32 devices in a mesh: replica: 2 (over x), fsdp: 16 (over z, y, core).
Axes of the slice: x: 2, y: 2, z: 4, core: 2. Of those that a mesh axis runs over, the one named last changes fastest.
Arguments:
- layer_in: bfloat16 [8192, 1152], P(('replica', 'fsdp')), may hold values from -6 to 6
- d_out: bfloat16 [8192, 1152], P(('replica', 'fsdp')), may hold values from -6 to 6
- segments: int32 [32, 256], P(('replica', 'fsdp')), may hold values from 0 to 255, as said below
- w_q: float32 [1152, 1024], P('fsdp'), may hold values from -0.1875 to 0.1875
- w_k: float32 [1152, 256], P('fsdp'), may hold values from -0.1875 to 0.1875
- w_v: float32 [1152, 256], P('fsdp'), may hold values from -0.1875 to 0.1875
- w_o: float32 [1024, 1152], P('fsdp'), may hold values from -0.1875 to 0.1875
- attn_pre: float32 [1152], P('fsdp'), may hold values from 0.5 to 1.5
- attn_post: float32 [1152], P('fsdp'), may hold values from 0.5 to 1.5
- q_gain: float32 [256], P('fsdp'), may hold values from 0.5 to 1.5
- k_gain: float32 [256], P('fsdp'), may hold values from 0.5 to 1.5
- w_gate: float32 [1152, 6912], P('fsdp'), may hold values from -0.1875 to 0.1875
- w_up: float32 [1152, 6912], P('fsdp'), may hold values from -0.1875 to 0.1875
- w_down: float32 [6912, 1152], P('fsdp'), may hold values from -0.078125 to 0.078125
- mlp_pre: float32 [1152], P('fsdp'), may hold values from 0.5 to 1.5
- mlp_post: float32 [1152], P('fsdp'), may hold values from 0.5 to 1.5
Outputs:
- layer_out: bfloat16 [8192, 1152], P(('replica', 'fsdp'))
- grad_x: bfloat16 [8192, 1152], P(('replica', 'fsdp'))
- grad_w_q: float32 [1152, 1024], P('fsdp')
- grad_w_k: float32 [1152, 256], P('fsdp')
- grad_w_v: float32 [1152, 256], P('fsdp')
- grad_w_o: float32 [1024, 1152], P('fsdp')
- grad_attn_pre: float32 [1152], P('fsdp')
- grad_attn_post: float32 [1152], P('fsdp')
- grad_q_gain: float32 [256], P('fsdp')
- grad_k_gain: float32 [256], P('fsdp')
- grad_w_gate: float32 [1152, 6912], P('fsdp')
- grad_w_up: float32 [1152, 6912], P('fsdp')
- grad_w_down: float32 [6912, 1152], P('fsdp')
- grad_mlp_pre: float32 [1152], P('fsdp')
- grad_mlp_post: float32 [1152], P('fsdp')
The draws below stay inside these ranges and needn't reach their ends.
Inputs may be any that keep to these rules, and one draw needn't show every extreme that they name: `segments`: within each sequence the numbers start at 0 and rise by 0 or 1 from one token to the next; tokens with one number form a document. The first sequence holds a single document; the last often holds a document for every token.
All inputs are finite; a program needn't handle non-finite values.
Results may differ from the reference program's by a relative error of at most 0.018.
The reference program's roundings to bfloat16 on the way count: a program that leaves them out, or rounds other values in their place, can miss the bound.
Values may be sent and summed in bfloat16 or wider, within the bound.
A program may use at most 256 MiB of HBM per device.

```python
import math
import jax
import jax.numpy as jnp
from jax import lax

D = 1152
FF = 6912
H = 4
HD = 256
SEQ = 256
SEQS = 32
TOKENS = 8192


def draw_segments(key, part):
    key = jax.random.fold_in(key, 7)
    kind_key, spread_key, flag_key = jax.random.split(key, 3)
    seq_kinds = jax.random.randint(kind_key, (SEQS, 1), 0, 8)
    powers = jax.random.randint(spread_key, (SEQS, 1), 3, 8)
    spacing = jnp.left_shift(jnp.ones_like(powers), powers)
    raw_draws = jax.random.randint(flag_key, (SEQS, SEQ), 0, 1 << 20)
    start_flags = jnp.remainder(raw_draws, spacing) == 0
    seq_rows = jnp.arange(SEQS, dtype=jnp.int32)[:, None]
    tok_columns = jnp.arange(SEQ, dtype=jnp.int32)[None, :]
    whole_doc = (seq_kinds == 0) | (seq_rows == 0)
    start_flags = (start_flags | (seq_rows == SEQS - 1)) & jnp.logical_not(whole_doc) & (tok_columns > 0)
    return jnp.cumsum(start_flags.astype(jnp.int32), axis=1).astype(jnp.int32)


def shard_levels(key, shape, shards, smallest, top_value):
    factor_of = 1.0
    for axis_at, parts in shards:
        heights = jax.random.uniform(jax.random.fold_in(jax.random.fold_in(key, 6), axis_at), (parts,), jnp.float32, smallest / len(shards), top_value / len(shards))
        factor_of = factor_of * jnp.repeat(jnp.exp(heights), shape[axis_at] // parts).reshape((-1,) + (1,) * (len(shape) - 1 - axis_at))
    return factor_of


def bell_draw(stream_key, shape, scale, reach, cuts=(), held_as=jnp.bfloat16):
    level = shard_levels(stream_key, shape, cuts, -0.22, 0.18) if cuts else 1.0
    values = jax.random.normal(stream_key, shape, jnp.float32) * scale * level
    return jnp.minimum(jnp.maximum(values, -reach), reach).astype(held_as)


def setup_inputs(seed: int = 0) -> dict:
    keys = jax.random.split(jax.random.key(seed), 17)
    layer_in = bell_draw(keys[0], (TOKENS, D), 1.0, 6.0, ((0, 32),))
    d_out = bell_draw(keys[1], (TOKENS, D), 1.0, 6.0, ((0, 32),))
    segments = draw_segments(jax.random.fold_in(keys[16], 71), 0)
    w_q = bell_draw(keys[3], (D, H * HD), D ** -0.5, 0.1875, ((0, 16),), jnp.float32)
    w_k = bell_draw(keys[4], (D, HD), D ** -0.5, 0.1875, ((0, 16),), jnp.float32)
    w_v = bell_draw(keys[5], (D, HD), D ** -0.5, 0.1875, ((0, 16),), jnp.float32)
    w_o = bell_draw(keys[6], (H * HD, D), (H * HD) ** -0.5, 0.1875, ((0, 16),), jnp.float32)
    attn_pre = jnp.clip(1.0 + 0.1 * jax.random.normal(keys[7], (D,), jnp.float32), 0.5, 1.5)
    attn_post = jnp.clip(1.0 + 0.1 * jax.random.normal(keys[8], (D,), jnp.float32), 0.5, 1.5)
    q_gain = jnp.clip(1.0 + 0.1 * jax.random.normal(keys[9], (HD,), jnp.float32), 0.5, 1.5)
    k_gain = jnp.clip(1.0 + 0.1 * jax.random.normal(keys[10], (HD,), jnp.float32), 0.5, 1.5)
    w_gate = bell_draw(keys[11], (D, FF), D ** -0.5, 0.1875, ((0, 16),), jnp.float32)
    w_up = bell_draw(keys[12], (D, FF), D ** -0.5, 0.1875, ((0, 16),), jnp.float32)
    w_down = bell_draw(keys[13], (FF, D), FF ** -0.5, 0.078125, ((0, 16),), jnp.float32)
    mlp_pre = jnp.clip(1.0 + 0.1 * jax.random.normal(keys[14], (D,), jnp.float32), 0.5, 1.5)
    mlp_post = jnp.clip(1.0 + 0.1 * jax.random.normal(keys[15], (D,), jnp.float32), 0.5, 1.5)
    return {"layer_in": layer_in, "d_out": d_out, "segments": segments, "w_q": w_q, "w_k": w_k, "w_v": w_v, "w_o": w_o, "attn_pre": attn_pre, "attn_post": attn_post, "q_gain": q_gain, "k_gain": k_gain, "w_gate": w_gate, "w_up": w_up, "w_down": w_down, "mlp_pre": mlp_pre, "mlp_post": mlp_post}


EPS = 1e-06
THETA = 1000000.0
SCALE = 0.0625
MASKED = -1e+30

@jax.custom_vjp
def low(v):
    return lax.optimization_barrier(v.astype(jnp.bfloat16)).astype(jnp.float32)

@jax.custom_vjp
def low_back(v):
    return v

def low_keep(v):
    return (low(v), None)

def low_pass(kept, grad):
    return (grad,)

def back_keep(v):
    return (v, None)

def back_low(kept, grad):
    return (low(grad),)
low.defvjp(low_keep, low_pass)
low_back.defvjp(back_keep, back_low)

def norm_rows(values, gain):
    return values * lax.rsqrt(lax.optimization_barrier(jnp.mean(values * values, axis=-1, keepdims=True)) + EPS) * gain

def positions_of(segments):
    length = segments.shape[-1]
    index = jnp.arange(length, dtype=jnp.int32)
    earlier = jnp.concatenate([segments[:, :1] - 1, segments[:, :-1]], axis=1)
    starts = jnp.where(segments != earlier, index[None, :], jnp.zeros_like(segments))
    return index[None, :] - lax.cummax(starts, axis=1)

def angle_tables(segments, head_size):
    half_size = head_size // 2
    rates = jnp.exp(jnp.arange(half_size, dtype=jnp.float32) * (-2.0 * math.log(THETA) / head_size))
    angles = positions_of(segments).astype(jnp.float32)[..., None] * rates
    return (jnp.cos(angles), jnp.sin(angles))

def rotate(values, cosine, sine):
    half_size = values.shape[-1] // 2
    first_half = values[..., :half_size]
    second_half = values[..., half_size:]
    return jnp.concatenate([first_half * cosine - second_half * sine, second_half * cosine + first_half * sine], axis=-1)

def matmul(left, right):
    return jnp.dot(left, right, precision=lax.Precision.HIGHEST)

def attend_one(pieces):
    q_low, k_low, v_low, seg_row = pieces
    length = seg_row.shape[0]
    scores = low_back(SCALE * jnp.einsum('qhd,kd->hqk', q_low, k_low, precision=lax.Precision.HIGHEST))
    index = jnp.arange(length, dtype=jnp.int32)
    allowed = (seg_row[:, None] == seg_row[None, :]) & (index[None, :] <= index[:, None])
    scores = jnp.where(allowed[None], scores, MASKED)
    top_val = lax.optimization_barrier(jnp.max(scores, axis=-1, keepdims=True))
    expo = jnp.exp(scores - top_val)
    probs = expo / lax.optimization_barrier(jnp.sum(expo, axis=-1, keepdims=True))
    return jnp.einsum('hqk,kd->qhd', low(probs), v_low, precision=lax.Precision.HIGHEST)

def forward(tok_in, segments, w_q, w_k, w_v, w_o, attn_pre, attn_post, q_gain, k_gain, w_gate, w_up, w_down, mlp_pre, mlp_post):
    seq_count, seq_len, width = tok_in.shape
    head_size = q_gain.shape[0]
    heads = w_q.shape[1] // head_size
    tok_flat = tok_in.reshape(seq_count * seq_len, width)
    a_low = low(norm_rows(tok_flat, low(attn_pre)))
    q_proj = low_back(matmul(a_low, low(w_q)))
    k_proj = low_back(matmul(a_low, low(w_k)))
    v_proj = low_back(matmul(a_low, low(w_v)))
    cosine, sine = angle_tables(segments, head_size)
    q_rot = rotate(norm_rows(q_proj.reshape(seq_count, seq_len, heads, head_size), low(q_gain)), cosine[:, :, None, :], sine[:, :, None, :])
    k_rot = rotate(norm_rows(k_proj.reshape(seq_count, seq_len, head_size), low(k_gain)), cosine, sine)
    q_low = low(q_rot)
    k_low = low(k_rot)
    v_low = low(v_proj.reshape(seq_count, seq_len, head_size))
    attn_mix = lax.map(jax.checkpoint(attend_one), (q_low, k_low, v_low, segments))
    o_low = low_back(low(attn_mix.reshape(seq_count * seq_len, heads * head_size)))
    attn_proj = low_back(matmul(o_low, low(w_o)))
    h_mid = tok_flat + norm_rows(attn_proj, low(attn_post))
    m_low = low(norm_rows(h_mid, low(mlp_pre)))
    gate_val = low_back(matmul(m_low, low(w_gate)))
    up_val = low_back(matmul(m_low, low(w_up)))
    hidden = low(jax.nn.gelu(gate_val, approximate=True) * up_val)
    down_val = low_back(matmul(hidden, low(w_down)))
    return (h_mid + norm_rows(down_val, low(mlp_post))).reshape(seq_count, seq_len, width)

def reference(layer_in, d_out, segments, w_q, w_k, w_v, w_o, attn_pre, attn_post, q_gain, k_gain, w_gate, w_up, w_down, mlp_pre, mlp_post):
    weights = (w_q, w_k, w_v, w_o, attn_pre, attn_post, q_gain, k_gain, w_gate, w_up, w_down, mlp_pre, mlp_post)
    seq_count, seq_len = segments.shape
    width = layer_in.shape[1]
    group = math.gcd(seq_count, max(1, 4096 // seq_len))
    rounds = seq_count // group
    inputs = layer_in.astype(jnp.float32).reshape(rounds, group, seq_len, width)
    cotangent = d_out.astype(jnp.float32).reshape(rounds, group, seq_len, width)
    seg_groups = segments.reshape(rounds, group, seq_len)

    def one_group(totals, pieces):
        tok_in, cot_in, seg_in = pieces

        def local_pass(tok_val, *params):
            return forward(tok_val, seg_in, *params)
        result, pullback = jax.vjp(local_pass, tok_in, *weights)
        grads = pullback(cot_in)
        totals = tuple((total + extra for total, extra in zip(totals, grads[1:])))
        return (totals, (result, grads[0]))
    starting = tuple((jnp.zeros(weight.shape, jnp.float32) for weight in weights))
    totals, (results, input_grads) = lax.scan(one_group, starting, (inputs, cotangent, seg_groups))
    layer_out = results.reshape(seq_count * seq_len, width).astype(jnp.bfloat16)
    grad_x = input_grads.reshape(seq_count * seq_len, width).astype(jnp.bfloat16)
    return (layer_out, grad_x, totals[0], totals[1], totals[2], totals[3], totals[4], totals[5], totals[6], totals[7], totals[8], totals[9], totals[10], totals[11], totals[12])
```

```python
from functools import partial
import math

import jax
import jax.numpy as jnp
from jax import lax
from jax.experimental import pallas as pl
from jax.experimental.pallas import tpu as pltpu
from jax.sharding import PartitionSpec as P

EPS = 1e-06
THETA = 1000000.0
SCALE = 0.0625
MASKED = -1e30


def norm_rows(values, gain):
    return values * lax.rsqrt(jnp.mean(values * values, axis=-1, keepdims=True) + EPS) * gain


def positions_of(segments):
    length = segments.shape[-1]
    index = jnp.arange(length, dtype=jnp.int32)
    earlier = jnp.concatenate([segments[:, :1] - 1, segments[:, :-1]], axis=1)
    starts = jnp.where(segments != earlier, index[None, :], jnp.zeros_like(segments))
    return index[None, :] - lax.cummax(starts, axis=1)


def angle_tables(segments, head_size):
    half_size = head_size // 2
    rates = jnp.exp(jnp.arange(half_size, dtype=jnp.float32) * (-2.0 * math.log(THETA) / head_size))
    angles = positions_of(segments).astype(jnp.float32)[..., None] * rates
    return (jnp.cos(angles), jnp.sin(angles))


def rotate(values, cosine, sine):
    half_size = values.shape[-1] // 2
    first_half = values[..., :half_size]
    second_half = values[..., half_size:]
    return jnp.concatenate(
        [first_half * cosine - second_half * sine, second_half * cosine + first_half * sine],
        axis=-1,
    )


def query_path(projected, gain, cosine, sine):
    shaped = projected.reshape(projected.shape[0], projected.shape[1], -1, gain.shape[0])
    return rotate(norm_rows(shaped, gain), cosine[:, :, None, :], sine[:, :, None, :])


def key_path(projected, gain, cosine, sine):
    return rotate(norm_rows(projected, gain), cosine, sine)


def gelu_product(gate_val, up_val):
    return jax.nn.gelu(gate_val, approximate=True) * up_val


def to_low(values):
    return values.astype(jnp.bfloat16)


def matmul(left, right):
    return jnp.dot(left, right, preferred_element_type=jnp.float32)


def matmul_left_t(left, right):
    return lax.dot_general(
        left, right, (((0,), (0,)), ((), ())), preferred_element_type=jnp.float32
    )


def matmul_right_t(left, right):
    return lax.dot_general(
        left, right, (((1,), (1,)), ((), ())), preferred_element_type=jnp.float32
    )


def attention_masks(segments):
    length = segments.shape[1]
    index = jnp.arange(length, dtype=jnp.int32)
    causal = index[None, :] <= index[:, None]
    return (segments[:, :, None] == segments[:, None, :]) & causal[None]


def scores_of(q_low, k_low, masks):
    scores = SCALE * jnp.einsum("nqhd,nkd->nhqk", q_low, k_low, preferred_element_type=jnp.float32)
    return jnp.where(masks[:, None], scores, MASKED)


def spread_gain(values):
    return jnp.broadcast_to(values[:, None], (values.shape[0], lax.axis_size("replica")))


def general_body(
    layer_in,
    d_out,
    segments,
    w_q,
    w_k,
    w_v,
    w_o,
    attn_pre,
    attn_post,
    q_gain,
    k_gain,
    w_gate,
    w_up,
    w_down,
    mlp_pre,
    mlp_post,
):
    attn_set = (
        lax.all_gather(to_low(w_q), "fsdp", axis=0, tiled=True),
        lax.all_gather(to_low(w_k), "fsdp", axis=0, tiled=True),
        lax.all_gather(to_low(w_v), "fsdp", axis=0, tiled=True),
        lax.all_gather(to_low(w_o), "fsdp", axis=0, tiled=True),
        lax.all_gather(to_low(attn_pre), "fsdp", axis=0, tiled=True),
        lax.all_gather(to_low(attn_post), "fsdp", axis=0, tiled=True),
        lax.all_gather(to_low(q_gain), "fsdp", axis=0, tiled=True),
        lax.all_gather(to_low(k_gain), "fsdp", axis=0, tiled=True),
    )
    q_full, k_full, v_full, o_full = (attn_set[0], attn_set[1], attn_set[2], attn_set[3])
    gain_apre = attn_set[4].astype(jnp.float32)
    gain_apost = attn_set[5].astype(jnp.float32)
    gain_q = attn_set[6].astype(jnp.float32)
    gain_k = attn_set[7].astype(jnp.float32)
    mlp_set = (
        lax.all_gather(to_low(w_gate), "fsdp", axis=0, tiled=True),
        lax.all_gather(to_low(w_up), "fsdp", axis=0, tiled=True),
        lax.all_gather(to_low(w_down), "fsdp", axis=0, tiled=True),
        lax.all_gather(to_low(mlp_pre), "fsdp", axis=0, tiled=True),
        lax.all_gather(to_low(mlp_post), "fsdp", axis=0, tiled=True),
    )
    gate_full, up_full, down_full = (mlp_set[0], mlp_set[1], mlp_set[2])
    gain_mpre = mlp_set[3].astype(jnp.float32)
    gain_mpost = mlp_set[4].astype(jnp.float32)
    seq_count, seq_len = segments.shape
    tok_flat = layer_in.astype(jnp.float32)
    cosine, sine = angle_tables(segments, gain_q.shape[0])
    masks = attention_masks(segments)
    normed_a, pull_a = jax.vjp(norm_rows, tok_flat, gain_apre)
    a_low = to_low(normed_a)
    q_proj = matmul(a_low, q_full).reshape(seq_count, seq_len, -1)
    k_proj = matmul(a_low, k_full).reshape(seq_count, seq_len, -1)
    v_proj = matmul(a_low, v_full)
    q_rot, pull_q = jax.vjp(partial(query_path, cosine=cosine, sine=sine), q_proj, gain_q)
    k_rot, pull_k = jax.vjp(partial(key_path, cosine=cosine, sine=sine), k_proj, gain_k)
    q_low = to_low(q_rot)
    k_low = to_low(k_rot)
    v_low = to_low(v_proj).reshape(seq_count, seq_len, -1)
    scores = scores_of(q_low, k_low, masks)
    top_val = jnp.max(scores, axis=-1, keepdims=True)
    log_total = top_val + jnp.log(jnp.sum(jnp.exp(scores - top_val), axis=-1, keepdims=True))
    p_low = to_low(jnp.exp(scores - log_total))
    attn_mix = jnp.einsum("nhqk,nkd->nqhd", p_low, v_low, preferred_element_type=jnp.float32)
    o_low = to_low(attn_mix.reshape(seq_count * seq_len, -1))
    attn_proj = matmul(o_low, o_full)
    post_attn, pull_pa = jax.vjp(norm_rows, attn_proj, gain_apost)
    h_mid = tok_flat + post_attn
    normed_m, pull_m = jax.vjp(norm_rows, h_mid, gain_mpre)
    m_low = to_low(normed_m)
    gate_val = matmul(m_low, gate_full)
    up_val = matmul(m_low, up_full)
    hidden, pull_h = jax.vjp(gelu_product, gate_val, up_val)
    h_low = to_low(hidden)
    down_val = matmul(h_low, down_full)
    post_mlp, pull_pm = jax.vjp(norm_rows, down_val, gain_mpost)
    layer_out = (h_mid + post_mlp).astype(jnp.bfloat16)
    gate_full, up_full, down_full = (
        lax.all_gather(to_low(w_gate), "fsdp", axis=0, tiled=True),
        lax.all_gather(to_low(w_up), "fsdp", axis=0, tiled=True),
        lax.all_gather(to_low(w_down), "fsdp", axis=0, tiled=True),
    )
    grad_top = d_out.astype(jnp.float32)
    d_down, grad_mpost = pull_pm(grad_top)
    d_down_low = to_low(d_down)
    grad_wdown = matmul_left_t(h_low, d_down_low)
    d_hidden = matmul_right_t(d_down_low, down_full)
    d_gate, d_up = pull_h(d_hidden)
    d_gate_low = to_low(d_gate)
    d_up_low = to_low(d_up)
    grad_wgate = matmul_left_t(m_low, d_gate_low)
    grad_wup = matmul_left_t(m_low, d_up_low)
    d_normed = matmul_right_t(d_gate_low, gate_full) + matmul_right_t(d_up_low, up_full)
    d_mid_norm, grad_mpre = pull_m(d_normed)
    d_mid = grad_top + d_mid_norm
    q_full, k_full, v_full, o_full = (
        lax.all_gather(to_low(w_q), "fsdp", axis=0, tiled=True),
        lax.all_gather(to_low(w_k), "fsdp", axis=0, tiled=True),
        lax.all_gather(to_low(w_v), "fsdp", axis=0, tiled=True),
        lax.all_gather(to_low(w_o), "fsdp", axis=0, tiled=True),
    )
    d_attn, grad_apost = pull_pa(d_mid)
    d_attn_low = to_low(d_attn)
    grad_wo = matmul_left_t(o_low, d_attn_low)
    d_mix_low = to_low(matmul_right_t(d_attn_low, o_full)).reshape(
        seq_count, seq_len, -1, k_low.shape[-1]
    )
    probs = jnp.exp(scores_of(q_low, k_low, masks) - log_total)
    d_probs = jnp.einsum("nqhd,nkd->nhqk", d_mix_low, v_low, preferred_element_type=jnp.float32)
    row_dot = jnp.sum(probs * d_probs, axis=-1, keepdims=True)
    d_scores_low = to_low(probs * (d_probs - row_dot))
    d_query = SCALE * jnp.einsum(
        "nhqk,nkd->nqhd", d_scores_low, k_low, preferred_element_type=jnp.float32
    )
    d_key = SCALE * jnp.einsum(
        "nhqk,nqhd->nkd", d_scores_low, q_low, preferred_element_type=jnp.float32
    )
    d_value = jnp.einsum("nhqk,nqhd->nkd", p_low, d_mix_low, preferred_element_type=jnp.float32)
    d_qproj, grad_qgain = pull_q(d_query)
    d_kproj, grad_kgain = pull_k(d_key)
    d_q_low = to_low(d_qproj.reshape(seq_count * seq_len, -1))
    d_k_low = to_low(d_kproj.reshape(seq_count * seq_len, -1))
    d_v_low = to_low(d_value.reshape(seq_count * seq_len, -1))
    grad_wq = matmul_left_t(a_low, d_q_low)
    grad_wk = matmul_left_t(a_low, d_k_low)
    grad_wv = matmul_left_t(a_low, d_v_low)
    d_normed_a = (
        matmul_right_t(d_q_low, q_full)
        + matmul_right_t(d_k_low, k_full)
        + matmul_right_t(d_v_low, v_full)
    )
    d_input_norm, grad_apre = pull_a(d_normed_a)
    grad_x = (d_mid + d_input_norm).astype(jnp.bfloat16)
    all_shards = (
        lax.psum_scatter(grad_wq, "fsdp", scatter_dimension=0, tiled=True),
        lax.psum_scatter(grad_wk, "fsdp", scatter_dimension=0, tiled=True),
        lax.psum_scatter(grad_wv, "fsdp", scatter_dimension=0, tiled=True),
        lax.psum_scatter(grad_wo, "fsdp", scatter_dimension=0, tiled=True),
        lax.psum_scatter(grad_apre, "fsdp", scatter_dimension=0, tiled=True),
        lax.psum_scatter(grad_apost, "fsdp", scatter_dimension=0, tiled=True),
        lax.psum_scatter(grad_qgain, "fsdp", scatter_dimension=0, tiled=True),
        lax.psum_scatter(grad_kgain, "fsdp", scatter_dimension=0, tiled=True),
        lax.psum_scatter(grad_wgate, "fsdp", scatter_dimension=0, tiled=True),
        lax.psum_scatter(grad_wup, "fsdp", scatter_dimension=0, tiled=True),
        lax.psum_scatter(grad_wdown, "fsdp", scatter_dimension=0, tiled=True),
        lax.psum_scatter(grad_mpre, "fsdp", scatter_dimension=0, tiled=True),
        lax.psum_scatter(grad_mpost, "fsdp", scatter_dimension=0, tiled=True),
    )
    all_cols = (
        lax.psum_scatter(
            all_shards[0].astype(jnp.bfloat16), "replica", scatter_dimension=1, tiled=True
        ).astype(jnp.float32),
        lax.psum_scatter(
            all_shards[1].astype(jnp.bfloat16), "replica", scatter_dimension=1, tiled=True
        ).astype(jnp.float32),
        lax.psum_scatter(
            all_shards[2].astype(jnp.bfloat16), "replica", scatter_dimension=1, tiled=True
        ).astype(jnp.float32),
        lax.psum_scatter(
            all_shards[3].astype(jnp.bfloat16), "replica", scatter_dimension=1, tiled=True
        ).astype(jnp.float32),
        lax.psum_scatter(
            all_shards[8].astype(jnp.bfloat16), "replica", scatter_dimension=1, tiled=True
        ).astype(jnp.float32),
        lax.psum_scatter(
            all_shards[9].astype(jnp.bfloat16), "replica", scatter_dimension=1, tiled=True
        ).astype(jnp.float32),
        lax.psum_scatter(
            all_shards[10].astype(jnp.bfloat16), "replica", scatter_dimension=1, tiled=True
        ).astype(jnp.float32),
        lax.psum_scatter(
            spread_gain(all_shards[4]).astype(jnp.bfloat16),
            "replica",
            scatter_dimension=1,
            tiled=True,
        ).astype(jnp.float32),
        lax.psum_scatter(
            spread_gain(all_shards[5]).astype(jnp.bfloat16),
            "replica",
            scatter_dimension=1,
            tiled=True,
        ).astype(jnp.float32),
        lax.psum_scatter(
            spread_gain(all_shards[6]).astype(jnp.bfloat16),
            "replica",
            scatter_dimension=1,
            tiled=True,
        ).astype(jnp.float32),
        lax.psum_scatter(
            spread_gain(all_shards[7]).astype(jnp.bfloat16),
            "replica",
            scatter_dimension=1,
            tiled=True,
        ).astype(jnp.float32),
        lax.psum_scatter(
            spread_gain(all_shards[11]).astype(jnp.bfloat16),
            "replica",
            scatter_dimension=1,
            tiled=True,
        ).astype(jnp.float32),
        lax.psum_scatter(
            spread_gain(all_shards[12]).astype(jnp.bfloat16),
            "replica",
            scatter_dimension=1,
            tiled=True,
        ).astype(jnp.float32),
    )
    all_mats = (
        lax.all_gather(all_cols[0].astype(jnp.bfloat16), "replica", axis=1, tiled=True).astype(
            jnp.float32
        ),
        lax.all_gather(all_cols[1].astype(jnp.bfloat16), "replica", axis=1, tiled=True).astype(
            jnp.float32
        ),
        lax.all_gather(all_cols[2].astype(jnp.bfloat16), "replica", axis=1, tiled=True).astype(
            jnp.float32
        ),
        lax.all_gather(all_cols[3].astype(jnp.bfloat16), "replica", axis=1, tiled=True).astype(
            jnp.float32
        ),
        lax.all_gather(all_cols[4].astype(jnp.bfloat16), "replica", axis=1, tiled=True).astype(
            jnp.float32
        ),
        lax.all_gather(all_cols[5].astype(jnp.bfloat16), "replica", axis=1, tiled=True).astype(
            jnp.float32
        ),
        lax.all_gather(all_cols[6].astype(jnp.bfloat16), "replica", axis=1, tiled=True).astype(
            jnp.float32
        ),
    )
    attn_sums = (
        all_mats[0],
        all_mats[1],
        all_mats[2],
        all_mats[3],
        all_cols[7][:, 0],
        all_cols[8][:, 0],
        all_cols[9][:, 0],
        all_cols[10][:, 0],
    )
    mlp_sums = (all_mats[4], all_mats[5], all_mats[6], all_cols[11][:, 0], all_cols[12][:, 0])
    return (
        layer_out,
        grad_x,
        attn_sums[0],
        attn_sums[1],
        attn_sums[2],
        attn_sums[3],
        attn_sums[4],
        attn_sums[5],
        attn_sums[6],
        attn_sums[7],
        mlp_sums[0],
        mlp_sums[1],
        mlp_sums[2],
        mlp_sums[3],
        mlp_sums[4],
    )


MESH = pl.DeviceIdType.MESH
VMEM_BYTES = 60 * 2**20
F32 = jnp.float32
BF16 = jnp.bfloat16


def fits_cubes(mesh):
    return dict(mesh.shape) == {"replica": 2, "fsdp": 16}


class Place:
    def __init__(self):
        shard = lax.axis_index("fsdp")
        self.x = lax.axis_index("replica")
        self.shard = shard
        self.c = lax.rem(shard, 2)
        self.y = lax.rem(lax.div(shard, 2), 2)
        self.z = lax.div(shard, 4)
        self.zl = lax.rem(self.z, 2)
        self.zh = lax.div(self.z, 2)

    def at(self, x=None, y=None, z=None, c=None):
        x = self.x if x is None else x
        y = self.y if y is None else y
        z = self.z if z is None else z
        c = self.c if c is None else c
        return (x, (z * 2 + y) * 2 + c)

    def z_xor(self, k):
        low = self.zl if k % 2 == 0 else 1 - self.zl
        high = self.zh if k // 2 == 0 else 1 - self.zh
        return 2 * high + low

    def cube(self, bits):
        return self.at(
            x=1 - self.x if bits & 4 else self.x,
            y=1 - self.y if bits & 2 else self.y,
            z=self.z_xor(1) if bits & 1 else self.z,
        )


class Wires:
    def __init__(self, send, recv):
        self.send, self.recv, self.used = send, recv, 0

    def remote(self, src, dst, device):
        i = self.used
        self.used += 1
        return pltpu.make_async_remote_copy(
            src_ref=src,
            dst_ref=dst,
            send_sem=self.send.at[i],
            recv_sem=self.recv.at[i],
            device_id=device,
            device_id_type=MESH,
        )

    def local(self, src, dst):
        i = self.used
        self.used += 1
        return pltpu.make_async_copy(src, dst, self.send.at[i])


def greet(devices):
    barrier = pltpu.get_barrier_semaphore()
    for device in devices:
        pl.semaphore_signal(barrier, inc=1, device_id=device, device_id_type=MESH)
    pl.semaphore_wait(barrier, len(devices))


def hbm():
    return pl.BlockSpec(memory_space=pl.ANY)


def vmem():
    return pl.BlockSpec(memory_space=pltpu.VMEM)


def sems(count):
    return [pltpu.SemaphoreType.DMA((count,)), pltpu.SemaphoreType.DMA((count,))]


def params(collective_id):
    return pltpu.CompilerParams(
        collective_id=collective_id, has_side_effects=True, vmem_limit_bytes=VMEM_BYTES
    )


def weights_kernel(qkv, out, gains, gu, dn, qkv_f, out_f, gains_f, gu_f, dn_f, send, recv):
    p = Place()
    w = Wires(send, recv)
    x, y, z, c = p.x, p.y, p.z, p.c
    sibling = p.at(c=1 - c)
    plane = [p.at(x=1 - x), p.at(y=1 - y), p.at(x=1 - x, y=1 - y)]
    lines = [p.at(y=yy, z=p.z_xor(k)) for yy in (y, 1 - y) for k in range(1, 4)]
    greet([sibling] + plane + lines)

    started, local = [], []

    def push(src, dst, device):
        copy = w.remote(src, dst, device)
        copy.start()
        started.append(copy)
        return copy

    def keep(src, dst):
        copy = w.local(src, dst)
        copy.start()
        local.append(copy)
        return copy

    line = []
    for k in range(1, 4):
        to = p.at(z=p.z_xor(k))
        line.append(
            (
                push(qkv.at[x], qkv_f.at[x, z, y, c], to),
                push(out.at[x], out_f.at[z, y, c, x], to),
                push(gains, gains_f.at[z, y, c], to),
            )
        )
    own = [
        keep(qkv, qkv_f.at[:, z, y, c]),
        keep(out, out_f.at[z, y, c]),
        keep(gains, gains_f.at[z, y, c]),
    ]
    across = [
        [
            push(qkv, qkv_f.at[:, z, y, c], plane[1]),
            push(out, out_f.at[z, y, c], plane[1]),
            push(gains, gains_f.at[z, y, c], plane[1]),
        ]
    ]
    wide = []
    for k in (3, 2, 1, 0):
        for other in (1, 0):
            if k == 0 and other == 0:
                continue
            yy = 1 - y if other else y
            zz = p.z_xor(k)
            part = (lax.rem(zz, 2) * 2 + x) * 2 + yy
            copy = push(gu.at[:, part], gu_f.at[:, z, y, c], p.at(y=yy, z=zz))
            wide.append((k, other, copy))
    part = (p.zl * 2 + x) * 2 + y
    own_wide = keep(gu.at[:, part], gu_f.at[:, z, y, c])
    source_z = 2 * p.zl + x
    down_sends = []
    down_first = w.used
    w.used += 3
    for half in range(2):
        zz = 2 * half + p.zh
        copy = pltpu.make_async_remote_copy(
            src_ref=dn,
            dst_ref=dn_f.at[c],
            send_sem=send.at[down_first + half],
            recv_sem=recv.at[down_first],
            device_id=p.at(z=zz),
            device_id_type=MESH,
        )
        need = (x == p.zl) & (zz != z)
        pl.when(need)(copy.start)
        down_sends.append((need, copy))
    own_down = pltpu.make_async_copy(dn, dn_f.at[c], send.at[down_first + 2])
    pl.when(source_z == z)(own_down.start)

    for copy in own:
        copy.wait()
    for k in range(1, 4):
        zz = p.z_xor(k)
        for copy in line[k - 1]:
            copy.wait_recv()
        batch = []
        for to in plane:
            batch.append(push(qkv_f.at[x, zz, y, c], qkv_f.at[x, zz, y, c], to))
            batch.append(push(out_f.at[zz, y, c, x], out_f.at[zz, y, c, x], to))
        batch.append(push(gains_f.at[zz, y, c], gains_f.at[zz, y, c], plane[1]))
        across.append(batch)
    pairs = []
    for k in range(4):
        zz = p.z_xor(k)
        for copy in across[k]:
            copy.wait_recv()
        pairs.append(push(qkv_f.at[:, zz, :, c], qkv_f.at[:, zz, :, c], sibling))
        pairs.append(push(out_f.at[zz, :, c], out_f.at[zz, :, c], sibling))
        pairs.append(push(gains_f.at[zz, :, c], gains_f.at[zz, :, c], sibling))
    own_wide.wait()
    pairs.append(push(gu_f.at[:, z, y, c], gu_f.at[:, z, y, c], sibling))
    for k, other, copy in reversed(wide):
        copy.wait_recv()
        zz = p.z_xor(k)
        yy = 1 - y if other else y
        pairs.append(push(gu_f.at[:, zz, yy, c], gu_f.at[:, zz, yy, c], sibling))
    pl.when(source_z == z)(own_down.wait)
    pl.when(source_z != z)(down_sends[0][1].wait_recv)
    pairs.append(push(dn_f.at[c], dn_f.at[c], sibling))
    for copy in pairs:
        copy.wait_recv()
    for need, copy in down_sends:
        pl.when(need)(copy.wait_send)
    for copy in started:
        copy.wait_send()


def gather_weights(qkv, out, gains, gu, dn):
    _, rows, columns = qkv.shape
    _, out_rows, out_columns = out.shape
    shapes = (
        jax.ShapeDtypeStruct((2, 4, 2, 2, rows, columns), BF16),
        jax.ShapeDtypeStruct((4, 2, 2, 2, out_rows, out_columns), BF16),
        jax.ShapeDtypeStruct((4, 2, 2) + gains.shape, F32),
        jax.ShapeDtypeStruct((2, 4, 2, 2) + gu.shape[2:], BF16),
        jax.ShapeDtypeStruct((2,) + dn.shape, BF16),
    )
    return pl.pallas_call(
        weights_kernel,
        out_shape=shapes,
        in_specs=[hbm()] * 5,
        out_specs=(hbm(),) * 5,
        scratch_shapes=sems(96),
        compiler_params=params(0),
        name="gather_weights",
    )(qkv, out, gains, gu, dn)


X, Y, Z = 4, 2, 1


def thirds(rows):
    first = -(-rows // 48) * 16
    return ((0, first), (first, first), (2 * first, rows - 2 * first))


def cube_gather_kernel(block, every, send, recv):
    p = Place()
    w = Wires(send, recv)
    near = {bit: p.cube(bit) for bit in (X, Y, Z)}
    greet([near[X], near[Y], near[Z]])
    started = []

    def push(src, dst, bit):
        copy = w.remote(src, dst, near[bit])
        copy.start()
        started.append(copy)
        return copy

    rows = block.shape[0]
    half = rows // 2
    own = w.local(block, every.at[0])
    own.start()
    arrivals = {}
    for h in range(2):
        at = pl.ds(h * half, half)
        for bit in (X, Y, Z):
            arrivals[bit, h] = push(block.at[at], every.at[bit, at], bit)
    for h in range(2):
        at = pl.ds(h * half, half)
        for link, relay in ((X, Y), (Y, Z), (Z, X)):
            arrivals[relay, h].wait_recv()
            arrivals[link | relay, h] = push(every.at[relay, at], every.at[link | relay, at], link)
    last = []
    for h in range(2):
        for (start, size), link, relay in zip(thirds(half), (X, Y, Z), (Y | Z, X | Z, X | Y)):
            at = pl.ds(h * half + start, size)
            arrivals[relay, h].wait_recv()
            last.append(push(every.at[relay, at], every.at[7, at], link))
    for copy in last:
        copy.wait_recv()
    own.wait()
    for copy in started:
        copy.wait_send()


def cube_gather(block):
    return pl.pallas_call(
        cube_gather_kernel,
        out_shape=jax.ShapeDtypeStruct((8,) + block.shape, block.dtype),
        in_specs=[hbm()],
        out_specs=hbm(),
        scratch_shapes=sems(24),
        compiler_params=params(1),
        name="cube_gather",
    )(block)


def cube_sum_kernel(parts, total, ready, third, second, first, send, recv):
    p = Place()
    w = Wires(send, recv)
    near = {bit: p.cube(bit) for bit in (X, Y, Z)}
    greet([near[X], near[Y], near[Z]])
    started = []

    def push(src, dst, bit):
        copy = w.remote(src, dst, near[bit])
        copy.start()
        started.append(copy)
        return copy

    rows = total.shape[0]
    half = rows // 2
    far, mid, end = {}, {}, {}
    for h in range(2):
        for (start, size), link in zip(thirds(half), (X, Y, Z)):
            at = pl.ds(h * half + start, size)
            far[link, h] = push(parts.at[7, at], third.at[at], link)
    for h in range(2):
        for i, (link, onward, place) in enumerate(((X, Y, Y | Z), (Y, Z, X | Z), (Z, X, X | Y))):
            start, size = thirds(half)[i]
            at = pl.ds(h * half + start, size)
            all_at = pl.ds(h * half, half)
            far[link, h].wait_recv()
            ready[i, all_at] = parts[place, all_at]
            ready[i, at] = (parts[place, at].astype(F32) + third[at].astype(F32)).astype(BF16)
            mid[onward, h] = push(ready.at[i, all_at], second.at[i, all_at], onward)
    for h in range(2):
        at = pl.ds(h * half, half)
        for i, (came, place) in enumerate(((Y, Z), (Z, X), (X, Y))):
            mid[came, h].wait_recv()
            ready[3 + i, at] = (parts[place, at].astype(F32) + second[i, at].astype(F32)).astype(BF16)
            end[place, h] = push(ready.at[3 + i, at], first.at[i, at], place)
    for h in range(2):
        at = pl.ds(h * half, half)
        value = parts[0, at].astype(F32)
        for i, place in enumerate((Z, X, Y)):
            end[place, h].wait_recv()
            value = value + first[i, at].astype(F32)
        total[at, :] = value
    for copy in started:
        copy.wait_send()


def cube_sum(parts):
    _, rows, columns = parts.shape
    return pl.pallas_call(
        cube_sum_kernel,
        out_shape=jax.ShapeDtypeStruct((rows, columns), F32),
        in_specs=[vmem()],
        out_specs=vmem(),
        scratch_shapes=[
            pltpu.VMEM((6, rows, columns), BF16),
            pltpu.VMEM((rows, columns), BF16),
            pltpu.VMEM((3, rows, columns), BF16),
            pltpu.VMEM((3, rows, columns), BF16),
        ]
        + sems(24),
        compiler_params=params(2),
        name="cube_sum",
    )(parts)


def add(left, right):
    return (left.astype(F32) + right.astype(F32)).astype(BF16)


def mlp_grads_kernel(gu, dn, gu_out, dn_out, sum1, got1, dsum1, dgot1, got2, dgot2, sum2, dsum2, send, recv):
    p = Place()
    w = Wires(send, recv)
    x, y, z, c, zl, zh = p.x, p.y, p.z, p.c, p.zl, p.zh
    sibling = p.at(c=1 - c)
    partner = p.at(z=p.z_xor(2))
    cube = [p.cube(bits) for bits in range(1, 8)]
    greet([sibling, partner] + cube)
    one = w.remote(gu.at[:, :, :, 1 - c], got1, sibling)
    one.start()
    two = w.remote(dn.at[1 - c], dgot1, sibling)
    two.start()
    one.wait_recv()
    for part in range(2):
        for zz in range(2):
            for yy in range(2):
                at = 2 * (1 - zh) + zz
                sum1[part, 0, zz, yy] = add(gu[part, at, yy, c], got1[part, at, yy])
    over = w.remote(sum1.at[:, 0], got2, partner)
    over.start()
    two.wait_recv()
    dsum1[...] = add(dn[c], dgot1[...])
    down_over = w.remote(dsum1, dgot2, partner)
    mine = zl == zh
    pl.when(zl != zh)(down_over.start)
    for part in range(2):
        for zz in range(2):
            for yy in range(2):
                at = 2 * zh + zz
                sum1[part, 1, zz, yy] = add(gu[part, at, yy, c], got1[part, at, yy])
    over.wait_recv()
    sum2[...] = add(sum1[:, 1], got2[...])
    part = (zl * 2 + x) * 2 + y
    spread = []
    for bits in range(1, 8):
        zz = 1 - zl if bits & 1 else zl
        yy = 1 - y if bits & 2 else y
        copy = w.remote(sum2.at[:, zz, yy], gu_out.at[:, part], cube[bits - 1])
        copy.start()
        spread.append(copy)
    own = w.local(sum2.at[:, zl, y], gu_out.at[:, part])
    own.start()

    away = [mine & ((x != xx) | (zh != x)) for xx in range(2)]
    arrival = pltpu.make_async_remote_copy(
        src_ref=dsum2,
        dst_ref=dn_out,
        send_sem=send.at[w.used],
        recv_sem=recv.at[w.used],
        device_id=sibling,
        device_id_type=MESH,
    )
    arrive_sem = recv.at[w.used]
    w.used += 1
    down = [
        pltpu.make_async_remote_copy(
            src_ref=dsum2,
            dst_ref=dn_out,
            send_sem=send.at[w.used + xx],
            recv_sem=arrive_sem,
            device_id=p.at(x=xx, z=2 * zh + x),
            device_id_type=MESH,
        )
        for xx in range(2)
    ]
    w.used += 2
    own_down = w.local(dsum2, dn_out)
    self_down = mine & (x == zl)

    @pl.when(mine)
    def _():
        down_over.wait_recv()
        dsum2[...] = add(dsum1[...], dgot2[...])

    for need, copy in zip(away, down):
        pl.when(need)(copy.start)
    pl.when(self_down)(own_down.start)
    pl.when(self_down)(own_down.wait)
    pl.when(jnp.logical_not(self_down))(arrival.wait_recv)
    for need, copy in zip(away, down):
        pl.when(need)(copy.wait_send)
    own.wait()
    for copy in spread:
        copy.wait_recv()
    for copy in [one, two, over] + spread:
        copy.wait_send()
    pl.when(zl != zh)(down_over.wait_send)


def mlp_grads(gu, dn):
    rows, columns = gu.shape[-2:]
    down = dn.shape[1:]
    return pl.pallas_call(
        mlp_grads_kernel,
        out_shape=(
            jax.ShapeDtypeStruct((2, 8, rows, columns), BF16),
            jax.ShapeDtypeStruct(down, BF16),
        ),
        in_specs=[vmem(), vmem()],
        out_specs=(vmem(), vmem()),
        scratch_shapes=[
            pltpu.VMEM((2, 2, 2, 2, rows, columns), BF16),
            pltpu.VMEM((2, 4, 2, rows, columns), BF16),
            pltpu.VMEM(down, BF16),
            pltpu.VMEM(down, BF16),
            pltpu.VMEM((2, 2, 2, rows, columns), BF16),
            pltpu.VMEM(down, BF16),
            pltpu.VMEM((2, 2, 2, rows, columns), BF16),
            pltpu.VMEM(down, BF16),
        ]
        + sems(24),
        compiler_params=params(3),
        name="mlp_grads",
    )(gu, dn)


def attn_grads_kernel(
    qkv, out, gains, qkv_r, out_r, gains_r,
    q1, o1, g1, qs, os, gs, q2, o2, g2, qt, ot, gt, q3, o3, g3, send, recv,
):
    p = Place()
    w = Wires(send, recv)
    x, y, z, c = p.x, p.y, p.z, p.c
    sibling = p.at(c=1 - c)
    line = [p.at(z=p.z_xor(k)) for k in range(1, 4)]
    plane = [p.at(x=1 - x), p.at(y=1 - y), p.at(x=1 - x, y=1 - y)]
    greet([sibling] + line + plane)
    started = []

    def push(src, dst, device):
        copy = w.remote(src, dst, device)
        copy.start()
        started.append(copy)
        return copy

    first = [
        push(qkv.at[:, :, :, 1 - c], q1, sibling),
        push(out.at[:, :, 1 - c], o1, sibling),
        push(gains.at[:, :, 1 - c], g1, sibling),
    ]
    for copy in first:
        copy.wait_recv()
    second = []
    for i in (2, 0, 1):
        xx = x if i == 1 else 1 - x
        yy = y if i == 0 else 1 - y
        qs[i] = add(qkv[xx, :, yy, c], q1[xx, :, yy])
        os[i] = add(out[:, yy, c, xx], o1[:, yy, xx])
        gs[i] = gains[:, yy, c] + g1[:, yy]
        second += [
            push(qs.at[i], q2.at[i], plane[i]),
            push(os.at[i], o2.at[i], plane[i]),
            push(gs.at[i], g2.at[i], plane[i]),
        ]
    for copy in second:
        copy.wait_recv()
    qt[...] = add(
        qkv[x, :, y, c].astype(F32) + q1[x, :, y].astype(F32) + q2[0].astype(F32),
        q2[1].astype(F32) + q2[2].astype(F32),
    )
    ot[...] = add(
        out[:, y, c, x].astype(F32) + o1[:, y, x].astype(F32) + o2[0].astype(F32),
        o2[1].astype(F32) + o2[2].astype(F32),
    )
    gt[...] = gains[:, y, c] + g1[:, y] + g2[0] + g2[1] + g2[2]
    third = []
    for k in range(1, 4):
        zz = p.z_xor(k)
        third += [
            push(qt.at[zz], q3.at[k - 1], line[k - 1]),
            push(ot.at[zz], o3.at[k - 1], line[k - 1]),
            push(gt.at[zz], g3.at[k - 1], line[k - 1]),
        ]
    for copy in third:
        copy.wait_recv()
    qkv_r[x] = add(qt[z].astype(F32) + q3[0].astype(F32), q3[1].astype(F32) + q3[2].astype(F32))
    out_r[x] = add(ot[z].astype(F32) + o3[0].astype(F32), o3[1].astype(F32) + o3[2].astype(F32))
    gains_r[...] = gt[z] + g3[0] + g3[1] + g3[2]
    last = [
        push(qkv_r.at[x], qkv_r.at[x], plane[0]),
        push(out_r.at[x], out_r.at[x], plane[0]),
    ]
    for copy in last:
        copy.wait_recv()
    for copy in started:
        copy.wait_send()


def attn_grads(qkv, out, gains):
    rows, columns = qkv.shape[-2:]
    out_rows, out_columns = out.shape[-2:]
    gain = gains.shape[-2:]
    q, o = (rows, columns), (out_rows, out_columns)
    scratch = []
    for lead_q, lead_o, lead_g in (
        ((2, 4, 2), (4, 2, 2), (4, 2)),
        ((3, 4), (3, 4), (3, 4)),
        ((3, 4), (3, 4), (3, 4)),
        ((4,), (4,), (4,)),
        ((3,), (3,), (3,)),
    ):
        scratch += [
            pltpu.VMEM(lead_q + q, BF16),
            pltpu.VMEM(lead_o + o, BF16),
            pltpu.VMEM(lead_g + gain, F32),
        ]
    return pl.pallas_call(
        attn_grads_kernel,
        out_shape=(
            jax.ShapeDtypeStruct((2,) + q, BF16),
            jax.ShapeDtypeStruct((2,) + o, BF16),
            jax.ShapeDtypeStruct(gain, F32),
        ),
        in_specs=[vmem()] * 3,
        out_specs=(vmem(),) * 3,
        scratch_shapes=scratch + sems(32),
        compiler_params=params(4),
        name="attn_grads",
    )(qkv, out, gains)


def pack_gains(vectors):
    lead = vectors[0].shape[:-1]
    rows = [jnp.pad(v, [(0, 0)] * len(lead) + [(0, 128 - v.shape[-1])]) for v in vectors]
    rows += [jnp.zeros(lead + (128,), F32)] * (8 - len(rows))
    return jnp.stack(rows, axis=-2)


def unpack_gains(packed, sizes):
    lead = packed.shape[:-2]
    return [packed[..., i, :size] for i, size in enumerate(sizes)]


def cube_body(
    layer_in, d_out, segments, w_q, w_k, w_v, w_o, attn_pre, attn_post, q_gain, k_gain,
    w_gate, w_up, w_down, mlp_pre, mlp_post,
):
    width = layer_in.shape[1]
    head = q_gain.shape[0] * 16
    mix = w_o.shape[0] * 16
    hidden_units = w_gate.shape[1]
    rows = w_q.shape[0]
    qkv = to_low(jnp.concatenate([w_q, w_k, w_v], axis=1))
    half = qkv.shape[1] // 2
    qkv = jnp.stack([qkv[:, :half], qkv[:, half:]])
    out = to_low(w_o).reshape(2, -1, width)
    gain_list = [attn_pre, attn_post, mlp_pre, mlp_post, q_gain, k_gain]
    gain_sizes = [v.shape[0] for v in gain_list]
    gains = pack_gains([to_low(v).astype(F32) for v in gain_list])
    gu = jnp.stack(
        [to_low(w).reshape(rows, 8, -1).transpose(1, 0, 2) for w in (w_gate, w_up)]
    )
    qkv_f, out_f, gains_f, gu_f, dn_f = gather_weights(qkv, out, gains, gu, to_low(w_down))
    qkv_f = qkv_f.reshape(2, width, half)
    o_full = out_f.reshape(mix, width)
    gain_apre, gain_apost, gain_mpre, gain_mpost, gain_q, gain_k = [
        v.reshape(-1) for v in unpack_gains(gains_f, gain_sizes)
    ]
    gate_w, up_w = gu_f[0].reshape(width, -1), gu_f[1].reshape(width, -1)
    down_w = dn_f.reshape(-1, width)

    seq_count, seq_len = segments.shape
    tok_flat = layer_in.astype(F32)
    cosine, sine = angle_tables(segments, head)
    masks = attention_masks(segments)
    normed_a, pull_a = jax.vjp(norm_rows, tok_flat, gain_apre)
    a_low = to_low(normed_a)
    qkv_proj = jnp.concatenate([matmul(a_low, qkv_f[0]), matmul(a_low, qkv_f[1])], axis=1)
    q_proj = qkv_proj[:, :mix].reshape(seq_count, seq_len, -1)
    k_proj = qkv_proj[:, mix : mix + head].reshape(seq_count, seq_len, -1)
    v_proj = qkv_proj[:, mix + head :]
    q_rot, pull_q = jax.vjp(partial(query_path, cosine=cosine, sine=sine), q_proj, gain_q)
    k_rot, pull_k = jax.vjp(partial(key_path, cosine=cosine, sine=sine), k_proj, gain_k)
    q_low = to_low(q_rot)
    k_low = to_low(k_rot)
    v_low = to_low(v_proj).reshape(seq_count, seq_len, -1)
    scores = scores_of(q_low, k_low, masks)
    top_val = jnp.max(scores, axis=-1, keepdims=True)
    expo = jnp.exp(scores - top_val)
    probs = expo / jnp.sum(expo, axis=-1, keepdims=True)
    p_low = to_low(probs)
    attn_mix = jnp.einsum("nhqk,nkd->nqhd", p_low, v_low, preferred_element_type=F32)
    o_low = to_low(attn_mix.reshape(seq_count * seq_len, -1))
    attn_proj = matmul(o_low, o_full)
    post_attn, pull_pa = jax.vjp(norm_rows, attn_proj, gain_apost)
    h_mid = tok_flat + post_attn
    normed_m, pull_m = jax.vjp(norm_rows, h_mid, gain_mpre)
    m_all = cube_gather(to_low(normed_m)).reshape(-1, width)
    gate_val = matmul(m_all, gate_w)
    up_val = matmul(m_all, up_w)
    hidden, pull_h = jax.vjp(gelu_product, gate_val, up_val)
    h_low = to_low(hidden)
    down_val = cube_sum(to_low(matmul(h_low, down_w)).reshape(8, -1, width))
    post_mlp, pull_pm = jax.vjp(norm_rows, down_val, gain_mpost)
    layer_out = (h_mid + post_mlp).astype(BF16)

    grad_top = d_out.astype(F32)
    d_down, grad_mpost = pull_pm(grad_top)
    dd_all = cube_gather(to_low(d_down)).reshape(-1, width)
    grad_wdown = matmul_left_t(h_low, dd_all)
    d_hidden = matmul_right_t(dd_all, down_w)
    d_gate, d_up = pull_h(d_hidden)
    d_gate_low = to_low(d_gate)
    d_up_low = to_low(d_up)
    grad_gu = jnp.stack(
        [to_low(matmul_left_t(m_all, d_gate_low)), to_low(matmul_left_t(m_all, d_up_low))]
    )
    d_normed = cube_sum(
        to_low(matmul_right_t(d_gate_low, gate_w) + matmul_right_t(d_up_low, up_w)).reshape(
            8, -1, width
        )
    )
    gu_r, dn_r = mlp_grads(
        grad_gu.reshape(2, 4, 2, 2, rows, -1), to_low(grad_wdown).reshape(2, -1, width)
    )
    d_mid_norm, grad_mpre = pull_m(d_normed)
    d_mid = grad_top + d_mid_norm
    d_attn, grad_apost = pull_pa(d_mid)
    d_attn_low = to_low(d_attn)
    grad_wo = matmul_left_t(o_low, d_attn_low)
    d_mix_low = to_low(matmul_right_t(d_attn_low, o_full)).reshape(seq_count, seq_len, -1, head)
    d_probs = jnp.einsum("nqhd,nkd->nhqk", d_mix_low, v_low, preferred_element_type=F32)
    row_dot = jnp.sum(probs * d_probs, axis=-1, keepdims=True)
    d_scores_low = to_low(probs * (d_probs - row_dot))
    d_query = SCALE * jnp.einsum("nhqk,nkd->nqhd", d_scores_low, k_low, preferred_element_type=F32)
    d_key = SCALE * jnp.einsum("nhqk,nqhd->nkd", d_scores_low, q_low, preferred_element_type=F32)
    d_value = jnp.einsum("nhqk,nqhd->nkd", p_low, d_mix_low, preferred_element_type=F32)
    d_qproj, grad_qgain = pull_q(d_query)
    d_kproj, grad_kgain = pull_k(d_key)
    d_qkv = to_low(
        jnp.concatenate(
            [v.reshape(seq_count * seq_len, -1) for v in (d_qproj, d_kproj, d_value)], axis=1
        )
    )
    grad_qkv = jnp.stack(
        [to_low(matmul_left_t(a_low, d_qkv[:, :half])), to_low(matmul_left_t(a_low, d_qkv[:, half:]))]
    )
    d_normed_a = matmul_right_t(d_qkv[:, :half], qkv_f[0]) + matmul_right_t(d_qkv[:, half:], qkv_f[1])
    d_input_norm, grad_apre = pull_a(d_normed_a)
    grad_x = (d_mid + d_input_norm).astype(BF16)
    grad_gains = [grad_apre, grad_apost, grad_mpre, grad_mpost, grad_qgain, grad_kgain]
    packed = pack_gains([v.reshape(4, 2, 2, -1) for v in grad_gains])
    qkv_r, out_r, gains_r = attn_grads(
        grad_qkv.reshape(2, 4, 2, 2, rows, half),
        to_low(grad_wo).reshape(4, 2, 2, 2, -1, width),
        packed,
    )
    qkv_r = jnp.concatenate([qkv_r[0], qkv_r[1]], axis=1).astype(F32)
    g_apre, g_apost, g_mpre, g_mpost, g_q, g_k = unpack_gains(gains_r, gain_sizes)
    gu_r = gu_r.transpose(0, 2, 1, 3).reshape(2, rows, hidden_units).astype(F32)
    return (
        layer_out,
        grad_x,
        qkv_r[:, :mix],
        qkv_r[:, mix : mix + head],
        qkv_r[:, mix + head :],
        out_r.reshape(-1, width).astype(F32),
        g_apre,
        g_apost,
        g_q,
        g_k,
        gu_r[0],
        gu_r[1],
        dn_r.astype(F32),
        g_mpre,
        g_mpost,
    )


def solution(mesh):
    in_specs = (
        P(("replica", "fsdp"), None),
        P(("replica", "fsdp"), None),
        P(("replica", "fsdp"), None),
        P("fsdp", None),
        P("fsdp", None),
        P("fsdp", None),
        P("fsdp", None),
        P("fsdp"),
        P("fsdp"),
        P("fsdp"),
        P("fsdp"),
        P("fsdp", None),
        P("fsdp", None),
        P("fsdp", None),
        P("fsdp"),
        P("fsdp"),
    )
    out_specs = (
        P(("replica", "fsdp"), None),
        P(("replica", "fsdp"), None),
        P("fsdp", None),
        P("fsdp", None),
        P("fsdp", None),
        P("fsdp", None),
        P("fsdp"),
        P("fsdp"),
        P("fsdp"),
        P("fsdp"),
        P("fsdp", None),
        P("fsdp", None),
        P("fsdp", None),
        P("fsdp"),
        P("fsdp"),
    )
    body = cube_body if fits_cubes(mesh) else general_body
    return jax.shard_map(body, mesh=mesh, in_specs=in_specs, out_specs=out_specs, check_vma=False)
```

```python
from functools import partial
import math

import jax
import jax.numpy as jnp
from jax import lax
from jax.experimental import pallas as pl
from jax.experimental.pallas import tpu as pltpu
from jax.sharding import PartitionSpec as P

EPS = 1e-06
THETA = 1000000.0
SCALE = 0.0625
MASKED = -1e30


def norm_rows(values, gain):
    return values * lax.rsqrt(jnp.mean(values * values, axis=-1, keepdims=True) + EPS) * gain


def positions_of(segments):
    length = segments.shape[-1]
    index = jnp.arange(length, dtype=jnp.int32)
    earlier = jnp.concatenate([segments[:, :1] - 1, segments[:, :-1]], axis=1)
    starts = jnp.where(segments != earlier, index[None, :], jnp.zeros_like(segments))
    return index[None, :] - lax.cummax(starts, axis=1)


def angle_tables(segments, head_size):
    half_size = head_size // 2
    rates = jnp.exp(jnp.arange(half_size, dtype=jnp.float32) * (-2.0 * math.log(THETA) / head_size))
    angles = positions_of(segments).astype(jnp.float32)[..., None] * rates
    return (jnp.cos(angles), jnp.sin(angles))


def rotate(values, cosine, sine):
    half_size = values.shape[-1] // 2
    first_half = values[..., :half_size]
    second_half = values[..., half_size:]
    return jnp.concatenate(
        [first_half * cosine - second_half * sine, second_half * cosine + first_half * sine],
        axis=-1,
    )


def query_path(projected, gain, cosine, sine):
    shaped = projected.reshape(projected.shape[0], projected.shape[1], -1, gain.shape[0])
    return rotate(norm_rows(shaped, gain), cosine[:, :, None, :], sine[:, :, None, :])


def key_path(projected, gain, cosine, sine):
    return rotate(norm_rows(projected, gain), cosine, sine)


def gelu_product(gate_val, up_val):
    return jax.nn.gelu(gate_val, approximate=True) * up_val


def to_low(values):
    return values.astype(jnp.bfloat16)


def matmul(left, right):
    return jnp.dot(left, right, preferred_element_type=jnp.float32)


def matmul_left_t(left, right):
    return lax.dot_general(
        left, right, (((0,), (0,)), ((), ())), preferred_element_type=jnp.float32
    )


def matmul_right_t(left, right):
    return lax.dot_general(
        left, right, (((1,), (1,)), ((), ())), preferred_element_type=jnp.float32
    )


def attention_masks(segments):
    length = segments.shape[1]
    index = jnp.arange(length, dtype=jnp.int32)
    causal = index[None, :] <= index[:, None]
    return (segments[:, :, None] == segments[:, None, :]) & causal[None]


def scores_of(q_low, k_low, masks):
    scores = SCALE * jnp.einsum("nqhd,nkd->nhqk", q_low, k_low, preferred_element_type=jnp.float32)
    return jnp.where(masks[:, None], scores, MASKED)


def spread_gain(values):
    return jnp.broadcast_to(values[:, None], (values.shape[0], lax.axis_size("replica")))


def general_body(
    layer_in,
    d_out,
    segments,
    w_q,
    w_k,
    w_v,
    w_o,
    attn_pre,
    attn_post,
    q_gain,
    k_gain,
    w_gate,
    w_up,
    w_down,
    mlp_pre,
    mlp_post,
):
    attn_set = (
        lax.all_gather(to_low(w_q), "fsdp", axis=0, tiled=True),
        lax.all_gather(to_low(w_k), "fsdp", axis=0, tiled=True),
        lax.all_gather(to_low(w_v), "fsdp", axis=0, tiled=True),
        lax.all_gather(to_low(w_o), "fsdp", axis=0, tiled=True),
        lax.all_gather(to_low(attn_pre), "fsdp", axis=0, tiled=True),
        lax.all_gather(to_low(attn_post), "fsdp", axis=0, tiled=True),
        lax.all_gather(to_low(q_gain), "fsdp", axis=0, tiled=True),
        lax.all_gather(to_low(k_gain), "fsdp", axis=0, tiled=True),
    )
    q_full, k_full, v_full, o_full = (attn_set[0], attn_set[1], attn_set[2], attn_set[3])
    gain_apre = attn_set[4].astype(jnp.float32)
    gain_apost = attn_set[5].astype(jnp.float32)
    gain_q = attn_set[6].astype(jnp.float32)
    gain_k = attn_set[7].astype(jnp.float32)
    mlp_set = (
        lax.all_gather(to_low(w_gate), "fsdp", axis=0, tiled=True),
        lax.all_gather(to_low(w_up), "fsdp", axis=0, tiled=True),
        lax.all_gather(to_low(w_down), "fsdp", axis=0, tiled=True),
        lax.all_gather(to_low(mlp_pre), "fsdp", axis=0, tiled=True),
        lax.all_gather(to_low(mlp_post), "fsdp", axis=0, tiled=True),
    )
    gate_full, up_full, down_full = (mlp_set[0], mlp_set[1], mlp_set[2])
    gain_mpre = mlp_set[3].astype(jnp.float32)
    gain_mpost = mlp_set[4].astype(jnp.float32)
    seq_count, seq_len = segments.shape
    tok_flat = layer_in.astype(jnp.float32)
    cosine, sine = angle_tables(segments, gain_q.shape[0])
    masks = attention_masks(segments)
    normed_a, pull_a = jax.vjp(norm_rows, tok_flat, gain_apre)
    a_low = to_low(normed_a)
    q_proj = matmul(a_low, q_full).reshape(seq_count, seq_len, -1)
    k_proj = matmul(a_low, k_full).reshape(seq_count, seq_len, -1)
    v_proj = matmul(a_low, v_full)
    q_rot, pull_q = jax.vjp(partial(query_path, cosine=cosine, sine=sine), q_proj, gain_q)
    k_rot, pull_k = jax.vjp(partial(key_path, cosine=cosine, sine=sine), k_proj, gain_k)
    q_low = to_low(q_rot)
    k_low = to_low(k_rot)
    v_low = to_low(v_proj).reshape(seq_count, seq_len, -1)
    scores = scores_of(q_low, k_low, masks)
    top_val = jnp.max(scores, axis=-1, keepdims=True)
    log_total = top_val + jnp.log(jnp.sum(jnp.exp(scores - top_val), axis=-1, keepdims=True))
    p_low = to_low(jnp.exp(scores - log_total))
    attn_mix = jnp.einsum("nhqk,nkd->nqhd", p_low, v_low, preferred_element_type=jnp.float32)
    o_low = to_low(attn_mix.reshape(seq_count * seq_len, -1))
    attn_proj = matmul(o_low, o_full)
    post_attn, pull_pa = jax.vjp(norm_rows, attn_proj, gain_apost)
    h_mid = tok_flat + post_attn
    normed_m, pull_m = jax.vjp(norm_rows, h_mid, gain_mpre)
    m_low = to_low(normed_m)
    gate_val = matmul(m_low, gate_full)
    up_val = matmul(m_low, up_full)
    hidden, pull_h = jax.vjp(gelu_product, gate_val, up_val)
    h_low = to_low(hidden)
    down_val = matmul(h_low, down_full)
    post_mlp, pull_pm = jax.vjp(norm_rows, down_val, gain_mpost)
    layer_out = (h_mid + post_mlp).astype(jnp.bfloat16)
    gate_full, up_full, down_full = (
        lax.all_gather(to_low(w_gate), "fsdp", axis=0, tiled=True),
        lax.all_gather(to_low(w_up), "fsdp", axis=0, tiled=True),
        lax.all_gather(to_low(w_down), "fsdp", axis=0, tiled=True),
    )
    grad_top = d_out.astype(jnp.float32)
    d_down, grad_mpost = pull_pm(grad_top)
    d_down_low = to_low(d_down)
    grad_wdown = matmul_left_t(h_low, d_down_low)
    d_hidden = matmul_right_t(d_down_low, down_full)
    d_gate, d_up = pull_h(d_hidden)
    d_gate_low = to_low(d_gate)
    d_up_low = to_low(d_up)
    grad_wgate = matmul_left_t(m_low, d_gate_low)
    grad_wup = matmul_left_t(m_low, d_up_low)
    d_normed = matmul_right_t(d_gate_low, gate_full) + matmul_right_t(d_up_low, up_full)
    d_mid_norm, grad_mpre = pull_m(d_normed)
    d_mid = grad_top + d_mid_norm
    q_full, k_full, v_full, o_full = (
        lax.all_gather(to_low(w_q), "fsdp", axis=0, tiled=True),
        lax.all_gather(to_low(w_k), "fsdp", axis=0, tiled=True),
        lax.all_gather(to_low(w_v), "fsdp", axis=0, tiled=True),
        lax.all_gather(to_low(w_o), "fsdp", axis=0, tiled=True),
    )
    d_attn, grad_apost = pull_pa(d_mid)
    d_attn_low = to_low(d_attn)
    grad_wo = matmul_left_t(o_low, d_attn_low)
    d_mix_low = to_low(matmul_right_t(d_attn_low, o_full)).reshape(
        seq_count, seq_len, -1, k_low.shape[-1]
    )
    probs = jnp.exp(scores_of(q_low, k_low, masks) - log_total)
    d_probs = jnp.einsum("nqhd,nkd->nhqk", d_mix_low, v_low, preferred_element_type=jnp.float32)
    row_dot = jnp.sum(probs * d_probs, axis=-1, keepdims=True)
    d_scores_low = to_low(probs * (d_probs - row_dot))
    d_query = SCALE * jnp.einsum(
        "nhqk,nkd->nqhd", d_scores_low, k_low, preferred_element_type=jnp.float32
    )
    d_key = SCALE * jnp.einsum(
        "nhqk,nqhd->nkd", d_scores_low, q_low, preferred_element_type=jnp.float32
    )
    d_value = jnp.einsum("nhqk,nqhd->nkd", p_low, d_mix_low, preferred_element_type=jnp.float32)
    d_qproj, grad_qgain = pull_q(d_query)
    d_kproj, grad_kgain = pull_k(d_key)
    d_q_low = to_low(d_qproj.reshape(seq_count * seq_len, -1))
    d_k_low = to_low(d_kproj.reshape(seq_count * seq_len, -1))
    d_v_low = to_low(d_value.reshape(seq_count * seq_len, -1))
    grad_wq = matmul_left_t(a_low, d_q_low)
    grad_wk = matmul_left_t(a_low, d_k_low)
    grad_wv = matmul_left_t(a_low, d_v_low)
    d_normed_a = (
        matmul_right_t(d_q_low, q_full)
        + matmul_right_t(d_k_low, k_full)
        + matmul_right_t(d_v_low, v_full)
    )
    d_input_norm, grad_apre = pull_a(d_normed_a)
    grad_x = (d_mid + d_input_norm).astype(jnp.bfloat16)
    all_shards = (
        lax.psum_scatter(grad_wq, "fsdp", scatter_dimension=0, tiled=True),
        lax.psum_scatter(grad_wk, "fsdp", scatter_dimension=0, tiled=True),
        lax.psum_scatter(grad_wv, "fsdp", scatter_dimension=0, tiled=True),
        lax.psum_scatter(grad_wo, "fsdp", scatter_dimension=0, tiled=True),
        lax.psum_scatter(grad_apre, "fsdp", scatter_dimension=0, tiled=True),
        lax.psum_scatter(grad_apost, "fsdp", scatter_dimension=0, tiled=True),
        lax.psum_scatter(grad_qgain, "fsdp", scatter_dimension=0, tiled=True),
        lax.psum_scatter(grad_kgain, "fsdp", scatter_dimension=0, tiled=True),
        lax.psum_scatter(grad_wgate, "fsdp", scatter_dimension=0, tiled=True),
        lax.psum_scatter(grad_wup, "fsdp", scatter_dimension=0, tiled=True),
        lax.psum_scatter(grad_wdown, "fsdp", scatter_dimension=0, tiled=True),
        lax.psum_scatter(grad_mpre, "fsdp", scatter_dimension=0, tiled=True),
        lax.psum_scatter(grad_mpost, "fsdp", scatter_dimension=0, tiled=True),
    )
    all_cols = (
        lax.psum_scatter(
            all_shards[0].astype(jnp.bfloat16), "replica", scatter_dimension=1, tiled=True
        ).astype(jnp.float32),
        lax.psum_scatter(
            all_shards[1].astype(jnp.bfloat16), "replica", scatter_dimension=1, tiled=True
        ).astype(jnp.float32),
        lax.psum_scatter(
            all_shards[2].astype(jnp.bfloat16), "replica", scatter_dimension=1, tiled=True
        ).astype(jnp.float32),
        lax.psum_scatter(
            all_shards[3].astype(jnp.bfloat16), "replica", scatter_dimension=1, tiled=True
        ).astype(jnp.float32),
        lax.psum_scatter(
            all_shards[8].astype(jnp.bfloat16), "replica", scatter_dimension=1, tiled=True
        ).astype(jnp.float32),
        lax.psum_scatter(
            all_shards[9].astype(jnp.bfloat16), "replica", scatter_dimension=1, tiled=True
        ).astype(jnp.float32),
        lax.psum_scatter(
            all_shards[10].astype(jnp.bfloat16), "replica", scatter_dimension=1, tiled=True
        ).astype(jnp.float32),
        lax.psum_scatter(
            spread_gain(all_shards[4]).astype(jnp.bfloat16),
            "replica",
            scatter_dimension=1,
            tiled=True,
        ).astype(jnp.float32),
        lax.psum_scatter(
            spread_gain(all_shards[5]).astype(jnp.bfloat16),
            "replica",
            scatter_dimension=1,
            tiled=True,
        ).astype(jnp.float32),
        lax.psum_scatter(
            spread_gain(all_shards[6]).astype(jnp.bfloat16),
            "replica",
            scatter_dimension=1,
            tiled=True,
        ).astype(jnp.float32),
        lax.psum_scatter(
            spread_gain(all_shards[7]).astype(jnp.bfloat16),
            "replica",
            scatter_dimension=1,
            tiled=True,
        ).astype(jnp.float32),
        lax.psum_scatter(
            spread_gain(all_shards[11]).astype(jnp.bfloat16),
            "replica",
            scatter_dimension=1,
            tiled=True,
        ).astype(jnp.float32),
        lax.psum_scatter(
            spread_gain(all_shards[12]).astype(jnp.bfloat16),
            "replica",
            scatter_dimension=1,
            tiled=True,
        ).astype(jnp.float32),
    )
    all_mats = (
        lax.all_gather(all_cols[0].astype(jnp.bfloat16), "replica", axis=1, tiled=True).astype(
            jnp.float32
        ),
        lax.all_gather(all_cols[1].astype(jnp.bfloat16), "replica", axis=1, tiled=True).astype(
            jnp.float32
        ),
        lax.all_gather(all_cols[2].astype(jnp.bfloat16), "replica", axis=1, tiled=True).astype(
            jnp.float32
        ),
        lax.all_gather(all_cols[3].astype(jnp.bfloat16), "replica", axis=1, tiled=True).astype(
            jnp.float32
        ),
        lax.all_gather(all_cols[4].astype(jnp.bfloat16), "replica", axis=1, tiled=True).astype(
            jnp.float32
        ),
        lax.all_gather(all_cols[5].astype(jnp.bfloat16), "replica", axis=1, tiled=True).astype(
            jnp.float32
        ),
        lax.all_gather(all_cols[6].astype(jnp.bfloat16), "replica", axis=1, tiled=True).astype(
            jnp.float32
        ),
    )
    attn_sums = (
        all_mats[0],
        all_mats[1],
        all_mats[2],
        all_mats[3],
        all_cols[7][:, 0],
        all_cols[8][:, 0],
        all_cols[9][:, 0],
        all_cols[10][:, 0],
    )
    mlp_sums = (all_mats[4], all_mats[5], all_mats[6], all_cols[11][:, 0], all_cols[12][:, 0])
    return (
        layer_out,
        grad_x,
        attn_sums[0],
        attn_sums[1],
        attn_sums[2],
        attn_sums[3],
        attn_sums[4],
        attn_sums[5],
        attn_sums[6],
        attn_sums[7],
        mlp_sums[0],
        mlp_sums[1],
        mlp_sums[2],
        mlp_sums[3],
        mlp_sums[4],
    )


MESH = pl.DeviceIdType.MESH
VMEM_BYTES = 60 * 2**20
F32 = jnp.float32
BF16 = jnp.bfloat16


def fits_cubes(mesh):
    return dict(mesh.shape) == {"replica": 2, "fsdp": 16}


class Place:
    def __init__(self):
        shard = lax.axis_index("fsdp")
        self.x = lax.axis_index("replica")
        self.shard = shard
        self.c = lax.rem(shard, 2)
        self.y = lax.rem(lax.div(shard, 2), 2)
        self.z = lax.div(shard, 4)
        self.zl = lax.rem(self.z, 2)
        self.zh = lax.div(self.z, 2)

    def at(self, x=None, y=None, z=None, c=None):
        x = self.x if x is None else x
        y = self.y if y is None else y
        z = self.z if z is None else z
        c = self.c if c is None else c
        return (x, (z * 2 + y) * 2 + c)

    def z_xor(self, k):
        low = self.zl if k % 2 == 0 else 1 - self.zl
        high = self.zh if k // 2 == 0 else 1 - self.zh
        return 2 * high + low

    def cube(self, bits):
        return self.at(
            x=1 - self.x if bits & 4 else self.x,
            y=1 - self.y if bits & 2 else self.y,
            z=self.z_xor(1) if bits & 1 else self.z,
        )


class Wires:
    def __init__(self, send, recv):
        self.send, self.recv, self.used = send, recv, 0

    def remote(self, src, dst, device):
        i = self.used
        self.used += 1
        return pltpu.make_async_remote_copy(
            src_ref=src,
            dst_ref=dst,
            send_sem=self.send.at[i],
            recv_sem=self.recv.at[i],
            device_id=device,
            device_id_type=MESH,
        )

    def local(self, src, dst):
        i = self.used
        self.used += 1
        return pltpu.make_async_copy(src, dst, self.send.at[i])


def greet(devices):
    barrier = pltpu.get_barrier_semaphore()
    for device in devices:
        pl.semaphore_signal(barrier, inc=1, device_id=device, device_id_type=MESH)
    pl.semaphore_wait(barrier, len(devices))


def hbm():
    return pl.BlockSpec(memory_space=pl.ANY)


def vmem():
    return pl.BlockSpec(memory_space=pltpu.VMEM)


def sems(count):
    return [pltpu.SemaphoreType.DMA((count,)), pltpu.SemaphoreType.DMA((count,))]


def params(collective_id):
    return pltpu.CompilerParams(
        collective_id=collective_id, has_side_effects=True, vmem_limit_bytes=VMEM_BYTES
    )


X, Y, Z = 4, 2, 1


def thirds(rows):
    first = -(-rows // 48) * 16
    return ((0, first), (first, first), (2 * first, rows - 2 * first))


def cube_gather_kernel(block, every, send, recv, local):
    p = Place()
    w = Wires(send, recv)
    greet([p.cube(X), p.cube(Y), p.cube(Z)])
    started = []
    for _ in cube_gather_steps(p, w, block, every, local.at[0], started):
        pass
    for copy in started:
        copy.wait_send()


def cube_gather(block):
    return pl.pallas_call(
        cube_gather_kernel,
        out_shape=jax.ShapeDtypeStruct((8,) + block.shape, block.dtype),
        in_specs=[hbm()],
        out_specs=hbm(),
        scratch_shapes=sems(24) + [pltpu.SemaphoreType.DMA((1,))],
        compiler_params=params(1),
        name="cube_gather",
    )(block)


def cube_sum_kernel(parts, total, ready, third, second, first, send, recv):
    p = Place()
    w = Wires(send, recv)
    near = {bit: p.cube(bit) for bit in (X, Y, Z)}
    greet([near[X], near[Y], near[Z]])
    started = []

    def push(src, dst, bit):
        copy = w.remote(src, dst, near[bit])
        copy.start()
        started.append(copy)
        return copy

    rows = total.shape[0]
    half = rows // 2
    far, mid, end = {}, {}, {}
    for h in range(2):
        for (start, size), link in zip(thirds(half), (X, Y, Z)):
            at = pl.ds(h * half + start, size)
            far[link, h] = push(parts.at[7, at], third.at[at], link)
    for h in range(2):
        for i, (link, onward, place) in enumerate(((X, Y, Y | Z), (Y, Z, X | Z), (Z, X, X | Y))):
            start, size = thirds(half)[i]
            at = pl.ds(h * half + start, size)
            all_at = pl.ds(h * half, half)
            far[link, h].wait_recv()
            ready[i, all_at] = parts[place, all_at]
            ready[i, at] = (parts[place, at].astype(F32) + third[at].astype(F32)).astype(BF16)
            mid[onward, h] = push(ready.at[i, all_at], second.at[i, all_at], onward)
    for h in range(2):
        at = pl.ds(h * half, half)
        for i, (came, place) in enumerate(((Y, Z), (Z, X), (X, Y))):
            mid[came, h].wait_recv()
            ready[3 + i, at] = (parts[place, at].astype(F32) + second[i, at].astype(F32)).astype(BF16)
            end[place, h] = push(ready.at[3 + i, at], first.at[i, at], place)
    for h in range(2):
        at = pl.ds(h * half, half)
        value = parts[0, at].astype(F32)
        for i, place in enumerate((Z, X, Y)):
            end[place, h].wait_recv()
            value = value + first[i, at].astype(F32)
        total[at, :] = value
    for copy in started:
        copy.wait_send()


def cube_sum(parts):
    _, rows, columns = parts.shape
    return pl.pallas_call(
        cube_sum_kernel,
        out_shape=jax.ShapeDtypeStruct((rows, columns), F32),
        in_specs=[vmem()],
        out_specs=vmem(),
        scratch_shapes=[
            pltpu.VMEM((6, rows, columns), BF16),
            pltpu.VMEM((rows, columns), BF16),
            pltpu.VMEM((3, rows, columns), BF16),
            pltpu.VMEM((3, rows, columns), BF16),
        ]
        + sems(24),
        compiler_params=params(2),
        name="cube_sum",
    )(parts)


def add(left, right):
    return (left.astype(F32) + right.astype(F32)).astype(BF16)


def norm_scale(values):
    return lax.rsqrt(jnp.mean(values * values, axis=-1, keepdims=True) + EPS)


def norm_pull(values, scale, gain, cotangent):
    weighted = gain * cotangent
    lean = jnp.mean(values * weighted, axis=-1, keepdims=True)
    d_values = scale * weighted - values * (scale * scale * scale * lean)
    return d_values, jnp.sum(values * scale * cotangent, axis=0, keepdims=True)


def spread_matrix(width, per):
    column = lax.broadcasted_iota(jnp.int32, (128, width), 1)
    row = lax.broadcasted_iota(jnp.int32, (128, width), 0)
    place = (lax.rem(column, per) == row).astype(F32)
    column = lax.broadcasted_iota(jnp.int32, (16, width), 1)
    row = lax.broadcasted_iota(jnp.int32, (16, width), 0)
    owner = (lax.div(column, per) == row).astype(F32)
    return place, owner


def join_gains(packed, which, width, per):
    place, owner = spread_matrix(width, per)
    shards = packed[:, which, :].astype(BF16)
    wide = jnp.dot(shards, place.astype(BF16), preferred_element_type=F32)
    return jnp.sum(wide * owner, axis=0, keepdims=True)


def turn(values, cosine, sine):
    half = values.shape[-1] // 2
    u, w = values[:, :half], values[:, half:]
    return jnp.concatenate([u * cosine - w * sine, w * cosine + u * sine], axis=1)


def turn_back(values, cosine, sine):
    half = values.shape[-1] // 2
    u, w = values[:, :half], values[:, half:]
    return jnp.concatenate([u * cosine + w * sine, w * cosine - u * sine], axis=1)


def front_kernel(
    tok, seg_row, seg_col, w_q, w_k, w_v, w_o, gains, w_gate, w_up, w_down,
    qkv_w, out_w, gu_w, dn_w, every, gains_full, a_low, qk_proj, q_low, k_low, v_low,
    probs, o_low, attn_proj, h_mid, tables,
    qkv_s, qkv_own, qkv_send, qkv_got, out_own, gains_own, gains_s, wide_in, wide_send, wide_got,
    wide_out, down_in, down_out, m_low, out_s, send, recv, local,
):
    p = Place()
    w = Wires(send, recv)
    x, y, z, c, zl, zh = p.x, p.y, p.z, p.c, p.zl, p.zh
    sibling = p.at(c=1 - c)
    plane = [p.at(x=1 - x), p.at(y=1 - y)]
    lines = [p.at(y=yy, z=p.z_xor(k)) for yy in (y, 1 - y) for k in range(1, 4)]
    started = []

    def push(src, dst, device):
        copy = w.remote(src, dst, device)
        copy.start()
        started.append(copy)
        return copy

    loads = [
        pltpu.make_async_copy(w_gate, wide_in.at[0], local.at[0]),
        pltpu.make_async_copy(w_up, wide_in.at[1], local.at[1]),
        pltpu.make_async_copy(w_down, down_in, local.at[2]),
    ]
    for copy in loads:
        copy.start()

    rows = w_q.shape[0]
    columns = qkv_s.shape[1] // 4
    out_rows = w_o.shape[0] // 2
    mine = 2 * x + c
    theirs = 2 * x + 1 - c

    all_own = jnp.concatenate([w_q[...], w_k[...], w_v[...]], axis=1)
    for quarter in range(4):
        qkv_own[quarter] = all_own[:, quarter * columns : (quarter + 1) * columns]
    qkv_send[...] = qkv_own[theirs].astype(BF16)
    out_own[...] = w_o[...].astype(BF16)
    gains_own[...] = gains[...].astype(BF16).astype(F32)
    greet([sibling] + plane + lines)

    def qkv_at(zz, yy, quarter):
        return qkv_s.at[
            pl.ds(pl.multiple_of((2 * zz + yy) * 2 * rows, 16), 2 * rows),
            pl.ds(pl.multiple_of(quarter * columns, 128), columns),
        ]

    def out_at(zz, yy, quarter):
        return out_s.at[
            pl.ds(pl.multiple_of((2 * zz + yy) * 4 * out_rows + quarter * out_rows, 16), out_rows)
        ]

    swap = push(qkv_send, qkv_got, sibling)

    def gains_at(zz, yy, cc):
        return gains_s.at[(2 * zz + yy) * 2 + cc]

    gains_s[(2 * z + y) * 2 + c] = gains_own[...]
    gain_line = [push(gains_own, gains_at(z, y, c), p.at(z=p.z_xor(k))) for k in range(1, 4)]
    gain_side = [push(gains_own, gains_at(z, y, c), plane[1])]
    holds = x == c
    out_theirs = out_own.at[pl.ds(pl.multiple_of((1 - c) * out_rows, 16), out_rows)]
    out_swap = w.remote(out_theirs, out_at(z, y, theirs), sibling)
    pl.when(holds)(out_swap.start)

    @pl.when(holds)
    def _():
        out_s[pl.ds(pl.multiple_of((2 * z + y) * 4 * out_rows + mine * out_rows, 16), out_rows)] = (
            out_own[pl.ds(pl.multiple_of(c * out_rows, 16), out_rows)]
        )

    swap.wait_recv()
    top, low = qkv_own[mine], qkv_got[...].astype(F32)
    first = jnp.where(c == 0, top, low)
    second = jnp.where(c == 0, low, top)
    base = pl.multiple_of((2 * z + y) * 2 * rows, 16)
    joined = jnp.concatenate([first, second], axis=0).astype(BF16)
    qkv_s[pl.ds(base, 2 * rows), pl.ds(pl.multiple_of(mine * columns, 128), columns)] = joined

    pl.when(jnp.logical_not(holds))(out_swap.wait_recv)
    pl.when(holds)(out_swap.wait_send)

    line = [None]
    for k in range(1, 4):
        to = p.at(z=p.z_xor(k))
        line.append(
            (
                push(qkv_at(z, y, mine), qkv_at(z, y, mine), to),
                push(out_at(z, y, mine), out_at(z, y, mine), to),
            )
        )
    side_x, side_y, corner = {}, {}, {}

    def spread(k):
        zz = p.z_xor(k)
        if k:
            for copy in line[k]:
                copy.wait_recv()
        qkv, out = qkv_at(zz, y, mine), out_at(zz, y, mine)
        side_x[k] = (push(qkv, qkv, plane[0]), push(out, out, plane[0]))
        side_y[k] = (push(qkv, qkv, plane[1]), push(out, out, plane[1]))

    def relay(k):
        zz = p.z_xor(k)
        if k % 2:
            for copy in side_y[k]:
                copy.wait_recv()
            qkv, out, to = qkv_at(zz, 1 - y, mine), out_at(zz, 1 - y, mine), plane[0]
        else:
            for copy in side_x[k]:
                copy.wait_recv()
            other = 2 * (1 - x) + c
            qkv, out, to = qkv_at(zz, y, other), out_at(zz, y, other), plane[1]
        corner[k] = (push(qkv, qkv, to), push(out, out, to))

    pairs = []

    def share(k):
        zz = p.z_xor(k)
        for copy in (side_x[k] if k % 2 else side_y[k]) + corner[k]:
            copy.wait_recv()
        for xx in range(2):
            at = qkv_s.at[
                pl.ds(pl.multiple_of(2 * zz * 2 * rows, 16), 4 * rows),
                pl.ds(pl.multiple_of((2 * xx + c) * columns, 128), columns),
            ]
            pairs.append(push(at, at, sibling))
            for yy in range(2):
                at = out_at(zz, yy, 2 * xx + c)
                pairs.append(push(at, at, sibling))

    spread(0)
    loads[0].wait()
    loads[1].wait()
    part_columns = wide_out.shape[-1]
    for xx in range(2):

        @pl.when(x == xx)
        def _():
            for zz in range(2):
                for yy in range(2):
                    part = (2 * zz + xx) * 2 + yy
                    at = slice(part * part_columns, (part + 1) * part_columns)
                    for matrix in range(2):

                        @pl.when(c == 1 - matrix)
                        def _():
                            wide_send[2 * zz + yy] = wide_in[matrix, :, at].astype(BF16)

    wide_swap = push(wide_send, wide_got, sibling)
    loads[2].wait()
    down_out[...] = down_in[...].astype(BF16)
    relay(0)
    spread(1)
    wide_swap.wait_recv()
    for xx in range(2):

        @pl.when(x == xx)
        def _():
            for zz in range(2):
                for yy in range(2):
                    part = (2 * zz + xx) * 2 + yy
                    at = slice(part * part_columns, (part + 1) * part_columns)
                    got = wide_got[2 * zz + yy].astype(F32)
                    for matrix in range(2):

                        @pl.when(c == matrix)
                        def _():
                            own = wide_in[matrix, :, at]
                            both = [own, got] if matrix == 0 else [got, own]
                            wide_out[2 * zz + yy] = jnp.concatenate(both, axis=0).astype(BF16)

    def gu_at(zz, yy):
        return gu_w.at[c, pl.ds(pl.multiple_of((2 * zz + yy) * 2 * rows, 16), 2 * rows)]

    wide = []
    for k in (3, 2, 1, 0):
        for other in (1, 0):
            yy = 1 - y if other else y
            zz = p.z_xor(k)
            src = wide_out.at[2 * lax.rem(zz, 2) + yy]
            if k == 0 and other == 0:
                own_wide = pltpu.make_async_copy(src, gu_at(z, y), local.at[0])
                own_wide.start()
            else:
                wide.append((zz, yy, push(src, gu_at(z, y), p.at(y=yy, z=zz))))
    down_rows = down_out.shape[0]
    down_at = dn_w.at[pl.ds(pl.multiple_of(c * down_rows, 16), down_rows)]
    source_z = 2 * zl + x
    first_down = w.used
    w.used += 2
    down_sends = []
    for half in range(2):
        zz = 2 * half + zh
        copy = pltpu.make_async_remote_copy(
            src_ref=down_out,
            dst_ref=down_at,
            send_sem=send.at[first_down + half],
            recv_sem=recv.at[first_down],
            device_id=p.at(z=zz),
            device_id_type=MESH,
        )
        need = (x == zl) & (zz != z)
        pl.when(need)(copy.start)
        down_sends.append((need, copy))
    own_down = pltpu.make_async_copy(down_out, down_at, local.at[1])
    pl.when(source_z == z)(own_down.start)

    tok_f = tok[...].astype(F32)
    length, width = tok_f.shape
    head = k_low.shape[1]
    spread(2)
    relay(1)
    for copy in gain_line:
        copy.wait_recv()
    for k in range(1, 4):
        zz = p.z_xor(k)
        gain_side.append(push(gains_at(zz, y, c), gains_at(zz, y, c), plane[1]))
    row_seg = seg_row[...].astype(F32)
    col_seg = seg_col[...].astype(F32)
    earlier = jnp.sum((row_seg < col_seg).astype(F32), axis=1, keepdims=True)
    index = lax.broadcasted_iota(jnp.int32, (length, 1), 0).astype(F32)
    rate_at = lax.broadcasted_iota(jnp.int32, (1, head // 2), 1).astype(F32)
    rates = jnp.exp(rate_at * (-2.0 * math.log(THETA) / head))
    angles = (index - earlier) * rates
    tables[0] = jnp.cos(angles)
    tables[1] = jnp.sin(angles)
    spread(3)
    relay(2)
    share(0)
    relay(3)
    for copy in gain_side:
        copy.wait_recv()
    gain_pair = []
    for zz in range(4):
        for yy in range(2):
            gain_pair.append(push(gains_at(zz, yy, c), gains_at(zz, yy, c), sibling))
    share(1)
    for copy in gain_pair:
        copy.wait_recv()
    packed = gains_s[...]
    for i, (size, per) in enumerate(
        ((width, rows),) * 4 + ((head, head // 16),) * 2
    ):
        gains_full[i, :, :size] = join_gains(packed, i, size, per)
    a_low[...] = (tok_f * norm_scale(tok_f) * gains_full[0]).astype(BF16)
    share(2)
    share(3)
    for copy in pairs:
        copy.wait_recv()
    saves = [
        pltpu.make_async_copy(qkv_s, qkv_w, local.at[2]),
        pltpu.make_async_copy(out_s, out_w, local.at[3]),
    ]
    for copy in saves:
        copy.start()

    cosine, sine = tables[0], tables[1]
    heads = q_low.shape[1] // head
    for i in range(heads + 2):
        at = slice(i * head, (i + 1) * head)
        value = jnp.dot(a_low[...], qkv_s[:, at], preferred_element_type=F32)
        if i < heads:
            qk_proj[:, at] = value
            q_low[:, at] = turn(
                value * norm_scale(value) * gains_full[4, :, :head], cosine, sine
            ).astype(BF16)
        elif i == heads:
            qk_proj[:, at] = value
            k_low[...] = turn(
                value * norm_scale(value) * gains_full[5, :, :head], cosine, sine
            ).astype(BF16)
        else:
            v_low[...] = value.astype(BF16)
    i_at = lax.broadcasted_iota(jnp.int32, (length, length), 0)
    j_at = lax.broadcasted_iota(jnp.int32, (length, length), 1)
    allowed = (row_seg == col_seg) & (j_at <= i_at)
    for i in range(heads):
        at = slice(i * head, (i + 1) * head)
        scores = SCALE * lax.dot_general(
            q_low[:, at], k_low[...], (((1,), (1,)), ((), ())), preferred_element_type=F32
        )
        scores = jnp.where(allowed, scores, MASKED)
        expo = jnp.exp(scores - jnp.max(scores, axis=1, keepdims=True))
        prob = expo / jnp.sum(expo, axis=1, keepdims=True)
        probs[i] = prob
        o_low[:, at] = jnp.dot(
            prob.astype(BF16), v_low[...], preferred_element_type=F32
        ).astype(BF16)
    third = width // 3
    for i in range(3):
        at = slice(i * third, (i + 1) * third)
        attn_proj[:, at] = jnp.dot(o_low[...], out_s[:, at], preferred_element_type=F32)
    proj = attn_proj[...]
    mid = tok_f + proj * norm_scale(proj) * gains_full[1]
    h_mid[...] = mid
    m_low[...] = (mid * norm_scale(mid) * gains_full[2]).astype(BF16)

    finish = cube_gather_steps(p, w, m_low, every, local.at[4], started)
    next(finish)
    own_wide.wait()
    shared = [push(gu_at(z, y), gu_at(z, y), sibling)]
    next(finish)
    for zz, yy, copy in reversed(wide):
        copy.wait_recv()
        shared.append(push(gu_at(zz, yy), gu_at(zz, yy), sibling))
    next(finish)
    pl.when(source_z == z)(own_down.wait)
    pl.when(source_z != z)(down_sends[0][1].wait_recv)
    shared.append(push(down_at, down_at, sibling))
    for _ in finish:
        pass
    for copy in shared:
        copy.wait_recv()
    for copy in saves:
        copy.wait()
    for need, copy in down_sends:
        pl.when(need)(copy.wait_send)
    for copy in started:
        copy.wait_send()


def cube_gather_steps(p, w, block, every, own_sem, started):
    near = {bit: p.cube(bit) for bit in (X, Y, Z)}

    def push(src, dst, bit):
        copy = w.remote(src, dst, near[bit])
        copy.start()
        started.append(copy)
        return copy

    rows = block.shape[0]
    half = rows // 2
    own = pltpu.make_async_copy(block, every.at[0], own_sem)
    own.start()
    arrivals = {}
    for h in range(2):
        at = pl.ds(h * half, half)
        for bit in (X, Y, Z):
            arrivals[bit, h] = push(block.at[at], every.at[bit, at], bit)
    yield
    for h in range(2):
        at = pl.ds(h * half, half)
        for link, relay in ((X, Y), (Y, Z), (Z, X)):
            arrivals[relay, h].wait_recv()
            arrivals[link | relay, h] = push(every.at[relay, at], every.at[link | relay, at], link)
    yield
    last = []
    for h in range(2):
        for (start, size), link, relay in zip(thirds(half), (X, Y, Z), (Y | Z, X | Z, X | Y)):
            at = pl.ds(h * half + start, size)
            arrivals[relay, h].wait_recv()
            last.append(push(every.at[relay, at], every.at[7, at], link))
    yield
    for copy in last:
        copy.wait_recv()
    own.wait()


def front(tok, segments, w_q, w_k, w_v, w_o, gains, w_gate, w_up, w_down, head):
    length, width = tok.shape
    rows, mix = w_q.shape
    hidden = w_gate.shape[1]
    part = hidden // 8
    down_rows = w_down.shape[0]
    total = mix + 2 * head
    heads = mix // head
    columns = total // 4
    struct = jax.ShapeDtypeStruct
    shapes = (
        struct((16 * rows, total), BF16),
        struct((16 * w_o.shape[0], width), BF16),
        struct((2, 16 * rows, part), BF16),
        struct((2 * down_rows, width), BF16),
        struct((8, length, width), BF16),
        struct((8, 1, width), F32),
        struct((length, width), BF16),
        struct((length, mix + head), F32),
        struct((length, mix), BF16),
        struct((length, head), BF16),
        struct((length, head), BF16),
        struct((heads, length, length), F32),
        struct((length, mix), BF16),
        struct((length, width), F32),
        struct((length, width), F32),
        struct((2, length, head // 2), F32),
    )
    scratch = [
        pltpu.VMEM((16 * rows, total), BF16),
        pltpu.VMEM((4, rows, columns), F32),
        pltpu.VMEM((rows, columns), BF16),
        pltpu.VMEM((rows, columns), BF16),
        pltpu.VMEM(w_o.shape, BF16),
        pltpu.VMEM(gains.shape, F32),
        pltpu.VMEM((16,) + gains.shape, F32),
        pltpu.VMEM((2, rows, hidden), F32),
        pltpu.VMEM((4, rows, part), BF16),
        pltpu.VMEM((4, rows, part), BF16),
        pltpu.VMEM((4, 2 * rows, part), BF16),
        pltpu.VMEM((down_rows, width), F32),
        pltpu.VMEM((down_rows, width), BF16),
        pltpu.VMEM((length, width), BF16),
        pltpu.VMEM((16 * w_o.shape[0], width), BF16),
    ]
    return pl.pallas_call(
        front_kernel,
        out_shape=shapes,
        in_specs=[vmem()] * 8 + [hbm()] * 3,
        out_specs=(hbm(),) * 5 + (vmem(),) * 11,
        scratch_shapes=scratch + sems(128) + [pltpu.SemaphoreType.DMA((5,))],
        compiler_params=params(0),
        name="front",
    )(
        tok, segments, segments.reshape(-1, 1), w_q, w_k, w_v, w_o, gains, w_gate, w_up, w_down
    )


def dot_rows(left, right):
    return lax.dot_general(left, right, (((0,), (0,)), ((), ())), preferred_element_type=F32)


def dot_columns(left, right):
    return lax.dot_general(left, right, (((1,), (1,)), ((), ())), preferred_element_type=F32)


def back_kernel(
    tok, d_out, d_normed, gains_full, a_low, qk_proj, q_low, k_low, v_low, probs, o_low, attn_proj,
    h_mid, tables, g_mpost, qkv_hbm, out_hbm, gu, dn,
    grad_x, grad_qkv, grad_out, grad_gains, grad_gu, grad_dn,
    qkv_w, out_w, wide_in, wide_got, wide_sum, wide_far, down_in, down_got, down_sum, down_far,
    down_end, d_input, wide_end, wide_swap, wide_back, d_attn, d_mid, d_mix, d_qkv, dqkv, dout, q1, o1, q2, o2, q3, o3, qe, oe,
    gain_acc, gain_got, send, recv, local,
):
    p = Place()
    w = Wires(send, recv)
    x, y, z, c, zl, zh = p.x, p.y, p.z, p.c, p.zl, p.zh
    sibling = p.at(c=1 - c)
    plane = [p.at(x=1 - x), p.at(y=1 - y), p.at(x=1 - x, y=1 - y)]
    line = [p.at(z=p.z_xor(k)) for k in range(1, 4)]
    cube = [p.cube(bits) for bits in range(1, 8)]
    started = []

    def push(src, dst, device):
        copy = w.remote(src, dst, device)
        copy.start()
        started.append(copy)
        return copy

    def rows_of(ref, start, size):
        return ref.at[pl.ds(pl.multiple_of(start, 16), size)]

    loads = [
        pltpu.make_async_copy(gu.at[c], wide_in, local.at[0]),
        pltpu.make_async_copy(dn, down_in, local.at[1]),
        pltpu.make_async_copy(out_hbm, out_w, local.at[2]),
        pltpu.make_async_copy(qkv_hbm, qkv_w, local.at[3]),
    ]
    for copy in loads:
        copy.start()
    greet([sibling] + plane + line + [p.cube(5), p.cube(7), p.cube(3)])

    width = tok.shape[1]
    chip_rows = wide_in.shape[0] // 8
    down_rows = down_sum.shape[0]
    half_rows = 4 * chip_rows
    far_half = half_rows * (1 - zh)
    near_half = half_rows * zh
    wide_one = [
        push(rows_of(gu.at[1 - c], start, half_rows), rows_of(wide_got, start, half_rows), sibling)
        for start in (far_half, near_half)
    ]
    down_one = push(rows_of(dn, down_rows * (1 - c), down_rows), down_got, sibling)

    mid = h_mid[...]
    d_value, g_mpre = norm_pull(mid, norm_scale(mid), gains_full[2], d_normed[...])
    d_mid[...] = d_out[...].astype(F32) + d_value
    proj = attn_proj[...]
    d_value, g_apost = norm_pull(proj, norm_scale(proj), gains_full[1], d_mid[...])
    d_attn[...] = d_value.astype(BF16)
    gain_acc[0, 2:3, :] = g_mpre
    gain_acc[0, 1:2, :] = g_apost

    loads[0].wait()
    loads[1].wait()
    wide_one[0].wait_recv()
    order = (3, 1, 2, 0)

    def piece(i):
        to_z = 1 - zl if i // 2 else zl
        to_y = 1 - y if i % 2 else y
        return (2 * to_z + to_y) * chip_rows

    wide_two = {}
    for i in order:
        rows = pl.ds(pl.multiple_of(far_half + piece(i), 16), chip_rows)
        at = pl.ds(i * chip_rows, chip_rows)
        wide_sum[at, :] = add(wide_in[rows, :], wide_got[rows, :])
        wide_two[i] = push(wide_sum.at[at], wide_far.at[at], line[1])
    down_one.wait_recv()
    down_sum[...] = add(down_in[pl.ds(pl.multiple_of(down_rows * c, 16), down_rows), :], down_got[...])
    down_two = w.remote(down_sum, down_far, line[1])
    mine = zl == zh
    pl.when(zl != zh)(down_two.start)

    third = width // 3
    for i in range(3):
        at = slice(i * third, (i + 1) * third)
        dout[:, at] = dot_rows(o_low[...], d_attn[:, at]).astype(BF16)
    out_rows = dout.shape[0] // 32
    columns = dqkv.shape[1] // 4

    def out_at(ref, zz, yy, quarter):
        return rows_of(ref, (2 * zz + yy) * 4 * out_rows + quarter * out_rows, out_rows)

    out_one = [
        push(
            out_at(dout, zz, yy, 2 * xx + 1 - c),
            o1.at[xx, yy, pl.ds(zz * out_rows, out_rows)],
            sibling,
        )
        for zz in range(4)
        for yy in range(2)
        for xx in range(2)
    ]
    loads[2].wait()
    d_mix[...] = dot_columns(d_attn[...], out_w[...]).astype(BF16)

    cosine, sine = tables[0], tables[1]
    head = k_low.shape[1]
    heads = q_low.shape[1] // head
    d_k, d_v, g_q = 0.0, 0.0, 0.0
    for i in range(heads):
        at = slice(i * head, (i + 1) * head)
        prob = probs[i]
        d_probs = dot_columns(d_mix[:, at], v_low[...])
        row_dot = jnp.sum(prob * d_probs, axis=1, keepdims=True)
        d_scores = (prob * (d_probs - row_dot)).astype(BF16)
        d_q = SCALE * jnp.dot(d_scores, k_low[...], preferred_element_type=F32)
        d_k = d_k + dot_rows(d_scores, q_low[:, at])
        d_v = d_v + dot_rows(prob.astype(BF16), d_mix[:, at])
        value = qk_proj[:, at]
        d_value, gain = norm_pull(
            value, norm_scale(value), gains_full[4, :, :head], turn_back(d_q, cosine, sine)
        )
        g_q = g_q + gain
        d_qkv[:, at] = d_value.astype(BF16)
    at = slice(heads * head, (heads + 1) * head)
    value = qk_proj[:, at]
    d_value, g_k = norm_pull(
        value, norm_scale(value), gains_full[5, :, :head], turn_back(SCALE * d_k, cosine, sine)
    )
    d_qkv[:, at] = d_value.astype(BF16)
    d_qkv[:, (heads + 1) * head :] = d_v.astype(BF16)
    gain_acc[0, 4:5, :] = jnp.zeros((1, width), F32)
    gain_acc[0, 5:8, :] = jnp.zeros((3, width), F32)
    gain_acc[0, 4:5, :head] = g_q
    gain_acc[0, 5:6, :head] = g_k
    for i in range(heads + 2):
        at = slice(i * head, (i + 1) * head)
        dqkv[:, at] = dot_rows(a_low[...], d_qkv[:, at]).astype(BF16)

    def qkv_columns(ref, quarter):
        return ref.at[:, pl.ds(pl.multiple_of(quarter * columns, 128), columns)]

    qkv_one = [push(qkv_columns(dqkv, 2 * xx + 1 - c), q1.at[xx], sibling) for xx in range(2)]

    loads[3].wait()
    tok_f = tok[...].astype(F32)
    for i in range(3):
        at = slice(i * third, (i + 1) * third)
        d_input[:, at] = dot_columns(d_qkv[...], qkv_w[at, :])
    d_value, g_apre = norm_pull(tok_f, norm_scale(tok_f), gains_full[0], d_input[...])
    grad_x[...] = (d_mid[...] + d_value).astype(BF16)
    gain_acc[0, 0:1, :] = g_apre
    gain_acc[0, 3:4, :] = g_mpost[...]
    gain_one = push(gain_acc.at[0], gain_got.at[0], sibling)

    for copy in out_one + qkv_one:
        copy.wait_recv()

    def plane_part(xx, yy, q_ref, o_ref):
        at = pl.ds(pl.multiple_of((2 * xx + c) * columns, 128), columns)
        for zz in range(4):
            rows = pl.ds(pl.multiple_of((2 * zz + yy) * chip_rows, 16), chip_rows)
            q_ref[zz * chip_rows : (zz + 1) * chip_rows, :] = add(dqkv[rows, at], q1[xx, rows, :])
            start = pl.multiple_of(((2 * zz + yy) * 4 + 2 * xx + c) * out_rows, 16)
            here = slice(zz * out_rows, (zz + 1) * out_rows)
            o_ref[here, :] = add(dout[pl.ds(start, out_rows), :], o1[xx, yy, here, :])

    second = {}
    for i in (2, 0, 1):
        plane_part(x if i == 1 else 1 - x, y if i == 0 else 1 - y, q2.at[i], o2.at[i])
        second[i] = (push(q2.at[i], q2.at[3 + i], plane[i]), push(o2.at[i], o2.at[3 + i], plane[i]))
    gain_one.wait_recv()
    gain_acc[1] = gain_acc[0] + gain_got[0]
    gain_two = [push(gain_acc.at[1], gain_got.at[1 + i], plane[i]) for i in range(3)]
    plane_part(x, y, q3, o3)

    part = (2 * zl + x) * 2 + y
    wide_three, own_wide = [], []

    def wide_on(i):
        at = pl.ds(i * chip_rows, chip_rows)
        rows = pl.ds(pl.multiple_of(near_half + piece(i), 16), chip_rows)
        wide_two[i].wait_recv()
        own = wide_in[rows, :].astype(F32) + wide_got[rows, :].astype(F32)
        wide_far[at, :] = (own + wide_far[at, :].astype(F32)).astype(BF16)
        for over in (1, 0):
            bits = 4 * over + 2 * (i % 2) + i // 2
            if bits:
                wide_three.append(push(wide_far.at[at], wide_end.at[part], p.cube(bits)))
            else:
                own_wide.append(
                    pltpu.make_async_copy(wide_far.at[at], wide_end.at[part], local.at[4])
                )
                own_wide[0].start()

    wide_one[1].wait_recv()
    wide_on(3)
    for i in range(3):
        for copy in second[i]:
            copy.wait_recv()
    q3[...] = add(
        q3[...].astype(F32) + q2[3].astype(F32), q2[4].astype(F32) + q2[5].astype(F32)
    )
    o3[...] = add(
        o3[...].astype(F32) + o2[3].astype(F32), o2[4].astype(F32) + o2[5].astype(F32)
    )
    third_step = []
    for k in range(1, 4):
        zz = p.z_xor(k)
        third_step += [
            push(rows_of(q3, zz * chip_rows, chip_rows), qe.at[k], line[k - 1]),
            push(rows_of(o3, zz * out_rows, out_rows), oe.at[k], line[k - 1]),
        ]
    for copy in gain_two:
        copy.wait_recv()
    gain_acc[2] = gain_acc[1] + gain_got[1] + gain_got[2] + gain_got[3]
    gain_three = [push(gain_acc.at[2], gain_got.at[3 + k], line[k - 1]) for k in range(1, 4)]
    wide_on(1)
    for copy in third_step:
        copy.wait_recv()
    start = pl.multiple_of(z * chip_rows, 16)
    qe[0] = add(
        q3[pl.ds(start, chip_rows), :].astype(F32) + qe[1].astype(F32),
        qe[2].astype(F32) + qe[3].astype(F32),
    )
    start = pl.multiple_of(z * out_rows, 16)
    oe[0] = add(
        o3[pl.ds(start, out_rows), :].astype(F32) + oe[1].astype(F32),
        oe[2].astype(F32) + oe[3].astype(F32),
    )
    last = [
        push(qe.at[0], qe.at[4 + i], device)
        for i, device in enumerate((sibling, plane[0]))
    ] + [
        push(oe.at[0], oe.at[4 + i], device)
        for i, device in enumerate((sibling, plane[0]))
    ]
    wide_on(2)
    for copy in last:
        copy.wait_recv()
    relay = [push(qe.at[5], qe.at[6], sibling), push(oe.at[5], oe.at[6], sibling)]
    wide_on(0)

    arrive = w.used
    w.used += 3
    down_three = []
    for xx in range(2):
        copy = pltpu.make_async_remote_copy(
            src_ref=down_far,
            dst_ref=down_end,
            send_sem=send.at[arrive + xx],
            recv_sem=recv.at[arrive],
            device_id=p.at(x=xx, z=2 * zh + x),
            device_id_type=MESH,
        )
        down_three.append((mine & ((x != xx) | (zh != x)), copy))
    down_here = mine & (x == zl)

    @pl.when(mine)
    def _():
        down_two.wait_recv()
        down_far[...] = add(down_sum[...], down_far[...])

    down_own = pltpu.make_async_copy(down_far, down_end, local.at[5])
    for need, copy in down_three:
        pl.when(need)(copy.start)
    pl.when(down_here)(down_own.start)

    for copy in relay:
        copy.wait_recv()
    rows = chip_rows // 2
    for xx in range(2):
        for cc in range(2):

            @pl.when((x == xx) & (c == cc))
            def _():
                for i, q in ((0, 2 * xx + cc), (4, 2 * xx + 1 - cc), (5, 2 * (1 - xx) + cc), (6, 2 * (1 - xx) + 1 - cc)):
                    both = qe[i].astype(F32)
                    grad_qkv[:, q * columns : (q + 1) * columns] = both[cc * rows : (cc + 1) * rows]
                    if q // 2 == cc:
                        grad_out[(q % 2) * out_rows : (q % 2 + 1) * out_rows, :] = oe[i].astype(F32)

    for copy in gain_three:
        copy.wait_recv()
    grad_gains[...] = gain_acc[2] + gain_got[4] + gain_got[5] + gain_got[6]

    own_wide[0].wait()
    for copy in wide_three:
        copy.wait_recv()
    for cc in range(2):

        @pl.when(c == cc)
        def _():
            for s in range(8):
                extra = (rows + 15) // 16 * 16
                at = slice(0, extra) if cc == 1 else slice(2 * rows - extra, 2 * rows)
                wide_swap[s] = wide_end[s, at, :]

    final = push(wide_swap, wide_back, sibling)
    pl.when(down_here)(down_own.wait)
    pl.when(jnp.logical_not(down_here))(down_three[0][1].wait_recv)
    grad_dn[...] = down_end[...].astype(F32)
    final.wait_recv()
    for cc in range(2):

        @pl.when(c == cc)
        def _():
            extra = (rows + 15) // 16 * 16
            size = wide_end.shape[2]
            for s in range(8):
                at = slice(s * size, (s + 1) * size)
                own = wide_end[s].astype(F32)[cc * rows : (cc + 1) * rows]
                other = wide_back[s].astype(F32)
                other = other[:rows] if cc == 0 else other[extra - rows :]
                grad_gu[cc, :, at] = own
                grad_gu[1 - cc, :, at] = other

    for need, copy in down_three:
        pl.when(need)(copy.wait_send)
    pl.when(zl != zh)(down_two.wait_send)
    for copy in started:
        copy.wait_send()


def back(
    tok, d_out, d_normed, gains_full, saved, g_mpost, qkv_w, out_w, grad_gu, grad_dn, rows, out_rows
):
    length, width = tok.shape
    total = qkv_w.shape[1]
    columns = total // 4
    mix = out_w.shape[0]
    _, _, part = grad_gu.shape
    down_rows = grad_dn.shape[0] // 2
    chip_rows = 2 * rows
    extra = (rows + 15) // 16 * 16
    piece = out_rows // 2
    struct = jax.ShapeDtypeStruct
    shapes = (
        struct((length, width), BF16),
        struct((rows, total), F32),
        struct((out_rows, width), F32),
        struct((8, width), F32),
        struct((2, rows, 8 * part), F32),
        struct((down_rows, width), F32),
    )
    scratch = [
        pltpu.VMEM(qkv_w.shape, BF16),
        pltpu.VMEM(out_w.shape, BF16),
        pltpu.VMEM((width, part), BF16),
        pltpu.VMEM((width, part), BF16),
        pltpu.VMEM((width // 2, part), BF16),
        pltpu.VMEM((width // 2, part), BF16),
        pltpu.VMEM(grad_dn.shape, BF16),
        pltpu.VMEM((down_rows, width), BF16),
        pltpu.VMEM((down_rows, width), BF16),
        pltpu.VMEM((down_rows, width), BF16),
        pltpu.VMEM((down_rows, width), BF16),
        pltpu.VMEM((length, width), F32),
        pltpu.VMEM((8, chip_rows, part), BF16),
        pltpu.VMEM((8, extra, part), BF16),
        pltpu.VMEM((8, extra, part), BF16),
        pltpu.VMEM((length, width), BF16),
        pltpu.VMEM((length, width), F32),
        pltpu.VMEM((length, mix), BF16),
        pltpu.VMEM((length, total), BF16),
        pltpu.VMEM((width, total), BF16),
        pltpu.VMEM((mix, width), BF16),
        pltpu.VMEM((2, width, columns), BF16),
        pltpu.VMEM((2, 2, 4 * piece, width), BF16),
        pltpu.VMEM((6, 4 * chip_rows, columns), BF16),
        pltpu.VMEM((6, 4 * piece, width), BF16),
        pltpu.VMEM((4 * chip_rows, columns), BF16),
        pltpu.VMEM((4 * piece, width), BF16),
        pltpu.VMEM((7, chip_rows, columns), BF16),
        pltpu.VMEM((7, piece, width), BF16),
        pltpu.VMEM((3, 8, width), F32),
        pltpu.VMEM((7, 8, width), F32),
    ]
    return pl.pallas_call(
        back_kernel,
        out_shape=shapes,
        in_specs=[vmem()] * 15 + [hbm()] * 4,
        out_specs=(vmem(),) * 6,
        scratch_shapes=scratch + sems(96) + [pltpu.SemaphoreType.DMA((6,))],
        compiler_params=params(3),
        name="back",
    )(tok, d_out, d_normed, gains_full, *saved, g_mpost, qkv_w, out_w, grad_gu, grad_dn)


def pack_gains(vectors):
    rows = [jnp.pad(v, (0, 128 - v.shape[0])) for v in vectors]
    return jnp.concatenate(rows + [jnp.zeros(((8 - len(rows)) * 128,), F32)]).reshape(8, 128)


def cube_body(
    layer_in, d_out, segments, w_q, w_k, w_v, w_o, attn_pre, attn_post, q_gain, k_gain,
    w_gate, w_up, w_down, mlp_pre, mlp_post,
):
    width = layer_in.shape[1]
    head = q_gain.shape[0] * 16
    rows, mix = w_q.shape
    gain_list = [attn_pre, attn_post, mlp_pre, mlp_post, q_gain, k_gain]
    (
        qkv_w, out_w, gu_w, down_w, m_all, gains_full, a_low, qk_proj, q_low, k_low, v_low,
        probs, o_low, attn_proj, h_mid, tables,
    ) = front(
        layer_in, segments, w_q, w_k, w_v, w_o, pack_gains(gain_list), w_gate, w_up, w_down, head
    )
    gate_w, up_w = gu_w[0], gu_w[1]
    m_all = m_all.reshape(-1, width)
    gate_val = matmul(m_all, gate_w)
    up_val = matmul(m_all, up_w)
    hidden, pull_h = jax.vjp(gelu_product, gate_val, up_val)
    h_low = to_low(hidden)
    down_val = cube_sum(to_low(matmul(h_low, down_w)).reshape(8, -1, width))
    post_mlp, pull_pm = jax.vjp(norm_rows, down_val, gains_full[3, 0])
    layer_out = (h_mid + post_mlp).astype(BF16)

    d_down, g_mpost = pull_pm(d_out.astype(F32))
    dd_all = cube_gather(to_low(d_down)).reshape(-1, width)
    grad_wdown = to_low(matmul_left_t(h_low, dd_all))
    d_hidden = matmul_right_t(dd_all, down_w)
    d_gate, d_up = pull_h(d_hidden)
    d_gate_low = to_low(d_gate)
    d_up_low = to_low(d_up)
    grad_gu = jnp.stack(
        [to_low(matmul_left_t(m_all, d_gate_low)), to_low(matmul_left_t(m_all, d_up_low))]
    )
    d_normed = cube_sum(
        to_low(matmul_right_t(d_gate_low, gate_w) + matmul_right_t(d_up_low, up_w)).reshape(
            8, -1, width
        )
    )
    saved = (a_low, qk_proj, q_low, k_low, v_low, probs, o_low, attn_proj, h_mid, tables)
    grad_x, grad_qkv, grad_out, grad_gains, grad_gu, grad_dn = back(
        layer_in, d_out, d_normed, gains_full, saved, g_mpost[None], qkv_w, out_w, grad_gu,
        grad_wdown, rows, w_o.shape[0],
    )
    shard = lax.axis_index("fsdp")
    g_apre, g_apost, g_mpre, g_mpost, g_q, g_k = [
        lax.dynamic_slice(grad_gains[i], (shard * v.shape[0],), (v.shape[0],))
        for i, v in enumerate(gain_list)
    ]
    return (
        layer_out,
        grad_x,
        grad_qkv[:, :mix],
        grad_qkv[:, mix : mix + head],
        grad_qkv[:, mix + head :],
        grad_out,
        g_apre,
        g_apost,
        g_q,
        g_k,
        grad_gu[0],
        grad_gu[1],
        grad_dn,
        g_mpre,
        g_mpost,
    )


def solution(mesh):
    in_specs = (
        P(("replica", "fsdp"), None),
        P(("replica", "fsdp"), None),
        P(("replica", "fsdp"), None),
        P("fsdp", None),
        P("fsdp", None),
        P("fsdp", None),
        P("fsdp", None),
        P("fsdp"),
        P("fsdp"),
        P("fsdp"),
        P("fsdp"),
        P("fsdp", None),
        P("fsdp", None),
        P("fsdp", None),
        P("fsdp"),
        P("fsdp"),
    )
    out_specs = (
        P(("replica", "fsdp"), None),
        P(("replica", "fsdp"), None),
        P("fsdp", None),
        P("fsdp", None),
        P("fsdp", None),
        P("fsdp", None),
        P("fsdp"),
        P("fsdp"),
        P("fsdp"),
        P("fsdp"),
        P("fsdp", None),
        P("fsdp", None),
        P("fsdp", None),
        P("fsdp"),
        P("fsdp"),
    )
    body = cube_body if fits_cubes(mesh) else general_body
    return jax.shard_map(body, mesh=mesh, in_specs=in_specs, out_specs=out_specs, check_vma=False)
```

```python
from functools import partial
import math

import jax
import jax.numpy as jnp
from jax import lax
from jax.experimental import pallas as pl
from jax.experimental.pallas import tpu as pltpu
from jax.sharding import PartitionSpec as P

EPS = 1e-06
THETA = 1000000.0
SCALE = 0.0625
MASKED = -1e30


def norm_rows(values, gain):
    return values * lax.rsqrt(jnp.mean(values * values, axis=-1, keepdims=True) + EPS) * gain


def positions_of(segments):
    length = segments.shape[-1]
    index = jnp.arange(length, dtype=jnp.int32)
    earlier = jnp.concatenate([segments[:, :1] - 1, segments[:, :-1]], axis=1)
    starts = jnp.where(segments != earlier, index[None, :], jnp.zeros_like(segments))
    return index[None, :] - lax.cummax(starts, axis=1)


def angle_tables(segments, head_size):
    half_size = head_size // 2
    rates = jnp.exp(jnp.arange(half_size, dtype=jnp.float32) * (-2.0 * math.log(THETA) / head_size))
    angles = positions_of(segments).astype(jnp.float32)[..., None] * rates
    return (jnp.cos(angles), jnp.sin(angles))


def rotate(values, cosine, sine):
    half_size = values.shape[-1] // 2
    first_half = values[..., :half_size]
    second_half = values[..., half_size:]
    return jnp.concatenate(
        [first_half * cosine - second_half * sine, second_half * cosine + first_half * sine],
        axis=-1,
    )


def query_path(projected, gain, cosine, sine):
    shaped = projected.reshape(projected.shape[0], projected.shape[1], -1, gain.shape[0])
    return rotate(norm_rows(shaped, gain), cosine[:, :, None, :], sine[:, :, None, :])


def key_path(projected, gain, cosine, sine):
    return rotate(norm_rows(projected, gain), cosine, sine)


def gelu_product(gate_val, up_val):
    return jax.nn.gelu(gate_val, approximate=True) * up_val


def to_low(values):
    return values.astype(jnp.bfloat16)


def matmul(left, right):
    return jnp.dot(left, right, preferred_element_type=jnp.float32)


def matmul_left_t(left, right):
    return lax.dot_general(
        left, right, (((0,), (0,)), ((), ())), preferred_element_type=jnp.float32
    )


def matmul_right_t(left, right):
    return lax.dot_general(
        left, right, (((1,), (1,)), ((), ())), preferred_element_type=jnp.float32
    )


def attention_masks(segments):
    length = segments.shape[1]
    index = jnp.arange(length, dtype=jnp.int32)
    causal = index[None, :] <= index[:, None]
    return (segments[:, :, None] == segments[:, None, :]) & causal[None]


def scores_of(q_low, k_low, masks):
    scores = SCALE * jnp.einsum("nqhd,nkd->nhqk", q_low, k_low, preferred_element_type=jnp.float32)
    return jnp.where(masks[:, None], scores, MASKED)


def spread_gain(values):
    return jnp.broadcast_to(values[:, None], (values.shape[0], lax.axis_size("replica")))


def general_body(
    layer_in,
    d_out,
    segments,
    w_q,
    w_k,
    w_v,
    w_o,
    attn_pre,
    attn_post,
    q_gain,
    k_gain,
    w_gate,
    w_up,
    w_down,
    mlp_pre,
    mlp_post,
):
    attn_set = (
        lax.all_gather(to_low(w_q), "fsdp", axis=0, tiled=True),
        lax.all_gather(to_low(w_k), "fsdp", axis=0, tiled=True),
        lax.all_gather(to_low(w_v), "fsdp", axis=0, tiled=True),
        lax.all_gather(to_low(w_o), "fsdp", axis=0, tiled=True),
        lax.all_gather(to_low(attn_pre), "fsdp", axis=0, tiled=True),
        lax.all_gather(to_low(attn_post), "fsdp", axis=0, tiled=True),
        lax.all_gather(to_low(q_gain), "fsdp", axis=0, tiled=True),
        lax.all_gather(to_low(k_gain), "fsdp", axis=0, tiled=True),
    )
    q_full, k_full, v_full, o_full = (attn_set[0], attn_set[1], attn_set[2], attn_set[3])
    gain_apre = attn_set[4].astype(jnp.float32)
    gain_apost = attn_set[5].astype(jnp.float32)
    gain_q = attn_set[6].astype(jnp.float32)
    gain_k = attn_set[7].astype(jnp.float32)
    mlp_set = (
        lax.all_gather(to_low(w_gate), "fsdp", axis=0, tiled=True),
        lax.all_gather(to_low(w_up), "fsdp", axis=0, tiled=True),
        lax.all_gather(to_low(w_down), "fsdp", axis=0, tiled=True),
        lax.all_gather(to_low(mlp_pre), "fsdp", axis=0, tiled=True),
        lax.all_gather(to_low(mlp_post), "fsdp", axis=0, tiled=True),
    )
    gate_full, up_full, down_full = (mlp_set[0], mlp_set[1], mlp_set[2])
    gain_mpre = mlp_set[3].astype(jnp.float32)
    gain_mpost = mlp_set[4].astype(jnp.float32)
    seq_count, seq_len = segments.shape
    tok_flat = layer_in.astype(jnp.float32)
    cosine, sine = angle_tables(segments, gain_q.shape[0])
    masks = attention_masks(segments)
    normed_a, pull_a = jax.vjp(norm_rows, tok_flat, gain_apre)
    a_low = to_low(normed_a)
    q_proj = matmul(a_low, q_full).reshape(seq_count, seq_len, -1)
    k_proj = matmul(a_low, k_full).reshape(seq_count, seq_len, -1)
    v_proj = matmul(a_low, v_full)
    q_rot, pull_q = jax.vjp(partial(query_path, cosine=cosine, sine=sine), q_proj, gain_q)
    k_rot, pull_k = jax.vjp(partial(key_path, cosine=cosine, sine=sine), k_proj, gain_k)
    q_low = to_low(q_rot)
    k_low = to_low(k_rot)
    v_low = to_low(v_proj).reshape(seq_count, seq_len, -1)
    scores = scores_of(q_low, k_low, masks)
    top_val = jnp.max(scores, axis=-1, keepdims=True)
    log_total = top_val + jnp.log(jnp.sum(jnp.exp(scores - top_val), axis=-1, keepdims=True))
    p_low = to_low(jnp.exp(scores - log_total))
    attn_mix = jnp.einsum("nhqk,nkd->nqhd", p_low, v_low, preferred_element_type=jnp.float32)
    o_low = to_low(attn_mix.reshape(seq_count * seq_len, -1))
    attn_proj = matmul(o_low, o_full)
    post_attn, pull_pa = jax.vjp(norm_rows, attn_proj, gain_apost)
    h_mid = tok_flat + post_attn
    normed_m, pull_m = jax.vjp(norm_rows, h_mid, gain_mpre)
    m_low = to_low(normed_m)
    gate_val = matmul(m_low, gate_full)
    up_val = matmul(m_low, up_full)
    hidden, pull_h = jax.vjp(gelu_product, gate_val, up_val)
    h_low = to_low(hidden)
    down_val = matmul(h_low, down_full)
    post_mlp, pull_pm = jax.vjp(norm_rows, down_val, gain_mpost)
    layer_out = (h_mid + post_mlp).astype(jnp.bfloat16)
    gate_full, up_full, down_full = (
        lax.all_gather(to_low(w_gate), "fsdp", axis=0, tiled=True),
        lax.all_gather(to_low(w_up), "fsdp", axis=0, tiled=True),
        lax.all_gather(to_low(w_down), "fsdp", axis=0, tiled=True),
    )
    grad_top = d_out.astype(jnp.float32)
    d_down, grad_mpost = pull_pm(grad_top)
    d_down_low = to_low(d_down)
    grad_wdown = matmul_left_t(h_low, d_down_low)
    d_hidden = matmul_right_t(d_down_low, down_full)
    d_gate, d_up = pull_h(d_hidden)
    d_gate_low = to_low(d_gate)
    d_up_low = to_low(d_up)
    grad_wgate = matmul_left_t(m_low, d_gate_low)
    grad_wup = matmul_left_t(m_low, d_up_low)
    d_normed = matmul_right_t(d_gate_low, gate_full) + matmul_right_t(d_up_low, up_full)
    d_mid_norm, grad_mpre = pull_m(d_normed)
    d_mid = grad_top + d_mid_norm
    q_full, k_full, v_full, o_full = (
        lax.all_gather(to_low(w_q), "fsdp", axis=0, tiled=True),
        lax.all_gather(to_low(w_k), "fsdp", axis=0, tiled=True),
        lax.all_gather(to_low(w_v), "fsdp", axis=0, tiled=True),
        lax.all_gather(to_low(w_o), "fsdp", axis=0, tiled=True),
    )
    d_attn, grad_apost = pull_pa(d_mid)
    d_attn_low = to_low(d_attn)
    grad_wo = matmul_left_t(o_low, d_attn_low)
    d_mix_low = to_low(matmul_right_t(d_attn_low, o_full)).reshape(
        seq_count, seq_len, -1, k_low.shape[-1]
    )
    probs = jnp.exp(scores_of(q_low, k_low, masks) - log_total)
    d_probs = jnp.einsum("nqhd,nkd->nhqk", d_mix_low, v_low, preferred_element_type=jnp.float32)
    row_dot = jnp.sum(probs * d_probs, axis=-1, keepdims=True)
    d_scores_low = to_low(probs * (d_probs - row_dot))
    d_query = SCALE * jnp.einsum(
        "nhqk,nkd->nqhd", d_scores_low, k_low, preferred_element_type=jnp.float32
    )
    d_key = SCALE * jnp.einsum(
        "nhqk,nqhd->nkd", d_scores_low, q_low, preferred_element_type=jnp.float32
    )
    d_value = jnp.einsum("nhqk,nqhd->nkd", p_low, d_mix_low, preferred_element_type=jnp.float32)
    d_qproj, grad_qgain = pull_q(d_query)
    d_kproj, grad_kgain = pull_k(d_key)
    d_q_low = to_low(d_qproj.reshape(seq_count * seq_len, -1))
    d_k_low = to_low(d_kproj.reshape(seq_count * seq_len, -1))
    d_v_low = to_low(d_value.reshape(seq_count * seq_len, -1))
    grad_wq = matmul_left_t(a_low, d_q_low)
    grad_wk = matmul_left_t(a_low, d_k_low)
    grad_wv = matmul_left_t(a_low, d_v_low)
    d_normed_a = (
        matmul_right_t(d_q_low, q_full)
        + matmul_right_t(d_k_low, k_full)
        + matmul_right_t(d_v_low, v_full)
    )
    d_input_norm, grad_apre = pull_a(d_normed_a)
    grad_x = (d_mid + d_input_norm).astype(jnp.bfloat16)
    all_shards = (
        lax.psum_scatter(grad_wq, "fsdp", scatter_dimension=0, tiled=True),
        lax.psum_scatter(grad_wk, "fsdp", scatter_dimension=0, tiled=True),
        lax.psum_scatter(grad_wv, "fsdp", scatter_dimension=0, tiled=True),
        lax.psum_scatter(grad_wo, "fsdp", scatter_dimension=0, tiled=True),
        lax.psum_scatter(grad_apre, "fsdp", scatter_dimension=0, tiled=True),
        lax.psum_scatter(grad_apost, "fsdp", scatter_dimension=0, tiled=True),
        lax.psum_scatter(grad_qgain, "fsdp", scatter_dimension=0, tiled=True),
        lax.psum_scatter(grad_kgain, "fsdp", scatter_dimension=0, tiled=True),
        lax.psum_scatter(grad_wgate, "fsdp", scatter_dimension=0, tiled=True),
        lax.psum_scatter(grad_wup, "fsdp", scatter_dimension=0, tiled=True),
        lax.psum_scatter(grad_wdown, "fsdp", scatter_dimension=0, tiled=True),
        lax.psum_scatter(grad_mpre, "fsdp", scatter_dimension=0, tiled=True),
        lax.psum_scatter(grad_mpost, "fsdp", scatter_dimension=0, tiled=True),
    )
    all_cols = (
        lax.psum_scatter(
            all_shards[0].astype(jnp.bfloat16), "replica", scatter_dimension=1, tiled=True
        ).astype(jnp.float32),
        lax.psum_scatter(
            all_shards[1].astype(jnp.bfloat16), "replica", scatter_dimension=1, tiled=True
        ).astype(jnp.float32),
        lax.psum_scatter(
            all_shards[2].astype(jnp.bfloat16), "replica", scatter_dimension=1, tiled=True
        ).astype(jnp.float32),
        lax.psum_scatter(
            all_shards[3].astype(jnp.bfloat16), "replica", scatter_dimension=1, tiled=True
        ).astype(jnp.float32),
        lax.psum_scatter(
            all_shards[8].astype(jnp.bfloat16), "replica", scatter_dimension=1, tiled=True
        ).astype(jnp.float32),
        lax.psum_scatter(
            all_shards[9].astype(jnp.bfloat16), "replica", scatter_dimension=1, tiled=True
        ).astype(jnp.float32),
        lax.psum_scatter(
            all_shards[10].astype(jnp.bfloat16), "replica", scatter_dimension=1, tiled=True
        ).astype(jnp.float32),
        lax.psum_scatter(
            spread_gain(all_shards[4]).astype(jnp.bfloat16),
            "replica",
            scatter_dimension=1,
            tiled=True,
        ).astype(jnp.float32),
        lax.psum_scatter(
            spread_gain(all_shards[5]).astype(jnp.bfloat16),
            "replica",
            scatter_dimension=1,
            tiled=True,
        ).astype(jnp.float32),
        lax.psum_scatter(
            spread_gain(all_shards[6]).astype(jnp.bfloat16),
            "replica",
            scatter_dimension=1,
            tiled=True,
        ).astype(jnp.float32),
        lax.psum_scatter(
            spread_gain(all_shards[7]).astype(jnp.bfloat16),
            "replica",
            scatter_dimension=1,
            tiled=True,
        ).astype(jnp.float32),
        lax.psum_scatter(
            spread_gain(all_shards[11]).astype(jnp.bfloat16),
            "replica",
            scatter_dimension=1,
            tiled=True,
        ).astype(jnp.float32),
        lax.psum_scatter(
            spread_gain(all_shards[12]).astype(jnp.bfloat16),
            "replica",
            scatter_dimension=1,
            tiled=True,
        ).astype(jnp.float32),
    )
    all_mats = (
        lax.all_gather(all_cols[0].astype(jnp.bfloat16), "replica", axis=1, tiled=True).astype(
            jnp.float32
        ),
        lax.all_gather(all_cols[1].astype(jnp.bfloat16), "replica", axis=1, tiled=True).astype(
            jnp.float32
        ),
        lax.all_gather(all_cols[2].astype(jnp.bfloat16), "replica", axis=1, tiled=True).astype(
            jnp.float32
        ),
        lax.all_gather(all_cols[3].astype(jnp.bfloat16), "replica", axis=1, tiled=True).astype(
            jnp.float32
        ),
        lax.all_gather(all_cols[4].astype(jnp.bfloat16), "replica", axis=1, tiled=True).astype(
            jnp.float32
        ),
        lax.all_gather(all_cols[5].astype(jnp.bfloat16), "replica", axis=1, tiled=True).astype(
            jnp.float32
        ),
        lax.all_gather(all_cols[6].astype(jnp.bfloat16), "replica", axis=1, tiled=True).astype(
            jnp.float32
        ),
    )
    attn_sums = (
        all_mats[0],
        all_mats[1],
        all_mats[2],
        all_mats[3],
        all_cols[7][:, 0],
        all_cols[8][:, 0],
        all_cols[9][:, 0],
        all_cols[10][:, 0],
    )
    mlp_sums = (all_mats[4], all_mats[5], all_mats[6], all_cols[11][:, 0], all_cols[12][:, 0])
    return (
        layer_out,
        grad_x,
        attn_sums[0],
        attn_sums[1],
        attn_sums[2],
        attn_sums[3],
        attn_sums[4],
        attn_sums[5],
        attn_sums[6],
        attn_sums[7],
        mlp_sums[0],
        mlp_sums[1],
        mlp_sums[2],
        mlp_sums[3],
        mlp_sums[4],
    )


MESH = pl.DeviceIdType.MESH
VMEM_BYTES = 60 * 2**20
F32 = jnp.float32
BF16 = jnp.bfloat16


def fits_cubes(mesh):
    return dict(mesh.shape) == {"replica": 2, "fsdp": 16}


class Place:
    def __init__(self):
        shard = lax.axis_index("fsdp")
        self.x = lax.axis_index("replica")
        self.shard = shard
        self.c = lax.rem(shard, 2)
        self.y = lax.rem(lax.div(shard, 2), 2)
        self.z = lax.div(shard, 4)
        self.zl = lax.rem(self.z, 2)
        self.zh = lax.div(self.z, 2)

    def at(self, x=None, y=None, z=None, c=None):
        x = self.x if x is None else x
        y = self.y if y is None else y
        z = self.z if z is None else z
        c = self.c if c is None else c
        return (x, (z * 2 + y) * 2 + c)

    def z_xor(self, k):
        low = self.zl if k % 2 == 0 else 1 - self.zl
        high = self.zh if k // 2 == 0 else 1 - self.zh
        return 2 * high + low

    def cube(self, bits):
        return self.at(
            x=1 - self.x if bits & 4 else self.x,
            y=1 - self.y if bits & 2 else self.y,
            z=self.z_xor(1) if bits & 1 else self.z,
        )


class Wires:
    def __init__(self, send, recv):
        self.send, self.recv, self.used = send, recv, 0

    def remote(self, src, dst, device):
        i = self.used
        self.used += 1
        return pltpu.make_async_remote_copy(
            src_ref=src,
            dst_ref=dst,
            send_sem=self.send.at[i],
            recv_sem=self.recv.at[i],
            device_id=device,
            device_id_type=MESH,
        )

    def local(self, src, dst):
        i = self.used
        self.used += 1
        return pltpu.make_async_copy(src, dst, self.send.at[i])


def greet(devices):
    barrier = pltpu.get_barrier_semaphore()
    for device in devices:
        pl.semaphore_signal(barrier, inc=1, device_id=device, device_id_type=MESH)
    pl.semaphore_wait(barrier, len(devices))


def hbm():
    return pl.BlockSpec(memory_space=pl.ANY)


def vmem():
    return pl.BlockSpec(memory_space=pltpu.VMEM)


def sems(count):
    return [pltpu.SemaphoreType.DMA((count,)), pltpu.SemaphoreType.DMA((count,))]


def params(collective_id):
    return pltpu.CompilerParams(
        collective_id=collective_id, has_side_effects=True, vmem_limit_bytes=VMEM_BYTES
    )


X, Y, Z = 4, 2, 1


def thirds(rows):
    first = -(-rows // 48) * 16
    return ((0, first), (first, first), (2 * first, rows - 2 * first))


def add(left, right):
    return (left.astype(F32) + right.astype(F32)).astype(BF16)


def norm_scale(values):
    return lax.rsqrt(jnp.mean(values * values, axis=-1, keepdims=True) + EPS)


def norm_pull(values, scale, gain, cotangent):
    weighted = gain * cotangent
    lean = jnp.mean(values * weighted, axis=-1, keepdims=True)
    d_values = scale * weighted - values * (scale * scale * scale * lean)
    return d_values, jnp.sum(values * scale * cotangent, axis=0, keepdims=True)


def spread_matrix(width, per):
    column = lax.broadcasted_iota(jnp.int32, (128, width), 1)
    row = lax.broadcasted_iota(jnp.int32, (128, width), 0)
    place = (lax.rem(column, per) == row).astype(F32)
    column = lax.broadcasted_iota(jnp.int32, (16, width), 1)
    row = lax.broadcasted_iota(jnp.int32, (16, width), 0)
    owner = (lax.div(column, per) == row).astype(F32)
    return place, owner


def join_gains(packed, which, width, per):
    place, owner = spread_matrix(width, per)
    shards = packed[:, which, :].astype(BF16)
    wide = jnp.dot(shards, place.astype(BF16), preferred_element_type=F32)
    return jnp.sum(wide * owner, axis=0, keepdims=True)


def turn(values, cosine, sine):
    half = values.shape[-1] // 2
    u, w = values[:, :half], values[:, half:]
    return jnp.concatenate([u * cosine - w * sine, w * cosine + u * sine], axis=1)


def turn_back(values, cosine, sine):
    half = values.shape[-1] // 2
    u, w = values[:, :half], values[:, half:]
    return jnp.concatenate([u * cosine + w * sine, w * cosine - u * sine], axis=1)


def front_kernel(
    tok, seg_row, seg_col, w_q, w_k, w_v, w_o, gains, w_gate, w_up, w_down,
    qkv_w, out_w, gu_w, dn_w, every, gains_full, a_low, qk_proj, q_low, k_low, v_low,
    probs, o_low, attn_proj, h_mid, tables,
    qkv_s, qkv_own, qkv_send, qkv_got, out_own, gains_own, gains_s, wide_in, wide_send, wide_got,
    wide_out, down_in, down_out, m_low, out_s, send, recv, local,
):
    p = Place()
    w = Wires(send, recv)
    x, y, z, c, zl, zh = p.x, p.y, p.z, p.c, p.zl, p.zh
    sibling = p.at(c=1 - c)
    plane = [p.at(x=1 - x), p.at(y=1 - y)]
    lines = [p.at(y=yy, z=p.z_xor(k)) for yy in (y, 1 - y) for k in range(1, 4)]
    started = []

    def push(src, dst, device):
        copy = w.remote(src, dst, device)
        copy.start()
        started.append(copy)
        return copy

    loads = [
        pltpu.make_async_copy(w_gate, wide_in.at[0], local.at[0]),
        pltpu.make_async_copy(w_up, wide_in.at[1], local.at[1]),
        pltpu.make_async_copy(w_down, down_in, local.at[2]),
    ]
    for copy in loads:
        copy.start()

    rows = w_q.shape[0]
    columns = qkv_s.shape[1] // 4
    out_rows = w_o.shape[0] // 2
    mine = 2 * x + c
    theirs = 2 * x + 1 - c

    all_own = jnp.concatenate([w_q[...], w_k[...], w_v[...]], axis=1)
    for quarter in range(4):
        qkv_own[quarter] = all_own[:, quarter * columns : (quarter + 1) * columns]
    qkv_send[...] = qkv_own[theirs].astype(BF16)
    out_own[...] = w_o[...].astype(BF16)
    gains_own[...] = gains[...].astype(BF16).astype(F32)
    greet([sibling] + plane + lines)

    def qkv_at(zz, yy, quarter):
        return qkv_s.at[
            pl.ds(pl.multiple_of((2 * zz + yy) * 2 * rows, 16), 2 * rows),
            pl.ds(pl.multiple_of(quarter * columns, 128), columns),
        ]

    def out_at(zz, yy, quarter):
        return out_s.at[
            pl.ds(pl.multiple_of((2 * zz + yy) * 4 * out_rows + quarter * out_rows, 16), out_rows)
        ]

    swap = push(qkv_send, qkv_got, sibling)

    def gains_at(zz, yy, cc):
        return gains_s.at[(2 * zz + yy) * 2 + cc]

    gains_s[(2 * z + y) * 2 + c] = gains_own[...]
    gain_line = [push(gains_own, gains_at(z, y, c), p.at(z=p.z_xor(k))) for k in range(1, 4)]
    gain_side = [push(gains_own, gains_at(z, y, c), plane[1])]
    holds = x == c
    out_theirs = out_own.at[pl.ds(pl.multiple_of((1 - c) * out_rows, 16), out_rows)]
    out_swap = w.remote(out_theirs, out_at(z, y, theirs), sibling)
    pl.when(holds)(out_swap.start)

    @pl.when(holds)
    def _():
        out_s[pl.ds(pl.multiple_of((2 * z + y) * 4 * out_rows + mine * out_rows, 16), out_rows)] = (
            out_own[pl.ds(pl.multiple_of(c * out_rows, 16), out_rows)]
        )

    swap.wait_recv()
    top, low = qkv_own[mine], qkv_got[...].astype(F32)
    first = jnp.where(c == 0, top, low)
    second = jnp.where(c == 0, low, top)
    base = pl.multiple_of((2 * z + y) * 2 * rows, 16)
    joined = jnp.concatenate([first, second], axis=0).astype(BF16)
    qkv_s[pl.ds(base, 2 * rows), pl.ds(pl.multiple_of(mine * columns, 128), columns)] = joined

    pl.when(jnp.logical_not(holds))(out_swap.wait_recv)
    pl.when(holds)(out_swap.wait_send)

    line = [None]
    for k in range(1, 4):
        to = p.at(z=p.z_xor(k))
        line.append(
            (
                push(qkv_at(z, y, mine), qkv_at(z, y, mine), to),
                push(out_at(z, y, mine), out_at(z, y, mine), to),
            )
        )
    side_x, side_y, corner = {}, {}, {}

    def spread(k):
        zz = p.z_xor(k)
        if k:
            for copy in line[k]:
                copy.wait_recv()
        qkv, out = qkv_at(zz, y, mine), out_at(zz, y, mine)
        side_x[k] = (push(qkv, qkv, plane[0]), push(out, out, plane[0]))
        side_y[k] = (push(qkv, qkv, plane[1]), push(out, out, plane[1]))

    def relay(k):
        zz = p.z_xor(k)
        if k % 2:
            for copy in side_y[k]:
                copy.wait_recv()
            qkv, out, to = qkv_at(zz, 1 - y, mine), out_at(zz, 1 - y, mine), plane[0]
        else:
            for copy in side_x[k]:
                copy.wait_recv()
            other = 2 * (1 - x) + c
            qkv, out, to = qkv_at(zz, y, other), out_at(zz, y, other), plane[1]
        corner[k] = (push(qkv, qkv, to), push(out, out, to))

    pairs = []

    def share(k):
        zz = p.z_xor(k)
        for copy in (side_x[k] if k % 2 else side_y[k]) + corner[k]:
            copy.wait_recv()
        for xx in range(2):
            at = qkv_s.at[
                pl.ds(pl.multiple_of(2 * zz * 2 * rows, 16), 4 * rows),
                pl.ds(pl.multiple_of((2 * xx + c) * columns, 128), columns),
            ]
            pairs.append(push(at, at, sibling))
            for yy in range(2):
                at = out_at(zz, yy, 2 * xx + c)
                pairs.append(push(at, at, sibling))

    spread(0)
    loads[0].wait()
    loads[1].wait()
    part_columns = wide_out.shape[-1]
    for xx in range(2):

        @pl.when(x == xx)
        def _():
            for zz in range(2):
                for yy in range(2):
                    part = (2 * zz + xx) * 2 + yy
                    at = slice(part * part_columns, (part + 1) * part_columns)
                    for matrix in range(2):

                        @pl.when(c == 1 - matrix)
                        def _():
                            wide_send[2 * zz + yy] = wide_in[matrix, :, at].astype(BF16)

    wide_swap = push(wide_send, wide_got, sibling)
    loads[2].wait()
    down_out[...] = down_in[...].astype(BF16)
    relay(0)
    spread(1)
    wide_swap.wait_recv()
    for xx in range(2):

        @pl.when(x == xx)
        def _():
            for zz in range(2):
                for yy in range(2):
                    part = (2 * zz + xx) * 2 + yy
                    at = slice(part * part_columns, (part + 1) * part_columns)
                    got = wide_got[2 * zz + yy].astype(F32)
                    for matrix in range(2):

                        @pl.when(c == matrix)
                        def _():
                            own = wide_in[matrix, :, at]
                            both = [own, got] if matrix == 0 else [got, own]
                            wide_out[2 * zz + yy] = jnp.concatenate(both, axis=0).astype(BF16)

    def gu_at(zz, yy):
        return gu_w.at[c, pl.ds(pl.multiple_of((2 * zz + yy) * 2 * rows, 16), 2 * rows)]

    wide = []
    for k in (3, 2, 1, 0):
        for other in (1, 0):
            yy = 1 - y if other else y
            zz = p.z_xor(k)
            src = wide_out.at[2 * lax.rem(zz, 2) + yy]
            if k == 0 and other == 0:
                own_wide = pltpu.make_async_copy(src, gu_at(z, y), local.at[0])
                own_wide.start()
            else:
                wide.append((zz, yy, push(src, gu_at(z, y), p.at(y=yy, z=zz))))
    down_rows = down_out.shape[0]
    down_at = dn_w.at[pl.ds(pl.multiple_of(c * down_rows, 16), down_rows)]
    source_z = 2 * zl + x
    first_down = w.used
    w.used += 2
    down_sends = []
    for half in range(2):
        zz = 2 * half + zh
        copy = pltpu.make_async_remote_copy(
            src_ref=down_out,
            dst_ref=down_at,
            send_sem=send.at[first_down + half],
            recv_sem=recv.at[first_down],
            device_id=p.at(z=zz),
            device_id_type=MESH,
        )
        need = (x == zl) & (zz != z)
        pl.when(need)(copy.start)
        down_sends.append((need, copy))
    own_down = pltpu.make_async_copy(down_out, down_at, local.at[1])
    pl.when(source_z == z)(own_down.start)

    tok_f = tok[...].astype(F32)
    length, width = tok_f.shape
    head = k_low.shape[1]
    spread(2)
    relay(1)
    for copy in gain_line:
        copy.wait_recv()
    for k in range(1, 4):
        zz = p.z_xor(k)
        gain_side.append(push(gains_at(zz, y, c), gains_at(zz, y, c), plane[1]))
    row_seg = seg_row[...].astype(F32)
    col_seg = seg_col[...].astype(F32)
    earlier = jnp.sum((row_seg < col_seg).astype(F32), axis=1, keepdims=True)
    index = lax.broadcasted_iota(jnp.int32, (length, 1), 0).astype(F32)
    rate_at = lax.broadcasted_iota(jnp.int32, (1, head // 2), 1).astype(F32)
    rates = jnp.exp(rate_at * (-2.0 * math.log(THETA) / head))
    angles = (index - earlier) * rates
    tables[0] = jnp.cos(angles)
    tables[1] = jnp.sin(angles)
    spread(3)
    relay(2)
    share(0)
    relay(3)
    for copy in gain_side:
        copy.wait_recv()
    gain_pair = []
    for zz in range(4):
        for yy in range(2):
            gain_pair.append(push(gains_at(zz, yy, c), gains_at(zz, yy, c), sibling))
    share(1)
    for copy in gain_pair:
        copy.wait_recv()
    packed = gains_s[...]
    for i, (size, per) in enumerate(
        ((width, rows),) * 4 + ((head, head // 16),) * 2
    ):
        gains_full[i, :, :size] = join_gains(packed, i, size, per)
    a_low[...] = (tok_f * norm_scale(tok_f) * gains_full[0]).astype(BF16)
    share(2)
    share(3)
    for copy in pairs:
        copy.wait_recv()
    saves = [
        pltpu.make_async_copy(qkv_s, qkv_w, local.at[2]),
        pltpu.make_async_copy(out_s, out_w, local.at[3]),
    ]
    for copy in saves:
        copy.start()

    cosine, sine = tables[0], tables[1]
    heads = q_low.shape[1] // head
    for i in range(heads + 2):
        at = slice(i * head, (i + 1) * head)
        value = jnp.dot(a_low[...], qkv_s[:, at], preferred_element_type=F32)
        if i < heads:
            qk_proj[:, at] = value
            q_low[:, at] = turn(
                value * norm_scale(value) * gains_full[4, :, :head], cosine, sine
            ).astype(BF16)
        elif i == heads:
            qk_proj[:, at] = value
            k_low[...] = turn(
                value * norm_scale(value) * gains_full[5, :, :head], cosine, sine
            ).astype(BF16)
        else:
            v_low[...] = value.astype(BF16)
    i_at = lax.broadcasted_iota(jnp.int32, (length, length), 0)
    j_at = lax.broadcasted_iota(jnp.int32, (length, length), 1)
    allowed = (row_seg == col_seg) & (j_at <= i_at)
    for i in range(heads):
        at = slice(i * head, (i + 1) * head)
        scores = SCALE * lax.dot_general(
            q_low[:, at], k_low[...], (((1,), (1,)), ((), ())), preferred_element_type=F32
        )
        scores = jnp.where(allowed, scores, MASKED)
        expo = jnp.exp(scores - jnp.max(scores, axis=1, keepdims=True))
        prob = expo / jnp.sum(expo, axis=1, keepdims=True)
        probs[i] = prob
        o_low[:, at] = jnp.dot(
            prob.astype(BF16), v_low[...], preferred_element_type=F32
        ).astype(BF16)
    third = width // 3
    for i in range(3):
        at = slice(i * third, (i + 1) * third)
        attn_proj[:, at] = jnp.dot(o_low[...], out_s[:, at], preferred_element_type=F32)
    proj = attn_proj[...]
    mid = tok_f + proj * norm_scale(proj) * gains_full[1]
    h_mid[...] = mid
    m_low[...] = (mid * norm_scale(mid) * gains_full[2]).astype(BF16)

    finish = cube_gather_steps(p, w, m_low, every, local.at[4], started)
    next(finish)
    own_wide.wait()
    shared = [push(gu_at(z, y), gu_at(z, y), sibling)]
    next(finish)
    for zz, yy, copy in reversed(wide):
        copy.wait_recv()
        shared.append(push(gu_at(zz, yy), gu_at(zz, yy), sibling))
    next(finish)
    pl.when(source_z == z)(own_down.wait)
    pl.when(source_z != z)(down_sends[0][1].wait_recv)
    shared.append(push(down_at, down_at, sibling))
    for _ in finish:
        pass
    for copy in shared:
        copy.wait_recv()
    for copy in saves:
        copy.wait()
    for need, copy in down_sends:
        pl.when(need)(copy.wait_send)
    for copy in started:
        copy.wait_send()


def cube_gather_steps(p, w, block, every, own_sem, started):
    near = {bit: p.cube(bit) for bit in (X, Y, Z)}

    def push(src, dst, bit):
        copy = w.remote(src, dst, near[bit])
        copy.start()
        started.append(copy)
        return copy

    rows = block.shape[0]
    half = rows // 2
    own = pltpu.make_async_copy(block, every.at[0], own_sem)
    own.start()
    arrivals = {}
    for h in range(2):
        at = pl.ds(h * half, half)
        for bit in (X, Y, Z):
            arrivals[bit, h] = push(block.at[at], every.at[bit, at], bit)
    yield
    for h in range(2):
        at = pl.ds(h * half, half)
        for link, relay in ((X, Y), (Y, Z), (Z, X)):
            arrivals[relay, h].wait_recv()
            arrivals[link | relay, h] = push(every.at[relay, at], every.at[link | relay, at], link)
    yield
    last = []
    for h in range(2):
        for (start, size), link, relay in zip(thirds(half), (X, Y, Z), (Y | Z, X | Z, X | Y)):
            at = pl.ds(h * half + start, size)
            arrivals[relay, h].wait_recv()
            last.append(push(every.at[relay, at], every.at[7, at], link))
    yield
    for copy in last:
        copy.wait_recv()
    own.wait()


def front(tok, segments, w_q, w_k, w_v, w_o, gains, w_gate, w_up, w_down, head):
    length, width = tok.shape
    rows, mix = w_q.shape
    hidden = w_gate.shape[1]
    part = hidden // 8
    down_rows = w_down.shape[0]
    total = mix + 2 * head
    heads = mix // head
    columns = total // 4
    struct = jax.ShapeDtypeStruct
    shapes = (
        struct((16 * rows, total), BF16),
        struct((16 * w_o.shape[0], width), BF16),
        struct((2, 16 * rows, part), BF16),
        struct((2 * down_rows, width), BF16),
        struct((8, length, width), BF16),
        struct((8, 1, width), F32),
        struct((length, width), BF16),
        struct((length, mix + head), F32),
        struct((length, mix), BF16),
        struct((length, head), BF16),
        struct((length, head), BF16),
        struct((heads, length, length), F32),
        struct((length, mix), BF16),
        struct((length, width), F32),
        struct((length, width), F32),
        struct((2, length, head // 2), F32),
    )
    scratch = [
        pltpu.VMEM((16 * rows, total), BF16),
        pltpu.VMEM((4, rows, columns), F32),
        pltpu.VMEM((rows, columns), BF16),
        pltpu.VMEM((rows, columns), BF16),
        pltpu.VMEM(w_o.shape, BF16),
        pltpu.VMEM(gains.shape, F32),
        pltpu.VMEM((16,) + gains.shape, F32),
        pltpu.VMEM((2, rows, hidden), F32),
        pltpu.VMEM((4, rows, part), BF16),
        pltpu.VMEM((4, rows, part), BF16),
        pltpu.VMEM((4, 2 * rows, part), BF16),
        pltpu.VMEM((down_rows, width), F32),
        pltpu.VMEM((down_rows, width), BF16),
        pltpu.VMEM((length, width), BF16),
        pltpu.VMEM((16 * w_o.shape[0], width), BF16),
    ]
    return pl.pallas_call(
        front_kernel,
        out_shape=shapes,
        in_specs=[vmem()] * 8 + [hbm()] * 3,
        out_specs=(hbm(),) * 5 + (vmem(),) * 11,
        scratch_shapes=scratch + sems(128) + [pltpu.SemaphoreType.DMA((5,))],
        compiler_params=params(0),
        name="front",
    )(
        tok, segments, segments.reshape(-1, 1), w_q, w_k, w_v, w_o, gains, w_gate, w_up, w_down
    )


def dot_rows(left, right):
    return lax.dot_general(left, right, (((0,), (0,)), ((), ())), preferred_element_type=F32)


def dot_columns(left, right):
    return lax.dot_general(left, right, (((1,), (1,)), ((), ())), preferred_element_type=F32)


def back_kernel(
    tok, d_out, d_normed, gains_full, a_low, qk_proj, q_low, k_low, v_low, probs, o_low, attn_proj,
    h_mid, tables, g_mpost, qkv_hbm, out_hbm, gu, dn,
    grad_x, grad_qkv, grad_out, grad_gains, grad_gu, grad_dn,
    qkv_w, out_w, wide_in, wide_got, wide_sum, wide_far, down_in, down_got, down_sum, down_far,
    down_end, d_input, wide_end, wide_swap, wide_back, d_attn, d_mid, d_mix, d_qkv, dqkv, dout, q1, o1, q2, o2, q3, o3, qe, oe,
    gain_acc, gain_got, send, recv, local,
):
    p = Place()
    w = Wires(send, recv)
    x, y, z, c, zl, zh = p.x, p.y, p.z, p.c, p.zl, p.zh
    sibling = p.at(c=1 - c)
    plane = [p.at(x=1 - x), p.at(y=1 - y), p.at(x=1 - x, y=1 - y)]
    line = [p.at(z=p.z_xor(k)) for k in range(1, 4)]
    cube = [p.cube(bits) for bits in range(1, 8)]
    started = []

    def push(src, dst, device):
        copy = w.remote(src, dst, device)
        copy.start()
        started.append(copy)
        return copy

    def rows_of(ref, start, size):
        return ref.at[pl.ds(pl.multiple_of(start, 16), size)]

    loads = [
        pltpu.make_async_copy(gu.at[c], wide_in, local.at[0]),
        pltpu.make_async_copy(dn, down_in, local.at[1]),
        pltpu.make_async_copy(out_hbm, out_w, local.at[2]),
        pltpu.make_async_copy(qkv_hbm, qkv_w, local.at[3]),
    ]
    for copy in loads:
        copy.start()
    greet([sibling] + plane + line + [p.cube(5), p.cube(7), p.cube(3)])

    width = tok.shape[1]
    chip_rows = wide_in.shape[0] // 8
    down_rows = down_sum.shape[0]
    half_rows = 4 * chip_rows
    far_half = half_rows * (1 - zh)
    near_half = half_rows * zh
    wide_one = [
        push(rows_of(gu.at[1 - c], start, half_rows), rows_of(wide_got, start, half_rows), sibling)
        for start in (far_half, near_half)
    ]
    down_one = push(rows_of(dn, down_rows * (1 - c), down_rows), down_got, sibling)

    mid = h_mid[...]
    d_value, g_mpre = norm_pull(mid, norm_scale(mid), gains_full[2], d_normed[...])
    d_mid[...] = d_out[...].astype(F32) + d_value
    proj = attn_proj[...]
    d_value, g_apost = norm_pull(proj, norm_scale(proj), gains_full[1], d_mid[...])
    d_attn[...] = d_value.astype(BF16)
    gain_acc[0, 2:3, :] = g_mpre
    gain_acc[0, 1:2, :] = g_apost

    loads[0].wait()
    loads[1].wait()
    wide_one[0].wait_recv()
    order = (3, 1, 2, 0)

    def piece(i):
        to_z = 1 - zl if i // 2 else zl
        to_y = 1 - y if i % 2 else y
        return (2 * to_z + to_y) * chip_rows

    wide_two = {}
    for i in order:
        rows = pl.ds(pl.multiple_of(far_half + piece(i), 16), chip_rows)
        at = pl.ds(i * chip_rows, chip_rows)
        wide_sum[at, :] = add(wide_in[rows, :], wide_got[rows, :])
        wide_two[i] = push(wide_sum.at[at], wide_far.at[at], line[1])
    down_one.wait_recv()
    down_sum[...] = add(down_in[pl.ds(pl.multiple_of(down_rows * c, 16), down_rows), :], down_got[...])
    down_two = w.remote(down_sum, down_far, line[1])
    mine = zl == zh
    pl.when(zl != zh)(down_two.start)

    third = width // 3
    for i in range(3):
        at = slice(i * third, (i + 1) * third)
        dout[:, at] = dot_rows(o_low[...], d_attn[:, at]).astype(BF16)
    out_rows = dout.shape[0] // 32
    columns = dqkv.shape[1] // 4

    def out_at(ref, zz, yy, quarter):
        return rows_of(ref, (2 * zz + yy) * 4 * out_rows + quarter * out_rows, out_rows)

    out_one = [
        push(
            out_at(dout, zz, yy, 2 * xx + 1 - c),
            o1.at[xx, yy, pl.ds(zz * out_rows, out_rows)],
            sibling,
        )
        for zz in range(4)
        for yy in range(2)
        for xx in range(2)
    ]
    loads[2].wait()
    d_mix[...] = dot_columns(d_attn[...], out_w[...]).astype(BF16)

    cosine, sine = tables[0], tables[1]
    head = k_low.shape[1]
    heads = q_low.shape[1] // head
    d_k, d_v, g_q = 0.0, 0.0, 0.0
    for i in range(heads):
        at = slice(i * head, (i + 1) * head)
        prob = probs[i]
        d_probs = dot_columns(d_mix[:, at], v_low[...])
        row_dot = jnp.sum(prob * d_probs, axis=1, keepdims=True)
        d_scores = (prob * (d_probs - row_dot)).astype(BF16)
        d_q = SCALE * jnp.dot(d_scores, k_low[...], preferred_element_type=F32)
        d_k = d_k + dot_rows(d_scores, q_low[:, at])
        d_v = d_v + dot_rows(prob.astype(BF16), d_mix[:, at])
        value = qk_proj[:, at]
        d_value, gain = norm_pull(
            value, norm_scale(value), gains_full[4, :, :head], turn_back(d_q, cosine, sine)
        )
        g_q = g_q + gain
        d_qkv[:, at] = d_value.astype(BF16)
    at = slice(heads * head, (heads + 1) * head)
    value = qk_proj[:, at]
    d_value, g_k = norm_pull(
        value, norm_scale(value), gains_full[5, :, :head], turn_back(SCALE * d_k, cosine, sine)
    )
    d_qkv[:, at] = d_value.astype(BF16)
    d_qkv[:, (heads + 1) * head :] = d_v.astype(BF16)
    gain_acc[0, 4:5, :] = jnp.zeros((1, width), F32)
    gain_acc[0, 5:8, :] = jnp.zeros((3, width), F32)
    gain_acc[0, 4:5, :head] = g_q
    gain_acc[0, 5:6, :head] = g_k
    for i in range(heads + 2):
        at = slice(i * head, (i + 1) * head)
        dqkv[:, at] = dot_rows(a_low[...], d_qkv[:, at]).astype(BF16)

    def qkv_columns(ref, quarter):
        return ref.at[:, pl.ds(pl.multiple_of(quarter * columns, 128), columns)]

    qkv_one = [push(qkv_columns(dqkv, 2 * xx + 1 - c), q1.at[xx], sibling) for xx in range(2)]

    loads[3].wait()
    tok_f = tok[...].astype(F32)
    for i in range(3):
        at = slice(i * third, (i + 1) * third)
        d_input[:, at] = dot_columns(d_qkv[...], qkv_w[at, :])
    d_value, g_apre = norm_pull(tok_f, norm_scale(tok_f), gains_full[0], d_input[...])
    grad_x[...] = (d_mid[...] + d_value).astype(BF16)
    gain_acc[0, 0:1, :] = g_apre
    gain_acc[0, 3:4, :] = g_mpost[...]
    gain_one = push(gain_acc.at[0], gain_got.at[0], sibling)

    for copy in out_one + qkv_one:
        copy.wait_recv()

    def plane_part(xx, yy, q_ref, o_ref):
        at = pl.ds(pl.multiple_of((2 * xx + c) * columns, 128), columns)
        for zz in range(4):
            rows = pl.ds(pl.multiple_of((2 * zz + yy) * chip_rows, 16), chip_rows)
            q_ref[zz * chip_rows : (zz + 1) * chip_rows, :] = add(dqkv[rows, at], q1[xx, rows, :])
            start = pl.multiple_of(((2 * zz + yy) * 4 + 2 * xx + c) * out_rows, 16)
            here = slice(zz * out_rows, (zz + 1) * out_rows)
            o_ref[here, :] = add(dout[pl.ds(start, out_rows), :], o1[xx, yy, here, :])

    second = {}
    for i in (2, 0, 1):
        plane_part(x if i == 1 else 1 - x, y if i == 0 else 1 - y, q2.at[i], o2.at[i])
        second[i] = (push(q2.at[i], q2.at[3 + i], plane[i]), push(o2.at[i], o2.at[3 + i], plane[i]))
    gain_one.wait_recv()
    gain_acc[1] = gain_acc[0] + gain_got[0]
    gain_two = [push(gain_acc.at[1], gain_got.at[1 + i], plane[i]) for i in range(3)]
    plane_part(x, y, q3, o3)

    part = (2 * zl + x) * 2 + y
    wide_three, own_wide = [], []

    def wide_on(i):
        at = pl.ds(i * chip_rows, chip_rows)
        rows = pl.ds(pl.multiple_of(near_half + piece(i), 16), chip_rows)
        wide_two[i].wait_recv()
        own = wide_in[rows, :].astype(F32) + wide_got[rows, :].astype(F32)
        wide_far[at, :] = (own + wide_far[at, :].astype(F32)).astype(BF16)
        for over in (1, 0):
            bits = 4 * over + 2 * (i % 2) + i // 2
            if bits:
                wide_three.append(push(wide_far.at[at], wide_end.at[part], p.cube(bits)))
            else:
                own_wide.append(
                    pltpu.make_async_copy(wide_far.at[at], wide_end.at[part], local.at[4])
                )
                own_wide[0].start()

    wide_one[1].wait_recv()
    wide_on(3)
    for i in range(3):
        for copy in second[i]:
            copy.wait_recv()
    q3[...] = add(
        q3[...].astype(F32) + q2[3].astype(F32), q2[4].astype(F32) + q2[5].astype(F32)
    )
    o3[...] = add(
        o3[...].astype(F32) + o2[3].astype(F32), o2[4].astype(F32) + o2[5].astype(F32)
    )
    third_step = []
    for k in range(1, 4):
        zz = p.z_xor(k)
        third_step += [
            push(rows_of(q3, zz * chip_rows, chip_rows), qe.at[k], line[k - 1]),
            push(rows_of(o3, zz * out_rows, out_rows), oe.at[k], line[k - 1]),
        ]
    for copy in gain_two:
        copy.wait_recv()
    gain_acc[2] = gain_acc[1] + gain_got[1] + gain_got[2] + gain_got[3]
    gain_three = [push(gain_acc.at[2], gain_got.at[3 + k], line[k - 1]) for k in range(1, 4)]
    wide_on(1)
    for copy in third_step:
        copy.wait_recv()
    start = pl.multiple_of(z * chip_rows, 16)
    qe[0] = add(
        q3[pl.ds(start, chip_rows), :].astype(F32) + qe[1].astype(F32),
        qe[2].astype(F32) + qe[3].astype(F32),
    )
    start = pl.multiple_of(z * out_rows, 16)
    oe[0] = add(
        o3[pl.ds(start, out_rows), :].astype(F32) + oe[1].astype(F32),
        oe[2].astype(F32) + oe[3].astype(F32),
    )
    last = [
        push(qe.at[0], qe.at[4 + i], device)
        for i, device in enumerate((sibling, plane[0]))
    ] + [
        push(oe.at[0], oe.at[4 + i], device)
        for i, device in enumerate((sibling, plane[0]))
    ]
    wide_on(2)
    for copy in last:
        copy.wait_recv()
    relay = [push(qe.at[5], qe.at[6], sibling), push(oe.at[5], oe.at[6], sibling)]
    wide_on(0)

    arrive = w.used
    w.used += 3
    down_three = []
    for xx in range(2):
        copy = pltpu.make_async_remote_copy(
            src_ref=down_far,
            dst_ref=down_end,
            send_sem=send.at[arrive + xx],
            recv_sem=recv.at[arrive],
            device_id=p.at(x=xx, z=2 * zh + x),
            device_id_type=MESH,
        )
        down_three.append((mine & ((x != xx) | (zh != x)), copy))
    down_here = mine & (x == zl)

    @pl.when(mine)
    def _():
        down_two.wait_recv()
        down_far[...] = add(down_sum[...], down_far[...])

    down_own = pltpu.make_async_copy(down_far, down_end, local.at[5])
    for need, copy in down_three:
        pl.when(need)(copy.start)
    pl.when(down_here)(down_own.start)

    for copy in relay:
        copy.wait_recv()
    rows = chip_rows // 2
    for xx in range(2):
        for cc in range(2):

            @pl.when((x == xx) & (c == cc))
            def _():
                for i, q in ((0, 2 * xx + cc), (4, 2 * xx + 1 - cc), (5, 2 * (1 - xx) + cc), (6, 2 * (1 - xx) + 1 - cc)):
                    both = qe[i].astype(F32)
                    grad_qkv[:, q * columns : (q + 1) * columns] = both[cc * rows : (cc + 1) * rows]
                    if q // 2 == cc:
                        grad_out[(q % 2) * out_rows : (q % 2 + 1) * out_rows, :] = oe[i].astype(F32)

    for copy in gain_three:
        copy.wait_recv()
    grad_gains[...] = gain_acc[2] + gain_got[4] + gain_got[5] + gain_got[6]

    own_wide[0].wait()
    for copy in wide_three:
        copy.wait_recv()
    for cc in range(2):

        @pl.when(c == cc)
        def _():
            for s in range(8):
                extra = (rows + 15) // 16 * 16
                at = slice(0, extra) if cc == 1 else slice(2 * rows - extra, 2 * rows)
                wide_swap[s] = wide_end[s, at, :]

    final = push(wide_swap, wide_back, sibling)
    pl.when(down_here)(down_own.wait)
    pl.when(jnp.logical_not(down_here))(down_three[0][1].wait_recv)
    grad_dn[...] = down_end[...].astype(F32)
    final.wait_recv()
    for cc in range(2):

        @pl.when(c == cc)
        def _():
            extra = (rows + 15) // 16 * 16
            size = wide_end.shape[2]
            for s in range(8):
                at = slice(s * size, (s + 1) * size)
                own = wide_end[s].astype(F32)[cc * rows : (cc + 1) * rows]
                other = wide_back[s].astype(F32)
                other = other[:rows] if cc == 0 else other[extra - rows :]
                grad_gu[cc, :, at] = own
                grad_gu[1 - cc, :, at] = other

    for need, copy in down_three:
        pl.when(need)(copy.wait_send)
    pl.when(zl != zh)(down_two.wait_send)
    for copy in started:
        copy.wait_send()


def back(
    tok, d_out, d_normed, gains_full, saved, g_mpost, qkv_w, out_w, grad_gu, grad_dn, rows, out_rows
):
    length, width = tok.shape
    total = qkv_w.shape[1]
    columns = total // 4
    mix = out_w.shape[0]
    _, _, part = grad_gu.shape
    down_rows = grad_dn.shape[0] // 2
    chip_rows = 2 * rows
    extra = (rows + 15) // 16 * 16
    piece = out_rows // 2
    struct = jax.ShapeDtypeStruct
    shapes = (
        struct((length, width), BF16),
        struct((rows, total), F32),
        struct((out_rows, width), F32),
        struct((8, width), F32),
        struct((2, rows, 8 * part), F32),
        struct((down_rows, width), F32),
    )
    scratch = [
        pltpu.VMEM(qkv_w.shape, BF16),
        pltpu.VMEM(out_w.shape, BF16),
        pltpu.VMEM((width, part), BF16),
        pltpu.VMEM((width, part), BF16),
        pltpu.VMEM((width // 2, part), BF16),
        pltpu.VMEM((width // 2, part), BF16),
        pltpu.VMEM(grad_dn.shape, BF16),
        pltpu.VMEM((down_rows, width), BF16),
        pltpu.VMEM((down_rows, width), BF16),
        pltpu.VMEM((down_rows, width), BF16),
        pltpu.VMEM((down_rows, width), BF16),
        pltpu.VMEM((length, width), F32),
        pltpu.VMEM((8, chip_rows, part), BF16),
        pltpu.VMEM((8, extra, part), BF16),
        pltpu.VMEM((8, extra, part), BF16),
        pltpu.VMEM((length, width), BF16),
        pltpu.VMEM((length, width), F32),
        pltpu.VMEM((length, mix), BF16),
        pltpu.VMEM((length, total), BF16),
        pltpu.VMEM((width, total), BF16),
        pltpu.VMEM((mix, width), BF16),
        pltpu.VMEM((2, width, columns), BF16),
        pltpu.VMEM((2, 2, 4 * piece, width), BF16),
        pltpu.VMEM((6, 4 * chip_rows, columns), BF16),
        pltpu.VMEM((6, 4 * piece, width), BF16),
        pltpu.VMEM((4 * chip_rows, columns), BF16),
        pltpu.VMEM((4 * piece, width), BF16),
        pltpu.VMEM((7, chip_rows, columns), BF16),
        pltpu.VMEM((7, piece, width), BF16),
        pltpu.VMEM((3, 8, width), F32),
        pltpu.VMEM((7, 8, width), F32),
    ]
    return pl.pallas_call(
        back_kernel,
        out_shape=shapes,
        in_specs=[vmem()] * 15 + [hbm()] * 4,
        out_specs=(vmem(),) * 6,
        scratch_shapes=scratch + sems(96) + [pltpu.SemaphoreType.DMA((6,))],
        compiler_params=params(3),
        name="back",
    )(tok, d_out, d_normed, gains_full, *saved, g_mpost, qkv_w, out_w, grad_gu, grad_dn)


GELU_ROOT = math.sqrt(2.0 / math.pi)


def gelu_parts(gate):
    square = gate * gate
    bend = jnp.tanh(GELU_ROOT * gate * (1.0 + 0.044715 * square))
    half = 0.5 * (1.0 + bend)
    slope = half + 0.5 * gate * (1.0 - bend * bend) * GELU_ROOT * (1.0 + 3 * 0.044715 * square)
    return half * gate, slope


def tiles(size, step):
    return [slice(at, min(at + step, size)) for at in range(0, size, step)]


class CubeSum:
    MIDDLE = ((X, Y, Y | Z), (Y, Z, X | Z), (Z, X, X | Y))
    NEAR = ((Y, Z), (Z, X), (X, Y))

    def __init__(self, p, w, parts, third, second, first):
        self.p, self.w, self.parts = p, w, parts
        self.third, self.second, self.first = third, second, first
        self.half = parts.shape[1] // 2
        self.started = []
        self.far, self.mid, self.end = {}, {}, {}

    def push(self, src, dst, bit):
        copy = self.w.remote(src, dst, self.p.cube(bit))
        copy.start()
        self.started.append(copy)
        return copy

    def send_far(self):
        for h in range(2):
            for (start, size), link in zip(thirds(self.half), (X, Y, Z)):
                at = pl.ds(h * self.half + start, size)
                self.far[link, h] = self.push(self.parts.at[7, at], self.third.at[at], link)

    def send_middle(self):
        for h in range(2):
            for i, (link, onward, place) in enumerate(self.MIDDLE):
                start, size = thirds(self.half)[i]
                at = pl.ds(h * self.half + start, size)
                all_at = pl.ds(h * self.half, self.half)
                self.far[link, h].wait_recv()
                self.parts[place, at] = add(self.parts[place, at], self.third[at, :])
                self.mid[onward, h] = self.push(
                    self.parts.at[place, all_at], self.second.at[i, all_at], onward
                )

    def send_near(self):
        for h in range(2):
            at = pl.ds(h * self.half, self.half)
            for i, (came, place) in enumerate(self.NEAR):
                self.mid[came, h].wait_recv()
                self.parts[place, at] = add(self.parts[place, at], self.second[i, at])
                self.end[place, h] = self.push(
                    self.parts.at[place, at], self.first.at[i, at], place
                )

    def finish(self):
        for h in range(2):
            at = pl.ds(h * self.half, self.half)
            value = self.parts[0, at].astype(F32)
            for i, (_, place) in enumerate(self.NEAR):
                self.end[place, h].wait_recv()
                value = value + self.first[i, at].astype(F32)
            yield at, value

    def wait_sent(self):
        for copy in self.started:
            copy.wait_send()
        self.started = []


class CubeGather:
    def __init__(self, p, w, block, every):
        self.p, self.w, self.block, self.every = p, w, block, every
        self.half = block.shape[0] // 2
        self.started = []
        self.near, self.middle, self.far = {}, {}, {}

    def push(self, src, dst, bit):
        copy = self.w.remote(src, dst, self.p.cube(bit))
        copy.start()
        self.started.append(copy)
        return copy

    def send_near(self, h):
        at = pl.ds(h * self.half, self.half)
        for bit in (X, Y, Z):
            self.near[bit, h] = self.push(self.block.at[at], self.every.at[bit, at], bit)

    def send_middle(self, h):
        at = pl.ds(h * self.half, self.half)
        for link, relay in ((X, Y), (Y, Z), (Z, X)):
            self.near[relay, h].wait_recv()
            self.middle[link | relay, h] = self.push(
                self.every.at[relay, at], self.every.at[link | relay, at], link
            )

    def send_far(self, h):
        for (start, size), link, relay in zip(thirds(self.half), (X, Y, Z), (Y | Z, X | Z, X | Y)):
            at = pl.ds(h * self.half + start, size)
            self.middle[relay, h].wait_recv()
            self.far[link, h] = self.push(self.every.at[relay, at], self.every.at[7, at], link)

    def wait_far(self):
        for copy in self.far.values():
            copy.wait_recv()

    def wait_sent(self):
        for copy in self.started:
            copy.wait_send()
        self.started = []


def mlp_kernel(
    every, gu, dn, h_mid, d_out, gains_full,
    layer_out, d_normed, g_mpost, grad_gu, grad_dn,
    m_all, wide_w, down_w, gate, up, hidden, dd_own, dd_all, parts, third, second, first,
    send, recv, local,
):
    p = Place()
    w = Wires(send, recv)
    order = (7, 3, 5, 6, 4, 2, 1, 0)
    loads = {r: pltpu.make_async_copy(every.at[r], m_all.at[r], local.at[r]) for r in order}
    wide_load = pltpu.make_async_copy(gu, wide_w, local.at[8])
    down_load = pltpu.make_async_copy(dn, down_w, local.at[9])
    wide_load.start()
    loads[7].start()
    down_load.start()
    for r in order[1:]:
        loads[r].start()
    greet([p.cube(X), p.cube(Y), p.cube(Z)])

    length, width = m_all.shape[1:]
    part = gate.shape[-1]
    wide_tiles = tiles(part, 256)
    down_tiles = tiles(width, 384)

    def forward(r):
        for at in wide_tiles:
            g = jnp.dot(m_all[r], wide_w[0, :, at], preferred_element_type=F32)
            u = jnp.dot(m_all[r], wide_w[1, :, at], preferred_element_type=F32)
            gate[r, :, at] = g
            up[r, :, at] = u
            value, _ = gelu_parts(g)
            hidden[r, :, at] = (value * u).astype(BF16)
        for at in down_tiles:
            parts[r, :, at] = jnp.dot(
                hidden[r], down_w[:, at], preferred_element_type=F32
            ).astype(BF16)

    def backward(r):
        for at in wide_tiles:
            d_hidden = dot_columns(dd_all[r], down_w[at, :])
            value, slope = gelu_parts(gate[r, :, at])
            d_gate = d_hidden * up[r, :, at] * slope
            gate[r, :, at] = d_gate.astype(BF16).astype(F32)
            up[r, :, at] = (d_hidden * value).astype(BF16).astype(F32)
        d_gate = gate[r].astype(BF16)
        d_up = up[r].astype(BF16)
        for at in down_tiles:
            parts[r, :, at] = (
                dot_columns(d_gate, wide_w[0, at, :]) + dot_columns(d_up, wide_w[1, at, :])
            ).astype(BF16)

    def several(step, places):
        lax.fori_loop(0, 3, lambda i, _: (step(places(i)), 0)[1], 0)

    def middles(i):
        return 7 - lax.shift_right_logical(jnp.int32(4), i)

    def nears(i):
        return lax.shift_right_logical(jnp.int32(4), i)

    total = CubeSum(p, w, parts, third, second, first)
    wide_load.wait()
    loads[7].wait()
    down_load.wait()
    forward(7)
    total.send_far()
    for r in order[1:]:
        loads[r].wait()
    several(forward, middles)
    total.send_middle()
    several(forward, nears)
    total.send_near()
    forward(0)

    gather = CubeGather(p, w, dd_own, dd_all)
    gain = gains_full[3]
    g_rows = 0.0
    for h, (at, value) in enumerate(total.finish()):
        scale = norm_scale(value)
        layer_out[at, :] = (h_mid[at, :] + value * scale * gain).astype(BF16)
        d_value, g_part = norm_pull(value, scale, gain, d_out[at, :].astype(F32))
        dd_own[at, :] = d_value.astype(BF16)
        g_rows = g_rows + g_part
        gather.send_near(h)
    g_mpost[...] = g_rows
    dd_all[0] = dd_own[...]
    total.wait_sent()
    backward(0)
    gather.send_middle(0)
    gather.send_middle(1)
    several(backward, nears)
    gather.send_far(0)
    gather.send_far(1)
    several(backward, middles)
    gather.wait_far()
    backward(7)

    total = CubeSum(p, w, parts, third, second, first)
    total.send_far()
    grad_rows = 384

    all_rows = 8 * length
    for at in down_tiles:
        grad_dn[:, at] = dot_rows(
            hidden[...].reshape(all_rows, part), dd_all[:, :, at].reshape(all_rows, -1)
        ).astype(BF16)
    total.send_middle()
    for matrix, held in ((0, gate), (1, up)):
        hidden[...] = held[...].astype(BF16)

        def grad_wide(i, _):
            at = pl.ds(pl.multiple_of(i * grad_rows, 128), grad_rows)
            left = m_all[:, :, at].reshape(all_rows, grad_rows)
            grad_gu[matrix, at, :] = dot_rows(left, hidden[...].reshape(all_rows, part)).astype(BF16)
            return 0

        lax.fori_loop(0, width // grad_rows, grad_wide, 0)
        if matrix == 0:
            total.send_near()
    for at, value in total.finish():
        d_normed[at, :] = value
    total.wait_sent()
    gather.wait_sent()


def mlp(every, gu, dn, h_mid, d_out, gains_full):
    _, length, width = every.shape
    part = dn.shape[0]
    struct = jax.ShapeDtypeStruct
    blocks = (8, length, width)
    return pl.pallas_call(
        mlp_kernel,
        out_shape=(
            struct((length, width), BF16),
            struct((length, width), F32),
            struct((1, width), F32),
            struct(gu.shape, BF16),
            struct(dn.shape, BF16),
        ),
        in_specs=[hbm()] * 3 + [vmem()] * 3,
        out_specs=(vmem(),) * 5,
        scratch_shapes=[
            pltpu.VMEM(blocks, BF16),
            pltpu.VMEM(gu.shape, BF16),
            pltpu.VMEM(dn.shape, BF16),
            pltpu.VMEM((8, length, part), F32),
            pltpu.VMEM((8, length, part), F32),
            pltpu.VMEM((8, length, part), BF16),
            pltpu.VMEM((length, width), BF16),
            pltpu.VMEM(blocks, BF16),
            pltpu.VMEM(blocks, BF16),
            pltpu.VMEM((length, width), BF16),
            pltpu.VMEM((3, length, width), BF16),
            pltpu.VMEM((3, length, width), BF16),
        ]
        + sems(64)
        + [pltpu.SemaphoreType.DMA((10,))],
        compiler_params=params(1),
        name="mlp",
    )(every, gu, dn, h_mid, d_out, gains_full)


def pack_gains(vectors):
    rows = [jnp.pad(v, (0, 128 - v.shape[0])) for v in vectors]
    return jnp.concatenate(rows + [jnp.zeros(((8 - len(rows)) * 128,), F32)]).reshape(8, 128)


def cube_body(
    layer_in, d_out, segments, w_q, w_k, w_v, w_o, attn_pre, attn_post, q_gain, k_gain,
    w_gate, w_up, w_down, mlp_pre, mlp_post,
):
    width = layer_in.shape[1]
    head = q_gain.shape[0] * 16
    rows, mix = w_q.shape
    gain_list = [attn_pre, attn_post, mlp_pre, mlp_post, q_gain, k_gain]
    (
        qkv_w, out_w, gu_w, down_w, m_all, gains_full, a_low, qk_proj, q_low, k_low, v_low,
        probs, o_low, attn_proj, h_mid, tables,
    ) = front(
        layer_in, segments, w_q, w_k, w_v, w_o, pack_gains(gain_list), w_gate, w_up, w_down, head
    )
    layer_out, d_normed, g_mpost, grad_gu, grad_wdown = mlp(
        m_all, gu_w, down_w, h_mid, d_out, gains_full
    )
    saved = (a_low, qk_proj, q_low, k_low, v_low, probs, o_low, attn_proj, h_mid, tables)
    grad_x, grad_qkv, grad_out, grad_gains, grad_gu, grad_dn = back(
        layer_in, d_out, d_normed, gains_full, saved, g_mpost, qkv_w, out_w, grad_gu,
        grad_wdown, rows, w_o.shape[0],
    )
    shard = lax.axis_index("fsdp")
    g_apre, g_apost, g_mpre, g_mpost, g_q, g_k = [
        lax.dynamic_slice(grad_gains[i], (shard * v.shape[0],), (v.shape[0],))
        for i, v in enumerate(gain_list)
    ]
    return (
        layer_out,
        grad_x,
        grad_qkv[:, :mix],
        grad_qkv[:, mix : mix + head],
        grad_qkv[:, mix + head :],
        grad_out,
        g_apre,
        g_apost,
        g_q,
        g_k,
        grad_gu[0],
        grad_gu[1],
        grad_dn,
        g_mpre,
        g_mpost,
    )


def solution(mesh):
    in_specs = (
        P(("replica", "fsdp"), None),
        P(("replica", "fsdp"), None),
        P(("replica", "fsdp"), None),
        P("fsdp", None),
        P("fsdp", None),
        P("fsdp", None),
        P("fsdp", None),
        P("fsdp"),
        P("fsdp"),
        P("fsdp"),
        P("fsdp"),
        P("fsdp", None),
        P("fsdp", None),
        P("fsdp", None),
        P("fsdp"),
        P("fsdp"),
    )
    out_specs = (
        P(("replica", "fsdp"), None),
        P(("replica", "fsdp"), None),
        P("fsdp", None),
        P("fsdp", None),
        P("fsdp", None),
        P("fsdp", None),
        P("fsdp"),
        P("fsdp"),
        P("fsdp"),
        P("fsdp"),
        P("fsdp", None),
        P("fsdp", None),
        P("fsdp", None),
        P("fsdp"),
        P("fsdp"),
    )
    body = cube_body if fits_cubes(mesh) else general_body
    return jax.shard_map(body, mesh=mesh, in_specs=in_specs, out_specs=out_specs, check_vma=False)
```

```python
from functools import partial
import math

import jax
import jax.numpy as jnp
from jax import lax
from jax.experimental import pallas as pl
from jax.experimental.pallas import tpu as pltpu
from jax.sharding import PartitionSpec as P

EPS = 1e-06
THETA = 1000000.0
SCALE = 0.0625
MASKED = -1e30


def norm_rows(values, gain):
    return values * lax.rsqrt(jnp.mean(values * values, axis=-1, keepdims=True) + EPS) * gain


def positions_of(segments):
    length = segments.shape[-1]
    index = jnp.arange(length, dtype=jnp.int32)
    earlier = jnp.concatenate([segments[:, :1] - 1, segments[:, :-1]], axis=1)
    starts = jnp.where(segments != earlier, index[None, :], jnp.zeros_like(segments))
    return index[None, :] - lax.cummax(starts, axis=1)


def angle_tables(segments, head_size):
    half_size = head_size // 2
    rates = jnp.exp(jnp.arange(half_size, dtype=jnp.float32) * (-2.0 * math.log(THETA) / head_size))
    angles = positions_of(segments).astype(jnp.float32)[..., None] * rates
    return (jnp.cos(angles), jnp.sin(angles))


def rotate(values, cosine, sine):
    half_size = values.shape[-1] // 2
    first_half = values[..., :half_size]
    second_half = values[..., half_size:]
    return jnp.concatenate(
        [first_half * cosine - second_half * sine, second_half * cosine + first_half * sine],
        axis=-1,
    )


def query_path(projected, gain, cosine, sine):
    shaped = projected.reshape(projected.shape[0], projected.shape[1], -1, gain.shape[0])
    return rotate(norm_rows(shaped, gain), cosine[:, :, None, :], sine[:, :, None, :])


def key_path(projected, gain, cosine, sine):
    return rotate(norm_rows(projected, gain), cosine, sine)


def gelu_product(gate_val, up_val):
    return jax.nn.gelu(gate_val, approximate=True) * up_val


def to_low(values):
    return values.astype(jnp.bfloat16)


def matmul(left, right):
    return jnp.dot(left, right, preferred_element_type=jnp.float32)


def matmul_left_t(left, right):
    return lax.dot_general(
        left, right, (((0,), (0,)), ((), ())), preferred_element_type=jnp.float32
    )


def matmul_right_t(left, right):
    return lax.dot_general(
        left, right, (((1,), (1,)), ((), ())), preferred_element_type=jnp.float32
    )


def attention_masks(segments):
    length = segments.shape[1]
    index = jnp.arange(length, dtype=jnp.int32)
    causal = index[None, :] <= index[:, None]
    return (segments[:, :, None] == segments[:, None, :]) & causal[None]


def scores_of(q_low, k_low, masks):
    scores = SCALE * jnp.einsum("nqhd,nkd->nhqk", q_low, k_low, preferred_element_type=jnp.float32)
    return jnp.where(masks[:, None], scores, MASKED)


def spread_gain(values):
    return jnp.broadcast_to(values[:, None], (values.shape[0], lax.axis_size("replica")))


def general_body(
    layer_in,
    d_out,
    segments,
    w_q,
    w_k,
    w_v,
    w_o,
    attn_pre,
    attn_post,
    q_gain,
    k_gain,
    w_gate,
    w_up,
    w_down,
    mlp_pre,
    mlp_post,
):
    attn_set = (
        lax.all_gather(to_low(w_q), "fsdp", axis=0, tiled=True),
        lax.all_gather(to_low(w_k), "fsdp", axis=0, tiled=True),
        lax.all_gather(to_low(w_v), "fsdp", axis=0, tiled=True),
        lax.all_gather(to_low(w_o), "fsdp", axis=0, tiled=True),
        lax.all_gather(to_low(attn_pre), "fsdp", axis=0, tiled=True),
        lax.all_gather(to_low(attn_post), "fsdp", axis=0, tiled=True),
        lax.all_gather(to_low(q_gain), "fsdp", axis=0, tiled=True),
        lax.all_gather(to_low(k_gain), "fsdp", axis=0, tiled=True),
    )
    q_full, k_full, v_full, o_full = (attn_set[0], attn_set[1], attn_set[2], attn_set[3])
    gain_apre = attn_set[4].astype(jnp.float32)
    gain_apost = attn_set[5].astype(jnp.float32)
    gain_q = attn_set[6].astype(jnp.float32)
    gain_k = attn_set[7].astype(jnp.float32)
    mlp_set = (
        lax.all_gather(to_low(w_gate), "fsdp", axis=0, tiled=True),
        lax.all_gather(to_low(w_up), "fsdp", axis=0, tiled=True),
        lax.all_gather(to_low(w_down), "fsdp", axis=0, tiled=True),
        lax.all_gather(to_low(mlp_pre), "fsdp", axis=0, tiled=True),
        lax.all_gather(to_low(mlp_post), "fsdp", axis=0, tiled=True),
    )
    gate_full, up_full, down_full = (mlp_set[0], mlp_set[1], mlp_set[2])
    gain_mpre = mlp_set[3].astype(jnp.float32)
    gain_mpost = mlp_set[4].astype(jnp.float32)
    seq_count, seq_len = segments.shape
    tok_flat = layer_in.astype(jnp.float32)
    cosine, sine = angle_tables(segments, gain_q.shape[0])
    masks = attention_masks(segments)
    normed_a, pull_a = jax.vjp(norm_rows, tok_flat, gain_apre)
    a_low = to_low(normed_a)
    q_proj = matmul(a_low, q_full).reshape(seq_count, seq_len, -1)
    k_proj = matmul(a_low, k_full).reshape(seq_count, seq_len, -1)
    v_proj = matmul(a_low, v_full)
    q_rot, pull_q = jax.vjp(partial(query_path, cosine=cosine, sine=sine), q_proj, gain_q)
    k_rot, pull_k = jax.vjp(partial(key_path, cosine=cosine, sine=sine), k_proj, gain_k)
    q_low = to_low(q_rot)
    k_low = to_low(k_rot)
    v_low = to_low(v_proj).reshape(seq_count, seq_len, -1)
    scores = scores_of(q_low, k_low, masks)
    top_val = jnp.max(scores, axis=-1, keepdims=True)
    log_total = top_val + jnp.log(jnp.sum(jnp.exp(scores - top_val), axis=-1, keepdims=True))
    p_low = to_low(jnp.exp(scores - log_total))
    attn_mix = jnp.einsum("nhqk,nkd->nqhd", p_low, v_low, preferred_element_type=jnp.float32)
    o_low = to_low(attn_mix.reshape(seq_count * seq_len, -1))
    attn_proj = matmul(o_low, o_full)
    post_attn, pull_pa = jax.vjp(norm_rows, attn_proj, gain_apost)
    h_mid = tok_flat + post_attn
    normed_m, pull_m = jax.vjp(norm_rows, h_mid, gain_mpre)
    m_low = to_low(normed_m)
    gate_val = matmul(m_low, gate_full)
    up_val = matmul(m_low, up_full)
    hidden, pull_h = jax.vjp(gelu_product, gate_val, up_val)
    h_low = to_low(hidden)
    down_val = matmul(h_low, down_full)
    post_mlp, pull_pm = jax.vjp(norm_rows, down_val, gain_mpost)
    layer_out = (h_mid + post_mlp).astype(jnp.bfloat16)
    gate_full, up_full, down_full = (
        lax.all_gather(to_low(w_gate), "fsdp", axis=0, tiled=True),
        lax.all_gather(to_low(w_up), "fsdp", axis=0, tiled=True),
        lax.all_gather(to_low(w_down), "fsdp", axis=0, tiled=True),
    )
    grad_top = d_out.astype(jnp.float32)
    d_down, grad_mpost = pull_pm(grad_top)
    d_down_low = to_low(d_down)
    grad_wdown = matmul_left_t(h_low, d_down_low)
    d_hidden = matmul_right_t(d_down_low, down_full)
    d_gate, d_up = pull_h(d_hidden)
    d_gate_low = to_low(d_gate)
    d_up_low = to_low(d_up)
    grad_wgate = matmul_left_t(m_low, d_gate_low)
    grad_wup = matmul_left_t(m_low, d_up_low)
    d_normed = matmul_right_t(d_gate_low, gate_full) + matmul_right_t(d_up_low, up_full)
    d_mid_norm, grad_mpre = pull_m(d_normed)
    d_mid = grad_top + d_mid_norm
    q_full, k_full, v_full, o_full = (
        lax.all_gather(to_low(w_q), "fsdp", axis=0, tiled=True),
        lax.all_gather(to_low(w_k), "fsdp", axis=0, tiled=True),
        lax.all_gather(to_low(w_v), "fsdp", axis=0, tiled=True),
        lax.all_gather(to_low(w_o), "fsdp", axis=0, tiled=True),
    )
    d_attn, grad_apost = pull_pa(d_mid)
    d_attn_low = to_low(d_attn)
    grad_wo = matmul_left_t(o_low, d_attn_low)
    d_mix_low = to_low(matmul_right_t(d_attn_low, o_full)).reshape(
        seq_count, seq_len, -1, k_low.shape[-1]
    )
    probs = jnp.exp(scores_of(q_low, k_low, masks) - log_total)
    d_probs = jnp.einsum("nqhd,nkd->nhqk", d_mix_low, v_low, preferred_element_type=jnp.float32)
    row_dot = jnp.sum(probs * d_probs, axis=-1, keepdims=True)
    d_scores_low = to_low(probs * (d_probs - row_dot))
    d_query = SCALE * jnp.einsum(
        "nhqk,nkd->nqhd", d_scores_low, k_low, preferred_element_type=jnp.float32
    )
    d_key = SCALE * jnp.einsum(
        "nhqk,nqhd->nkd", d_scores_low, q_low, preferred_element_type=jnp.float32
    )
    d_value = jnp.einsum("nhqk,nqhd->nkd", p_low, d_mix_low, preferred_element_type=jnp.float32)
    d_qproj, grad_qgain = pull_q(d_query)
    d_kproj, grad_kgain = pull_k(d_key)
    d_q_low = to_low(d_qproj.reshape(seq_count * seq_len, -1))
    d_k_low = to_low(d_kproj.reshape(seq_count * seq_len, -1))
    d_v_low = to_low(d_value.reshape(seq_count * seq_len, -1))
    grad_wq = matmul_left_t(a_low, d_q_low)
    grad_wk = matmul_left_t(a_low, d_k_low)
    grad_wv = matmul_left_t(a_low, d_v_low)
    d_normed_a = (
        matmul_right_t(d_q_low, q_full)
        + matmul_right_t(d_k_low, k_full)
        + matmul_right_t(d_v_low, v_full)
    )
    d_input_norm, grad_apre = pull_a(d_normed_a)
    grad_x = (d_mid + d_input_norm).astype(jnp.bfloat16)
    all_shards = (
        lax.psum_scatter(grad_wq, "fsdp", scatter_dimension=0, tiled=True),
        lax.psum_scatter(grad_wk, "fsdp", scatter_dimension=0, tiled=True),
        lax.psum_scatter(grad_wv, "fsdp", scatter_dimension=0, tiled=True),
        lax.psum_scatter(grad_wo, "fsdp", scatter_dimension=0, tiled=True),
        lax.psum_scatter(grad_apre, "fsdp", scatter_dimension=0, tiled=True),
        lax.psum_scatter(grad_apost, "fsdp", scatter_dimension=0, tiled=True),
        lax.psum_scatter(grad_qgain, "fsdp", scatter_dimension=0, tiled=True),
        lax.psum_scatter(grad_kgain, "fsdp", scatter_dimension=0, tiled=True),
        lax.psum_scatter(grad_wgate, "fsdp", scatter_dimension=0, tiled=True),
        lax.psum_scatter(grad_wup, "fsdp", scatter_dimension=0, tiled=True),
        lax.psum_scatter(grad_wdown, "fsdp", scatter_dimension=0, tiled=True),
        lax.psum_scatter(grad_mpre, "fsdp", scatter_dimension=0, tiled=True),
        lax.psum_scatter(grad_mpost, "fsdp", scatter_dimension=0, tiled=True),
    )
    all_cols = (
        lax.psum_scatter(
            all_shards[0].astype(jnp.bfloat16), "replica", scatter_dimension=1, tiled=True
        ).astype(jnp.float32),
        lax.psum_scatter(
            all_shards[1].astype(jnp.bfloat16), "replica", scatter_dimension=1, tiled=True
        ).astype(jnp.float32),
        lax.psum_scatter(
            all_shards[2].astype(jnp.bfloat16), "replica", scatter_dimension=1, tiled=True
        ).astype(jnp.float32),
        lax.psum_scatter(
            all_shards[3].astype(jnp.bfloat16), "replica", scatter_dimension=1, tiled=True
        ).astype(jnp.float32),
        lax.psum_scatter(
            all_shards[8].astype(jnp.bfloat16), "replica", scatter_dimension=1, tiled=True
        ).astype(jnp.float32),
        lax.psum_scatter(
            all_shards[9].astype(jnp.bfloat16), "replica", scatter_dimension=1, tiled=True
        ).astype(jnp.float32),
        lax.psum_scatter(
            all_shards[10].astype(jnp.bfloat16), "replica", scatter_dimension=1, tiled=True
        ).astype(jnp.float32),
        lax.psum_scatter(
            spread_gain(all_shards[4]).astype(jnp.bfloat16),
            "replica",
            scatter_dimension=1,
            tiled=True,
        ).astype(jnp.float32),
        lax.psum_scatter(
            spread_gain(all_shards[5]).astype(jnp.bfloat16),
            "replica",
            scatter_dimension=1,
            tiled=True,
        ).astype(jnp.float32),
        lax.psum_scatter(
            spread_gain(all_shards[6]).astype(jnp.bfloat16),
            "replica",
            scatter_dimension=1,
            tiled=True,
        ).astype(jnp.float32),
        lax.psum_scatter(
            spread_gain(all_shards[7]).astype(jnp.bfloat16),
            "replica",
            scatter_dimension=1,
            tiled=True,
        ).astype(jnp.float32),
        lax.psum_scatter(
            spread_gain(all_shards[11]).astype(jnp.bfloat16),
            "replica",
            scatter_dimension=1,
            tiled=True,
        ).astype(jnp.float32),
        lax.psum_scatter(
            spread_gain(all_shards[12]).astype(jnp.bfloat16),
            "replica",
            scatter_dimension=1,
            tiled=True,
        ).astype(jnp.float32),
    )
    all_mats = (
        lax.all_gather(all_cols[0].astype(jnp.bfloat16), "replica", axis=1, tiled=True).astype(
            jnp.float32
        ),
        lax.all_gather(all_cols[1].astype(jnp.bfloat16), "replica", axis=1, tiled=True).astype(
            jnp.float32
        ),
        lax.all_gather(all_cols[2].astype(jnp.bfloat16), "replica", axis=1, tiled=True).astype(
            jnp.float32
        ),
        lax.all_gather(all_cols[3].astype(jnp.bfloat16), "replica", axis=1, tiled=True).astype(
            jnp.float32
        ),
        lax.all_gather(all_cols[4].astype(jnp.bfloat16), "replica", axis=1, tiled=True).astype(
            jnp.float32
        ),
        lax.all_gather(all_cols[5].astype(jnp.bfloat16), "replica", axis=1, tiled=True).astype(
            jnp.float32
        ),
        lax.all_gather(all_cols[6].astype(jnp.bfloat16), "replica", axis=1, tiled=True).astype(
            jnp.float32
        ),
    )
    attn_sums = (
        all_mats[0],
        all_mats[1],
        all_mats[2],
        all_mats[3],
        all_cols[7][:, 0],
        all_cols[8][:, 0],
        all_cols[9][:, 0],
        all_cols[10][:, 0],
    )
    mlp_sums = (all_mats[4], all_mats[5], all_mats[6], all_cols[11][:, 0], all_cols[12][:, 0])
    return (
        layer_out,
        grad_x,
        attn_sums[0],
        attn_sums[1],
        attn_sums[2],
        attn_sums[3],
        attn_sums[4],
        attn_sums[5],
        attn_sums[6],
        attn_sums[7],
        mlp_sums[0],
        mlp_sums[1],
        mlp_sums[2],
        mlp_sums[3],
        mlp_sums[4],
    )


MESH = pl.DeviceIdType.MESH
VMEM_BYTES = 60 * 2**20
F32 = jnp.float32
BF16 = jnp.bfloat16


def fits_cubes(mesh):
    return dict(mesh.shape) == {"replica": 2, "fsdp": 16}


class Place:
    def __init__(self):
        shard = lax.axis_index("fsdp")
        self.x = lax.axis_index("replica")
        self.shard = shard
        self.c = lax.rem(shard, 2)
        self.y = lax.rem(lax.div(shard, 2), 2)
        self.z = lax.div(shard, 4)
        self.zl = lax.rem(self.z, 2)
        self.zh = lax.div(self.z, 2)

    def at(self, x=None, y=None, z=None, c=None):
        x = self.x if x is None else x
        y = self.y if y is None else y
        z = self.z if z is None else z
        c = self.c if c is None else c
        return (x, (z * 2 + y) * 2 + c)

    def z_xor(self, k):
        low = self.zl if k % 2 == 0 else 1 - self.zl
        high = self.zh if k // 2 == 0 else 1 - self.zh
        return 2 * high + low

    def cube(self, bits):
        return self.at(
            x=1 - self.x if bits & 4 else self.x,
            y=1 - self.y if bits & 2 else self.y,
            z=self.z_xor(1) if bits & 1 else self.z,
        )


class Wires:
    def __init__(self, send, recv):
        self.send, self.recv, self.used = send, recv, 0

    def remote(self, src, dst, device):
        i = self.used
        self.used += 1
        return pltpu.make_async_remote_copy(
            src_ref=src,
            dst_ref=dst,
            send_sem=self.send.at[i],
            recv_sem=self.recv.at[i],
            device_id=device,
            device_id_type=MESH,
        )

    def local(self, src, dst):
        i = self.used
        self.used += 1
        return pltpu.make_async_copy(src, dst, self.send.at[i])


def greet(devices):
    barrier = pltpu.get_barrier_semaphore()
    for device in devices:
        pl.semaphore_signal(barrier, inc=1, device_id=device, device_id_type=MESH)
    pl.semaphore_wait(barrier, len(devices))


def hbm():
    return pl.BlockSpec(memory_space=pl.ANY)


def vmem():
    return pl.BlockSpec(memory_space=pltpu.VMEM)


def sems(count):
    return [pltpu.SemaphoreType.DMA((count,)), pltpu.SemaphoreType.DMA((count,))]


def params(collective_id):
    return pltpu.CompilerParams(
        collective_id=collective_id, has_side_effects=True, vmem_limit_bytes=VMEM_BYTES
    )


X, Y, Z = 4, 2, 1


def thirds(rows):
    first = -(-rows // 48) * 16
    return ((0, first), (first, first), (2 * first, rows - 2 * first))


def add(left, right):
    return (left.astype(F32) + right.astype(F32)).astype(BF16)


def norm_scale(values):
    return lax.rsqrt(jnp.mean(values * values, axis=-1, keepdims=True) + EPS)


def norm_pull(values, scale, gain, cotangent):
    weighted = gain * cotangent
    lean = jnp.mean(values * weighted, axis=-1, keepdims=True)
    d_values = scale * weighted - values * (scale * scale * scale * lean)
    return d_values, jnp.sum(values * scale * cotangent, axis=0, keepdims=True)


def spread_matrix(width, per):
    column = lax.broadcasted_iota(jnp.int32, (128, width), 1)
    row = lax.broadcasted_iota(jnp.int32, (128, width), 0)
    place = (lax.rem(column, per) == row).astype(F32)
    column = lax.broadcasted_iota(jnp.int32, (16, width), 1)
    row = lax.broadcasted_iota(jnp.int32, (16, width), 0)
    owner = (lax.div(column, per) == row).astype(F32)
    return place, owner


def join_gains(packed, which, width, per):
    place, owner = spread_matrix(width, per)
    shards = packed[:, which, :].astype(BF16)
    wide = jnp.dot(shards, place.astype(BF16), preferred_element_type=F32)
    return jnp.sum(wide * owner, axis=0, keepdims=True)


def turn(values, cosine, sine):
    half = values.shape[-1] // 2
    u, w = values[:, :half], values[:, half:]
    return jnp.concatenate([u * cosine - w * sine, w * cosine + u * sine], axis=1)


def turn_back(values, cosine, sine):
    half = values.shape[-1] // 2
    u, w = values[:, :half], values[:, half:]
    return jnp.concatenate([u * cosine + w * sine, w * cosine - u * sine], axis=1)


def front_kernel(
    tok, seg_row, w_q, w_k, w_v, w_o, g_apre, g_apost, g_mpre, g_mpost, g_q, g_k, w_gate, w_up, w_down,
    qkv_w, out_w, gu_w, dn_w, every, gains_full, a_low, qk_proj, q_low, k_low, v_low,
    probs, o_low, attn_proj, h_mid, tables,
    qkv_s, qkv_own, qkv_send, qkv_got, out_own, gains_own, gains_s, wide_in, wide_send, wide_got,
    wide_out, down_in, down_out, m_low, out_s, send, recv, local,
):
    p = Place()
    w = Wires(send, recv)
    x, y, z, c, zl, zh = p.x, p.y, p.z, p.c, p.zl, p.zh
    sibling = p.at(c=1 - c)
    plane = [p.at(x=1 - x), p.at(y=1 - y)]
    lines = [p.at(y=yy, z=p.z_xor(k)) for yy in (y, 1 - y) for k in range(1, 4)]
    started = []

    def push(src, dst, device):
        copy = w.remote(src, dst, device)
        copy.start()
        started.append(copy)
        return copy

    loads = [
        pltpu.make_async_copy(w_gate, wide_in.at[0], local.at[0]),
        pltpu.make_async_copy(w_up, wide_in.at[1], local.at[1]),
        pltpu.make_async_copy(w_down, down_in, local.at[2]),
    ]
    for copy in loads:
        copy.start()

    rows = w_q.shape[0]
    columns = qkv_s.shape[1] // 4
    out_rows = w_o.shape[0] // 2
    mine = 2 * x + c
    theirs = 2 * x + 1 - c

    all_own = jnp.concatenate([w_q[...], w_k[...], w_v[...]], axis=1)
    for quarter in range(4):
        qkv_own[quarter] = all_own[:, quarter * columns : (quarter + 1) * columns]
    qkv_send[...] = qkv_own[theirs].astype(BF16)
    out_own[...] = w_o[...].astype(BF16)
    gains_own[...] = jnp.zeros_like(gains_own)
    for i, gain in enumerate((g_apre, g_apost, g_mpre, g_mpost, g_q, g_k)):
        gains_own[i, : gain.shape[0]] = gain[...].astype(BF16).astype(F32)
    greet([sibling] + plane + lines)

    def qkv_at(zz, yy, quarter):
        return qkv_s.at[
            pl.ds(pl.multiple_of((2 * zz + yy) * 2 * rows, 16), 2 * rows),
            pl.ds(pl.multiple_of(quarter * columns, 128), columns),
        ]

    def out_at(zz, yy, quarter):
        return out_s.at[
            pl.ds(pl.multiple_of((2 * zz + yy) * 4 * out_rows + quarter * out_rows, 16), out_rows)
        ]

    swap = push(qkv_send, qkv_got, sibling)

    def gains_at(zz, yy, cc):
        return gains_s.at[(2 * zz + yy) * 2 + cc]

    gains_s[(2 * z + y) * 2 + c] = gains_own[...]
    gain_line = [push(gains_own, gains_at(z, y, c), p.at(z=p.z_xor(k))) for k in range(1, 4)]
    gain_side = [push(gains_own, gains_at(z, y, c), plane[1])]
    holds = x == c
    out_theirs = out_own.at[pl.ds(pl.multiple_of((1 - c) * out_rows, 16), out_rows)]
    out_swap = w.remote(out_theirs, out_at(z, y, theirs), sibling)
    pl.when(holds)(out_swap.start)

    @pl.when(holds)
    def _():
        out_s[pl.ds(pl.multiple_of((2 * z + y) * 4 * out_rows + mine * out_rows, 16), out_rows)] = (
            out_own[pl.ds(pl.multiple_of(c * out_rows, 16), out_rows)]
        )

    swap.wait_recv()
    top, low = qkv_own[mine], qkv_got[...].astype(F32)
    first = jnp.where(c == 0, top, low)
    second = jnp.where(c == 0, low, top)
    base = pl.multiple_of((2 * z + y) * 2 * rows, 16)
    joined = jnp.concatenate([first, second], axis=0).astype(BF16)
    qkv_s[pl.ds(base, 2 * rows), pl.ds(pl.multiple_of(mine * columns, 128), columns)] = joined

    pl.when(jnp.logical_not(holds))(out_swap.wait_recv)
    pl.when(holds)(out_swap.wait_send)

    line = [None]
    for k in range(1, 4):
        to = p.at(z=p.z_xor(k))
        line.append(
            (
                push(qkv_at(z, y, mine), qkv_at(z, y, mine), to),
                push(out_at(z, y, mine), out_at(z, y, mine), to),
            )
        )
    side_x, side_y, corner = {}, {}, {}

    def spread(k):
        zz = p.z_xor(k)
        if k:
            for copy in line[k]:
                copy.wait_recv()
        qkv, out = qkv_at(zz, y, mine), out_at(zz, y, mine)
        side_x[k] = (push(qkv, qkv, plane[0]), push(out, out, plane[0]))
        side_y[k] = (push(qkv, qkv, plane[1]), push(out, out, plane[1]))

    def relay(k):
        zz = p.z_xor(k)
        if k % 2:
            for copy in side_y[k]:
                copy.wait_recv()
            qkv, out, to = qkv_at(zz, 1 - y, mine), out_at(zz, 1 - y, mine), plane[0]
        else:
            for copy in side_x[k]:
                copy.wait_recv()
            other = 2 * (1 - x) + c
            qkv, out, to = qkv_at(zz, y, other), out_at(zz, y, other), plane[1]
        corner[k] = (push(qkv, qkv, to), push(out, out, to))

    pairs = []

    def share(k):
        zz = p.z_xor(k)
        for copy in (side_x[k] if k % 2 else side_y[k]) + corner[k]:
            copy.wait_recv()
        for xx in range(2):
            at = qkv_s.at[
                pl.ds(pl.multiple_of(2 * zz * 2 * rows, 16), 4 * rows),
                pl.ds(pl.multiple_of((2 * xx + c) * columns, 128), columns),
            ]
            pairs.append(push(at, at, sibling))
            for yy in range(2):
                at = out_at(zz, yy, 2 * xx + c)
                pairs.append(push(at, at, sibling))

    spread(0)
    loads[0].wait()
    loads[1].wait()
    part_columns = wide_out.shape[-1]
    for xx in range(2):

        @pl.when(x == xx)
        def _():
            for zz in range(2):
                for yy in range(2):
                    part = (2 * zz + xx) * 2 + yy
                    at = slice(part * part_columns, (part + 1) * part_columns)
                    for matrix in range(2):

                        @pl.when(c == 1 - matrix)
                        def _():
                            wide_send[2 * zz + yy] = wide_in[matrix, :, at].astype(BF16)

    wide_swap = push(wide_send, wide_got, sibling)
    loads[2].wait()
    down_out[...] = down_in[...].astype(BF16)
    relay(0)
    spread(1)
    wide_swap.wait_recv()
    for xx in range(2):

        @pl.when(x == xx)
        def _():
            for zz in range(2):
                for yy in range(2):
                    part = (2 * zz + xx) * 2 + yy
                    at = slice(part * part_columns, (part + 1) * part_columns)
                    got = wide_got[2 * zz + yy].astype(F32)
                    for matrix in range(2):

                        @pl.when(c == matrix)
                        def _():
                            own = wide_in[matrix, :, at]
                            both = [own, got] if matrix == 0 else [got, own]
                            wide_out[2 * zz + yy] = jnp.concatenate(both, axis=0).astype(BF16)

    def gu_at(zz, yy):
        return gu_w.at[c, pl.ds(pl.multiple_of((2 * zz + yy) * 2 * rows, 16), 2 * rows)]

    wide = []
    for k in (3, 2, 1, 0):
        for other in (1, 0):
            yy = 1 - y if other else y
            zz = p.z_xor(k)
            src = wide_out.at[2 * lax.rem(zz, 2) + yy]
            if k == 0 and other == 0:
                own_wide = pltpu.make_async_copy(src, gu_at(z, y), local.at[0])
                own_wide.start()
            else:
                wide.append((zz, yy, push(src, gu_at(z, y), p.at(y=yy, z=zz))))
    down_rows = down_out.shape[0]
    down_at = dn_w.at[pl.ds(pl.multiple_of(c * down_rows, 16), down_rows)]
    source_z = 2 * zl + x
    first_down = w.used
    w.used += 2
    down_sends = []
    for half in range(2):
        zz = 2 * half + zh
        copy = pltpu.make_async_remote_copy(
            src_ref=down_out,
            dst_ref=down_at,
            send_sem=send.at[first_down + half],
            recv_sem=recv.at[first_down],
            device_id=p.at(z=zz),
            device_id_type=MESH,
        )
        need = (x == zl) & (zz != z)
        pl.when(need)(copy.start)
        down_sends.append((need, copy))
    own_down = pltpu.make_async_copy(down_out, down_at, local.at[1])
    pl.when(source_z == z)(own_down.start)

    tok_f = tok[...].astype(F32)
    length, width = tok_f.shape
    head = k_low.shape[1]
    spread(2)
    relay(1)
    for copy in gain_line:
        copy.wait_recv()
    for k in range(1, 4):
        zz = p.z_xor(k)
        gain_side.append(push(gains_at(zz, y, c), gains_at(zz, y, c), plane[1]))
    row_seg = seg_row[...].astype(F32)
    i_at = lax.broadcasted_iota(jnp.int32, (length, length), 0)
    j_at = lax.broadcasted_iota(jnp.int32, (length, length), 1)
    col_seg = jnp.sum(jnp.where(i_at == j_at, row_seg, 0.0), axis=1, keepdims=True)
    earlier = jnp.sum((row_seg < col_seg).astype(F32), axis=1, keepdims=True)
    index = lax.broadcasted_iota(jnp.int32, (length, 1), 0).astype(F32)
    rate_at = lax.broadcasted_iota(jnp.int32, (1, head // 2), 1).astype(F32)
    rates = jnp.exp(rate_at * (-2.0 * math.log(THETA) / head))
    angles = (index - earlier) * rates
    tables[0] = jnp.cos(angles)
    tables[1] = jnp.sin(angles)
    spread(3)
    relay(2)
    share(0)
    relay(3)
    for copy in gain_side:
        copy.wait_recv()
    gain_pair = []
    for zz in range(4):
        for yy in range(2):
            gain_pair.append(push(gains_at(zz, yy, c), gains_at(zz, yy, c), sibling))
    share(1)
    for copy in gain_pair:
        copy.wait_recv()
    packed = gains_s[...]
    for i, (size, per) in enumerate(
        ((width, rows),) * 4 + ((head, head // 16),) * 2
    ):
        gains_full[i, :, :size] = join_gains(packed, i, size, per)
    a_low[...] = (tok_f * norm_scale(tok_f) * gains_full[0]).astype(BF16)
    share(2)
    share(3)
    for copy in pairs:
        copy.wait_recv()
    saves = [
        pltpu.make_async_copy(qkv_s, qkv_w, local.at[2]),
        pltpu.make_async_copy(out_s, out_w, local.at[3]),
    ]
    for copy in saves:
        copy.start()

    cosine, sine = tables[0], tables[1]
    heads = q_low.shape[1] // head
    for i in range(heads + 2):
        at = slice(i * head, (i + 1) * head)
        value = jnp.dot(a_low[...], qkv_s[:, at], preferred_element_type=F32)
        if i < heads:
            qk_proj[:, at] = value
            q_low[:, at] = turn(
                value * norm_scale(value) * gains_full[4, :, :head], cosine, sine
            ).astype(BF16)
        elif i == heads:
            qk_proj[:, at] = value
            k_low[...] = turn(
                value * norm_scale(value) * gains_full[5, :, :head], cosine, sine
            ).astype(BF16)
        else:
            v_low[...] = value.astype(BF16)
    allowed = (row_seg == col_seg) & (j_at <= i_at)
    for i in range(heads):
        at = slice(i * head, (i + 1) * head)
        scores = SCALE * lax.dot_general(
            q_low[:, at], k_low[...], (((1,), (1,)), ((), ())), preferred_element_type=F32
        )
        scores = jnp.where(allowed, scores, MASKED)
        expo = jnp.exp(scores - jnp.max(scores, axis=1, keepdims=True))
        prob = expo / jnp.sum(expo, axis=1, keepdims=True)
        probs[i] = prob
        o_low[:, at] = jnp.dot(
            prob.astype(BF16), v_low[...], preferred_element_type=F32
        ).astype(BF16)
    third = width // 3
    for i in range(3):
        at = slice(i * third, (i + 1) * third)
        attn_proj[:, at] = jnp.dot(o_low[...], out_s[:, at], preferred_element_type=F32)
    proj = attn_proj[...]
    mid = tok_f + proj * norm_scale(proj) * gains_full[1]
    h_mid[...] = mid
    m_low[...] = (mid * norm_scale(mid) * gains_full[2]).astype(BF16)

    finish = cube_gather_steps(p, w, m_low, every, local.at[4], started)
    next(finish)
    own_wide.wait()
    shared = [push(gu_at(z, y), gu_at(z, y), sibling)]
    next(finish)
    for zz, yy, copy in reversed(wide):
        copy.wait_recv()
        shared.append(push(gu_at(zz, yy), gu_at(zz, yy), sibling))
    next(finish)
    pl.when(source_z == z)(own_down.wait)
    pl.when(source_z != z)(down_sends[0][1].wait_recv)
    shared.append(push(down_at, down_at, sibling))
    for _ in finish:
        pass
    for copy in shared:
        copy.wait_recv()
    for copy in saves:
        copy.wait()
    for need, copy in down_sends:
        pl.when(need)(copy.wait_send)
    for copy in started:
        copy.wait_send()


def cube_gather_steps(p, w, block, every, own_sem, started):
    near = {bit: p.cube(bit) for bit in (X, Y, Z)}

    def push(src, dst, bit):
        copy = w.remote(src, dst, near[bit])
        copy.start()
        started.append(copy)
        return copy

    rows = block.shape[0]
    half = rows // 2
    own = pltpu.make_async_copy(block, every.at[0], own_sem)
    own.start()
    arrivals = {}
    for h in range(2):
        at = pl.ds(h * half, half)
        for bit in (X, Y, Z):
            arrivals[bit, h] = push(block.at[at], every.at[bit, at], bit)
    yield
    for h in range(2):
        at = pl.ds(h * half, half)
        for link, relay in ((X, Y), (Y, Z), (Z, X)):
            arrivals[relay, h].wait_recv()
            arrivals[link | relay, h] = push(every.at[relay, at], every.at[link | relay, at], link)
    yield
    last = []
    for h in range(2):
        for (start, size), link, relay in zip(thirds(half), (X, Y, Z), (Y | Z, X | Z, X | Y)):
            at = pl.ds(h * half + start, size)
            arrivals[relay, h].wait_recv()
            last.append(push(every.at[relay, at], every.at[7, at], link))
    yield
    for copy in last:
        copy.wait_recv()
    own.wait()


def front(tok, segments, w_q, w_k, w_v, w_o, gains, w_gate, w_up, w_down, head):
    length, width = tok.shape
    rows, mix = w_q.shape
    hidden = w_gate.shape[1]
    part = hidden // 8
    down_rows = w_down.shape[0]
    total = mix + 2 * head
    heads = mix // head
    columns = total // 4
    struct = jax.ShapeDtypeStruct
    shapes = (
        struct((16 * rows, total), BF16),
        struct((16 * w_o.shape[0], width), BF16),
        struct((2, 16 * rows, part), BF16),
        struct((2 * down_rows, width), BF16),
        struct((8, length, width), BF16),
        struct((8, 1, width), F32),
        struct((length, width), BF16),
        struct((length, mix + head), F32),
        struct((length, mix), BF16),
        struct((length, head), BF16),
        struct((length, head), BF16),
        struct((heads, length, length), F32),
        struct((length, mix), BF16),
        struct((length, width), F32),
        struct((length, width), F32),
        struct((2, length, head // 2), F32),
    )
    scratch = [
        pltpu.VMEM((16 * rows, total), BF16),
        pltpu.VMEM((4, rows, columns), F32),
        pltpu.VMEM((rows, columns), BF16),
        pltpu.VMEM((rows, columns), BF16),
        pltpu.VMEM(w_o.shape, BF16),
        pltpu.VMEM((8, 128), F32),
        pltpu.VMEM((16, 8, 128), F32),
        pltpu.VMEM((2, rows, hidden), F32),
        pltpu.VMEM((4, rows, part), BF16),
        pltpu.VMEM((4, rows, part), BF16),
        pltpu.VMEM((4, 2 * rows, part), BF16),
        pltpu.VMEM((down_rows, width), F32),
        pltpu.VMEM((down_rows, width), BF16),
        pltpu.VMEM((length, width), BF16),
        pltpu.VMEM((16 * w_o.shape[0], width), BF16),
    ]
    return pl.pallas_call(
        front_kernel,
        out_shape=shapes,
        in_specs=[vmem()] * 12 + [hbm()] * 3,
        out_specs=(hbm(),) * 5 + (vmem(),) * 11,
        scratch_shapes=scratch + sems(128) + [pltpu.SemaphoreType.DMA((5,))],
        compiler_params=params(0),
        name="front",
    )(
        tok, segments, w_q, w_k, w_v, w_o, *gains, w_gate, w_up, w_down
    )


def dot_rows(left, right):
    return lax.dot_general(left, right, (((0,), (0,)), ((), ())), preferred_element_type=F32)


def dot_columns(left, right):
    return lax.dot_general(left, right, (((1,), (1,)), ((), ())), preferred_element_type=F32)


def back_kernel(
    tok, d_out, d_normed, gains_full, a_low, qk_proj, q_low, k_low, v_low, probs, o_low, attn_proj,
    h_mid, tables, g_mpost, down_two, qkv_hbm, out_hbm, wide_one,
    grad_x, qe, oe, gains_sum, wide_end, wide_back, down_end,
    qkv_w, out_w, wide_in, wide_far, d_input, wide_swap, d_attn, d_mid, d_mix, d_qkv, dqkv, dout,
    q1, o1, q2, o2, q3, o3,
    gain_acc, gain_got, send, recv, local,
):
    p = Place()
    w = Wires(send, recv)
    x, y, z, c, zl, zh = p.x, p.y, p.z, p.c, p.zl, p.zh
    sibling = p.at(c=1 - c)
    plane = [p.at(x=1 - x), p.at(y=1 - y), p.at(x=1 - x, y=1 - y)]
    line = [p.at(z=p.z_xor(k)) for k in range(1, 4)]
    cube = [p.cube(bits) for bits in range(1, 8)]
    started = []

    def push(src, dst, device):
        copy = w.remote(src, dst, device)
        copy.start()
        started.append(copy)
        return copy

    def rows_of(ref, start, size):
        return ref.at[pl.ds(pl.multiple_of(start, 16), size)]

    width = tok.shape[1]
    chip_rows = wide_one.shape[0] // 8
    half_rows = 4 * chip_rows
    far_half = half_rows * (1 - zh)
    near_half = half_rows * zh
    loads = [
        pltpu.make_async_copy(rows_of(wide_one, near_half, half_rows), wide_in, local.at[0]),
        pltpu.make_async_copy(out_hbm, out_w, local.at[2]),
        pltpu.make_async_copy(qkv_hbm, qkv_w, local.at[3]),
    ]
    for copy in loads:
        copy.start()
    greet([sibling] + plane + line + [p.cube(5), p.cube(7), p.cube(3)])

    order = (3, 1, 2, 0)

    def piece(i):
        to_z = 1 - zl if i // 2 else zl
        to_y = 1 - y if i % 2 else y
        return (2 * to_z + to_y) * chip_rows

    wide_two = {}
    for i in order:
        at = pl.ds(i * chip_rows, chip_rows)
        wide_two[i] = push(
            rows_of(wide_one, far_half + piece(i), chip_rows), wide_far.at[at], line[1]
        )
    mine = zl == zh
    arrive = w.used
    w.used += 3
    down_three = []
    for xx in range(2):
        copy = pltpu.make_async_remote_copy(
            src_ref=down_two,
            dst_ref=down_end,
            send_sem=send.at[arrive + xx],
            recv_sem=recv.at[arrive],
            device_id=p.at(x=xx, z=2 * zh + x),
            device_id_type=MESH,
        )
        need = mine & ((x != xx) | (zh != x))
        pl.when(need)(copy.start)
        down_three.append((need, copy))
    down_here = mine & (x == zl)
    down_own = pltpu.make_async_copy(down_two, down_end, local.at[5])
    pl.when(down_here)(down_own.start)

    mid = h_mid[...]
    d_value, g_mpre = norm_pull(mid, norm_scale(mid), gains_full[2], d_normed[...])
    d_mid[...] = d_out[...].astype(F32) + d_value
    proj = attn_proj[...]
    d_value, g_apost = norm_pull(proj, norm_scale(proj), gains_full[1], d_mid[...])
    d_attn[...] = d_value.astype(BF16)
    gain_acc[0, 2:3, :] = g_mpre
    gain_acc[0, 1:2, :] = g_apost

    third = width // 3
    for i in range(3):
        at = slice(i * third, (i + 1) * third)
        dout[:, at] = dot_rows(o_low[...], d_attn[:, at]).astype(BF16)
    out_rows = dout.shape[0] // 32
    columns = dqkv.shape[1] // 4

    def out_at(ref, zz, yy, quarter):
        return rows_of(ref, (2 * zz + yy) * 4 * out_rows + quarter * out_rows, out_rows)

    out_one = [
        push(
            out_at(dout, zz, yy, 2 * xx + 1 - c),
            o1.at[xx, yy, pl.ds(zz * out_rows, out_rows)],
            sibling,
        )
        for zz in range(4)
        for yy in range(2)
        for xx in range(2)
    ]
    loads[1].wait()
    d_mix[...] = dot_columns(d_attn[...], out_w[...]).astype(BF16)

    cosine, sine = tables[0], tables[1]
    head = k_low.shape[1]
    heads = q_low.shape[1] // head
    d_k, d_v, g_q = 0.0, 0.0, 0.0
    for i in range(heads):
        at = slice(i * head, (i + 1) * head)
        prob = probs[i]
        d_probs = dot_columns(d_mix[:, at], v_low[...])
        row_dot = jnp.sum(prob * d_probs, axis=1, keepdims=True)
        d_scores = (prob * (d_probs - row_dot)).astype(BF16)
        d_q = SCALE * jnp.dot(d_scores, k_low[...], preferred_element_type=F32)
        d_k = d_k + dot_rows(d_scores, q_low[:, at])
        d_v = d_v + dot_rows(prob.astype(BF16), d_mix[:, at])
        value = qk_proj[:, at]
        d_value, gain = norm_pull(
            value, norm_scale(value), gains_full[4, :, :head], turn_back(d_q, cosine, sine)
        )
        g_q = g_q + gain
        d_qkv[:, at] = d_value.astype(BF16)
    at = slice(heads * head, (heads + 1) * head)
    value = qk_proj[:, at]
    d_value, g_k = norm_pull(
        value, norm_scale(value), gains_full[5, :, :head], turn_back(SCALE * d_k, cosine, sine)
    )
    d_qkv[:, at] = d_value.astype(BF16)
    d_qkv[:, (heads + 1) * head :] = d_v.astype(BF16)
    gain_acc[0, 4:5, :] = jnp.zeros((1, width), F32)
    gain_acc[0, 5:8, :] = jnp.zeros((3, width), F32)
    gain_acc[0, 4:5, :head] = g_q
    gain_acc[0, 5:6, :head] = g_k
    for i in range(heads + 2):
        at = slice(i * head, (i + 1) * head)
        dqkv[:, at] = dot_rows(a_low[...], d_qkv[:, at]).astype(BF16)

    def qkv_columns(ref, quarter):
        return ref.at[:, pl.ds(pl.multiple_of(quarter * columns, 128), columns)]

    qkv_one = [push(qkv_columns(dqkv, 2 * xx + 1 - c), q1.at[xx], sibling) for xx in range(2)]

    loads[2].wait()
    tok_f = tok[...].astype(F32)
    for i in range(3):
        at = slice(i * third, (i + 1) * third)
        d_input[:, at] = dot_columns(d_qkv[...], qkv_w[at, :])
    d_value, g_apre = norm_pull(tok_f, norm_scale(tok_f), gains_full[0], d_input[...])
    grad_x[...] = (d_mid[...] + d_value).astype(BF16)
    gain_acc[0, 0:1, :] = g_apre
    gain_acc[0, 3:4, :] = g_mpost[...]
    gain_one = push(gain_acc.at[0], gain_got.at[0], sibling)

    for copy in out_one + qkv_one:
        copy.wait_recv()

    def plane_part(xx, yy, q_ref, o_ref):
        at = pl.ds(pl.multiple_of((2 * xx + c) * columns, 128), columns)
        for zz in range(4):
            rows = pl.ds(pl.multiple_of((2 * zz + yy) * chip_rows, 16), chip_rows)
            q_ref[zz * chip_rows : (zz + 1) * chip_rows, :] = add(dqkv[rows, at], q1[xx, rows, :])
            start = pl.multiple_of(((2 * zz + yy) * 4 + 2 * xx + c) * out_rows, 16)
            here = slice(zz * out_rows, (zz + 1) * out_rows)
            o_ref[here, :] = add(dout[pl.ds(start, out_rows), :], o1[xx, yy, here, :])

    second = {}
    for i in (2, 0, 1):
        plane_part(x if i == 1 else 1 - x, y if i == 0 else 1 - y, q2.at[i], o2.at[i])
        second[i] = (push(q2.at[i], q2.at[3 + i], plane[i]), push(o2.at[i], o2.at[3 + i], plane[i]))
    gain_one.wait_recv()
    gain_acc[1] = gain_acc[0] + gain_got[0]
    gain_two = [push(gain_acc.at[1], gain_got.at[1 + i], plane[i]) for i in range(3)]
    plane_part(x, y, q3, o3)

    part = (2 * zl + x) * 2 + y
    wide_three, own_wide = [], []

    def wide_on(i):
        at = pl.ds(i * chip_rows, chip_rows)
        rows = pl.ds(pl.multiple_of(piece(i), 16), chip_rows)
        wide_two[i].wait_recv()
        wide_far[at, :] = add(wide_in[rows, :], wide_far[at, :])
        for over in (1, 0):
            bits = 4 * over + 2 * (i % 2) + i // 2
            if bits:
                wide_three.append(push(wide_far.at[at], wide_end.at[part], p.cube(bits)))
            else:
                own_wide.append(
                    pltpu.make_async_copy(wide_far.at[at], wide_end.at[part], local.at[4])
                )
                own_wide[0].start()

    loads[0].wait()
    wide_on(3)
    for i in range(3):
        for copy in second[i]:
            copy.wait_recv()
    q3[...] = add(
        q3[...].astype(F32) + q2[3].astype(F32), q2[4].astype(F32) + q2[5].astype(F32)
    )
    o3[...] = add(
        o3[...].astype(F32) + o2[3].astype(F32), o2[4].astype(F32) + o2[5].astype(F32)
    )
    third_step = []
    for k in range(1, 4):
        zz = p.z_xor(k)
        third_step += [
            push(rows_of(q3, zz * chip_rows, chip_rows), qe.at[k], line[k - 1]),
            push(rows_of(o3, zz * out_rows, out_rows), oe.at[k], line[k - 1]),
        ]
    for copy in gain_two:
        copy.wait_recv()
    gain_acc[2] = gain_acc[1] + gain_got[1] + gain_got[2] + gain_got[3]
    gain_three = [push(gain_acc.at[2], gain_got.at[3 + k], line[k - 1]) for k in range(1, 4)]
    wide_on(1)
    for copy in third_step:
        copy.wait_recv()
    start = pl.multiple_of(z * chip_rows, 16)
    qe[0] = add(
        q3[pl.ds(start, chip_rows), :].astype(F32) + qe[1].astype(F32),
        qe[2].astype(F32) + qe[3].astype(F32),
    )
    start = pl.multiple_of(z * out_rows, 16)
    oe[0] = add(
        o3[pl.ds(start, out_rows), :].astype(F32) + oe[1].astype(F32),
        oe[2].astype(F32) + oe[3].astype(F32),
    )
    last = [
        push(qe.at[0], qe.at[4 + i], device)
        for i, device in enumerate((sibling, plane[0]))
    ] + [
        push(oe.at[0], oe.at[4 + i], device)
        for i, device in enumerate((sibling, plane[0]))
    ]
    wide_on(2)
    for copy in last:
        copy.wait_recv()
    relay = [push(qe.at[5], qe.at[6], sibling), push(oe.at[5], oe.at[6], sibling)]
    wide_on(0)

    for copy in relay:
        copy.wait_recv()
    rows = chip_rows // 2
    for copy in gain_three:
        copy.wait_recv()
    gains_sum[...] = gain_acc[2] + gain_got[4] + gain_got[5] + gain_got[6]

    own_wide[0].wait()
    for copy in wide_three:
        copy.wait_recv()
    for cc in range(2):

        @pl.when(c == cc)
        def _():
            for s in range(8):
                extra = (rows + 15) // 16 * 16
                at = slice(0, extra) if cc == 1 else slice(2 * rows - extra, 2 * rows)
                wide_swap[s] = wide_end[s, at, :]

    final = push(wide_swap, wide_back, sibling)
    pl.when(down_here)(down_own.wait)
    pl.when(jnp.logical_not(down_here))(down_three[0][1].wait_recv)
    final.wait_recv()
    for need, copy in down_three:
        pl.when(need)(copy.wait_send)
    for copy in started:
        copy.wait_send()


def back(tok, d_out, d_normed, gains_full, saved, g_mpost, down_two, qkv_w, out_w, wide_one):
    length, width = tok.shape
    total = qkv_w.shape[1]
    columns = total // 4
    mix = out_w.shape[0]
    part = wide_one.shape[1]
    chip_rows = width // 8
    rows = chip_rows // 2
    extra = (rows + 15) // 16 * 16
    piece = mix // 32
    struct = jax.ShapeDtypeStruct
    shapes = (
        struct((length, width), BF16),
        struct((7, chip_rows, columns), BF16),
        struct((7, piece, width), BF16),
        struct((8, width), F32),
        struct((8, chip_rows, part), BF16),
        struct((8, extra, part), BF16),
        struct(down_two.shape, BF16),
    )
    scratch = [
        pltpu.VMEM(qkv_w.shape, BF16),
        pltpu.VMEM(out_w.shape, BF16),
        pltpu.VMEM((width // 2, part), BF16),
        pltpu.VMEM((width // 2, part), BF16),
        pltpu.VMEM((length, width), F32),
        pltpu.VMEM((8, extra, part), BF16),
        pltpu.VMEM((length, width), BF16),
        pltpu.VMEM((length, width), F32),
        pltpu.VMEM((length, mix), BF16),
        pltpu.VMEM((length, total), BF16),
        pltpu.VMEM((width, total), BF16),
        pltpu.VMEM((mix, width), BF16),
        pltpu.VMEM((2, width, columns), BF16),
        pltpu.VMEM((2, 2, 4 * piece, width), BF16),
        pltpu.VMEM((6, 4 * chip_rows, columns), BF16),
        pltpu.VMEM((6, 4 * piece, width), BF16),
        pltpu.VMEM((4 * chip_rows, columns), BF16),
        pltpu.VMEM((4 * piece, width), BF16),
        pltpu.VMEM((3, 8, width), F32),
        pltpu.VMEM((7, 8, width), F32),
    ]
    return pl.pallas_call(
        back_kernel,
        out_shape=shapes,
        in_specs=[vmem()] * 16 + [hbm()] * 3,
        out_specs=(vmem(),) * 7,
        scratch_shapes=scratch + sems(96) + [pltpu.SemaphoreType.DMA((6,))],
        compiler_params=params(3),
        name="back",
    )(tok, d_out, d_normed, gains_full, *saved, g_mpost, down_two, qkv_w, out_w, wide_one)


def place_kernel(
    qe, oe, gains, wide_end, wide_back, down_end,
    w_q, w_k, w_v, w_o, w_gate, w_up, w_down, a_pre, a_post, m_pre, m_post, q_gain, k_gain,
):
    p = Place()
    rows, mix = w_q.shape
    head = w_k.shape[1]
    columns = qe.shape[2]
    piece = oe.shape[1]
    size = wide_end.shape[2]
    extra = wide_back.shape[1]

    def put_columns(start, value):
        for ref, first, width in ((w_q, 0, mix), (w_k, mix, head), (w_v, mix + head, head)):
            low, high = max(start, first), min(start + columns, first + width)
            if low < high:
                ref[:, low - first : high - first] = value[:, low - start : high - start]

    for xx in range(2):
        for cc in range(2):

            @pl.when((p.x == xx) & (p.c == cc))
            def _():
                for i, q in (
                    (0, 2 * xx + cc),
                    (4, 2 * xx + 1 - cc),
                    (5, 2 * (1 - xx) + cc),
                    (6, 2 * (1 - xx) + 1 - cc),
                ):
                    both = qe[i].astype(F32)
                    put_columns(q * columns, both[cc * rows : (cc + 1) * rows])
                    if q // 2 == cc:
                        w_o[(q % 2) * piece : (q % 2 + 1) * piece, :] = oe[i].astype(F32)

    for cc in range(2):

        @pl.when(p.c == cc)
        def _():
            own_ref, other_ref = (w_gate, w_up) if cc == 0 else (w_up, w_gate)
            for s in range(8):
                at = slice(s * size, (s + 1) * size)
                own_ref[:, at] = wide_end[s].astype(F32)[cc * rows : (cc + 1) * rows]
                other = wide_back[s].astype(F32)
                other_ref[:, at] = other[:rows] if cc == 0 else other[extra - rows :]

    w_down[...] = down_end[...].astype(F32)
    sums = gains[...]
    for i, ref in enumerate((a_pre, a_post, m_pre, m_post, q_gain, k_gain)):
        per = ref.shape[0]
        full = 16 * per
        turned = pltpu.roll(sums[:, :full], lax.rem(full - p.shard * per, full), 1)
        ref[...] = turned[i, :per]


def place(summed, shapes):
    return pl.pallas_call(
        place_kernel,
        out_shape=tuple(jax.ShapeDtypeStruct(shape, F32) for shape in shapes),
        in_specs=[vmem()] * 6,
        out_specs=(vmem(),) * 13,
        compiler_params=pltpu.CompilerParams(vmem_limit_bytes=VMEM_BYTES),
        name="place",
    )(*summed)


GELU_ROOT = math.sqrt(2.0 / math.pi)


def gelu_parts(gate):
    square = gate * gate
    bend = jnp.tanh(GELU_ROOT * gate * (1.0 + 0.044715 * square))
    half = 0.5 * (1.0 + bend)
    slope = half + 0.5 * gate * (1.0 - bend * bend) * GELU_ROOT * (1.0 + 3 * 0.044715 * square)
    return half * gate, slope


def tiles(size, step):
    return [slice(at, min(at + step, size)) for at in range(0, size, step)]


class CubeSum:
    MIDDLE = ((X, Y, Y | Z), (Y, Z, X | Z), (Z, X, X | Y))
    NEAR = ((Y, Z), (Z, X), (X, Y))

    def __init__(self, p, w, parts, third, second, first):
        self.p, self.w, self.parts = p, w, parts
        self.third, self.second, self.first = third, second, first
        self.half = parts.shape[1] // 2
        self.started = []
        self.far, self.mid, self.end = {}, {}, {}

    def push(self, src, dst, bit):
        copy = self.w.remote(src, dst, self.p.cube(bit))
        copy.start()
        self.started.append(copy)
        return copy

    def send_far(self):
        for h in range(2):
            for (start, size), link in zip(thirds(self.half), (X, Y, Z)):
                at = pl.ds(h * self.half + start, size)
                self.far[link, h] = self.push(self.parts.at[7, at], self.third.at[at], link)

    def send_middle(self):
        for h in range(2):
            for i, (link, onward, place) in enumerate(self.MIDDLE):
                start, size = thirds(self.half)[i]
                at = pl.ds(h * self.half + start, size)
                all_at = pl.ds(h * self.half, self.half)
                self.far[link, h].wait_recv()
                self.parts[place, at] = add(self.parts[place, at], self.third[at, :])
                self.mid[onward, h] = self.push(
                    self.parts.at[place, all_at], self.second.at[i, all_at], onward
                )

    def send_near(self):
        for h in range(2):
            at = pl.ds(h * self.half, self.half)
            for i, (came, place) in enumerate(self.NEAR):
                self.mid[came, h].wait_recv()
                self.parts[place, at] = add(self.parts[place, at], self.second[i, at])
                self.end[place, h] = self.push(
                    self.parts.at[place, at], self.first.at[i, at], place
                )

    def finish(self):
        for h in range(2):
            at = pl.ds(h * self.half, self.half)
            value = self.parts[0, at].astype(F32)
            for i, (_, place) in enumerate(self.NEAR):
                self.end[place, h].wait_recv()
                value = value + self.first[i, at].astype(F32)
            yield at, value

    def wait_sent(self):
        for copy in self.started:
            copy.wait_send()
        self.started = []


class CubeGather:
    def __init__(self, p, w, block, every):
        self.p, self.w, self.block, self.every = p, w, block, every
        self.half = block.shape[0] // 2
        self.started = []
        self.near, self.middle, self.far = {}, {}, {}

    def push(self, src, dst, bit):
        copy = self.w.remote(src, dst, self.p.cube(bit))
        copy.start()
        self.started.append(copy)
        return copy

    def send_near(self, h):
        at = pl.ds(h * self.half, self.half)
        for bit in (X, Y, Z):
            self.near[bit, h] = self.push(self.block.at[at], self.every.at[bit, at], bit)

    def send_middle(self, h):
        at = pl.ds(h * self.half, self.half)
        for link, relay in ((X, Y), (Y, Z), (Z, X)):
            self.near[relay, h].wait_recv()
            self.middle[link | relay, h] = self.push(
                self.every.at[relay, at], self.every.at[link | relay, at], link
            )

    def send_far(self, h):
        for (start, size), link, relay in zip(thirds(self.half), (X, Y, Z), (Y | Z, X | Z, X | Y)):
            at = pl.ds(h * self.half + start, size)
            self.middle[relay, h].wait_recv()
            self.far[link, h] = self.push(self.every.at[relay, at], self.every.at[7, at], link)

    def wait_far(self):
        for copy in self.far.values():
            copy.wait_recv()

    def wait_sent(self):
        for copy in self.started:
            copy.wait_send()
        self.started = []


def mlp_kernel(
    every, gu, dn, h_mid, d_out, gains_full,
    layer_out, d_normed, g_mpost, wide_one, down_two,
    m_all, wide_w, down_w, wide, hidden, dd_own, dd_all, parts, third, second, first,
    wide_out, wide_got, grad_dn, down_got, down_sum, down_far,
    send, recv, local,
):
    p = Place()
    w = Wires(send, recv)
    order = (7, 3, 5, 6, 4, 2, 1, 0)
    loads = {r: pltpu.make_async_copy(every.at[r], m_all.at[r], local.at[r]) for r in order}
    wide_load = pltpu.make_async_copy(gu, wide_w, local.at[8])
    down_load = pltpu.make_async_copy(dn, down_w, local.at[9])
    wide_load.start()
    loads[7].start()
    down_load.start()
    for r in order[1:]:
        loads[r].start()
    c = p.c
    sibling, partner = p.at(c=1 - c), p.at(z=p.z_xor(2))
    greet([p.cube(X), p.cube(Y), p.cube(Z), sibling, partner])

    length, width = m_all.shape[1:]
    part = wide.shape[-1]
    wide_tiles = tiles(part, 256)
    down_tiles = tiles(width, 384)

    def forward(r):
        for at in wide_tiles:
            g = jnp.dot(m_all[r], wide_w[0, :, at], preferred_element_type=F32)
            u = jnp.dot(m_all[r], wide_w[1, :, at], preferred_element_type=F32)
            wide[0, r, :, at] = g.astype(BF16)
            wide[1, r, :, at] = u.astype(BF16)
            value, _ = gelu_parts(g)
            hidden[r, :, at] = (value * u).astype(BF16)
        for at in down_tiles:
            parts[r, :, at] = jnp.dot(
                hidden[r], down_w[:, at], preferred_element_type=F32
            ).astype(BF16)

    def backward(r):
        for at in wide_tiles:
            d_hidden = dot_columns(dd_all[r], down_w[at, :])
            value, slope = gelu_parts(wide[0, r, :, at].astype(F32))
            up = wide[1, r, :, at].astype(F32)
            wide[0, r, :, at] = (d_hidden * up * slope).astype(BF16)
            wide[1, r, :, at] = (d_hidden * value).astype(BF16)
        d_gate = wide[0, r]
        d_up = wide[1, r]
        for at in down_tiles:
            parts[r, :, at] = (
                dot_columns(d_gate, wide_w[0, at, :]) + dot_columns(d_up, wide_w[1, at, :])
            ).astype(BF16)

    def several(step, places):
        lax.fori_loop(0, 3, lambda i, _: (step(places(i)), 0)[1], 0)

    def middles(i):
        return 7 - lax.shift_right_logical(jnp.int32(4), i)

    def nears(i):
        return lax.shift_right_logical(jnp.int32(4), i)

    total = CubeSum(p, w, parts, third, second, first)
    wide_load.wait()
    loads[7].wait()
    down_load.wait()
    forward(7)
    total.send_far()
    for r in order[1:]:
        loads[r].wait()
    several(forward, middles)
    total.send_middle()
    several(forward, nears)
    total.send_near()
    forward(0)

    gather = CubeGather(p, w, dd_own, dd_all)
    gain = gains_full[3]
    g_rows = 0.0
    for h, (at, value) in enumerate(total.finish()):
        scale = norm_scale(value)
        layer_out[at, :] = (h_mid[at, :] + value * scale * gain).astype(BF16)
        d_value, g_part = norm_pull(value, scale, gain, d_out[at, :].astype(F32))
        dd_own[at, :] = d_value.astype(BF16)
        g_rows = g_rows + g_part
        gather.send_near(h)
    g_mpost[...] = g_rows
    dd_all[0] = dd_own[...]
    total.wait_sent()
    backward(0)
    gather.send_middle(0)
    gather.send_middle(1)
    several(backward, nears)
    gather.send_far(0)
    gather.send_far(1)
    several(backward, middles)
    gather.wait_far()
    backward(7)

    total = CubeSum(p, w, parts, third, second, first)
    total.send_far()
    grad_rows = 384
    all_rows = 8 * length
    for at in down_tiles:
        grad_dn[:, at] = dot_rows(
            hidden[...].reshape(all_rows, part), dd_all[:, :, at].reshape(all_rows, -1)
        ).astype(BF16)
    down_rows = down_sum.shape[0]
    give = grad_dn.at[pl.ds(pl.multiple_of((1 - c) * down_rows, 16), down_rows)]
    down_one = w.remote(give, down_got, sibling)
    down_one.start()
    total.send_middle()

    def grad_wide(matrix, out):
        def step(i, _):
            at = pl.ds(pl.multiple_of(i * grad_rows, 128), grad_rows)
            left = m_all[:, :, at].reshape(all_rows, grad_rows)
            out[at, :] = dot_rows(left, wide[matrix].reshape(all_rows, part)).astype(BF16)
            return 0

        lax.fori_loop(0, width // grad_rows, step, 0)

    grad_wide(1 - c, wide_out)
    wide_swap = w.remote(wide_out, wide_got, sibling)
    wide_swap.start()
    down_one.wait_recv()
    keep = pl.ds(pl.multiple_of(c * down_rows, 16), down_rows)
    down_sum[...] = add(grad_dn[keep, :], down_got[...])
    down_over = w.remote(down_sum, down_far, partner)
    mine = p.zl == p.zh
    pl.when(p.zl != p.zh)(down_over.start)
    total.send_near()
    grad_wide(c, wide_one)
    wide_swap.wait_recv()
    wide_one[...] = add(wide_one[...], wide_got[...])
    for at, value in total.finish():
        d_normed[at, :] = value
    pl.when(mine)(down_over.wait_recv)

    @pl.when(mine)
    def _():
        down_two[...] = add(down_sum[...], down_far[...])

    pl.when(p.zl != p.zh)(down_over.wait_send)
    down_one.wait_send()
    wide_swap.wait_send()
    total.wait_sent()
    gather.wait_sent()


def mlp(every, gu, dn, h_mid, d_out, gains_full):
    _, length, width = every.shape
    part = dn.shape[0]
    struct = jax.ShapeDtypeStruct
    blocks = (8, length, width)
    return pl.pallas_call(
        mlp_kernel,
        out_shape=(
            struct((length, width), BF16),
            struct((length, width), F32),
            struct((1, width), F32),
            struct((width, part), BF16),
            struct((part // 2, width), BF16),
        ),
        in_specs=[hbm()] * 3 + [vmem()] * 3,
        out_specs=(vmem(),) * 5,
        scratch_shapes=[
            pltpu.VMEM(blocks, BF16),
            pltpu.VMEM(gu.shape, BF16),
            pltpu.VMEM(dn.shape, BF16),
            pltpu.VMEM((2, 8, length, part), BF16),
            pltpu.VMEM((8, length, part), BF16),
            pltpu.VMEM((length, width), BF16),
            pltpu.VMEM(blocks, BF16),
            pltpu.VMEM(blocks, BF16),
            pltpu.VMEM((length, width), BF16),
            pltpu.VMEM((3, length, width), BF16),
            pltpu.VMEM((3, length, width), BF16),
            pltpu.VMEM((width, part), BF16),
            pltpu.VMEM((width, part), BF16),
            pltpu.VMEM(dn.shape, BF16),
            pltpu.VMEM((part // 2, width), BF16),
            pltpu.VMEM((part // 2, width), BF16),
            pltpu.VMEM((part // 2, width), BF16),
        ]
        + sems(64)
        + [pltpu.SemaphoreType.DMA((10,))],
        compiler_params=params(1),
        name="mlp",
    )(every, gu, dn, h_mid, d_out, gains_full)


def cube_body(
    layer_in, d_out, segments, w_q, w_k, w_v, w_o, attn_pre, attn_post, q_gain, k_gain,
    w_gate, w_up, w_down, mlp_pre, mlp_post,
):
    width = layer_in.shape[1]
    head = q_gain.shape[0] * 16
    rows, mix = w_q.shape
    gain_list = [attn_pre, attn_post, mlp_pre, mlp_post, q_gain, k_gain]
    (
        qkv_w, out_w, gu_w, down_w, m_all, gains_full, a_low, qk_proj, q_low, k_low, v_low,
        probs, o_low, attn_proj, h_mid, tables,
    ) = front(
        layer_in, segments, w_q, w_k, w_v, w_o, gain_list, w_gate, w_up, w_down, head
    )
    layer_out, d_normed, g_mpost, wide_one, down_two = mlp(
        m_all, gu_w, down_w, h_mid, d_out, gains_full
    )
    saved = (a_low, qk_proj, q_low, k_low, v_low, probs, o_low, attn_proj, h_mid, tables)
    grad_x, *summed = back(
        layer_in, d_out, d_normed, gains_full, saved, g_mpost, down_two, qkv_w, out_w, wide_one
    )
    matrices = [w_q, w_k, w_v, w_o, w_gate, w_up, w_down]
    grads = place(summed, [v.shape for v in matrices + gain_list])
    g_apre, g_apost, g_mpre, g_mpost, g_q, g_k = grads[7:]
    return (
        layer_out,
        grad_x,
        *grads[:4],
        g_apre,
        g_apost,
        g_q,
        g_k,
        *grads[4:7],
        g_mpre,
        g_mpost,
    )


def solution(mesh):
    in_specs = (
        P(("replica", "fsdp"), None),
        P(("replica", "fsdp"), None),
        P(("replica", "fsdp"), None),
        P("fsdp", None),
        P("fsdp", None),
        P("fsdp", None),
        P("fsdp", None),
        P("fsdp"),
        P("fsdp"),
        P("fsdp"),
        P("fsdp"),
        P("fsdp", None),
        P("fsdp", None),
        P("fsdp", None),
        P("fsdp"),
        P("fsdp"),
    )
    out_specs = (
        P(("replica", "fsdp"), None),
        P(("replica", "fsdp"), None),
        P("fsdp", None),
        P("fsdp", None),
        P("fsdp", None),
        P("fsdp", None),
        P("fsdp"),
        P("fsdp"),
        P("fsdp"),
        P("fsdp"),
        P("fsdp", None),
        P("fsdp", None),
        P("fsdp", None),
        P("fsdp"),
        P("fsdp"),
    )
    body = cube_body if fits_cubes(mesh) else general_body
    return jax.shard_map(body, mesh=mesh, in_specs=in_specs, out_specs=out_specs, check_vma=False)
```

```python
from functools import partial
import math

import jax
import jax.numpy as jnp
from jax import lax
from jax.experimental import pallas as pl
from jax.experimental.pallas import tpu as pltpu
from jax.sharding import PartitionSpec as P

EPS = 1e-06
THETA = 1000000.0
SCALE = 0.0625
MASKED = -1e30


def norm_rows(values, gain):
    return values * lax.rsqrt(jnp.mean(values * values, axis=-1, keepdims=True) + EPS) * gain


def positions_of(segments):
    length = segments.shape[-1]
    index = jnp.arange(length, dtype=jnp.int32)
    earlier = jnp.concatenate([segments[:, :1] - 1, segments[:, :-1]], axis=1)
    starts = jnp.where(segments != earlier, index[None, :], jnp.zeros_like(segments))
    return index[None, :] - lax.cummax(starts, axis=1)


def angle_tables(segments, head_size):
    half_size = head_size // 2
    rates = jnp.exp(jnp.arange(half_size, dtype=jnp.float32) * (-2.0 * math.log(THETA) / head_size))
    angles = positions_of(segments).astype(jnp.float32)[..., None] * rates
    return (jnp.cos(angles), jnp.sin(angles))


def rotate(values, cosine, sine):
    half_size = values.shape[-1] // 2
    first_half = values[..., :half_size]
    second_half = values[..., half_size:]
    return jnp.concatenate(
        [first_half * cosine - second_half * sine, second_half * cosine + first_half * sine],
        axis=-1,
    )


def query_path(projected, gain, cosine, sine):
    shaped = projected.reshape(projected.shape[0], projected.shape[1], -1, gain.shape[0])
    return rotate(norm_rows(shaped, gain), cosine[:, :, None, :], sine[:, :, None, :])


def key_path(projected, gain, cosine, sine):
    return rotate(norm_rows(projected, gain), cosine, sine)


def gelu_product(gate_val, up_val):
    return jax.nn.gelu(gate_val, approximate=True) * up_val


def to_low(values):
    return values.astype(jnp.bfloat16)


def matmul(left, right):
    return jnp.dot(left, right, preferred_element_type=jnp.float32)


def matmul_left_t(left, right):
    return lax.dot_general(
        left, right, (((0,), (0,)), ((), ())), preferred_element_type=jnp.float32
    )


def matmul_right_t(left, right):
    return lax.dot_general(
        left, right, (((1,), (1,)), ((), ())), preferred_element_type=jnp.float32
    )


def attention_masks(segments):
    length = segments.shape[1]
    index = jnp.arange(length, dtype=jnp.int32)
    causal = index[None, :] <= index[:, None]
    return (segments[:, :, None] == segments[:, None, :]) & causal[None]


def scores_of(q_low, k_low, masks):
    scores = SCALE * jnp.einsum("nqhd,nkd->nhqk", q_low, k_low, preferred_element_type=jnp.float32)
    return jnp.where(masks[:, None], scores, MASKED)


def spread_gain(values):
    return jnp.broadcast_to(values[:, None], (values.shape[0], lax.axis_size("replica")))


def general_body(
    layer_in,
    d_out,
    segments,
    w_q,
    w_k,
    w_v,
    w_o,
    attn_pre,
    attn_post,
    q_gain,
    k_gain,
    w_gate,
    w_up,
    w_down,
    mlp_pre,
    mlp_post,
):
    attn_set = (
        lax.all_gather(to_low(w_q), "fsdp", axis=0, tiled=True),
        lax.all_gather(to_low(w_k), "fsdp", axis=0, tiled=True),
        lax.all_gather(to_low(w_v), "fsdp", axis=0, tiled=True),
        lax.all_gather(to_low(w_o), "fsdp", axis=0, tiled=True),
        lax.all_gather(to_low(attn_pre), "fsdp", axis=0, tiled=True),
        lax.all_gather(to_low(attn_post), "fsdp", axis=0, tiled=True),
        lax.all_gather(to_low(q_gain), "fsdp", axis=0, tiled=True),
        lax.all_gather(to_low(k_gain), "fsdp", axis=0, tiled=True),
    )
    q_full, k_full, v_full, o_full = (attn_set[0], attn_set[1], attn_set[2], attn_set[3])
    gain_apre = attn_set[4].astype(jnp.float32)
    gain_apost = attn_set[5].astype(jnp.float32)
    gain_q = attn_set[6].astype(jnp.float32)
    gain_k = attn_set[7].astype(jnp.float32)
    mlp_set = (
        lax.all_gather(to_low(w_gate), "fsdp", axis=0, tiled=True),
        lax.all_gather(to_low(w_up), "fsdp", axis=0, tiled=True),
        lax.all_gather(to_low(w_down), "fsdp", axis=0, tiled=True),
        lax.all_gather(to_low(mlp_pre), "fsdp", axis=0, tiled=True),
        lax.all_gather(to_low(mlp_post), "fsdp", axis=0, tiled=True),
    )
    gate_full, up_full, down_full = (mlp_set[0], mlp_set[1], mlp_set[2])
    gain_mpre = mlp_set[3].astype(jnp.float32)
    gain_mpost = mlp_set[4].astype(jnp.float32)
    seq_count, seq_len = segments.shape
    tok_flat = layer_in.astype(jnp.float32)
    cosine, sine = angle_tables(segments, gain_q.shape[0])
    masks = attention_masks(segments)
    normed_a, pull_a = jax.vjp(norm_rows, tok_flat, gain_apre)
    a_low = to_low(normed_a)
    q_proj = matmul(a_low, q_full).reshape(seq_count, seq_len, -1)
    k_proj = matmul(a_low, k_full).reshape(seq_count, seq_len, -1)
    v_proj = matmul(a_low, v_full)
    q_rot, pull_q = jax.vjp(partial(query_path, cosine=cosine, sine=sine), q_proj, gain_q)
    k_rot, pull_k = jax.vjp(partial(key_path, cosine=cosine, sine=sine), k_proj, gain_k)
    q_low = to_low(q_rot)
    k_low = to_low(k_rot)
    v_low = to_low(v_proj).reshape(seq_count, seq_len, -1)
    scores = scores_of(q_low, k_low, masks)
    top_val = jnp.max(scores, axis=-1, keepdims=True)
    log_total = top_val + jnp.log(jnp.sum(jnp.exp(scores - top_val), axis=-1, keepdims=True))
    p_low = to_low(jnp.exp(scores - log_total))
    attn_mix = jnp.einsum("nhqk,nkd->nqhd", p_low, v_low, preferred_element_type=jnp.float32)
    o_low = to_low(attn_mix.reshape(seq_count * seq_len, -1))
    attn_proj = matmul(o_low, o_full)
    post_attn, pull_pa = jax.vjp(norm_rows, attn_proj, gain_apost)
    h_mid = tok_flat + post_attn
    normed_m, pull_m = jax.vjp(norm_rows, h_mid, gain_mpre)
    m_low = to_low(normed_m)
    gate_val = matmul(m_low, gate_full)
    up_val = matmul(m_low, up_full)
    hidden, pull_h = jax.vjp(gelu_product, gate_val, up_val)
    h_low = to_low(hidden)
    down_val = matmul(h_low, down_full)
    post_mlp, pull_pm = jax.vjp(norm_rows, down_val, gain_mpost)
    layer_out = (h_mid + post_mlp).astype(jnp.bfloat16)
    gate_full, up_full, down_full = (
        lax.all_gather(to_low(w_gate), "fsdp", axis=0, tiled=True),
        lax.all_gather(to_low(w_up), "fsdp", axis=0, tiled=True),
        lax.all_gather(to_low(w_down), "fsdp", axis=0, tiled=True),
    )
    grad_top = d_out.astype(jnp.float32)
    d_down, grad_mpost = pull_pm(grad_top)
    d_down_low = to_low(d_down)
    grad_wdown = matmul_left_t(h_low, d_down_low)
    d_hidden = matmul_right_t(d_down_low, down_full)
    d_gate, d_up = pull_h(d_hidden)
    d_gate_low = to_low(d_gate)
    d_up_low = to_low(d_up)
    grad_wgate = matmul_left_t(m_low, d_gate_low)
    grad_wup = matmul_left_t(m_low, d_up_low)
    d_normed = matmul_right_t(d_gate_low, gate_full) + matmul_right_t(d_up_low, up_full)
    d_mid_norm, grad_mpre = pull_m(d_normed)
    d_mid = grad_top + d_mid_norm
    q_full, k_full, v_full, o_full = (
        lax.all_gather(to_low(w_q), "fsdp", axis=0, tiled=True),
        lax.all_gather(to_low(w_k), "fsdp", axis=0, tiled=True),
        lax.all_gather(to_low(w_v), "fsdp", axis=0, tiled=True),
        lax.all_gather(to_low(w_o), "fsdp", axis=0, tiled=True),
    )
    d_attn, grad_apost = pull_pa(d_mid)
    d_attn_low = to_low(d_attn)
    grad_wo = matmul_left_t(o_low, d_attn_low)
    d_mix_low = to_low(matmul_right_t(d_attn_low, o_full)).reshape(
        seq_count, seq_len, -1, k_low.shape[-1]
    )
    probs = jnp.exp(scores_of(q_low, k_low, masks) - log_total)
    d_probs = jnp.einsum("nqhd,nkd->nhqk", d_mix_low, v_low, preferred_element_type=jnp.float32)
    row_dot = jnp.sum(probs * d_probs, axis=-1, keepdims=True)
    d_scores_low = to_low(probs * (d_probs - row_dot))
    d_query = SCALE * jnp.einsum(
        "nhqk,nkd->nqhd", d_scores_low, k_low, preferred_element_type=jnp.float32
    )
    d_key = SCALE * jnp.einsum(
        "nhqk,nqhd->nkd", d_scores_low, q_low, preferred_element_type=jnp.float32
    )
    d_value = jnp.einsum("nhqk,nqhd->nkd", p_low, d_mix_low, preferred_element_type=jnp.float32)
    d_qproj, grad_qgain = pull_q(d_query)
    d_kproj, grad_kgain = pull_k(d_key)
    d_q_low = to_low(d_qproj.reshape(seq_count * seq_len, -1))
    d_k_low = to_low(d_kproj.reshape(seq_count * seq_len, -1))
    d_v_low = to_low(d_value.reshape(seq_count * seq_len, -1))
    grad_wq = matmul_left_t(a_low, d_q_low)
    grad_wk = matmul_left_t(a_low, d_k_low)
    grad_wv = matmul_left_t(a_low, d_v_low)
    d_normed_a = (
        matmul_right_t(d_q_low, q_full)
        + matmul_right_t(d_k_low, k_full)
        + matmul_right_t(d_v_low, v_full)
    )
    d_input_norm, grad_apre = pull_a(d_normed_a)
    grad_x = (d_mid + d_input_norm).astype(jnp.bfloat16)
    all_shards = (
        lax.psum_scatter(grad_wq, "fsdp", scatter_dimension=0, tiled=True),
        lax.psum_scatter(grad_wk, "fsdp", scatter_dimension=0, tiled=True),
        lax.psum_scatter(grad_wv, "fsdp", scatter_dimension=0, tiled=True),
        lax.psum_scatter(grad_wo, "fsdp", scatter_dimension=0, tiled=True),
        lax.psum_scatter(grad_apre, "fsdp", scatter_dimension=0, tiled=True),
        lax.psum_scatter(grad_apost, "fsdp", scatter_dimension=0, tiled=True),
        lax.psum_scatter(grad_qgain, "fsdp", scatter_dimension=0, tiled=True),
        lax.psum_scatter(grad_kgain, "fsdp", scatter_dimension=0, tiled=True),
        lax.psum_scatter(grad_wgate, "fsdp", scatter_dimension=0, tiled=True),
        lax.psum_scatter(grad_wup, "fsdp", scatter_dimension=0, tiled=True),
        lax.psum_scatter(grad_wdown, "fsdp", scatter_dimension=0, tiled=True),
        lax.psum_scatter(grad_mpre, "fsdp", scatter_dimension=0, tiled=True),
        lax.psum_scatter(grad_mpost, "fsdp", scatter_dimension=0, tiled=True),
    )
    all_cols = (
        lax.psum_scatter(
            all_shards[0].astype(jnp.bfloat16), "replica", scatter_dimension=1, tiled=True
        ).astype(jnp.float32),
        lax.psum_scatter(
            all_shards[1].astype(jnp.bfloat16), "replica", scatter_dimension=1, tiled=True
        ).astype(jnp.float32),
        lax.psum_scatter(
            all_shards[2].astype(jnp.bfloat16), "replica", scatter_dimension=1, tiled=True
        ).astype(jnp.float32),
        lax.psum_scatter(
            all_shards[3].astype(jnp.bfloat16), "replica", scatter_dimension=1, tiled=True
        ).astype(jnp.float32),
        lax.psum_scatter(
            all_shards[8].astype(jnp.bfloat16), "replica", scatter_dimension=1, tiled=True
        ).astype(jnp.float32),
        lax.psum_scatter(
            all_shards[9].astype(jnp.bfloat16), "replica", scatter_dimension=1, tiled=True
        ).astype(jnp.float32),
        lax.psum_scatter(
            all_shards[10].astype(jnp.bfloat16), "replica", scatter_dimension=1, tiled=True
        ).astype(jnp.float32),
        lax.psum_scatter(
            spread_gain(all_shards[4]).astype(jnp.bfloat16),
            "replica",
            scatter_dimension=1,
            tiled=True,
        ).astype(jnp.float32),
        lax.psum_scatter(
            spread_gain(all_shards[5]).astype(jnp.bfloat16),
            "replica",
            scatter_dimension=1,
            tiled=True,
        ).astype(jnp.float32),
        lax.psum_scatter(
            spread_gain(all_shards[6]).astype(jnp.bfloat16),
            "replica",
            scatter_dimension=1,
            tiled=True,
        ).astype(jnp.float32),
        lax.psum_scatter(
            spread_gain(all_shards[7]).astype(jnp.bfloat16),
            "replica",
            scatter_dimension=1,
            tiled=True,
        ).astype(jnp.float32),
        lax.psum_scatter(
            spread_gain(all_shards[11]).astype(jnp.bfloat16),
            "replica",
            scatter_dimension=1,
            tiled=True,
        ).astype(jnp.float32),
        lax.psum_scatter(
            spread_gain(all_shards[12]).astype(jnp.bfloat16),
            "replica",
            scatter_dimension=1,
            tiled=True,
        ).astype(jnp.float32),
    )
    all_mats = (
        lax.all_gather(all_cols[0].astype(jnp.bfloat16), "replica", axis=1, tiled=True).astype(
            jnp.float32
        ),
        lax.all_gather(all_cols[1].astype(jnp.bfloat16), "replica", axis=1, tiled=True).astype(
            jnp.float32
        ),
        lax.all_gather(all_cols[2].astype(jnp.bfloat16), "replica", axis=1, tiled=True).astype(
            jnp.float32
        ),
        lax.all_gather(all_cols[3].astype(jnp.bfloat16), "replica", axis=1, tiled=True).astype(
            jnp.float32
        ),
        lax.all_gather(all_cols[4].astype(jnp.bfloat16), "replica", axis=1, tiled=True).astype(
            jnp.float32
        ),
        lax.all_gather(all_cols[5].astype(jnp.bfloat16), "replica", axis=1, tiled=True).astype(
            jnp.float32
        ),
        lax.all_gather(all_cols[6].astype(jnp.bfloat16), "replica", axis=1, tiled=True).astype(
            jnp.float32
        ),
    )
    attn_sums = (
        all_mats[0],
        all_mats[1],
        all_mats[2],
        all_mats[3],
        all_cols[7][:, 0],
        all_cols[8][:, 0],
        all_cols[9][:, 0],
        all_cols[10][:, 0],
    )
    mlp_sums = (all_mats[4], all_mats[5], all_mats[6], all_cols[11][:, 0], all_cols[12][:, 0])
    return (
        layer_out,
        grad_x,
        attn_sums[0],
        attn_sums[1],
        attn_sums[2],
        attn_sums[3],
        attn_sums[4],
        attn_sums[5],
        attn_sums[6],
        attn_sums[7],
        mlp_sums[0],
        mlp_sums[1],
        mlp_sums[2],
        mlp_sums[3],
        mlp_sums[4],
    )


MESH = pl.DeviceIdType.MESH
VMEM_BYTES = 60 * 2**20
F32 = jnp.float32
BF16 = jnp.bfloat16


def fits_cubes(mesh):
    return dict(mesh.shape) == {"replica": 2, "fsdp": 16}


class Place:
    def __init__(self):
        shard = lax.axis_index("fsdp")
        self.x = lax.axis_index("replica")
        self.shard = shard
        self.c = lax.rem(shard, 2)
        self.y = lax.rem(lax.div(shard, 2), 2)
        self.z = lax.div(shard, 4)
        self.zl = lax.rem(self.z, 2)
        self.zh = lax.div(self.z, 2)

    def at(self, x=None, y=None, z=None, c=None):
        x = self.x if x is None else x
        y = self.y if y is None else y
        z = self.z if z is None else z
        c = self.c if c is None else c
        return (x, (z * 2 + y) * 2 + c)

    def z_xor(self, k):
        low = self.zl if k % 2 == 0 else 1 - self.zl
        high = self.zh if k // 2 == 0 else 1 - self.zh
        return 2 * high + low

    def slice_z(self, z=None):
        z = self.z if z is None else z
        inner = lax.rem(lax.rem(z, 2) + lax.div(z, 2), 2)
        return jnp.where(self.x == 0, 2 * inner, 3 - 2 * inner)

    def cube(self, bits):
        return self.at(
            x=1 - self.x if bits & 4 else self.x,
            y=1 - self.y if bits & 2 else self.y,
            z=self.z_xor(1) if bits & 1 else self.z,
        )


class Wires:
    def __init__(self, send, recv):
        self.send, self.recv, self.used = send, recv, 0

    def remote(self, src, dst, device):
        i = self.used
        self.used += 1
        return pltpu.make_async_remote_copy(
            src_ref=src,
            dst_ref=dst,
            send_sem=self.send.at[i],
            recv_sem=self.recv.at[i],
            device_id=device,
            device_id_type=MESH,
        )

    def local(self, src, dst):
        i = self.used
        self.used += 1
        return pltpu.make_async_copy(src, dst, self.send.at[i])


def greet(devices):
    barrier = pltpu.get_barrier_semaphore()
    for device in devices:
        pl.semaphore_signal(barrier, inc=1, device_id=device, device_id_type=MESH)
    pl.semaphore_wait(barrier, len(devices))


def hbm():
    return pl.BlockSpec(memory_space=pl.ANY)


def vmem():
    return pl.BlockSpec(memory_space=pltpu.VMEM)


def sems(count):
    return [pltpu.SemaphoreType.DMA((count,)), pltpu.SemaphoreType.DMA((count,))]


def params(collective_id):
    return pltpu.CompilerParams(
        collective_id=collective_id, has_side_effects=True, vmem_limit_bytes=VMEM_BYTES
    )


X, Y, Z = 4, 2, 1


def thirds(rows):
    first = -(-rows // 48) * 16
    return ((0, first), (first, first), (2 * first, rows - 2 * first))


def add(left, right):
    return (left.astype(F32) + right.astype(F32)).astype(BF16)


class CubeSum:
    MIDDLE = ((X, Y, Y | Z), (Y, Z, X | Z), (Z, X, X | Y))
    NEAR = ((Y, Z), (Z, X), (X, Y))

    def __init__(self, p, w, parts, third, second, first):
        self.p, self.w, self.parts = p, w, parts
        self.third, self.second, self.first = third, second, first
        self.half = parts.shape[1] // 2
        self.started = []
        self.far, self.mid, self.end = {}, {}, {}

    def push(self, src, dst, bit):
        copy = self.w.remote(src, dst, self.p.cube(bit))
        copy.start()
        self.started.append(copy)
        return copy

    def send_far(self):
        for h in range(2):
            for (start, size), link in zip(thirds(self.half), (X, Y, Z)):
                at = pl.ds(h * self.half + start, size)
                self.far[link, h] = self.push(self.parts.at[7, at], self.third.at[at], link)

    def send_middle(self):
        for h in range(2):
            for i, (link, onward, place) in enumerate(self.MIDDLE):
                start, size = thirds(self.half)[i]
                at = pl.ds(h * self.half + start, size)
                all_at = pl.ds(h * self.half, self.half)
                self.far[link, h].wait_recv()
                self.parts[place, at] = add(self.parts[place, at], self.third[at, :])
                self.mid[onward, h] = self.push(
                    self.parts.at[place, all_at], self.second.at[i, all_at], onward
                )

    def send_near(self):
        for h in range(2):
            at = pl.ds(h * self.half, self.half)
            for i, (came, place) in enumerate(self.NEAR):
                self.mid[came, h].wait_recv()
                self.parts[place, at] = add(self.parts[place, at], self.second[i, at])
                self.end[place, h] = self.push(
                    self.parts.at[place, at], self.first.at[i, at], place
                )

    def finish(self):
        for h in range(2):
            at = pl.ds(h * self.half, self.half)
            value = self.parts[0, at].astype(F32)
            for i, (_, place) in enumerate(self.NEAR):
                self.end[place, h].wait_recv()
                value = value + self.first[i, at].astype(F32)
            yield at, value

    def wait_sent(self):
        for copy in self.started:
            copy.wait_send()
        self.started = []


class LightSum(CubeSum):
    def send_far(self):
        for h, link in ((0, X), (1, Y)):
            at = pl.ds(h * self.half, self.half)
            self.far[link, h] = self.push(self.parts.at[7, at], self.third.at[at], link)

    def send_middle(self):
        for h, link, place in ((0, X, Y | Z), (1, Y, X | Z)):
            at = pl.ds(h * self.half, self.half)
            self.far[link, h].wait_recv()
            self.parts[place, at] = add(self.parts[place, at], self.third[at, :])
        for h in range(2):
            at = pl.ds(h * self.half, self.half)
            for i, (link, place) in enumerate(((X, X | Z), (Y, Y | Z))):
                self.mid[link, h] = self.push(self.parts.at[place, at], self.second.at[i, at], link)
            link = (X, Y)[h]
            self.mid[X | Y, h] = self.push(self.parts.at[X | Y, at], self.second.at[2, at], link)

    def send_near(self):
        for h in range(2):
            at = pl.ds(h * self.half, self.half)
            self.mid[X, h].wait_recv()
            self.mid[Y, h].wait_recv()
            total = self.second[0, at].astype(F32) + self.second[1, at].astype(F32)
            self.parts[Z, at] = add(self.parts[Z, at], total)
            self.end[Z, h] = self.push(self.parts.at[Z, at], self.first.at[0, at], Z)
            self.mid[X | Y, h].wait_recv()
            place = (Y, X)[h]
            self.parts[place, at] = add(self.parts[place, at], self.second[2, at])
            for i, bit in ((1, X), (2, Y)):
                self.end[bit, h] = self.push(self.parts.at[bit, at], self.first.at[i, at], bit)


class CubeGather:
    def __init__(self, p, w, block, every):
        self.p, self.w, self.block, self.every = p, w, block, every
        self.half = block.shape[0] // 2
        self.started = []
        self.near, self.middle, self.far = {}, {}, {}

    def push(self, src, dst, bit):
        copy = self.w.remote(src, dst, self.p.cube(bit))
        copy.start()
        self.started.append(copy)
        return copy

    def send_near(self, h):
        at = pl.ds(h * self.half, self.half)
        for bit in (X, Y, Z):
            self.near[bit, h] = self.push(self.block.at[at], self.every.at[bit, at], bit)

    def send_middle(self, h):
        at = pl.ds(h * self.half, self.half)
        for link, relay in ((X, Y), (Y, Z), (Z, X)):
            self.near[relay, h].wait_recv()
            self.middle[link | relay, h] = self.push(
                self.every.at[relay, at], self.every.at[link | relay, at], link
            )

    def send_far(self, h):
        for (start, size), link, relay in zip(thirds(self.half), (X, Y, Z), (Y | Z, X | Z, X | Y)):
            at = pl.ds(h * self.half + start, size)
            self.middle[relay, h].wait_recv()
            self.far[link, h] = self.push(self.every.at[relay, at], self.every.at[7, at], link)

    def wait_far(self):
        for copy in self.far.values():
            copy.wait_recv()

    def wait_sent(self):
        for copy in self.started:
            copy.wait_send()
        self.started = []


def norm_scale(values):
    return lax.rsqrt(jnp.mean(values * values, axis=-1, keepdims=True) + EPS)


def norm_pull(values, scale, gain, cotangent):
    weighted = gain * cotangent
    lean = jnp.mean(values * weighted, axis=-1, keepdims=True)
    d_values = scale * weighted - values * (scale * scale * scale * lean)
    return d_values, jnp.sum(values * scale * cotangent, axis=0, keepdims=True)


def spread_matrix(width, per):
    column = lax.broadcasted_iota(jnp.int32, (128, width), 1)
    row = lax.broadcasted_iota(jnp.int32, (128, width), 0)
    place = (lax.rem(column, per) == row).astype(F32)
    column = lax.broadcasted_iota(jnp.int32, (16, width), 1)
    row = lax.broadcasted_iota(jnp.int32, (16, width), 0)
    owner = (lax.div(column, per) == row).astype(F32)
    return place, owner


def join_gains(packed, which, width, per):
    place, owner = spread_matrix(width, per)
    shards = packed[:, which, :].astype(BF16)
    wide = jnp.dot(shards, place.astype(BF16), preferred_element_type=F32)
    return jnp.sum(wide * owner, axis=0, keepdims=True)


def turn(values, cosine, sine):
    half = values.shape[-1] // 2
    u, w = values[:, :half], values[:, half:]
    return jnp.concatenate([u * cosine - w * sine, w * cosine + u * sine], axis=1)


def turn_back(values, cosine, sine):
    half = values.shape[-1] // 2
    u, w = values[:, :half], values[:, half:]
    return jnp.concatenate([u * cosine + w * sine, w * cosine - u * sine], axis=1)


def front_kernel(
    tok, seg_row, w_q, w_k, w_v, w_o, g_apre, g_apost, g_mpre, g_mpost, g_q, g_k, w_gate, w_up, w_down,
    qkv_w, out_w, gu_w, dn_w, every, gains_full, a_low, qk_proj, q_low, k_low, v_low,
    probs, o_low, attn_proj, h_mid, tables,
    qkv_s, qkv_own, qkv_send, qkv_got, out_own, gains_own, gains_s, wide_in, wide_send, wide_got,
    wide_out, down_in, down_out, m_low, out_s, send, recv, local,
):
    p = Place()
    w = Wires(send, recv)
    x, y, z, c, zl, zh = p.x, p.y, p.z, p.c, p.zl, p.zh
    sibling = p.at(c=1 - c)
    plane = [p.at(x=1 - x), p.at(y=1 - y)]
    lines = [p.at(y=yy, z=p.z_xor(k)) for yy in (y, 1 - y) for k in range(1, 4)]
    started = []

    def push(src, dst, device):
        copy = w.remote(src, dst, device)
        copy.start()
        started.append(copy)
        return copy

    loads = [
        pltpu.make_async_copy(w_gate, wide_in.at[0], local.at[0]),
        pltpu.make_async_copy(w_up, wide_in.at[1], local.at[1]),
        pltpu.make_async_copy(w_down, down_in, local.at[2]),
    ]
    for copy in loads:
        copy.start()

    rows = w_q.shape[0]
    columns = qkv_s.shape[1] // 4
    out_rows = w_o.shape[0] // 2
    mine = 2 * x + c
    theirs = 2 * x + 1 - c

    all_own = jnp.concatenate([w_q[...], w_k[...], w_v[...]], axis=1)
    for quarter in range(4):
        qkv_own[quarter] = all_own[:, quarter * columns : (quarter + 1) * columns]
    qkv_send[...] = qkv_own[theirs].astype(BF16)
    out_own[...] = w_o[...].astype(BF16)
    gains_own[...] = jnp.zeros_like(gains_own)
    for i, gain in enumerate((g_apre, g_apost, g_mpre, g_mpost, g_q, g_k)):
        gains_own[i, : gain.shape[0]] = gain[...].astype(BF16).astype(F32)
    across = p.at(x=1 - x, z=p.z_xor(3))
    greet([sibling, across] + plane + lines)

    def qkv_at(zz, yy, quarter):
        return qkv_s.at[
            pl.ds(pl.multiple_of((2 * zz + yy) * 2 * rows, 16), 2 * rows),
            pl.ds(pl.multiple_of(quarter * columns, 128), columns),
        ]

    def out_at(zz, yy, quarter):
        return out_s.at[
            pl.ds(pl.multiple_of((2 * zz + yy) * 4 * out_rows + quarter * out_rows, 16), out_rows)
        ]

    swap = push(qkv_send, qkv_got, sibling)

    def gains_at(zz, yy, cc):
        return gains_s.at[(2 * zz + yy) * 2 + cc]

    gains_s[(2 * z + y) * 2 + c] = gains_own[...]
    gain_line = [push(gains_own, gains_at(z, y, c), p.at(z=p.z_xor(k))) for k in range(1, 4)]
    gain_side = [push(gains_own, gains_at(z, y, c), plane[1])]
    holds = x == c
    out_theirs = out_own.at[pl.ds(pl.multiple_of((1 - c) * out_rows, 16), out_rows)]
    out_swap = w.remote(out_theirs, out_at(z, y, theirs), sibling)
    pl.when(holds)(out_swap.start)

    @pl.when(holds)
    def _():
        out_s[pl.ds(pl.multiple_of((2 * z + y) * 4 * out_rows + mine * out_rows, 16), out_rows)] = (
            out_own[pl.ds(pl.multiple_of(c * out_rows, 16), out_rows)]
        )

    swap.wait_recv()
    top, low = qkv_own[mine], qkv_got[...].astype(F32)
    first = jnp.where(c == 0, top, low)
    second = jnp.where(c == 0, low, top)
    base = pl.multiple_of((2 * z + y) * 2 * rows, 16)
    joined = jnp.concatenate([first, second], axis=0).astype(BF16)
    qkv_s[pl.ds(base, 2 * rows), pl.ds(pl.multiple_of(mine * columns, 128), columns)] = joined

    pl.when(jnp.logical_not(holds))(out_swap.wait_recv)
    pl.when(holds)(out_swap.wait_send)

    line = [None]
    for k in range(1, 4):
        to = p.at(z=p.z_xor(k))
        line.append(
            (
                push(qkv_at(z, y, mine), qkv_at(z, y, mine), to),
                push(out_at(z, y, mine), out_at(z, y, mine), to),
            )
        )
    side_x, side_y, corner = {}, {}, {}

    def spread(k):
        zz = p.z_xor(k)
        if k:
            for copy in line[k]:
                copy.wait_recv()
        qkv, out = qkv_at(zz, y, mine), out_at(zz, y, mine)
        side_x[k] = (push(qkv, qkv, plane[0]), push(out, out, plane[0]))
        side_y[k] = (push(qkv, qkv, plane[1]), push(out, out, plane[1]))

    def relay(k):
        zz = p.z_xor(k)
        if k % 2:
            for copy in side_y[k]:
                copy.wait_recv()
            qkv, out, to = qkv_at(zz, 1 - y, mine), out_at(zz, 1 - y, mine), plane[0]
        else:
            for copy in side_x[k]:
                copy.wait_recv()
            other = 2 * (1 - x) + c
            qkv, out, to = qkv_at(zz, y, other), out_at(zz, y, other), plane[1]
        corner[k] = (push(qkv, qkv, to), push(out, out, to))

    pairs = []

    def share(k):
        zz = p.z_xor(k)
        for copy in (side_x[k] if k % 2 else side_y[k]) + corner[k]:
            copy.wait_recv()
        for xx in range(2):
            at = qkv_s.at[
                pl.ds(pl.multiple_of(2 * zz * 2 * rows, 16), 4 * rows),
                pl.ds(pl.multiple_of((2 * xx + c) * columns, 128), columns),
            ]
            pairs.append(push(at, at, sibling))
            for yy in range(2):
                at = out_at(zz, yy, 2 * xx + c)
                pairs.append(push(at, at, sibling))

    spread(0)
    loads[0].wait()
    loads[1].wait()
    part_columns = wide_out.shape[-1]
    for xx in range(2):

        @pl.when(x == xx)
        def _():
            for zz in range(2):
                for yy in range(2):
                    part = (3 - 2 * zz if xx else 2 * zz) * 2 + yy
                    at = slice(part * part_columns, (part + 1) * part_columns)
                    for matrix in range(2):

                        @pl.when(c == 1 - matrix)
                        def _():
                            wide_send[2 * zz + yy] = wide_in[matrix, :, at].astype(BF16)

    wide_swap = push(wide_send, wide_got, sibling)
    loads[2].wait()
    down_out[...] = down_in[...].astype(BF16)
    relay(0)
    spread(1)
    wide_swap.wait_recv()
    for xx in range(2):

        @pl.when(x == xx)
        def _():
            for zz in range(2):
                for yy in range(2):
                    part = (3 - 2 * zz if xx else 2 * zz) * 2 + yy
                    at = slice(part * part_columns, (part + 1) * part_columns)
                    got = wide_got[2 * zz + yy].astype(F32)
                    for matrix in range(2):

                        @pl.when(c == matrix)
                        def _():
                            own = wide_in[matrix, :, at]
                            both = [own, got] if matrix == 0 else [got, own]
                            wide_out[2 * zz + yy] = jnp.concatenate(both, axis=0).astype(BF16)

    def gu_at(zz, yy):
        return gu_w.at[c, pl.ds(pl.multiple_of((2 * zz + yy) * 2 * rows, 16), 2 * rows)]

    wide = []
    for k in range(4):
        for other in range(2):
            yy = 1 - y if other else y
            zz = p.z_xor(k)
            inner = lax.rem(lax.rem(zz, 2) + lax.div(zz, 2), 2)
            src = wide_out.at[2 * inner + yy]
            if k == 0 and other == 0:
                own_wide = pltpu.make_async_copy(src, gu_at(z, y), local.at[0])
                own_wide.start()
            else:
                wide.append((zz, yy, push(src, gu_at(z, y), p.at(y=yy, z=zz))))
    down_rows = down_out.shape[0]
    down_at = dn_w.at[pl.ds(pl.multiple_of(c * down_rows, 16), down_rows)]
    down_local = p.slice_z() == z
    down_sends = lax.rem(zl + c, 2) == x
    down_copy = w.remote(down_out, down_at, p.at(x=zl, z=p.z_xor(3)))
    pl.when(down_sends)(down_copy.start)
    own_down = pltpu.make_async_copy(down_out, down_at, local.at[1])
    pl.when(down_local)(own_down.start)

    tok_f = tok[...].astype(F32)
    length, width = tok_f.shape
    head = k_low.shape[1]
    spread(2)
    relay(1)
    for copy in gain_line:
        copy.wait_recv()
    for k in range(1, 4):
        zz = p.z_xor(k)
        gain_side.append(push(gains_at(zz, y, c), gains_at(zz, y, c), plane[1]))
    row_seg = seg_row[...].astype(F32)
    i_at = lax.broadcasted_iota(jnp.int32, (length, length), 0)
    j_at = lax.broadcasted_iota(jnp.int32, (length, length), 1)
    col_seg = jnp.sum(jnp.where(i_at == j_at, row_seg, 0.0), axis=1, keepdims=True)
    earlier = jnp.sum((row_seg < col_seg).astype(F32), axis=1, keepdims=True)
    index = lax.broadcasted_iota(jnp.int32, (length, 1), 0).astype(F32)
    rate_at = lax.broadcasted_iota(jnp.int32, (1, head // 2), 1).astype(F32)
    rates = jnp.exp(rate_at * (-2.0 * math.log(THETA) / head))
    angles = (index - earlier) * rates
    tables[0] = jnp.cos(angles)
    tables[1] = jnp.sin(angles)
    spread(3)
    relay(2)
    share(0)
    relay(3)
    for copy in gain_side:
        copy.wait_recv()
    gain_pair = []
    for zz in range(4):
        for yy in range(2):
            gain_pair.append(push(gains_at(zz, yy, c), gains_at(zz, yy, c), sibling))
    share(1)
    for copy in gain_pair:
        copy.wait_recv()
    packed = gains_s[...]
    for i, (size, per) in enumerate(
        ((width, rows),) * 4 + ((head, head // 16),) * 2
    ):
        gains_full[i, :, :size] = join_gains(packed, i, size, per)
    a_low[...] = (tok_f * norm_scale(tok_f) * gains_full[0]).astype(BF16)
    share(2)
    share(3)
    for copy in pairs:
        copy.wait_recv()
    saves = [
        pltpu.make_async_copy(qkv_s, qkv_w, local.at[2]),
        pltpu.make_async_copy(out_s, out_w, local.at[3]),
    ]
    for copy in saves:
        copy.start()

    cosine, sine = tables[0], tables[1]
    heads = q_low.shape[1] // head
    for i in range(heads + 2):
        at = slice(i * head, (i + 1) * head)
        value = jnp.dot(a_low[...], qkv_s[:, at], preferred_element_type=F32)
        if i < heads:
            qk_proj[:, at] = value
            q_low[:, at] = turn(
                value * norm_scale(value) * gains_full[4, :, :head], cosine, sine
            ).astype(BF16)
        elif i == heads:
            qk_proj[:, at] = value
            k_low[...] = turn(
                value * norm_scale(value) * gains_full[5, :, :head], cosine, sine
            ).astype(BF16)
        else:
            v_low[...] = value.astype(BF16)
    allowed = (row_seg == col_seg) & (j_at <= i_at)
    for i in range(heads):
        at = slice(i * head, (i + 1) * head)
        scores = SCALE * lax.dot_general(
            q_low[:, at], k_low[...], (((1,), (1,)), ((), ())), preferred_element_type=F32
        )
        scores = jnp.where(allowed, scores, MASKED)
        expo = jnp.exp(scores - jnp.max(scores, axis=1, keepdims=True))
        prob = expo / jnp.sum(expo, axis=1, keepdims=True)
        probs[i] = prob
        o_low[:, at] = jnp.dot(
            prob.astype(BF16), v_low[...], preferred_element_type=F32
        ).astype(BF16)
    third = width // 3
    for i in range(3):
        at = slice(i * third, (i + 1) * third)
        attn_proj[:, at] = jnp.dot(o_low[...], out_s[:, at], preferred_element_type=F32)
    proj = attn_proj[...]
    mid = tok_f + proj * norm_scale(proj) * gains_full[1]
    h_mid[...] = mid
    m_low[...] = (mid * norm_scale(mid) * gains_full[2]).astype(BF16)

    gather = CubeGather(p, w, m_low, every)
    own = pltpu.make_async_copy(m_low, every.at[0], local.at[4])
    own.start()
    gather.send_near(0)
    gather.send_near(1)
    own_wide.wait()
    shared = [push(gu_at(z, y), gu_at(z, y), sibling)]
    gather.send_middle(0)
    gather.send_middle(1)
    gather.send_far(0)
    gather.send_far(1)
    for zz, yy, copy in reversed(wide):
        copy.wait_recv()
        shared.append(push(gu_at(zz, yy), gu_at(zz, yy), sibling))
    pl.when(down_local)(own_down.wait)
    pl.when(jnp.logical_not(down_local))(down_copy.wait_recv)
    shared.append(push(down_at, down_at, sibling))
    gather.wait_far()
    own.wait()
    gather.wait_sent()
    for copy in shared:
        copy.wait_recv()
    for copy in saves:
        copy.wait()
    pl.when(down_sends)(down_copy.wait_send)
    for copy in started:
        copy.wait_send()


def front(tok, segments, w_q, w_k, w_v, w_o, gains, w_gate, w_up, w_down, head):
    length, width = tok.shape
    rows, mix = w_q.shape
    hidden = w_gate.shape[1]
    part = hidden // 8
    down_rows = w_down.shape[0]
    total = mix + 2 * head
    heads = mix // head
    columns = total // 4
    struct = jax.ShapeDtypeStruct
    shapes = (
        struct((16 * rows, total), BF16),
        struct((16 * w_o.shape[0], width), BF16),
        struct((2, 16 * rows, part), BF16),
        struct((2 * down_rows, width), BF16),
        struct((8, length, width), BF16),
        struct((8, 1, width), F32),
        struct((length, width), BF16),
        struct((length, mix + head), F32),
        struct((length, mix), BF16),
        struct((length, head), BF16),
        struct((length, head), BF16),
        struct((heads, length, length), F32),
        struct((length, mix), BF16),
        struct((length, width), F32),
        struct((length, width), F32),
        struct((2, length, head // 2), F32),
    )
    scratch = [
        pltpu.VMEM((16 * rows, total), BF16),
        pltpu.VMEM((4, rows, columns), F32),
        pltpu.VMEM((rows, columns), BF16),
        pltpu.VMEM((rows, columns), BF16),
        pltpu.VMEM(w_o.shape, BF16),
        pltpu.VMEM((8, 128), F32),
        pltpu.VMEM((16, 8, 128), F32),
        pltpu.VMEM((2, rows, hidden), F32),
        pltpu.VMEM((4, rows, part), BF16),
        pltpu.VMEM((4, rows, part), BF16),
        pltpu.VMEM((4, 2 * rows, part), BF16),
        pltpu.VMEM((down_rows, width), F32),
        pltpu.VMEM((down_rows, width), BF16),
        pltpu.VMEM((length, width), BF16),
        pltpu.VMEM((16 * w_o.shape[0], width), BF16),
    ]
    return pl.pallas_call(
        front_kernel,
        out_shape=shapes,
        in_specs=[vmem()] * 12 + [hbm()] * 3,
        out_specs=(hbm(),) * 5 + (vmem(),) * 11,
        scratch_shapes=scratch + sems(128) + [pltpu.SemaphoreType.DMA((5,))],
        compiler_params=params(0),
        name="front",
    )(
        tok, segments, w_q, w_k, w_v, w_o, *gains, w_gate, w_up, w_down
    )


def dot_rows(left, right):
    return lax.dot_general(left, right, (((0,), (0,)), ((), ())), preferred_element_type=F32)


def dot_columns(left, right):
    return lax.dot_general(left, right, (((1,), (1,)), ((), ())), preferred_element_type=F32)


def back_kernel(
    tok, d_out, d_normed, gains_full, a_low, qk_proj, q_low, k_low, v_low, probs, o_low, attn_proj,
    h_mid, tables, g_mpost, down_two, qkv_hbm, out_hbm, wide_one,
    grad_x, qe, oe, gains_sum, wide_end, wide_back, down_end,
    qkv_w, out_w, wide_in, wide_far, d_input, wide_swap, d_attn, d_mid, d_mix, d_qkv, dqkv, dout,
    q1, o1, qa, oa, qb, ob, qc, oc,
    gain_acc, gain_got, send, recv, local,
):
    p = Place()
    w = Wires(send, recv)
    x, y, z, c, zl, zh = p.x, p.y, p.z, p.c, p.zl, p.zh
    sibling = p.at(c=1 - c)
    plane = [p.at(x=1 - x), p.at(y=1 - y)]
    line = [p.at(z=p.z_xor(k)) for k in range(1, 4)]
    cube = [p.cube(bits) for bits in range(1, 8)]
    started = []

    def push(src, dst, device):
        copy = w.remote(src, dst, device)
        copy.start()
        started.append(copy)
        return copy

    def rows_of(ref, start, size):
        return ref.at[pl.ds(pl.multiple_of(start, 16), size)]

    width = tok.shape[1]
    chip_rows = wide_one.shape[0] // 8
    half_rows = 4 * chip_rows
    far_half = half_rows * (1 - zh)
    near_half = half_rows * zh
    loads = [
        pltpu.make_async_copy(rows_of(wide_one, near_half, half_rows), wide_in, local.at[0]),
        pltpu.make_async_copy(out_hbm, out_w, local.at[2]),
        pltpu.make_async_copy(qkv_hbm, qkv_w, local.at[3]),
    ]
    for copy in loads:
        copy.start()
    greet([sibling] + plane + line + [p.cube(3)])

    pieces = (0, 1, 2, 3)
    order = (3, 1, 2, 0)

    def piece(i, zl):
        to_z = 1 - zl if i // 2 else zl
        to_y = 1 - y if i % 2 else y
        return (2 * to_z + to_y) * chip_rows

    wide_two = {}
    for i in pieces:
        at = pl.ds(i * chip_rows, chip_rows)
        wide_two[i] = push(
            rows_of(wide_one, far_half + piece(i, 1 - zl), chip_rows), wide_far.at[at], line[2]
        )
    mine = p.slice_z() == z
    down_copy = w.remote(down_two, down_end, plane[0])
    down_own = pltpu.make_async_copy(down_two, down_end, local.at[5])

    @pl.when(mine)
    def _():
        down_copy.start()
        down_own.start()

    mid = h_mid[...]
    d_value, g_mpre = norm_pull(mid, norm_scale(mid), gains_full[2], d_normed[...])
    d_mid[...] = d_out[...].astype(F32) + d_value
    proj = attn_proj[...]
    d_value, g_apost = norm_pull(proj, norm_scale(proj), gains_full[1], d_mid[...])
    d_attn[...] = d_value.astype(BF16)
    gain_acc[0, 2:3, :] = g_mpre
    gain_acc[0, 1:2, :] = g_apost

    third = width // 3
    for i in range(3):
        at = slice(i * third, (i + 1) * third)
        dout[:, at] = dot_rows(o_low[...], d_attn[:, at]).astype(BF16)
    out_rows = dout.shape[0] // 32
    columns = dqkv.shape[1] // 4

    def out_at(ref, zz, yy, quarter):
        return rows_of(ref, (2 * zz + yy) * 4 * out_rows + quarter * out_rows, out_rows)

    out_one = {
        k: [
            push(
                out_at(dout, p.z_xor(k), yy, 2 * xx + 1 - c),
                o1.at[k, xx, yy],
                sibling,
            )
            for yy in range(2)
            for xx in range(2)
        ]
        for k in order
    }
    loads[1].wait()
    d_mix[...] = dot_columns(d_attn[...], out_w[...]).astype(BF16)

    cosine, sine = tables[0], tables[1]
    head = k_low.shape[1]
    heads = q_low.shape[1] // head
    d_k, d_v, g_q = 0.0, 0.0, 0.0
    for i in range(heads):
        at = slice(i * head, (i + 1) * head)
        prob = probs[i]
        d_probs = dot_columns(d_mix[:, at], v_low[...])
        row_dot = jnp.sum(prob * d_probs, axis=1, keepdims=True)
        d_scores = (prob * (d_probs - row_dot)).astype(BF16)
        d_q = SCALE * jnp.dot(d_scores, k_low[...], preferred_element_type=F32)
        d_k = d_k + dot_rows(d_scores, q_low[:, at])
        d_v = d_v + dot_rows(prob.astype(BF16), d_mix[:, at])
        value = qk_proj[:, at]
        d_value, gain = norm_pull(
            value, norm_scale(value), gains_full[4, :, :head], turn_back(d_q, cosine, sine)
        )
        g_q = g_q + gain
        d_qkv[:, at] = d_value.astype(BF16)
    at = slice(heads * head, (heads + 1) * head)
    value = qk_proj[:, at]
    d_value, g_k = norm_pull(
        value, norm_scale(value), gains_full[5, :, :head], turn_back(SCALE * d_k, cosine, sine)
    )
    d_qkv[:, at] = d_value.astype(BF16)
    d_qkv[:, (heads + 1) * head :] = d_v.astype(BF16)
    gain_acc[0, 4:5, :] = jnp.zeros((1, width), F32)
    gain_acc[0, 5:8, :] = jnp.zeros((3, width), F32)
    gain_acc[0, 4:5, :head] = g_q
    gain_acc[0, 5:6, :head] = g_k
    for i in range(heads + 2):
        at = slice(i * head, (i + 1) * head)
        dqkv[:, at] = dot_rows(a_low[...], d_qkv[:, at]).astype(BF16)

    qkv_one = {}
    for k in order:
        rows = pl.ds(pl.multiple_of(2 * p.z_xor(k) * chip_rows, 16), 2 * chip_rows)
        qkv_one[k] = [
            push(
                dqkv.at[
                    rows, pl.ds(pl.multiple_of((2 * xx + 1 - c) * columns, 128), columns)
                ],
                q1.at[k, xx],
                sibling,
            )
            for xx in range(2)
        ]

    def own_part(k, xx, yy):
        zz = p.z_xor(k)
        rows = pl.ds(pl.multiple_of((2 * zz + yy) * chip_rows, 16), chip_rows)
        at = pl.ds(pl.multiple_of((2 * xx + c) * columns, 128), columns)
        got = pl.ds(pl.multiple_of(yy * chip_rows, 16), chip_rows)
        start = pl.multiple_of(((2 * zz + yy) * 4 + 2 * xx + c) * out_rows, 16)
        return (
            dqkv[rows, at].astype(F32) + q1[k, xx, got, :].astype(F32),
            dout[pl.ds(start, out_rows), :].astype(F32) + o1[k, xx, yy].astype(F32),
        )

    first, then, last_step = {}, {}, {}

    def plane_first(k):
        for copy in out_one[k] + qkv_one[k]:
            copy.wait_recv()
        link = k % 2
        first[k] = []
        for j in range(2):
            xx = (x if j == 0 else 1 - x) if link else 1 - x
            yy = 1 - y if link else (y if j == 0 else 1 - y)
            q, o = own_part(k, xx, yy)
            qa[k, j] = q.astype(BF16)
            oa[k, j] = o.astype(BF16)
            first[k] += [
                push(qa.at[k, j], qa.at[k, 2 + j], plane[link]),
                push(oa.at[k, j], oa.at[k, 2 + j], plane[link]),
            ]

    def plane_then(k):
        for copy in first[k]:
            copy.wait_recv()
        link = k % 2
        q, o = own_part(k, 1 - x if link else x, y if link else 1 - y)
        qb[k, 0] = (q + qa[k, 3].astype(F32)).astype(BF16)
        ob[k, 0] = (o + oa[k, 3].astype(F32)).astype(BF16)
        then[k] = [
            push(qb.at[k, 0], qb.at[k, 1], plane[1 - link]),
            push(ob.at[k, 0], ob.at[k, 1], plane[1 - link]),
        ]

    def plane_last(k):
        for copy in then[k]:
            copy.wait_recv()
        q, o = own_part(k, x, y)
        q = q + qa[k, 2].astype(F32) + qb[k, 1].astype(F32)
        o = o + oa[k, 2].astype(F32) + ob[k, 1].astype(F32)
        if k == 0:
            return q, o
        qc[k, 0] = q.astype(BF16)
        oc[k, 0] = o.astype(BF16)
        last_step[k] = [
            push(qc.at[k, 0], qc.at[k, 1], line[k - 1]),
            push(oc.at[k, 0], oc.at[k, 1], line[k - 1]),
        ]

    for k in order:
        plane_first(k)

    loads[2].wait()
    tok_f = tok[...].astype(F32)
    for i in range(3):
        at = slice(i * third, (i + 1) * third)
        d_input[:, at] = dot_columns(d_qkv[...], qkv_w[at, :])
    d_value, g_apre = norm_pull(tok_f, norm_scale(tok_f), gains_full[0], d_input[...])
    grad_x[...] = (d_mid[...] + d_value).astype(BF16)
    gain_acc[0, 0:1, :] = g_apre
    gain_acc[0, 3:4, :] = g_mpost[...]
    gain_one = push(gain_acc.at[0], gain_got.at[0], sibling)

    wide_three, wide_four, own_wide = {}, [], []

    def part_of(i):
        return 2 * p.slice_z(2 * zh + (1 - zl if i // 2 else zl)) + (1 - y if i % 2 else y)

    def wide_on(i):
        at = pl.ds(i * chip_rows, chip_rows)
        rows = pl.ds(pl.multiple_of(piece(i, zl), 16), chip_rows)
        wide_two[i].wait_recv()
        wide_far[at, :] = add(wide_in[rows, :], wide_far[at, :])
        dst = wide_end.at[part_of(0)]
        if i:
            wide_three[i] = push(wide_far.at[at], dst, p.cube(2 * (i % 2) + i // 2))
        else:
            own_wide.append(pltpu.make_async_copy(wide_far.at[at], dst, local.at[4]))
            own_wide[0].start()
            wide_four.append(push(wide_far.at[at], dst, plane[0]))

    def wide_over(i):
        wide_three[i].wait_recv()
        dst = wide_end.at[part_of(i)]
        wide_four.append(push(dst, dst, plane[0]))

    for k in order[:2]:
        plane_then(k)
    gain_one.wait_recv()
    gain_acc[1] = gain_acc[0] + gain_got[0]
    gain_two = push(gain_acc.at[1], gain_got.at[1], plane[0])
    loads[0].wait()
    wide_on(pieces[0])
    for k in order[2:]:
        plane_then(k)
    for k in order[:3]:
        plane_last(k)
    gain_two.wait_recv()
    gain_acc[2] = gain_acc[1] + gain_got[1]
    gain_three = push(gain_acc.at[2], gain_got.at[2], plane[1])
    wide_on(pieces[1])
    q, o = plane_last(0)
    for k in order[:3]:
        for copy in last_step[k]:
            copy.wait_recv()
    qe[0] = (q + qc[1, 1].astype(F32) + qc[2, 1].astype(F32) + qc[3, 1].astype(F32)).astype(BF16)
    oe[0] = (o + oc[1, 1].astype(F32) + oc[2, 1].astype(F32) + oc[3, 1].astype(F32)).astype(BF16)
    last = [
        push(qe.at[0], qe.at[4 + i], device)
        for i, device in enumerate((sibling, plane[0]))
    ] + [
        push(oe.at[0], oe.at[4 + i], device)
        for i, device in enumerate((sibling, plane[0]))
    ]
    gain_three.wait_recv()
    gain_acc[3] = gain_acc[2] + gain_got[2]
    gain_four = [push(gain_acc.at[3], gain_got.at[2 + k], line[k - 1]) for k in range(1, 4)]
    wide_on(pieces[2])
    for copy in last:
        copy.wait_recv()
    for i in pieces[:3]:
        if i and i != pieces[2]:
            wide_over(i)
    relay = [push(qe.at[5], qe.at[6], sibling), push(oe.at[5], oe.at[6], sibling)]
    wide_on(pieces[3])
    for i in pieces[2:]:
        if i:
            wide_over(i)

    for copy in relay:
        copy.wait_recv()
    rows = chip_rows // 2
    for copy in gain_four:
        copy.wait_recv()
    gains_sum[...] = gain_acc[3] + gain_got[3] + gain_got[4] + gain_got[5]

    own_wide[0].wait()
    for copy in wide_four:
        copy.wait_recv()
    for cc in range(2):

        @pl.when(c == cc)
        def _():
            for s in range(8):
                extra = (rows + 15) // 16 * 16
                at = slice(0, extra) if cc == 1 else slice(2 * rows - extra, 2 * rows)
                wide_swap[s] = wide_end[s, at, :]

    final = push(wide_swap, wide_back, sibling)
    pl.when(mine)(down_own.wait)
    pl.when(jnp.logical_not(mine))(down_copy.wait_recv)
    final.wait_recv()
    pl.when(mine)(down_copy.wait_send)
    for copy in started:
        copy.wait_send()


def back(tok, d_out, d_normed, gains_full, saved, g_mpost, down_two, qkv_w, out_w, wide_one):
    length, width = tok.shape
    total = qkv_w.shape[1]
    columns = total // 4
    mix = out_w.shape[0]
    part = wide_one.shape[1]
    chip_rows = width // 8
    rows = chip_rows // 2
    extra = (rows + 15) // 16 * 16
    piece = mix // 32
    struct = jax.ShapeDtypeStruct
    shapes = (
        struct((length, width), BF16),
        struct((7, chip_rows, columns), BF16),
        struct((7, piece, width), BF16),
        struct((8, width), F32),
        struct((8, chip_rows, part), BF16),
        struct((8, extra, part), BF16),
        struct(down_two.shape, BF16),
    )
    scratch = [
        pltpu.VMEM(qkv_w.shape, BF16),
        pltpu.VMEM(out_w.shape, BF16),
        pltpu.VMEM((width // 2, part), BF16),
        pltpu.VMEM((width // 2, part), BF16),
        pltpu.VMEM((length, width), F32),
        pltpu.VMEM((8, extra, part), BF16),
        pltpu.VMEM((length, width), BF16),
        pltpu.VMEM((length, width), F32),
        pltpu.VMEM((length, mix), BF16),
        pltpu.VMEM((length, total), BF16),
        pltpu.VMEM((width, total), BF16),
        pltpu.VMEM((mix, width), BF16),
        pltpu.VMEM((4, 2, 2 * chip_rows, columns), BF16),
        pltpu.VMEM((4, 2, 2, piece, width), BF16),
        pltpu.VMEM((4, 4, chip_rows, columns), BF16),
        pltpu.VMEM((4, 4, piece, width), BF16),
        pltpu.VMEM((4, 2, chip_rows, columns), BF16),
        pltpu.VMEM((4, 2, piece, width), BF16),
        pltpu.VMEM((4, 2, chip_rows, columns), BF16),
        pltpu.VMEM((4, 2, piece, width), BF16),
        pltpu.VMEM((4, 8, width), F32),
        pltpu.VMEM((6, 8, width), F32),
    ]
    return pl.pallas_call(
        back_kernel,
        out_shape=shapes,
        in_specs=[vmem()] * 16 + [hbm()] * 3,
        out_specs=(vmem(),) * 7,
        scratch_shapes=scratch + sems(96) + [pltpu.SemaphoreType.DMA((6,))],
        compiler_params=params(3),
        name="back",
    )(tok, d_out, d_normed, gains_full, *saved, g_mpost, down_two, qkv_w, out_w, wide_one)


def place_kernel(
    qe, oe, gains, wide_end, wide_back, down_end,
    w_q, w_k, w_v, w_o, w_gate, w_up, w_down, a_pre, a_post, m_pre, m_post, q_gain, k_gain,
):
    p = Place()
    rows, mix = w_q.shape
    head = w_k.shape[1]
    columns = qe.shape[2]
    piece = oe.shape[1]
    size = wide_end.shape[2]
    extra = wide_back.shape[1]

    def put_columns(start, value):
        for ref, first, width in ((w_q, 0, mix), (w_k, mix, head), (w_v, mix + head, head)):
            low, high = max(start, first), min(start + columns, first + width)
            if low < high:
                ref[:, low - first : high - first] = value[:, low - start : high - start]

    for xx in range(2):
        for cc in range(2):

            @pl.when((p.x == xx) & (p.c == cc))
            def _():
                for i, q in (
                    (0, 2 * xx + cc),
                    (4, 2 * xx + 1 - cc),
                    (5, 2 * (1 - xx) + cc),
                    (6, 2 * (1 - xx) + 1 - cc),
                ):
                    both = qe[i].astype(F32)
                    put_columns(q * columns, both[cc * rows : (cc + 1) * rows])
                    if q // 2 == cc:
                        w_o[(q % 2) * piece : (q % 2 + 1) * piece, :] = oe[i].astype(F32)

    for cc in range(2):

        @pl.when(p.c == cc)
        def _():
            own_ref, other_ref = (w_gate, w_up) if cc == 0 else (w_up, w_gate)
            for s in range(8):
                at = slice(s * size, (s + 1) * size)
                own_ref[:, at] = wide_end[s].astype(F32)[cc * rows : (cc + 1) * rows]
                other = wide_back[s].astype(F32)
                other_ref[:, at] = other[:rows] if cc == 0 else other[extra - rows :]

    w_down[...] = down_end[...].astype(F32)
    sums = gains[...]
    for i, ref in enumerate((a_pre, a_post, m_pre, m_post, q_gain, k_gain)):
        per = ref.shape[0]
        full = 16 * per
        turned = pltpu.roll(sums[:, :full], lax.rem(full - p.shard * per, full), 1)
        ref[...] = turned[i, :per]


def place(summed, shapes):
    return pl.pallas_call(
        place_kernel,
        out_shape=tuple(jax.ShapeDtypeStruct(shape, F32) for shape in shapes),
        in_specs=[vmem()] * 6,
        out_specs=(vmem(),) * 13,
        compiler_params=pltpu.CompilerParams(vmem_limit_bytes=VMEM_BYTES),
        name="place",
    )(*summed)


GELU_ROOT = math.sqrt(2.0 / math.pi)


def gelu_parts(gate):
    square = gate * gate
    bend = jnp.tanh(GELU_ROOT * gate * (1.0 + 0.044715 * square))
    half = 0.5 * (1.0 + bend)
    slope = half + 0.5 * gate * (1.0 - bend * bend) * GELU_ROOT * (1.0 + 3 * 0.044715 * square)
    return half * gate, slope


def tiles(size, step):
    return [slice(at, min(at + step, size)) for at in range(0, size, step)]


def mlp_kernel(
    every, gu, dn, h_mid, d_out, gains_full,
    layer_out, d_normed, g_mpost, wide_one, down_two,
    m_all, wide_w, down_w, wide, hidden, dd_own, dd_all, parts, third, second, first,
    wide_out, wide_got, grad_dn, down_got, down_sum, down_far,
    send, recv, local,
):
    p = Place()
    w = Wires(send, recv)
    order = (7, 3, 5, 6, 4, 2, 1, 0)
    loads = {r: pltpu.make_async_copy(every.at[r], m_all.at[r], local.at[r]) for r in order}
    wide_load = pltpu.make_async_copy(gu, wide_w, local.at[8])
    down_load = pltpu.make_async_copy(dn, down_w, local.at[9])
    wide_load.start()
    loads[7].start()
    down_load.start()
    for r in order[1:]:
        loads[r].start()
    c = p.c
    sibling, partner = p.at(c=1 - c), p.at(z=p.z_xor(3))
    greet([p.cube(X), p.cube(Y), p.cube(Z), sibling, partner])

    length, width = m_all.shape[1:]
    part = wide.shape[-1]
    wide_tiles = tiles(part, 256)
    down_tiles = tiles(width, 384)

    def forward(r):
        for at in wide_tiles:
            g = jnp.dot(m_all[r], wide_w[0, :, at], preferred_element_type=F32)
            u = jnp.dot(m_all[r], wide_w[1, :, at], preferred_element_type=F32)
            wide[0, r, :, at] = g.astype(BF16)
            wide[1, r, :, at] = u.astype(BF16)
            value, _ = gelu_parts(g)
            hidden[r, :, at] = (value * u).astype(BF16)
        for at in down_tiles:
            parts[r, :, at] = jnp.dot(
                hidden[r], down_w[:, at], preferred_element_type=F32
            ).astype(BF16)

    def backward(r):
        for at in wide_tiles:
            d_hidden = dot_columns(dd_all[r], down_w[at, :])
            value, slope = gelu_parts(wide[0, r, :, at].astype(F32))
            up = wide[1, r, :, at].astype(F32)
            wide[0, r, :, at] = (d_hidden * up * slope).astype(BF16)
            wide[1, r, :, at] = (d_hidden * value).astype(BF16)
        d_gate = wide[0, r]
        d_up = wide[1, r]
        for at in down_tiles:
            parts[r, :, at] = (
                dot_columns(d_gate, wide_w[0, at, :]) + dot_columns(d_up, wide_w[1, at, :])
            ).astype(BF16)

    def several(step, places):
        lax.fori_loop(0, 3, lambda i, _: (step(places(i)), 0)[1], 0)

    def middles(i):
        return 7 - lax.shift_right_logical(jnp.int32(4), i)

    def nears(i):
        return lax.shift_right_logical(jnp.int32(4), i)

    total = CubeSum(p, w, parts, third, second, first)
    wide_load.wait()
    loads[7].wait()
    down_load.wait()
    forward(7)
    total.send_far()
    for r in order[1:]:
        loads[r].wait()
    several(forward, middles)
    total.send_middle()
    several(forward, nears)
    total.send_near()
    forward(0)

    gather = CubeGather(p, w, dd_own, dd_all)
    gain = gains_full[3]
    g_rows = 0.0
    for h, (at, value) in enumerate(total.finish()):
        scale = norm_scale(value)
        layer_out[at, :] = (h_mid[at, :] + value * scale * gain).astype(BF16)
        d_value, g_part = norm_pull(value, scale, gain, d_out[at, :].astype(F32))
        dd_own[at, :] = d_value.astype(BF16)
        g_rows = g_rows + g_part
        gather.send_near(h)
    g_mpost[...] = g_rows
    dd_all[0] = dd_own[...]
    total.wait_sent()
    backward(0)
    gather.send_middle(0)
    gather.send_middle(1)
    several(backward, nears)
    gather.send_far(0)
    gather.send_far(1)
    several(backward, middles)
    gather.wait_far()
    backward(7)

    total = LightSum(p, w, parts, third, second, first)
    total.send_far()
    grad_rows = 384
    all_rows = 8 * length
    for at in down_tiles:
        grad_dn[:, at] = dot_rows(
            hidden[...].reshape(all_rows, part), dd_all[:, :, at].reshape(all_rows, -1)
        ).astype(BF16)
    down_rows = down_sum.shape[0]
    give = grad_dn.at[pl.ds(pl.multiple_of((1 - c) * down_rows, 16), down_rows)]
    down_one = w.remote(give, down_got, sibling)
    down_one.start()
    total.send_middle()

    def grad_wide(matrix, out):
        def step(i, _):
            at = pl.ds(pl.multiple_of(i * grad_rows, 128), grad_rows)
            left = m_all[:, :, at].reshape(all_rows, grad_rows)
            out[at, :] = dot_rows(left, wide[matrix].reshape(all_rows, part)).astype(BF16)
            return 0

        lax.fori_loop(0, width // grad_rows, step, 0)

    grad_wide(1 - c, wide_out)
    wide_swap = w.remote(wide_out, wide_got, sibling)
    wide_swap.start()
    down_one.wait_recv()
    keep = pl.ds(pl.multiple_of(c * down_rows, 16), down_rows)
    down_sum[...] = add(grad_dn[keep, :], down_got[...])
    down_over = w.remote(down_sum, down_far, partner)
    mine = p.slice_z() == p.z
    pl.when(jnp.logical_not(mine))(down_over.start)
    total.send_near()
    grad_wide(c, wide_one)
    wide_swap.wait_recv()
    wide_one[...] = add(wide_one[...], wide_got[...])
    for at, value in total.finish():
        d_normed[at, :] = value
    pl.when(mine)(down_over.wait_recv)

    @pl.when(mine)
    def _():
        down_two[...] = add(down_sum[...], down_far[...])

    pl.when(jnp.logical_not(mine))(down_over.wait_send)
    down_one.wait_send()
    wide_swap.wait_send()
    total.wait_sent()
    gather.wait_sent()


def mlp(every, gu, dn, h_mid, d_out, gains_full):
    _, length, width = every.shape
    part = dn.shape[0]
    struct = jax.ShapeDtypeStruct
    blocks = (8, length, width)
    return pl.pallas_call(
        mlp_kernel,
        out_shape=(
            struct((length, width), BF16),
            struct((length, width), F32),
            struct((1, width), F32),
            struct((width, part), BF16),
            struct((part // 2, width), BF16),
        ),
        in_specs=[hbm()] * 3 + [vmem()] * 3,
        out_specs=(vmem(),) * 5,
        scratch_shapes=[
            pltpu.VMEM(blocks, BF16),
            pltpu.VMEM(gu.shape, BF16),
            pltpu.VMEM(dn.shape, BF16),
            pltpu.VMEM((2, 8, length, part), BF16),
            pltpu.VMEM((8, length, part), BF16),
            pltpu.VMEM((length, width), BF16),
            pltpu.VMEM(blocks, BF16),
            pltpu.VMEM(blocks, BF16),
            pltpu.VMEM((length, width), BF16),
            pltpu.VMEM((3, length, width), BF16),
            pltpu.VMEM((3, length, width), BF16),
            pltpu.VMEM((width, part), BF16),
            pltpu.VMEM((width, part), BF16),
            pltpu.VMEM(dn.shape, BF16),
            pltpu.VMEM((part // 2, width), BF16),
            pltpu.VMEM((part // 2, width), BF16),
            pltpu.VMEM((part // 2, width), BF16),
        ]
        + sems(64)
        + [pltpu.SemaphoreType.DMA((10,))],
        compiler_params=params(1),
        name="mlp",
    )(every, gu, dn, h_mid, d_out, gains_full)


def cube_body(
    layer_in, d_out, segments, w_q, w_k, w_v, w_o, attn_pre, attn_post, q_gain, k_gain,
    w_gate, w_up, w_down, mlp_pre, mlp_post,
):
    width = layer_in.shape[1]
    head = q_gain.shape[0] * 16
    rows, mix = w_q.shape
    gain_list = [attn_pre, attn_post, mlp_pre, mlp_post, q_gain, k_gain]
    (
        qkv_w, out_w, gu_w, down_w, m_all, gains_full, a_low, qk_proj, q_low, k_low, v_low,
        probs, o_low, attn_proj, h_mid, tables,
    ) = front(
        layer_in, segments, w_q, w_k, w_v, w_o, gain_list, w_gate, w_up, w_down, head
    )
    layer_out, d_normed, g_mpost, wide_one, down_two = mlp(
        m_all, gu_w, down_w, h_mid, d_out, gains_full
    )
    saved = (a_low, qk_proj, q_low, k_low, v_low, probs, o_low, attn_proj, h_mid, tables)
    grad_x, *summed = back(
        layer_in, d_out, d_normed, gains_full, saved, g_mpost, down_two, qkv_w, out_w, wide_one
    )
    matrices = [w_q, w_k, w_v, w_o, w_gate, w_up, w_down]
    grads = place(summed, [v.shape for v in matrices + gain_list])
    g_apre, g_apost, g_mpre, g_mpost, g_q, g_k = grads[7:]
    return (
        layer_out,
        grad_x,
        *grads[:4],
        g_apre,
        g_apost,
        g_q,
        g_k,
        *grads[4:7],
        g_mpre,
        g_mpost,
    )


def solution(mesh):
    in_specs = (
        P(("replica", "fsdp"), None),
        P(("replica", "fsdp"), None),
        P(("replica", "fsdp"), None),
        P("fsdp", None),
        P("fsdp", None),
        P("fsdp", None),
        P("fsdp", None),
        P("fsdp"),
        P("fsdp"),
        P("fsdp"),
        P("fsdp"),
        P("fsdp", None),
        P("fsdp", None),
        P("fsdp", None),
        P("fsdp"),
        P("fsdp"),
    )
    out_specs = (
        P(("replica", "fsdp"), None),
        P(("replica", "fsdp"), None),
        P("fsdp", None),
        P("fsdp", None),
        P("fsdp", None),
        P("fsdp", None),
        P("fsdp"),
        P("fsdp"),
        P("fsdp"),
        P("fsdp"),
        P("fsdp", None),
        P("fsdp", None),
        P("fsdp", None),
        P("fsdp"),
        P("fsdp"),
    )
    body = cube_body if fits_cubes(mesh) else general_body
    return jax.shard_map(body, mesh=mesh, in_specs=in_specs, out_specs=out_specs, check_vma=False)
```

```python
from functools import partial
import math

import jax
import jax.numpy as jnp
from jax import lax
from jax.experimental import pallas as pl
from jax.experimental.pallas import tpu as pltpu
from jax.sharding import PartitionSpec as P

EPS = 1e-06
THETA = 1000000.0
SCALE = 0.0625
MASKED = -1e30


def norm_rows(values, gain):
    return values * lax.rsqrt(jnp.mean(values * values, axis=-1, keepdims=True) + EPS) * gain


def positions_of(segments):
    length = segments.shape[-1]
    index = jnp.arange(length, dtype=jnp.int32)
    earlier = jnp.concatenate([segments[:, :1] - 1, segments[:, :-1]], axis=1)
    starts = jnp.where(segments != earlier, index[None, :], jnp.zeros_like(segments))
    return index[None, :] - lax.cummax(starts, axis=1)


def angle_tables(segments, head_size):
    half_size = head_size // 2
    rates = jnp.exp(jnp.arange(half_size, dtype=jnp.float32) * (-2.0 * math.log(THETA) / head_size))
    angles = positions_of(segments).astype(jnp.float32)[..., None] * rates
    return (jnp.cos(angles), jnp.sin(angles))


def rotate(values, cosine, sine):
    half_size = values.shape[-1] // 2
    first_half = values[..., :half_size]
    second_half = values[..., half_size:]
    return jnp.concatenate(
        [first_half * cosine - second_half * sine, second_half * cosine + first_half * sine],
        axis=-1,
    )


def query_path(projected, gain, cosine, sine):
    shaped = projected.reshape(projected.shape[0], projected.shape[1], -1, gain.shape[0])
    return rotate(norm_rows(shaped, gain), cosine[:, :, None, :], sine[:, :, None, :])


def key_path(projected, gain, cosine, sine):
    return rotate(norm_rows(projected, gain), cosine, sine)


def gelu_product(gate_val, up_val):
    return jax.nn.gelu(gate_val, approximate=True) * up_val


def to_low(values):
    return values.astype(jnp.bfloat16)


def matmul(left, right):
    return jnp.dot(left, right, preferred_element_type=jnp.float32)


def matmul_left_t(left, right):
    return lax.dot_general(
        left, right, (((0,), (0,)), ((), ())), preferred_element_type=jnp.float32
    )


def matmul_right_t(left, right):
    return lax.dot_general(
        left, right, (((1,), (1,)), ((), ())), preferred_element_type=jnp.float32
    )


def attention_masks(segments):
    length = segments.shape[1]
    index = jnp.arange(length, dtype=jnp.int32)
    causal = index[None, :] <= index[:, None]
    return (segments[:, :, None] == segments[:, None, :]) & causal[None]


def scores_of(q_low, k_low, masks):
    scores = SCALE * jnp.einsum("nqhd,nkd->nhqk", q_low, k_low, preferred_element_type=jnp.float32)
    return jnp.where(masks[:, None], scores, MASKED)


def spread_gain(values):
    return jnp.broadcast_to(values[:, None], (values.shape[0], lax.axis_size("replica")))


def general_body(
    layer_in,
    d_out,
    segments,
    w_q,
    w_k,
    w_v,
    w_o,
    attn_pre,
    attn_post,
    q_gain,
    k_gain,
    w_gate,
    w_up,
    w_down,
    mlp_pre,
    mlp_post,
):
    attn_set = (
        lax.all_gather(to_low(w_q), "fsdp", axis=0, tiled=True),
        lax.all_gather(to_low(w_k), "fsdp", axis=0, tiled=True),
        lax.all_gather(to_low(w_v), "fsdp", axis=0, tiled=True),
        lax.all_gather(to_low(w_o), "fsdp", axis=0, tiled=True),
        lax.all_gather(to_low(attn_pre), "fsdp", axis=0, tiled=True),
        lax.all_gather(to_low(attn_post), "fsdp", axis=0, tiled=True),
        lax.all_gather(to_low(q_gain), "fsdp", axis=0, tiled=True),
        lax.all_gather(to_low(k_gain), "fsdp", axis=0, tiled=True),
    )
    q_full, k_full, v_full, o_full = (attn_set[0], attn_set[1], attn_set[2], attn_set[3])
    gain_apre = attn_set[4].astype(jnp.float32)
    gain_apost = attn_set[5].astype(jnp.float32)
    gain_q = attn_set[6].astype(jnp.float32)
    gain_k = attn_set[7].astype(jnp.float32)
    mlp_set = (
        lax.all_gather(to_low(w_gate), "fsdp", axis=0, tiled=True),
        lax.all_gather(to_low(w_up), "fsdp", axis=0, tiled=True),
        lax.all_gather(to_low(w_down), "fsdp", axis=0, tiled=True),
        lax.all_gather(to_low(mlp_pre), "fsdp", axis=0, tiled=True),
        lax.all_gather(to_low(mlp_post), "fsdp", axis=0, tiled=True),
    )
    gate_full, up_full, down_full = (mlp_set[0], mlp_set[1], mlp_set[2])
    gain_mpre = mlp_set[3].astype(jnp.float32)
    gain_mpost = mlp_set[4].astype(jnp.float32)
    seq_count, seq_len = segments.shape
    tok_flat = layer_in.astype(jnp.float32)
    cosine, sine = angle_tables(segments, gain_q.shape[0])
    masks = attention_masks(segments)
    normed_a, pull_a = jax.vjp(norm_rows, tok_flat, gain_apre)
    a_low = to_low(normed_a)
    q_proj = matmul(a_low, q_full).reshape(seq_count, seq_len, -1)
    k_proj = matmul(a_low, k_full).reshape(seq_count, seq_len, -1)
    v_proj = matmul(a_low, v_full)
    q_rot, pull_q = jax.vjp(partial(query_path, cosine=cosine, sine=sine), q_proj, gain_q)
    k_rot, pull_k = jax.vjp(partial(key_path, cosine=cosine, sine=sine), k_proj, gain_k)
    q_low = to_low(q_rot)
    k_low = to_low(k_rot)
    v_low = to_low(v_proj).reshape(seq_count, seq_len, -1)
    scores = scores_of(q_low, k_low, masks)
    top_val = jnp.max(scores, axis=-1, keepdims=True)
    log_total = top_val + jnp.log(jnp.sum(jnp.exp(scores - top_val), axis=-1, keepdims=True))
    p_low = to_low(jnp.exp(scores - log_total))
    attn_mix = jnp.einsum("nhqk,nkd->nqhd", p_low, v_low, preferred_element_type=jnp.float32)
    o_low = to_low(attn_mix.reshape(seq_count * seq_len, -1))
    attn_proj = matmul(o_low, o_full)
    post_attn, pull_pa = jax.vjp(norm_rows, attn_proj, gain_apost)
    h_mid = tok_flat + post_attn
    normed_m, pull_m = jax.vjp(norm_rows, h_mid, gain_mpre)
    m_low = to_low(normed_m)
    gate_val = matmul(m_low, gate_full)
    up_val = matmul(m_low, up_full)
    hidden, pull_h = jax.vjp(gelu_product, gate_val, up_val)
    h_low = to_low(hidden)
    down_val = matmul(h_low, down_full)
    post_mlp, pull_pm = jax.vjp(norm_rows, down_val, gain_mpost)
    layer_out = (h_mid + post_mlp).astype(jnp.bfloat16)
    gate_full, up_full, down_full = (
        lax.all_gather(to_low(w_gate), "fsdp", axis=0, tiled=True),
        lax.all_gather(to_low(w_up), "fsdp", axis=0, tiled=True),
        lax.all_gather(to_low(w_down), "fsdp", axis=0, tiled=True),
    )
    grad_top = d_out.astype(jnp.float32)
    d_down, grad_mpost = pull_pm(grad_top)
    d_down_low = to_low(d_down)
    grad_wdown = matmul_left_t(h_low, d_down_low)
    d_hidden = matmul_right_t(d_down_low, down_full)
    d_gate, d_up = pull_h(d_hidden)
    d_gate_low = to_low(d_gate)
    d_up_low = to_low(d_up)
    grad_wgate = matmul_left_t(m_low, d_gate_low)
    grad_wup = matmul_left_t(m_low, d_up_low)
    d_normed = matmul_right_t(d_gate_low, gate_full) + matmul_right_t(d_up_low, up_full)
    d_mid_norm, grad_mpre = pull_m(d_normed)
    d_mid = grad_top + d_mid_norm
    q_full, k_full, v_full, o_full = (
        lax.all_gather(to_low(w_q), "fsdp", axis=0, tiled=True),
        lax.all_gather(to_low(w_k), "fsdp", axis=0, tiled=True),
        lax.all_gather(to_low(w_v), "fsdp", axis=0, tiled=True),
        lax.all_gather(to_low(w_o), "fsdp", axis=0, tiled=True),
    )
    d_attn, grad_apost = pull_pa(d_mid)
    d_attn_low = to_low(d_attn)
    grad_wo = matmul_left_t(o_low, d_attn_low)
    d_mix_low = to_low(matmul_right_t(d_attn_low, o_full)).reshape(
        seq_count, seq_len, -1, k_low.shape[-1]
    )
    probs = jnp.exp(scores_of(q_low, k_low, masks) - log_total)
    d_probs = jnp.einsum("nqhd,nkd->nhqk", d_mix_low, v_low, preferred_element_type=jnp.float32)
    row_dot = jnp.sum(probs * d_probs, axis=-1, keepdims=True)
    d_scores_low = to_low(probs * (d_probs - row_dot))
    d_query = SCALE * jnp.einsum(
        "nhqk,nkd->nqhd", d_scores_low, k_low, preferred_element_type=jnp.float32
    )
    d_key = SCALE * jnp.einsum(
        "nhqk,nqhd->nkd", d_scores_low, q_low, preferred_element_type=jnp.float32
    )
    d_value = jnp.einsum("nhqk,nqhd->nkd", p_low, d_mix_low, preferred_element_type=jnp.float32)
    d_qproj, grad_qgain = pull_q(d_query)
    d_kproj, grad_kgain = pull_k(d_key)
    d_q_low = to_low(d_qproj.reshape(seq_count * seq_len, -1))
    d_k_low = to_low(d_kproj.reshape(seq_count * seq_len, -1))
    d_v_low = to_low(d_value.reshape(seq_count * seq_len, -1))
    grad_wq = matmul_left_t(a_low, d_q_low)
    grad_wk = matmul_left_t(a_low, d_k_low)
    grad_wv = matmul_left_t(a_low, d_v_low)
    d_normed_a = (
        matmul_right_t(d_q_low, q_full)
        + matmul_right_t(d_k_low, k_full)
        + matmul_right_t(d_v_low, v_full)
    )
    d_input_norm, grad_apre = pull_a(d_normed_a)
    grad_x = (d_mid + d_input_norm).astype(jnp.bfloat16)
    all_shards = (
        lax.psum_scatter(grad_wq, "fsdp", scatter_dimension=0, tiled=True),
        lax.psum_scatter(grad_wk, "fsdp", scatter_dimension=0, tiled=True),
        lax.psum_scatter(grad_wv, "fsdp", scatter_dimension=0, tiled=True),
        lax.psum_scatter(grad_wo, "fsdp", scatter_dimension=0, tiled=True),
        lax.psum_scatter(grad_apre, "fsdp", scatter_dimension=0, tiled=True),
        lax.psum_scatter(grad_apost, "fsdp", scatter_dimension=0, tiled=True),
        lax.psum_scatter(grad_qgain, "fsdp", scatter_dimension=0, tiled=True),
        lax.psum_scatter(grad_kgain, "fsdp", scatter_dimension=0, tiled=True),
        lax.psum_scatter(grad_wgate, "fsdp", scatter_dimension=0, tiled=True),
        lax.psum_scatter(grad_wup, "fsdp", scatter_dimension=0, tiled=True),
        lax.psum_scatter(grad_wdown, "fsdp", scatter_dimension=0, tiled=True),
        lax.psum_scatter(grad_mpre, "fsdp", scatter_dimension=0, tiled=True),
        lax.psum_scatter(grad_mpost, "fsdp", scatter_dimension=0, tiled=True),
    )
    all_cols = (
        lax.psum_scatter(
            all_shards[0].astype(jnp.bfloat16), "replica", scatter_dimension=1, tiled=True
        ).astype(jnp.float32),
        lax.psum_scatter(
            all_shards[1].astype(jnp.bfloat16), "replica", scatter_dimension=1, tiled=True
        ).astype(jnp.float32),
        lax.psum_scatter(
            all_shards[2].astype(jnp.bfloat16), "replica", scatter_dimension=1, tiled=True
        ).astype(jnp.float32),
        lax.psum_scatter(
            all_shards[3].astype(jnp.bfloat16), "replica", scatter_dimension=1, tiled=True
        ).astype(jnp.float32),
        lax.psum_scatter(
            all_shards[8].astype(jnp.bfloat16), "replica", scatter_dimension=1, tiled=True
        ).astype(jnp.float32),
        lax.psum_scatter(
            all_shards[9].astype(jnp.bfloat16), "replica", scatter_dimension=1, tiled=True
        ).astype(jnp.float32),
        lax.psum_scatter(
            all_shards[10].astype(jnp.bfloat16), "replica", scatter_dimension=1, tiled=True
        ).astype(jnp.float32),
        lax.psum_scatter(
            spread_gain(all_shards[4]).astype(jnp.bfloat16),
            "replica",
            scatter_dimension=1,
            tiled=True,
        ).astype(jnp.float32),
        lax.psum_scatter(
            spread_gain(all_shards[5]).astype(jnp.bfloat16),
            "replica",
            scatter_dimension=1,
            tiled=True,
        ).astype(jnp.float32),
        lax.psum_scatter(
            spread_gain(all_shards[6]).astype(jnp.bfloat16),
            "replica",
            scatter_dimension=1,
            tiled=True,
        ).astype(jnp.float32),
        lax.psum_scatter(
            spread_gain(all_shards[7]).astype(jnp.bfloat16),
            "replica",
            scatter_dimension=1,
            tiled=True,
        ).astype(jnp.float32),
        lax.psum_scatter(
            spread_gain(all_shards[11]).astype(jnp.bfloat16),
            "replica",
            scatter_dimension=1,
            tiled=True,
        ).astype(jnp.float32),
        lax.psum_scatter(
            spread_gain(all_shards[12]).astype(jnp.bfloat16),
            "replica",
            scatter_dimension=1,
            tiled=True,
        ).astype(jnp.float32),
    )
    all_mats = (
        lax.all_gather(all_cols[0].astype(jnp.bfloat16), "replica", axis=1, tiled=True).astype(
            jnp.float32
        ),
        lax.all_gather(all_cols[1].astype(jnp.bfloat16), "replica", axis=1, tiled=True).astype(
            jnp.float32
        ),
        lax.all_gather(all_cols[2].astype(jnp.bfloat16), "replica", axis=1, tiled=True).astype(
            jnp.float32
        ),
        lax.all_gather(all_cols[3].astype(jnp.bfloat16), "replica", axis=1, tiled=True).astype(
            jnp.float32
        ),
        lax.all_gather(all_cols[4].astype(jnp.bfloat16), "replica", axis=1, tiled=True).astype(
            jnp.float32
        ),
        lax.all_gather(all_cols[5].astype(jnp.bfloat16), "replica", axis=1, tiled=True).astype(
            jnp.float32
        ),
        lax.all_gather(all_cols[6].astype(jnp.bfloat16), "replica", axis=1, tiled=True).astype(
            jnp.float32
        ),
    )
    attn_sums = (
        all_mats[0],
        all_mats[1],
        all_mats[2],
        all_mats[3],
        all_cols[7][:, 0],
        all_cols[8][:, 0],
        all_cols[9][:, 0],
        all_cols[10][:, 0],
    )
    mlp_sums = (all_mats[4], all_mats[5], all_mats[6], all_cols[11][:, 0], all_cols[12][:, 0])
    return (
        layer_out,
        grad_x,
        attn_sums[0],
        attn_sums[1],
        attn_sums[2],
        attn_sums[3],
        attn_sums[4],
        attn_sums[5],
        attn_sums[6],
        attn_sums[7],
        mlp_sums[0],
        mlp_sums[1],
        mlp_sums[2],
        mlp_sums[3],
        mlp_sums[4],
    )


MESH = pl.DeviceIdType.MESH
VMEM_BYTES = 63 * 2**20
F32 = jnp.float32
BF16 = jnp.bfloat16


def fits_cubes(mesh):
    return dict(mesh.shape) == {"replica": 2, "fsdp": 16}


class Place:
    def __init__(self):
        shard = lax.axis_index("fsdp")
        self.x = lax.axis_index("replica")
        self.shard = shard
        self.c = lax.rem(shard, 2)
        self.y = lax.rem(lax.div(shard, 2), 2)
        self.z = lax.div(shard, 4)
        self.zl = lax.rem(self.z, 2)
        self.zh = lax.div(self.z, 2)

    def at(self, x=None, y=None, z=None, c=None):
        x = self.x if x is None else x
        y = self.y if y is None else y
        z = self.z if z is None else z
        c = self.c if c is None else c
        return (x, (z * 2 + y) * 2 + c)

    def z_xor(self, k):
        low = self.zl if k % 2 == 0 else 1 - self.zl
        high = self.zh if k // 2 == 0 else 1 - self.zh
        return 2 * high + low

    def slice_z(self, z=None):
        z = self.z if z is None else z
        inner = lax.rem(lax.rem(z, 2) + lax.div(z, 2), 2)
        return jnp.where(self.x == 0, 2 * inner, 3 - 2 * inner)

    def cube(self, bits):
        return self.at(
            x=1 - self.x if bits & 4 else self.x,
            y=1 - self.y if bits & 2 else self.y,
            z=self.z_xor(1) if bits & 1 else self.z,
        )


class Wires:
    def __init__(self, send, recv):
        self.send, self.recv, self.used = send, recv, 0

    def remote(self, src, dst, device):
        i = self.used
        self.used += 1
        return pltpu.make_async_remote_copy(
            src_ref=src,
            dst_ref=dst,
            send_sem=self.send.at[i],
            recv_sem=self.recv.at[i],
            device_id=device,
            device_id_type=MESH,
        )

    def local(self, src, dst):
        i = self.used
        self.used += 1
        return pltpu.make_async_copy(src, dst, self.send.at[i])


def greet(devices):
    barrier = pltpu.get_barrier_semaphore()
    for device in devices:
        pl.semaphore_signal(barrier, inc=1, device_id=device, device_id_type=MESH)
    pl.semaphore_wait(barrier, len(devices))


def hbm():
    return pl.BlockSpec(memory_space=pl.ANY)


def vmem():
    return pl.BlockSpec(memory_space=pltpu.VMEM)


def sems(count):
    return [pltpu.SemaphoreType.DMA((count,)), pltpu.SemaphoreType.DMA((count,))]


def params(collective_id):
    return pltpu.CompilerParams(
        collective_id=collective_id, has_side_effects=True, vmem_limit_bytes=VMEM_BYTES
    )


X, Y, Z = 4, 2, 1


def thirds(rows):
    first = -(-rows // 48) * 16
    return ((0, first), (first, first), (2 * first, rows - 2 * first))


def add(left, right):
    return (left.astype(F32) + right.astype(F32)).astype(BF16)


class CubeSum:
    MIDDLE = ((X, Y, Y | Z), (Y, Z, X | Z), (Z, X, X | Y))
    NEAR = ((Y, Z), (Z, X), (X, Y))

    def __init__(self, p, w, parts, third, second, first):
        self.p, self.w, self.parts = p, w, parts
        self.third, self.second, self.first = third, second, first
        self.half = parts.shape[1] // 2
        self.started = []
        self.far, self.mid, self.end = {}, {}, {}

    def push(self, src, dst, bit):
        copy = self.w.remote(src, dst, self.p.cube(bit))
        copy.start()
        self.started.append(copy)
        return copy

    def send_far(self):
        for h in range(2):
            for (start, size), link in zip(thirds(self.half), (X, Y, Z)):
                at = pl.ds(h * self.half + start, size)
                self.far[link, h] = self.push(self.parts.at[7, at], self.third.at[at], link)

    def send_middle(self):
        for h in range(2):
            for i, (link, onward, place) in enumerate(self.MIDDLE):
                start, size = thirds(self.half)[i]
                at = pl.ds(h * self.half + start, size)
                all_at = pl.ds(h * self.half, self.half)
                self.far[link, h].wait_recv()
                self.parts[place, at] = add(self.parts[place, at], self.third[at, :])
                self.mid[onward, h] = self.push(
                    self.parts.at[place, all_at], self.second.at[i, all_at], onward
                )

    def send_near(self):
        for h in range(2):
            at = pl.ds(h * self.half, self.half)
            for i, (came, place) in enumerate(self.NEAR):
                self.mid[came, h].wait_recv()
                self.parts[place, at] = add(self.parts[place, at], self.second[i, at])
                self.end[place, h] = self.push(
                    self.parts.at[place, at], self.first.at[i, at], place
                )

    def finish(self):
        for h in range(2):
            at = pl.ds(h * self.half, self.half)
            value = self.parts[0, at].astype(F32)
            for i, (_, place) in enumerate(self.NEAR):
                self.end[place, h].wait_recv()
                value = value + self.first[i, at].astype(F32)
            yield at, value

    def wait_sent(self):
        for copy in self.started:
            copy.wait_send()
        self.started = []


class LightSum(CubeSum):
    def send_far(self):
        for h, link in ((0, X), (1, Y)):
            at = pl.ds(h * self.half, self.half)
            self.far[link, h] = self.push(self.parts.at[7, at], self.third.at[at], link)

    def send_middle(self):
        for h, link, place in ((0, X, Y | Z), (1, Y, X | Z)):
            at = pl.ds(h * self.half, self.half)
            self.far[link, h].wait_recv()
            self.parts[place, at] = add(self.parts[place, at], self.third[at, :])
        for h in range(2):
            at = pl.ds(h * self.half, self.half)
            for i, (link, place) in enumerate(((X, X | Z), (Y, Y | Z))):
                self.mid[link, h] = self.push(self.parts.at[place, at], self.second.at[i, at], link)
            link = (X, Y)[h]
            self.mid[X | Y, h] = self.push(self.parts.at[X | Y, at], self.second.at[2, at], link)

    def send_near(self):
        for h in range(2):
            at = pl.ds(h * self.half, self.half)
            self.mid[X, h].wait_recv()
            self.mid[Y, h].wait_recv()
            total = self.second[0, at].astype(F32) + self.second[1, at].astype(F32)
            self.parts[Z, at] = add(self.parts[Z, at], total)
            self.end[Z, h] = self.push(self.parts.at[Z, at], self.first.at[0, at], Z)
            self.mid[X | Y, h].wait_recv()
            place = (Y, X)[h]
            self.parts[place, at] = add(self.parts[place, at], self.second[2, at])
            for i, bit in ((1, X), (2, Y)):
                self.end[bit, h] = self.push(self.parts.at[bit, at], self.first.at[i, at], bit)


class CubeGather:
    def __init__(self, p, w, block, every):
        self.p, self.w, self.block, self.every = p, w, block, every
        self.half = block.shape[0] // 2
        self.started = []
        self.near, self.middle, self.far = {}, {}, {}

    def push(self, src, dst, bit):
        copy = self.w.remote(src, dst, self.p.cube(bit))
        copy.start()
        self.started.append(copy)
        return copy

    def send_near(self, h):
        at = pl.ds(h * self.half, self.half)
        for bit in (X, Y, Z):
            self.near[bit, h] = self.push(self.block.at[at], self.every.at[bit, at], bit)

    def send_middle(self, h):
        at = pl.ds(h * self.half, self.half)
        for link, relay in ((X, Y), (Y, Z), (Z, X)):
            self.near[relay, h].wait_recv()
            self.middle[link | relay, h] = self.push(
                self.every.at[relay, at], self.every.at[link | relay, at], link
            )

    def send_far(self, h):
        for (start, size), link, relay in zip(thirds(self.half), (X, Y, Z), (Y | Z, X | Z, X | Y)):
            at = pl.ds(h * self.half + start, size)
            self.middle[relay, h].wait_recv()
            self.far[link, h] = self.push(self.every.at[relay, at], self.every.at[7, at], link)

    def wait_far(self):
        for copy in self.far.values():
            copy.wait_recv()

    def wait_sent(self):
        for copy in self.started:
            copy.wait_send()
        self.started = []


def norm_scale(values):
    return lax.rsqrt(jnp.mean(values * values, axis=-1, keepdims=True) + EPS)


def norm_pull(values, scale, gain, cotangent):
    weighted = gain * cotangent
    lean = jnp.mean(values * weighted, axis=-1, keepdims=True)
    d_values = scale * weighted - values * (scale * scale * scale * lean)
    return d_values, jnp.sum(values * scale * cotangent, axis=0, keepdims=True)


def spread_matrix(width, per):
    column = lax.broadcasted_iota(jnp.int32, (128, width), 1)
    row = lax.broadcasted_iota(jnp.int32, (128, width), 0)
    place = (lax.rem(column, per) == row).astype(F32)
    column = lax.broadcasted_iota(jnp.int32, (16, width), 1)
    row = lax.broadcasted_iota(jnp.int32, (16, width), 0)
    owner = (lax.div(column, per) == row).astype(F32)
    return place, owner


def join_gains(packed, which, width, per):
    place, owner = spread_matrix(width, per)
    shards = packed[:, which, :].astype(BF16)
    wide = jnp.dot(shards, place.astype(BF16), preferred_element_type=F32)
    return jnp.sum(wide * owner, axis=0, keepdims=True)


def turn(values, cosine, sine):
    half = values.shape[-1] // 2
    u, w = values[:, :half], values[:, half:]
    return jnp.concatenate([u * cosine - w * sine, w * cosine + u * sine], axis=1)


def turn_back(values, cosine, sine):
    half = values.shape[-1] // 2
    u, w = values[:, :half], values[:, half:]
    return jnp.concatenate([u * cosine + w * sine, w * cosine - u * sine], axis=1)


def front_kernel(
    tok, seg_row, w_q, w_k, w_v, w_o, g_apre, g_apost, g_mpre, g_mpost, g_q, g_k, w_gate, w_up, w_down,
    qkv_w, out_w, gu_w, dn_w, every, gains_full, a_low, qk_proj, q_low, k_low, v_low,
    probs, o_low, attn_proj, h_mid, tables,
    qkv_s, qkv_own, qkv_send, qkv_got, out_own, gains_own, gains_s, wide_in, wide_send, wide_got,
    wide_out, down_in, down_out, m_low, out_s, send, recv, local,
):
    p = Place()
    w = Wires(send, recv)
    x, y, z, c, zl, zh = p.x, p.y, p.z, p.c, p.zl, p.zh
    sibling = p.at(c=1 - c)
    plane = [p.at(x=1 - x), p.at(y=1 - y)]
    lines = [p.at(y=yy, z=p.z_xor(k)) for yy in (y, 1 - y) for k in range(1, 4)]
    started = []

    def push(src, dst, device):
        copy = w.remote(src, dst, device)
        copy.start()
        started.append(copy)
        return copy

    loads = [
        pltpu.make_async_copy(w_gate, wide_in.at[0], local.at[0]),
        pltpu.make_async_copy(w_up, wide_in.at[1], local.at[1]),
        pltpu.make_async_copy(w_down, down_in, local.at[2]),
    ]
    for copy in loads:
        copy.start()

    rows = w_q.shape[0]
    columns = qkv_s.shape[1] // 4
    out_rows = w_o.shape[0] // 2
    mine = 2 * x + c
    theirs = 2 * x + 1 - c

    all_own = jnp.concatenate([w_q[...], w_k[...], w_v[...]], axis=1)
    for quarter in range(4):
        qkv_own[quarter] = all_own[:, quarter * columns : (quarter + 1) * columns]
    qkv_send[...] = qkv_own[theirs].astype(BF16)
    out_own[...] = w_o[...].astype(BF16)
    gains_own[...] = jnp.zeros_like(gains_own)
    for i, gain in enumerate((g_apre, g_apost, g_mpre, g_mpost, g_q, g_k)):
        gains_own[i, : gain.shape[0]] = gain[...].astype(BF16).astype(F32)
    across = p.at(x=1 - x, z=p.z_xor(3))
    greet([sibling, across] + plane + lines)

    def qkv_at(zz, yy, quarter):
        return qkv_s.at[
            pl.ds(pl.multiple_of((2 * zz + yy) * 2 * rows, 16), 2 * rows),
            pl.ds(pl.multiple_of(quarter * columns, 128), columns),
        ]

    def out_at(zz, yy, quarter):
        return out_s.at[
            pl.ds(pl.multiple_of((2 * zz + yy) * 4 * out_rows + quarter * out_rows, 16), out_rows)
        ]

    swap = push(qkv_send, qkv_got, sibling)

    def gains_at(zz, yy, cc):
        return gains_s.at[(2 * zz + yy) * 2 + cc]

    gains_s[(2 * z + y) * 2 + c] = gains_own[...]
    gain_line = [push(gains_own, gains_at(z, y, c), p.at(z=p.z_xor(k))) for k in range(1, 4)]
    gain_side = [push(gains_own, gains_at(z, y, c), plane[1])]
    holds = x == c
    out_theirs = out_own.at[pl.ds(pl.multiple_of((1 - c) * out_rows, 16), out_rows)]
    out_swap = w.remote(out_theirs, out_at(z, y, theirs), sibling)
    pl.when(holds)(out_swap.start)

    @pl.when(holds)
    def _():
        out_s[pl.ds(pl.multiple_of((2 * z + y) * 4 * out_rows + mine * out_rows, 16), out_rows)] = (
            out_own[pl.ds(pl.multiple_of(c * out_rows, 16), out_rows)]
        )

    swap.wait_recv()
    top, low = qkv_own[mine], qkv_got[...].astype(F32)
    first = jnp.where(c == 0, top, low)
    second = jnp.where(c == 0, low, top)
    base = pl.multiple_of((2 * z + y) * 2 * rows, 16)
    joined = jnp.concatenate([first, second], axis=0).astype(BF16)
    qkv_s[pl.ds(base, 2 * rows), pl.ds(pl.multiple_of(mine * columns, 128), columns)] = joined

    pl.when(jnp.logical_not(holds))(out_swap.wait_recv)
    pl.when(holds)(out_swap.wait_send)

    line = [None]
    for k in range(1, 4):
        to = p.at(z=p.z_xor(k))
        line.append(
            (
                push(qkv_at(z, y, mine), qkv_at(z, y, mine), to),
                push(out_at(z, y, mine), out_at(z, y, mine), to),
            )
        )
    side_x, side_y, corner = {}, {}, {}

    def spread(k):
        zz = p.z_xor(k)
        if k:
            for copy in line[k]:
                copy.wait_recv()
        qkv, out = qkv_at(zz, y, mine), out_at(zz, y, mine)
        side_x[k] = (push(qkv, qkv, plane[0]), push(out, out, plane[0]))
        side_y[k] = (push(qkv, qkv, plane[1]), push(out, out, plane[1]))

    def relay(k):
        zz = p.z_xor(k)
        if k % 2:
            for copy in side_y[k]:
                copy.wait_recv()
            qkv, out, to = qkv_at(zz, 1 - y, mine), out_at(zz, 1 - y, mine), plane[0]
        else:
            for copy in side_x[k]:
                copy.wait_recv()
            other = 2 * (1 - x) + c
            qkv, out, to = qkv_at(zz, y, other), out_at(zz, y, other), plane[1]
        corner[k] = (push(qkv, qkv, to), push(out, out, to))

    pairs = []

    def share(k):
        zz = p.z_xor(k)
        for copy in (side_x[k] if k % 2 else side_y[k]) + corner[k]:
            copy.wait_recv()
        for xx in range(2):
            at = qkv_s.at[
                pl.ds(pl.multiple_of(2 * zz * 2 * rows, 16), 4 * rows),
                pl.ds(pl.multiple_of((2 * xx + c) * columns, 128), columns),
            ]
            pairs.append(push(at, at, sibling))
            for yy in range(2):
                at = out_at(zz, yy, 2 * xx + c)
                pairs.append(push(at, at, sibling))

    spread(0)
    loads[0].wait()
    loads[1].wait()
    part_columns = wide_out.shape[-1]
    for xx in range(2):

        @pl.when(x == xx)
        def _():
            for zz in range(2):
                for yy in range(2):
                    part = (3 - 2 * zz if xx else 2 * zz) * 2 + yy
                    at = slice(part * part_columns, (part + 1) * part_columns)
                    for matrix in range(2):

                        @pl.when(c == 1 - matrix)
                        def _():
                            wide_send[2 * zz + yy] = wide_in[matrix, :, at].astype(BF16)

    wide_swap = push(wide_send, wide_got, sibling)
    loads[2].wait()
    down_out[...] = down_in[...].astype(BF16)
    relay(0)
    spread(1)
    wide_swap.wait_recv()
    for xx in range(2):

        @pl.when(x == xx)
        def _():
            for zz in range(2):
                for yy in range(2):
                    part = (3 - 2 * zz if xx else 2 * zz) * 2 + yy
                    at = slice(part * part_columns, (part + 1) * part_columns)
                    got = wide_got[2 * zz + yy].astype(F32)
                    for matrix in range(2):

                        @pl.when(c == matrix)
                        def _():
                            own = wide_in[matrix, :, at]
                            both = [own, got] if matrix == 0 else [got, own]
                            wide_out[2 * zz + yy] = jnp.concatenate(both, axis=0).astype(BF16)

    def gu_at(zz, yy):
        return gu_w.at[c, pl.ds(pl.multiple_of((2 * zz + yy) * 2 * rows, 16), 2 * rows)]

    wide = []
    for k in range(4):
        for other in range(2):
            yy = 1 - y if other else y
            zz = p.z_xor(k)
            inner = lax.rem(lax.rem(zz, 2) + lax.div(zz, 2), 2)
            src = wide_out.at[2 * inner + yy]
            if k == 0 and other == 0:
                own_wide = pltpu.make_async_copy(src, gu_at(z, y), local.at[0])
                own_wide.start()
            else:
                wide.append((zz, yy, push(src, gu_at(z, y), p.at(y=yy, z=zz))))
    down_rows = down_out.shape[0]
    down_at = dn_w.at[pl.ds(pl.multiple_of(c * down_rows, 16), down_rows)]
    down_local = p.slice_z() == z
    down_sends = lax.rem(zl + c, 2) == x
    down_copy = w.remote(down_out, down_at, p.at(x=zl, z=p.z_xor(3)))
    pl.when(down_sends)(down_copy.start)
    own_down = pltpu.make_async_copy(down_out, down_at, local.at[1])
    pl.when(down_local)(own_down.start)

    tok_f = tok[...].astype(F32)
    length, width = tok_f.shape
    head = k_low.shape[1]
    spread(2)
    relay(1)
    for copy in gain_line:
        copy.wait_recv()
    for k in range(1, 4):
        zz = p.z_xor(k)
        gain_side.append(push(gains_at(zz, y, c), gains_at(zz, y, c), plane[1]))
    row_seg = seg_row[...].astype(F32)
    i_at = lax.broadcasted_iota(jnp.int32, (length, length), 0)
    j_at = lax.broadcasted_iota(jnp.int32, (length, length), 1)
    col_seg = jnp.sum(jnp.where(i_at == j_at, row_seg, 0.0), axis=1, keepdims=True)
    earlier = jnp.sum((row_seg < col_seg).astype(F32), axis=1, keepdims=True)
    index = lax.broadcasted_iota(jnp.int32, (length, 1), 0).astype(F32)
    rate_at = lax.broadcasted_iota(jnp.int32, (1, head // 2), 1).astype(F32)
    rates = jnp.exp(rate_at * (-2.0 * math.log(THETA) / head))
    angles = (index - earlier) * rates
    tables[0] = jnp.cos(angles)
    tables[1] = jnp.sin(angles)
    spread(3)
    relay(2)
    share(0)
    relay(3)
    for copy in gain_side:
        copy.wait_recv()
    gain_pair = []
    for zz in range(4):
        for yy in range(2):
            gain_pair.append(push(gains_at(zz, yy, c), gains_at(zz, yy, c), sibling))
    share(1)
    for copy in gain_pair:
        copy.wait_recv()
    packed = gains_s[...]
    for i, (size, per) in enumerate(
        ((width, rows),) * 4 + ((head, head // 16),) * 2
    ):
        gains_full[i, :, :size] = join_gains(packed, i, size, per)
    a_low[...] = (tok_f * norm_scale(tok_f) * gains_full[0]).astype(BF16)
    share(2)
    share(3)
    for copy in pairs:
        copy.wait_recv()
    saves = [
        pltpu.make_async_copy(qkv_s, qkv_w, local.at[2]),
        pltpu.make_async_copy(out_s, out_w, local.at[3]),
    ]
    for copy in saves:
        copy.start()

    cosine, sine = tables[0], tables[1]
    heads = q_low.shape[1] // head
    for i in range(heads + 2):
        at = slice(i * head, (i + 1) * head)
        value = jnp.dot(a_low[...], qkv_s[:, at], preferred_element_type=F32)
        if i < heads:
            qk_proj[:, at] = value
            q_low[:, at] = turn(
                value * norm_scale(value) * gains_full[4, :, :head], cosine, sine
            ).astype(BF16)
        elif i == heads:
            qk_proj[:, at] = value
            k_low[...] = turn(
                value * norm_scale(value) * gains_full[5, :, :head], cosine, sine
            ).astype(BF16)
        else:
            v_low[...] = value.astype(BF16)
    allowed = (row_seg == col_seg) & (j_at <= i_at)
    for i in range(heads):
        at = slice(i * head, (i + 1) * head)
        scores = SCALE * lax.dot_general(
            q_low[:, at], k_low[...], (((1,), (1,)), ((), ())), preferred_element_type=F32
        )
        scores = jnp.where(allowed, scores, MASKED)
        expo = jnp.exp(scores - jnp.max(scores, axis=1, keepdims=True))
        prob = expo / jnp.sum(expo, axis=1, keepdims=True)
        probs[i] = prob
        o_low[:, at] = jnp.dot(
            prob.astype(BF16), v_low[...], preferred_element_type=F32
        ).astype(BF16)
    third = width // 3
    for i in range(3):
        at = slice(i * third, (i + 1) * third)
        attn_proj[:, at] = jnp.dot(o_low[...], out_s[:, at], preferred_element_type=F32)
    proj = attn_proj[...]
    mid = tok_f + proj * norm_scale(proj) * gains_full[1]
    h_mid[...] = mid
    m_low[...] = (mid * norm_scale(mid) * gains_full[2]).astype(BF16)

    gather = CubeGather(p, w, m_low, every)
    own = pltpu.make_async_copy(m_low, every.at[0], local.at[4])
    own.start()
    gather.send_near(0)
    gather.send_near(1)
    own_wide.wait()
    shared = [push(gu_at(z, y), gu_at(z, y), sibling)]
    gather.send_middle(0)
    gather.send_middle(1)
    gather.send_far(0)
    gather.send_far(1)
    for zz, yy, copy in reversed(wide):
        copy.wait_recv()
        shared.append(push(gu_at(zz, yy), gu_at(zz, yy), sibling))
    pl.when(down_local)(own_down.wait)
    pl.when(jnp.logical_not(down_local))(down_copy.wait_recv)
    shared.append(push(down_at, down_at, sibling))
    gather.wait_far()
    own.wait()
    gather.wait_sent()
    for copy in shared:
        copy.wait_recv()
    for copy in saves:
        copy.wait()
    pl.when(down_sends)(down_copy.wait_send)
    for copy in started:
        copy.wait_send()


def front(tok, segments, w_q, w_k, w_v, w_o, gains, w_gate, w_up, w_down, head):
    length, width = tok.shape
    rows, mix = w_q.shape
    hidden = w_gate.shape[1]
    part = hidden // 8
    down_rows = w_down.shape[0]
    total = mix + 2 * head
    heads = mix // head
    columns = total // 4
    struct = jax.ShapeDtypeStruct
    shapes = (
        struct((16 * rows, total), BF16),
        struct((16 * w_o.shape[0], width), BF16),
        struct((2, 16 * rows, part), BF16),
        struct((2 * down_rows, width), BF16),
        struct((8, length, width), BF16),
        struct((8, 1, width), F32),
        struct((length, width), BF16),
        struct((length, mix + head), F32),
        struct((length, mix), BF16),
        struct((length, head), BF16),
        struct((length, head), BF16),
        struct((heads, length, length), F32),
        struct((length, mix), BF16),
        struct((length, width), F32),
        struct((length, width), F32),
        struct((2, length, head // 2), F32),
    )
    scratch = [
        pltpu.VMEM((16 * rows, total), BF16),
        pltpu.VMEM((4, rows, columns), F32),
        pltpu.VMEM((rows, columns), BF16),
        pltpu.VMEM((rows, columns), BF16),
        pltpu.VMEM(w_o.shape, BF16),
        pltpu.VMEM((8, 128), F32),
        pltpu.VMEM((16, 8, 128), F32),
        pltpu.VMEM((2, rows, hidden), F32),
        pltpu.VMEM((4, rows, part), BF16),
        pltpu.VMEM((4, rows, part), BF16),
        pltpu.VMEM((4, 2 * rows, part), BF16),
        pltpu.VMEM((down_rows, width), F32),
        pltpu.VMEM((down_rows, width), BF16),
        pltpu.VMEM((length, width), BF16),
        pltpu.VMEM((16 * w_o.shape[0], width), BF16),
    ]
    return pl.pallas_call(
        front_kernel,
        out_shape=shapes,
        in_specs=[vmem()] * 12 + [hbm()] * 3,
        out_specs=(hbm(),) * 5 + (vmem(),) * 11,
        scratch_shapes=scratch + sems(128) + [pltpu.SemaphoreType.DMA((5,))],
        compiler_params=params(0),
        name="front",
    )(
        tok, segments, w_q, w_k, w_v, w_o, *gains, w_gate, w_up, w_down
    )


def dot_rows(left, right):
    return lax.dot_general(left, right, (((0,), (0,)), ((), ())), preferred_element_type=F32)


def dot_columns(left, right):
    return lax.dot_general(left, right, (((1,), (1,)), ((), ())), preferred_element_type=F32)


GELU_ROOT = math.sqrt(2.0 / math.pi)


def gelu_parts(gate):
    square = gate * gate
    bend = jnp.tanh(GELU_ROOT * gate * (1.0 + 0.044715 * square))
    half = 0.5 * (1.0 + bend)
    slope = half + 0.5 * gate * (1.0 - bend * bend) * GELU_ROOT * (1.0 + 3 * 0.044715 * square)
    return half * gate, slope


def tiles(size, step):
    return [slice(at, min(at + step, size)) for at in range(0, size, step)]


def tail_kernel(
    tok, d_out, h_mid, gains_full, every, gu, dn, proj_h, o_h, out_h, v_h, probs_h, k_h, q_h, qk_h,
    tables_h, a_h, qkv_h,
    layer_out, grad_x, qe, oe, gains_sum, wide_end, wide_back, down_end,
    dd_own, dd_all, third, second, first, wide_got, wide_sum, wide_far, down_got, down_sum, down_far,
    d_mid, q1, o1, qa, oa, qb, ob, qc, oc, gain_acc, gain_got, send, recv, local,
):
    p = Place()
    w = Wires(send, recv)
    x, y, z, c, zl, zh = p.x, p.y, p.z, p.c, p.zl, p.zh
    sibling = p.at(c=1 - c)
    plane = [p.at(x=1 - x), p.at(y=1 - y)]
    line = [p.at(z=p.z_xor(k)) for k in range(1, 4)]
    started = []

    def push(src, dst, device):
        copy = w.remote(src, dst, device)
        copy.start()
        started.append(copy)
        return copy

    def rows_of(ref, start, size):
        return ref.at[pl.ds(pl.multiple_of(start, 16), size)]

    chip_rows = wide_sum.shape[0] // 8
    half_rows = 4 * chip_rows
    far_half = half_rows * (1 - zh)
    near_half = half_rows * zh

    pieces = (0, 1, 2, 3)
    order = (3, 1, 2, 0)

    def piece(i, zl):
        to_z = 1 - zl if i // 2 else zl
        to_y = 1 - y if i % 2 else y
        return (2 * to_z + to_y) * chip_rows

    crossing = w.used
    w.used += 5

    def cross(i, src, dst):
        return pltpu.make_async_remote_copy(
            src_ref=src,
            dst_ref=dst,
            send_sem=send.at[crossing + i],
            recv_sem=recv.at[crossing + i],
            device_id=line[2],
            device_id_type=MESH,
        )

    def wide_two(i):
        return cross(
            i,
            rows_of(wide_sum, far_half + piece(i, 1 - zl), chip_rows),
            wide_far.at[pl.ds(i * chip_rows, chip_rows)],
        )

    def down_over():
        return cross(4, down_sum, down_far)

    mine = p.slice_z() == z

    def feed_forward(m_all, wide_w, down_w, wide, hidden, parts):
        blocks = (7, 3, 5, 6, 4, 2, 1, 0)
        loads = {r: pltpu.make_async_copy(every.at[r], m_all.at[r], local.at[r]) for r in blocks}
        wide_load = pltpu.make_async_copy(gu, wide_w, local.at[8])
        down_load = pltpu.make_async_copy(dn, down_w, local.at[9])
        wide_load.start()
        loads[7].start()
        down_load.start()
        for r in blocks[1:]:
            loads[r].start()
        greet([sibling] + plane + line + [p.cube(3)])
        length, width = m_all.shape[1:]
        part = wide.shape[-1]
        wide_tiles = tiles(part, 256)
        down_tiles = tiles(width, 384)

        def forward(r):
            for at in wide_tiles:
                g = jnp.dot(m_all[r], wide_w[0, :, at], preferred_element_type=F32)
                u = jnp.dot(m_all[r], wide_w[1, :, at], preferred_element_type=F32)
                wide[0, r, :, at] = g.astype(BF16)
                wide[1, r, :, at] = u.astype(BF16)
                value, _ = gelu_parts(g)
                hidden[r, :, at] = (value * u).astype(BF16)
            for at in down_tiles:
                parts[r, :, at] = jnp.dot(
                    hidden[r], down_w[:, at], preferred_element_type=F32
                ).astype(BF16)

        def backward(r):
            for at in wide_tiles:
                d_hidden = dot_columns(dd_all[r], down_w[at, :])
                value, slope = gelu_parts(wide[0, r, :, at].astype(F32))
                up = wide[1, r, :, at].astype(F32)
                wide[0, r, :, at] = (d_hidden * up * slope).astype(BF16)
                wide[1, r, :, at] = (d_hidden * value).astype(BF16)
            d_gate = wide[0, r]
            d_up = wide[1, r]
            for at in down_tiles:
                parts[r, :, at] = (
                    dot_columns(d_gate, wide_w[0, at, :]) + dot_columns(d_up, wide_w[1, at, :])
                ).astype(BF16)

        def several(step, places):
            lax.fori_loop(0, 3, lambda i, _: (step(places(i)), 0)[1], 0)

        def middles(i):
            return 7 - lax.shift_right_logical(jnp.int32(4), i)

        def nears(i):
            return lax.shift_right_logical(jnp.int32(4), i)

        total = CubeSum(p, w, parts, third, second, first)
        wide_load.wait()
        loads[7].wait()
        down_load.wait()
        forward(7)
        total.send_far()
        for r in blocks[1:]:
            loads[r].wait()
        several(forward, middles)
        total.send_middle()
        several(forward, nears)
        total.send_near()
        forward(0)

        gather = CubeGather(p, w, dd_own, dd_all)
        gain = gains_full[3]
        g_rows = 0.0
        for h, (at, value) in enumerate(total.finish()):
            scale = norm_scale(value)
            layer_out[at, :] = (h_mid[at, :] + value * scale * gain).astype(BF16)
            d_value, g_part = norm_pull(value, scale, gain, d_out[at, :].astype(F32))
            dd_own[at, :] = d_value.astype(BF16)
            g_rows = g_rows + g_part
            gather.send_near(h)
        gain_acc[0, 3:4, :] = g_rows
        dd_all[0] = dd_own[...]
        total.wait_sent()
        backward(0)
        gather.send_middle(0)
        gather.send_middle(1)
        several(backward, nears)
        gather.send_far(0)
        gather.send_far(1)
        several(backward, middles)
        gather.wait_far()
        backward(7)

        total = LightSum(p, w, parts, third, second, first)
        total.send_far()
        grad_rows = 384
        all_rows = 8 * length
        for at in down_tiles:
            down_w[:, at] = dot_rows(
                hidden[...].reshape(all_rows, part), dd_all[:, :, at].reshape(all_rows, -1)
            ).astype(BF16)
        down_rows = down_sum.shape[0]
        down_one = w.remote(rows_of(down_w, (1 - c) * down_rows, down_rows), down_got, sibling)
        down_one.start()
        total.send_middle()
        down_one.wait_recv()
        down_sum[...] = add(down_w[pl.ds(pl.multiple_of(c * down_rows, 16), down_rows), :], down_got[...])
        pl.when(jnp.logical_not(mine))(down_over().start)

        def grad_wide(matrix, out):
            def step(i, _):
                at = pl.ds(pl.multiple_of(i * grad_rows, 128), grad_rows)
                left = m_all[:, :, at].reshape(all_rows, grad_rows)
                out[at, :] = dot_rows(left, wide[matrix].reshape(all_rows, part)).astype(BF16)
                return 0

            lax.fori_loop(0, width // grad_rows, step, 0)

        other = wide_w.at[1 - c]
        grad_wide(1 - c, other)
        wide_one = w.remote(other, wide_got, sibling)
        wide_one.start()
        grad_wide(c, wide_sum)
        wide_one.wait_recv()
        wide_sum[...] = add(wide_sum[...], wide_got[...])
        total.send_near()
        for i in pieces:
            wide_two(i).start()
        g_rows = 0.0
        for at, value in total.finish():
            mid = h_mid[at, :]
            d_value, g_part = norm_pull(mid, norm_scale(mid), gains_full[2], value)
            d_mid[at, :] = d_out[at, :].astype(F32) + d_value
            g_rows = g_rows + g_part
        gain_acc[0, 2:3, :] = g_rows
        down_one.wait_send()
        wide_one.wait_send()
        total.wait_sent()
        gather.wait_sent()

    def attention(
        proj, o_low, out_w, v_low, probs, k_low, q_low, qk_proj, tables, a_low, qkv_w,
        d_input, wide_swap, d_attn, d_mix, d_qkv, dqkv, dout, qa_s, oa_s, qb_s, ob_s, qc_s, oc_s,
    ):
        loads = [
            pltpu.make_async_copy(src, dst, local.at[i])
            for i, (src, dst) in enumerate(
                zip(
                    (proj_h, o_h, out_h, v_h, probs_h, k_h, q_h, qk_h, tables_h, a_h, qkv_h),
                    (proj, o_low, out_w, v_low, probs, k_low, q_low, qk_proj, tables, a_low, qkv_w),
                )
            )
        ]
        for copy in loads:
            copy.start()
        loads[0].wait()
        value = proj[...]
        d_value, g_apost = norm_pull(value, norm_scale(value), gains_full[1], d_mid[...])
        d_attn[...] = d_value.astype(BF16)
        gain_acc[0, 1:2, :] = g_apost
        loads[1].wait()

        width = tok.shape[1]
        step = width // 3
        for i in range(3):
            at = slice(i * step, (i + 1) * step)
            dout[:, at] = dot_rows(o_low[...], d_attn[:, at]).astype(BF16)
        out_rows = dout.shape[0] // 32
        columns = dqkv.shape[1] // 4

        def out_at(ref, zz, yy, quarter):
            return rows_of(ref, (2 * zz + yy) * 4 * out_rows + quarter * out_rows, out_rows)

        out_one = {
            k: [
                push(
                    out_at(dout, p.z_xor(k), yy, 2 * xx + 1 - c),
                    o1.at[k, xx, yy],
                    sibling,
                )
                for yy in range(2)
                for xx in range(2)
            ]
            for k in order
        }
        loads[2].wait()
        d_mix[...] = dot_columns(d_attn[...], out_w[...]).astype(BF16)

        for copy in loads[3:9]:
            copy.wait()
        cosine, sine = tables[0], tables[1]
        head = k_low.shape[1]
        heads = q_low.shape[1] // head
        d_k, d_v, g_q = 0.0, 0.0, 0.0
        for i in range(heads):
            at = slice(i * head, (i + 1) * head)
            prob = probs[i]
            d_probs = dot_columns(d_mix[:, at], v_low[...])
            row_dot = jnp.sum(prob * d_probs, axis=1, keepdims=True)
            d_scores = (prob * (d_probs - row_dot)).astype(BF16)
            d_q = SCALE * jnp.dot(d_scores, k_low[...], preferred_element_type=F32)
            d_k = d_k + dot_rows(d_scores, q_low[:, at])
            d_v = d_v + dot_rows(prob.astype(BF16), d_mix[:, at])
            value = qk_proj[:, at]
            d_value, gain = norm_pull(
                value, norm_scale(value), gains_full[4, :, :head], turn_back(d_q, cosine, sine)
            )
            g_q = g_q + gain
            d_qkv[:, at] = d_value.astype(BF16)
        at = slice(heads * head, (heads + 1) * head)
        value = qk_proj[:, at]
        d_value, g_k = norm_pull(
            value, norm_scale(value), gains_full[5, :, :head], turn_back(SCALE * d_k, cosine, sine)
        )
        d_qkv[:, at] = d_value.astype(BF16)
        d_qkv[:, (heads + 1) * head :] = d_v.astype(BF16)
        gain_acc[0, 4:5, :] = jnp.zeros((1, width), F32)
        gain_acc[0, 5:8, :] = jnp.zeros((3, width), F32)
        gain_acc[0, 4:5, :head] = g_q
        gain_acc[0, 5:6, :head] = g_k
        loads[9].wait()
        for i in range(heads + 2):
            at = slice(i * head, (i + 1) * head)
            dqkv[:, at] = dot_rows(a_low[...], d_qkv[:, at]).astype(BF16)

        qkv_one = {}
        for k in order:
            rows = pl.ds(pl.multiple_of(2 * p.z_xor(k) * chip_rows, 16), 2 * chip_rows)
            qkv_one[k] = [
                push(
                    dqkv.at[
                        rows, pl.ds(pl.multiple_of((2 * xx + 1 - c) * columns, 128), columns)
                    ],
                    q1.at[k, xx],
                    sibling,
                )
                for xx in range(2)
            ]

        def own_part(k, xx, yy):
            zz = p.z_xor(k)
            rows = pl.ds(pl.multiple_of((2 * zz + yy) * chip_rows, 16), chip_rows)
            at = pl.ds(pl.multiple_of((2 * xx + c) * columns, 128), columns)
            got = pl.ds(pl.multiple_of(yy * chip_rows, 16), chip_rows)
            start = pl.multiple_of(((2 * zz + yy) * 4 + 2 * xx + c) * out_rows, 16)
            return (
                dqkv[rows, at].astype(F32) + q1[k, xx, got, :].astype(F32),
                dout[pl.ds(start, out_rows), :].astype(F32) + o1[k, xx, yy].astype(F32),
            )

        first, then, last_step = {}, {}, {}

        def plane_first(k):
            for copy in out_one[k] + qkv_one[k]:
                copy.wait_recv()
            first[k] = []
            for j in range(2):
                q, o = own_part(k, x if j == 0 else 1 - x, 1 - y)
                qa_s[k, j] = q.astype(BF16)
                oa_s[k, j] = o.astype(BF16)
                first[k] += [
                    push(qa_s.at[k, j], qa.at[k, j], plane[1]),
                    push(oa_s.at[k, j], oa.at[k, j], plane[1]),
                ]

        def plane_then(k):
            for copy in first[k]:
                copy.wait_recv()
            q, o = own_part(k, 1 - x, y)
            qb_s[k] = (q + qa[k, 1].astype(F32)).astype(BF16)
            ob_s[k] = (o + oa[k, 1].astype(F32)).astype(BF16)
            then[k] = [
                push(qb_s.at[k], qb.at[k], plane[0]),
                push(ob_s.at[k], ob.at[k], plane[0]),
            ]

        def plane_last(k):
            for copy in then[k]:
                copy.wait_recv()
            q, o = own_part(k, x, y)
            q = q + qa[k, 0].astype(F32) + qb[k].astype(F32)
            o = o + oa[k, 0].astype(F32) + ob[k].astype(F32)
            if k == 0:
                return q, o
            qc_s[k] = q.astype(BF16)
            oc_s[k] = o.astype(BF16)
            last_step[k] = [
                push(qc_s.at[k], qc.at[k], line[k - 1]),
                push(oc_s.at[k], oc.at[k], line[k - 1]),
            ]

        for k in order:
            plane_first(k)

        down_copy = w.remote(down_end, down_end, plane[0])

        @pl.when(mine)
        def _():
            down_over().wait_recv()
            down_end[...] = add(down_sum[...], down_far[...])
            down_copy.start()

        wide_three, wide_four, own_wide = {}, [], []

        def part_of(i):
            return 2 * p.slice_z(2 * zh + (1 - zl if i // 2 else zl)) + (1 - y if i % 2 else y)

        def wide_on(i):
            at = pl.ds(i * chip_rows, chip_rows)
            rows = pl.ds(pl.multiple_of(near_half + piece(i, zl), 16), chip_rows)
            wide_two(i).wait_recv()
            wide_far[at, :] = add(wide_sum[rows, :], wide_far[at, :])
            dst = wide_end.at[part_of(0)]
            if i:
                wide_three[i] = push(wide_far.at[at], dst, p.cube(2 * (i % 2) + i // 2))
            else:
                own_wide.append(pltpu.make_async_copy(wide_far.at[at], dst, local.at[11]))
                own_wide[0].start()
                wide_four.append(push(wide_far.at[at], dst, plane[0]))

        def wide_over(i):
            wide_three[i].wait_recv()
            dst = wide_end.at[part_of(i)]
            wide_four.append(push(dst, dst, plane[0]))

        wide_on(0)

        loads[10].wait()
        tok_f = tok[...].astype(F32)
        for i in range(3):
            at = slice(i * step, (i + 1) * step)
            d_input[:, at] = dot_columns(d_qkv[...], qkv_w[at, :])
        d_value, g_apre = norm_pull(tok_f, norm_scale(tok_f), gains_full[0], d_input[...])
        grad_x[...] = (d_mid[...] + d_value).astype(BF16)
        gain_acc[0, 0:1, :] = g_apre
        gain_one = push(gain_acc.at[0], gain_got.at[0], sibling)

        for k in order[:2]:
            plane_then(k)
        gain_one.wait_recv()
        gain_acc[1] = gain_acc[0] + gain_got[0]
        gain_two = push(gain_acc.at[1], gain_got.at[1], plane[0])
        wide_on(1)
        for k in order[2:]:
            plane_then(k)
        for k in order[:3]:
            plane_last(k)
        wide_on(2)
        wide_over(1)
        gain_two.wait_recv()
        gain_acc[2] = gain_acc[1] + gain_got[1]
        gain_three = push(gain_acc.at[2], gain_got.at[2], plane[1])
        q, o = plane_last(0)
        for k in order[:3]:
            for copy in last_step[k]:
                copy.wait_recv()
        qe[0] = (q + qc[1].astype(F32) + qc[2].astype(F32) + qc[3].astype(F32)).astype(BF16)
        oe[0] = (o + oc[1].astype(F32) + oc[2].astype(F32) + oc[3].astype(F32)).astype(BF16)
        last = [
            push(qe.at[0], qe.at[4 + i], device)
            for i, device in enumerate((sibling, plane[0]))
        ] + [
            push(oe.at[0], oe.at[4 + i], device)
            for i, device in enumerate((sibling, plane[0]))
        ]
        wide_on(3)
        wide_over(2)
        gain_three.wait_recv()
        gain_acc[3] = gain_acc[2] + gain_got[2]
        gain_four = [push(gain_acc.at[3], gain_got.at[2 + k], line[k - 1]) for k in range(1, 4)]
        for copy in last:
            copy.wait_recv()
        relay = [push(qe.at[5], qe.at[6], sibling), push(oe.at[5], oe.at[6], sibling)]

        wide_over(3)
        for copy in relay:
            copy.wait_recv()
        rows = chip_rows // 2
        for copy in gain_four:
            copy.wait_recv()
        gains_sum[...] = gain_acc[3] + gain_got[3] + gain_got[4] + gain_got[5]

        own_wide[0].wait()
        for copy in wide_four:
            copy.wait_recv()
        for cc in range(2):

            @pl.when(c == cc)
            def _():
                for s in range(8):
                    extra = (rows + 15) // 16 * 16
                    at = slice(0, extra) if cc == 1 else slice(2 * rows - extra, 2 * rows)
                    wide_swap[s] = wide_end[s, at, :]

        final = push(wide_swap, wide_back, sibling)
        pl.when(jnp.logical_not(mine))(down_copy.wait_recv)
        final.wait_recv()
        pl.when(mine)(down_copy.wait_send)
        pl.when(jnp.logical_not(mine))(down_over().wait_send)
        for i in pieces:
            wide_two(i).wait_send()
        for copy in started:
            copy.wait_send()


    length, width = tok.shape
    blocks = (8, length, width)
    part = wide_sum.shape[1]
    pl.run_scoped(
        feed_forward,
        pltpu.VMEM(blocks, BF16),
        pltpu.VMEM(gu.shape, BF16),
        pltpu.VMEM(dn.shape, BF16),
        pltpu.VMEM((2, 8, length, part), BF16),
        pltpu.VMEM((8, length, part), BF16),
        pltpu.VMEM(blocks, BF16),
    )
    total = qkv_h.shape[1]
    mix = o_h.shape[1]
    q_piece, o_piece = qa.shape[2:], oa.shape[2:]
    saved = (proj_h, o_h, out_h, v_h, probs_h, k_h, q_h, qk_h, tables_h, a_h, qkv_h)
    pl.run_scoped(
        attention,
        *[pltpu.VMEM(ref.shape, ref.dtype) for ref in saved],
        pltpu.VMEM((length, width), F32),
        pltpu.VMEM(wide_back.shape, BF16),
        pltpu.VMEM((length, width), BF16),
        pltpu.VMEM((length, mix), BF16),
        pltpu.VMEM((length, total), BF16),
        pltpu.VMEM((width, total), BF16),
        pltpu.VMEM((mix, width), BF16),
        pltpu.VMEM((4, 2) + q_piece, BF16),
        pltpu.VMEM((4, 2) + o_piece, BF16),
        pltpu.VMEM((4,) + q_piece, BF16),
        pltpu.VMEM((4,) + o_piece, BF16),
        pltpu.VMEM((4,) + q_piece, BF16),
        pltpu.VMEM((4,) + o_piece, BF16),
    )


def tail(tok, d_out, h_mid, gains_full, every, gu, dn, saved):
    length, width = tok.shape
    part = dn.shape[0]
    proj, o_low, out_w, *_, qkv_w = saved
    columns = qkv_w.shape[1] // 4
    mix = out_w.shape[0]
    chip_rows = width // 8
    rows = chip_rows // 2
    extra = (rows + 15) // 16 * 16
    piece = mix // 32
    blocks = (8, length, width)
    struct = jax.ShapeDtypeStruct
    shapes = (
        struct((length, width), BF16),
        struct((length, width), BF16),
        struct((7, chip_rows, columns), BF16),
        struct((7, piece, width), BF16),
        struct((8, width), F32),
        struct((8, chip_rows, part), BF16),
        struct((8, extra, part), BF16),
        struct((part // 2, width), BF16),
    )
    scratch = [
        pltpu.VMEM((length, width), BF16),
        pltpu.VMEM(blocks, BF16),
        pltpu.VMEM((length, width), BF16),
        pltpu.VMEM((3, length, width), BF16),
        pltpu.VMEM((3, length, width), BF16),
        pltpu.VMEM((width, part), BF16),
        pltpu.VMEM((width, part), BF16),
        pltpu.VMEM((width // 2, part), BF16),
        pltpu.VMEM((part // 2, width), BF16),
        pltpu.VMEM((part // 2, width), BF16),
        pltpu.VMEM((part // 2, width), BF16),
        pltpu.VMEM((length, width), F32),
        pltpu.VMEM((4, 2, 2 * chip_rows, columns), BF16),
        pltpu.VMEM((4, 2, 2, piece, width), BF16),
        pltpu.VMEM((4, 2, chip_rows, columns), BF16),
        pltpu.VMEM((4, 2, piece, width), BF16),
        pltpu.VMEM((4, chip_rows, columns), BF16),
        pltpu.VMEM((4, piece, width), BF16),
        pltpu.VMEM((4, chip_rows, columns), BF16),
        pltpu.VMEM((4, piece, width), BF16),
        pltpu.VMEM((4, 8, width), F32),
        pltpu.VMEM((6, 8, width), F32),
    ]
    return pl.pallas_call(
        tail_kernel,
        out_shape=shapes,
        in_specs=[vmem()] * 4 + [hbm()] * 14,
        out_specs=(vmem(),) * 8,
        scratch_shapes=scratch + sems(160) + [pltpu.SemaphoreType.DMA((12,))],
        compiler_params=params(1),
        name="tail",
    )(tok, d_out, h_mid, gains_full, every, gu, dn, *saved)


def place_kernel(
    qe, oe, gains, wide_end, wide_back, down_end,
    w_q, w_k, w_v, w_o, w_gate, w_up, w_down, a_pre, a_post, m_pre, m_post, q_gain, k_gain,
):
    p = Place()
    rows, mix = w_q.shape
    head = w_k.shape[1]
    columns = qe.shape[2]
    piece = oe.shape[1]
    size = wide_end.shape[2]
    extra = wide_back.shape[1]

    def put_columns(start, value):
        for ref, first, width in ((w_q, 0, mix), (w_k, mix, head), (w_v, mix + head, head)):
            low, high = max(start, first), min(start + columns, first + width)
            if low < high:
                ref[:, low - first : high - first] = value[:, low - start : high - start]

    for xx in range(2):
        for cc in range(2):

            @pl.when((p.x == xx) & (p.c == cc))
            def _():
                for i, q in (
                    (0, 2 * xx + cc),
                    (4, 2 * xx + 1 - cc),
                    (5, 2 * (1 - xx) + cc),
                    (6, 2 * (1 - xx) + 1 - cc),
                ):
                    both = qe[i].astype(F32)
                    put_columns(q * columns, both[cc * rows : (cc + 1) * rows])
                    if q // 2 == cc:
                        w_o[(q % 2) * piece : (q % 2 + 1) * piece, :] = oe[i].astype(F32)

    for cc in range(2):

        @pl.when(p.c == cc)
        def _():
            own_ref, other_ref = (w_gate, w_up) if cc == 0 else (w_up, w_gate)
            for s in range(8):
                at = slice(s * size, (s + 1) * size)
                own_ref[:, at] = wide_end[s].astype(F32)[cc * rows : (cc + 1) * rows]
                other = wide_back[s].astype(F32)
                other_ref[:, at] = other[:rows] if cc == 0 else other[extra - rows :]

    w_down[...] = down_end[...].astype(F32)
    sums = gains[...]
    for i, ref in enumerate((a_pre, a_post, m_pre, m_post, q_gain, k_gain)):
        per = ref.shape[0]
        full = 16 * per
        turned = pltpu.roll(sums[:, :full], lax.rem(full - p.shard * per, full), 1)
        ref[...] = turned[i, :per]


def place(summed, shapes):
    return pl.pallas_call(
        place_kernel,
        out_shape=tuple(jax.ShapeDtypeStruct(shape, F32) for shape in shapes),
        in_specs=[vmem()] * 6,
        out_specs=(vmem(),) * 13,
        compiler_params=pltpu.CompilerParams(vmem_limit_bytes=VMEM_BYTES),
        name="place",
    )(*summed)


def cube_body(
    layer_in, d_out, segments, w_q, w_k, w_v, w_o, attn_pre, attn_post, q_gain, k_gain,
    w_gate, w_up, w_down, mlp_pre, mlp_post,
):
    width = layer_in.shape[1]
    head = q_gain.shape[0] * 16
    rows, mix = w_q.shape
    gain_list = [attn_pre, attn_post, mlp_pre, mlp_post, q_gain, k_gain]
    (
        qkv_w, out_w, gu_w, down_w, m_all, gains_full, a_low, qk_proj, q_low, k_low, v_low,
        probs, o_low, attn_proj, h_mid, tables,
    ) = front(
        layer_in, segments, w_q, w_k, w_v, w_o, gain_list, w_gate, w_up, w_down, head
    )
    saved = (
        attn_proj, o_low, out_w, v_low, probs, k_low, q_low, qk_proj, tables, a_low, qkv_w,
    )
    layer_out, grad_x, *summed = tail(
        layer_in, d_out, h_mid, gains_full, m_all, gu_w, down_w, saved
    )
    matrices = [w_q, w_k, w_v, w_o, w_gate, w_up, w_down]
    grads = place(summed, [v.shape for v in matrices + gain_list])
    g_apre, g_apost, g_mpre, g_mpost, g_q, g_k = grads[7:]
    return (
        layer_out,
        grad_x,
        *grads[:4],
        g_apre,
        g_apost,
        g_q,
        g_k,
        *grads[4:7],
        g_mpre,
        g_mpost,
    )


def solution(mesh):
    in_specs = (
        P(("replica", "fsdp"), None),
        P(("replica", "fsdp"), None),
        P(("replica", "fsdp"), None),
        P("fsdp", None),
        P("fsdp", None),
        P("fsdp", None),
        P("fsdp", None),
        P("fsdp"),
        P("fsdp"),
        P("fsdp"),
        P("fsdp"),
        P("fsdp", None),
        P("fsdp", None),
        P("fsdp", None),
        P("fsdp"),
        P("fsdp"),
    )
    out_specs = (
        P(("replica", "fsdp"), None),
        P(("replica", "fsdp"), None),
        P("fsdp", None),
        P("fsdp", None),
        P("fsdp", None),
        P("fsdp", None),
        P("fsdp"),
        P("fsdp"),
        P("fsdp"),
        P("fsdp"),
        P("fsdp", None),
        P("fsdp", None),
        P("fsdp", None),
        P("fsdp"),
        P("fsdp"),
    )
    body = cube_body if fits_cubes(mesh) else general_body
    return jax.shard_map(body, mesh=mesh, in_specs=in_specs, out_specs=out_specs, check_vma=False)
```

```python
from functools import partial
import math

import jax
import jax.numpy as jnp
from jax import lax
from jax.experimental import pallas as pl
from jax.experimental.pallas import tpu as pltpu
from jax.sharding import PartitionSpec as P

EPS = 1e-06
THETA = 1000000.0
SCALE = 0.0625
MASKED = -1e30


def norm_rows(values, gain):
    return values * lax.rsqrt(jnp.mean(values * values, axis=-1, keepdims=True) + EPS) * gain


def positions_of(segments):
    length = segments.shape[-1]
    index = jnp.arange(length, dtype=jnp.int32)
    earlier = jnp.concatenate([segments[:, :1] - 1, segments[:, :-1]], axis=1)
    starts = jnp.where(segments != earlier, index[None, :], jnp.zeros_like(segments))
    return index[None, :] - lax.cummax(starts, axis=1)


def angle_tables(segments, head_size):
    half_size = head_size // 2
    rates = jnp.exp(jnp.arange(half_size, dtype=jnp.float32) * (-2.0 * math.log(THETA) / head_size))
    angles = positions_of(segments).astype(jnp.float32)[..., None] * rates
    return (jnp.cos(angles), jnp.sin(angles))


def rotate(values, cosine, sine):
    half_size = values.shape[-1] // 2
    first_half = values[..., :half_size]
    second_half = values[..., half_size:]
    return jnp.concatenate(
        [first_half * cosine - second_half * sine, second_half * cosine + first_half * sine],
        axis=-1,
    )


def query_path(projected, gain, cosine, sine):
    shaped = projected.reshape(projected.shape[0], projected.shape[1], -1, gain.shape[0])
    return rotate(norm_rows(shaped, gain), cosine[:, :, None, :], sine[:, :, None, :])


def key_path(projected, gain, cosine, sine):
    return rotate(norm_rows(projected, gain), cosine, sine)


def gelu_product(gate_val, up_val):
    return jax.nn.gelu(gate_val, approximate=True) * up_val


def to_low(values):
    return values.astype(jnp.bfloat16)


def matmul(left, right):
    return jnp.dot(left, right, preferred_element_type=jnp.float32)


def matmul_left_t(left, right):
    return lax.dot_general(
        left, right, (((0,), (0,)), ((), ())), preferred_element_type=jnp.float32
    )


def matmul_right_t(left, right):
    return lax.dot_general(
        left, right, (((1,), (1,)), ((), ())), preferred_element_type=jnp.float32
    )


def attention_masks(segments):
    length = segments.shape[1]
    index = jnp.arange(length, dtype=jnp.int32)
    causal = index[None, :] <= index[:, None]
    return (segments[:, :, None] == segments[:, None, :]) & causal[None]


def scores_of(q_low, k_low, masks):
    scores = SCALE * jnp.einsum("nqhd,nkd->nhqk", q_low, k_low, preferred_element_type=jnp.float32)
    return jnp.where(masks[:, None], scores, MASKED)


def spread_gain(values):
    return jnp.broadcast_to(values[:, None], (values.shape[0], lax.axis_size("replica")))


def general_body(
    layer_in,
    d_out,
    segments,
    w_q,
    w_k,
    w_v,
    w_o,
    attn_pre,
    attn_post,
    q_gain,
    k_gain,
    w_gate,
    w_up,
    w_down,
    mlp_pre,
    mlp_post,
):
    attn_set = (
        lax.all_gather(to_low(w_q), "fsdp", axis=0, tiled=True),
        lax.all_gather(to_low(w_k), "fsdp", axis=0, tiled=True),
        lax.all_gather(to_low(w_v), "fsdp", axis=0, tiled=True),
        lax.all_gather(to_low(w_o), "fsdp", axis=0, tiled=True),
        lax.all_gather(to_low(attn_pre), "fsdp", axis=0, tiled=True),
        lax.all_gather(to_low(attn_post), "fsdp", axis=0, tiled=True),
        lax.all_gather(to_low(q_gain), "fsdp", axis=0, tiled=True),
        lax.all_gather(to_low(k_gain), "fsdp", axis=0, tiled=True),
    )
    q_full, k_full, v_full, o_full = (attn_set[0], attn_set[1], attn_set[2], attn_set[3])
    gain_apre = attn_set[4].astype(jnp.float32)
    gain_apost = attn_set[5].astype(jnp.float32)
    gain_q = attn_set[6].astype(jnp.float32)
    gain_k = attn_set[7].astype(jnp.float32)
    mlp_set = (
        lax.all_gather(to_low(w_gate), "fsdp", axis=0, tiled=True),
        lax.all_gather(to_low(w_up), "fsdp", axis=0, tiled=True),
        lax.all_gather(to_low(w_down), "fsdp", axis=0, tiled=True),
        lax.all_gather(to_low(mlp_pre), "fsdp", axis=0, tiled=True),
        lax.all_gather(to_low(mlp_post), "fsdp", axis=0, tiled=True),
    )
    gate_full, up_full, down_full = (mlp_set[0], mlp_set[1], mlp_set[2])
    gain_mpre = mlp_set[3].astype(jnp.float32)
    gain_mpost = mlp_set[4].astype(jnp.float32)
    seq_count, seq_len = segments.shape
    tok_flat = layer_in.astype(jnp.float32)
    cosine, sine = angle_tables(segments, gain_q.shape[0])
    masks = attention_masks(segments)
    normed_a, pull_a = jax.vjp(norm_rows, tok_flat, gain_apre)
    a_low = to_low(normed_a)
    q_proj = matmul(a_low, q_full).reshape(seq_count, seq_len, -1)
    k_proj = matmul(a_low, k_full).reshape(seq_count, seq_len, -1)
    v_proj = matmul(a_low, v_full)
    q_rot, pull_q = jax.vjp(partial(query_path, cosine=cosine, sine=sine), q_proj, gain_q)
    k_rot, pull_k = jax.vjp(partial(key_path, cosine=cosine, sine=sine), k_proj, gain_k)
    q_low = to_low(q_rot)
    k_low = to_low(k_rot)
    v_low = to_low(v_proj).reshape(seq_count, seq_len, -1)
    scores = scores_of(q_low, k_low, masks)
    top_val = jnp.max(scores, axis=-1, keepdims=True)
    log_total = top_val + jnp.log(jnp.sum(jnp.exp(scores - top_val), axis=-1, keepdims=True))
    p_low = to_low(jnp.exp(scores - log_total))
    attn_mix = jnp.einsum("nhqk,nkd->nqhd", p_low, v_low, preferred_element_type=jnp.float32)
    o_low = to_low(attn_mix.reshape(seq_count * seq_len, -1))
    attn_proj = matmul(o_low, o_full)
    post_attn, pull_pa = jax.vjp(norm_rows, attn_proj, gain_apost)
    h_mid = tok_flat + post_attn
    normed_m, pull_m = jax.vjp(norm_rows, h_mid, gain_mpre)
    m_low = to_low(normed_m)
    gate_val = matmul(m_low, gate_full)
    up_val = matmul(m_low, up_full)
    hidden, pull_h = jax.vjp(gelu_product, gate_val, up_val)
    h_low = to_low(hidden)
    down_val = matmul(h_low, down_full)
    post_mlp, pull_pm = jax.vjp(norm_rows, down_val, gain_mpost)
    layer_out = (h_mid + post_mlp).astype(jnp.bfloat16)
    gate_full, up_full, down_full = (
        lax.all_gather(to_low(w_gate), "fsdp", axis=0, tiled=True),
        lax.all_gather(to_low(w_up), "fsdp", axis=0, tiled=True),
        lax.all_gather(to_low(w_down), "fsdp", axis=0, tiled=True),
    )
    grad_top = d_out.astype(jnp.float32)
    d_down, grad_mpost = pull_pm(grad_top)
    d_down_low = to_low(d_down)
    grad_wdown = matmul_left_t(h_low, d_down_low)
    d_hidden = matmul_right_t(d_down_low, down_full)
    d_gate, d_up = pull_h(d_hidden)
    d_gate_low = to_low(d_gate)
    d_up_low = to_low(d_up)
    grad_wgate = matmul_left_t(m_low, d_gate_low)
    grad_wup = matmul_left_t(m_low, d_up_low)
    d_normed = matmul_right_t(d_gate_low, gate_full) + matmul_right_t(d_up_low, up_full)
    d_mid_norm, grad_mpre = pull_m(d_normed)
    d_mid = grad_top + d_mid_norm
    q_full, k_full, v_full, o_full = (
        lax.all_gather(to_low(w_q), "fsdp", axis=0, tiled=True),
        lax.all_gather(to_low(w_k), "fsdp", axis=0, tiled=True),
        lax.all_gather(to_low(w_v), "fsdp", axis=0, tiled=True),
        lax.all_gather(to_low(w_o), "fsdp", axis=0, tiled=True),
    )
    d_attn, grad_apost = pull_pa(d_mid)
    d_attn_low = to_low(d_attn)
    grad_wo = matmul_left_t(o_low, d_attn_low)
    d_mix_low = to_low(matmul_right_t(d_attn_low, o_full)).reshape(
        seq_count, seq_len, -1, k_low.shape[-1]
    )
    probs = jnp.exp(scores_of(q_low, k_low, masks) - log_total)
    d_probs = jnp.einsum("nqhd,nkd->nhqk", d_mix_low, v_low, preferred_element_type=jnp.float32)
    row_dot = jnp.sum(probs * d_probs, axis=-1, keepdims=True)
    d_scores_low = to_low(probs * (d_probs - row_dot))
    d_query = SCALE * jnp.einsum(
        "nhqk,nkd->nqhd", d_scores_low, k_low, preferred_element_type=jnp.float32
    )
    d_key = SCALE * jnp.einsum(
        "nhqk,nqhd->nkd", d_scores_low, q_low, preferred_element_type=jnp.float32
    )
    d_value = jnp.einsum("nhqk,nqhd->nkd", p_low, d_mix_low, preferred_element_type=jnp.float32)
    d_qproj, grad_qgain = pull_q(d_query)
    d_kproj, grad_kgain = pull_k(d_key)
    d_q_low = to_low(d_qproj.reshape(seq_count * seq_len, -1))
    d_k_low = to_low(d_kproj.reshape(seq_count * seq_len, -1))
    d_v_low = to_low(d_value.reshape(seq_count * seq_len, -1))
    grad_wq = matmul_left_t(a_low, d_q_low)
    grad_wk = matmul_left_t(a_low, d_k_low)
    grad_wv = matmul_left_t(a_low, d_v_low)
    d_normed_a = (
        matmul_right_t(d_q_low, q_full)
        + matmul_right_t(d_k_low, k_full)
        + matmul_right_t(d_v_low, v_full)
    )
    d_input_norm, grad_apre = pull_a(d_normed_a)
    grad_x = (d_mid + d_input_norm).astype(jnp.bfloat16)
    all_shards = (
        lax.psum_scatter(grad_wq, "fsdp", scatter_dimension=0, tiled=True),
        lax.psum_scatter(grad_wk, "fsdp", scatter_dimension=0, tiled=True),
        lax.psum_scatter(grad_wv, "fsdp", scatter_dimension=0, tiled=True),
        lax.psum_scatter(grad_wo, "fsdp", scatter_dimension=0, tiled=True),
        lax.psum_scatter(grad_apre, "fsdp", scatter_dimension=0, tiled=True),
        lax.psum_scatter(grad_apost, "fsdp", scatter_dimension=0, tiled=True),
        lax.psum_scatter(grad_qgain, "fsdp", scatter_dimension=0, tiled=True),
        lax.psum_scatter(grad_kgain, "fsdp", scatter_dimension=0, tiled=True),
        lax.psum_scatter(grad_wgate, "fsdp", scatter_dimension=0, tiled=True),
        lax.psum_scatter(grad_wup, "fsdp", scatter_dimension=0, tiled=True),
        lax.psum_scatter(grad_wdown, "fsdp", scatter_dimension=0, tiled=True),
        lax.psum_scatter(grad_mpre, "fsdp", scatter_dimension=0, tiled=True),
        lax.psum_scatter(grad_mpost, "fsdp", scatter_dimension=0, tiled=True),
    )
    all_cols = (
        lax.psum_scatter(
            all_shards[0].astype(jnp.bfloat16), "replica", scatter_dimension=1, tiled=True
        ).astype(jnp.float32),
        lax.psum_scatter(
            all_shards[1].astype(jnp.bfloat16), "replica", scatter_dimension=1, tiled=True
        ).astype(jnp.float32),
        lax.psum_scatter(
            all_shards[2].astype(jnp.bfloat16), "replica", scatter_dimension=1, tiled=True
        ).astype(jnp.float32),
        lax.psum_scatter(
            all_shards[3].astype(jnp.bfloat16), "replica", scatter_dimension=1, tiled=True
        ).astype(jnp.float32),
        lax.psum_scatter(
            all_shards[8].astype(jnp.bfloat16), "replica", scatter_dimension=1, tiled=True
        ).astype(jnp.float32),
        lax.psum_scatter(
            all_shards[9].astype(jnp.bfloat16), "replica", scatter_dimension=1, tiled=True
        ).astype(jnp.float32),
        lax.psum_scatter(
            all_shards[10].astype(jnp.bfloat16), "replica", scatter_dimension=1, tiled=True
        ).astype(jnp.float32),
        lax.psum_scatter(
            spread_gain(all_shards[4]).astype(jnp.bfloat16),
            "replica",
            scatter_dimension=1,
            tiled=True,
        ).astype(jnp.float32),
        lax.psum_scatter(
            spread_gain(all_shards[5]).astype(jnp.bfloat16),
            "replica",
            scatter_dimension=1,
            tiled=True,
        ).astype(jnp.float32),
        lax.psum_scatter(
            spread_gain(all_shards[6]).astype(jnp.bfloat16),
            "replica",
            scatter_dimension=1,
            tiled=True,
        ).astype(jnp.float32),
        lax.psum_scatter(
            spread_gain(all_shards[7]).astype(jnp.bfloat16),
            "replica",
            scatter_dimension=1,
            tiled=True,
        ).astype(jnp.float32),
        lax.psum_scatter(
            spread_gain(all_shards[11]).astype(jnp.bfloat16),
            "replica",
            scatter_dimension=1,
            tiled=True,
        ).astype(jnp.float32),
        lax.psum_scatter(
            spread_gain(all_shards[12]).astype(jnp.bfloat16),
            "replica",
            scatter_dimension=1,
            tiled=True,
        ).astype(jnp.float32),
    )
    all_mats = (
        lax.all_gather(all_cols[0].astype(jnp.bfloat16), "replica", axis=1, tiled=True).astype(
            jnp.float32
        ),
        lax.all_gather(all_cols[1].astype(jnp.bfloat16), "replica", axis=1, tiled=True).astype(
            jnp.float32
        ),
        lax.all_gather(all_cols[2].astype(jnp.bfloat16), "replica", axis=1, tiled=True).astype(
            jnp.float32
        ),
        lax.all_gather(all_cols[3].astype(jnp.bfloat16), "replica", axis=1, tiled=True).astype(
            jnp.float32
        ),
        lax.all_gather(all_cols[4].astype(jnp.bfloat16), "replica", axis=1, tiled=True).astype(
            jnp.float32
        ),
        lax.all_gather(all_cols[5].astype(jnp.bfloat16), "replica", axis=1, tiled=True).astype(
            jnp.float32
        ),
        lax.all_gather(all_cols[6].astype(jnp.bfloat16), "replica", axis=1, tiled=True).astype(
            jnp.float32
        ),
    )
    attn_sums = (
        all_mats[0],
        all_mats[1],
        all_mats[2],
        all_mats[3],
        all_cols[7][:, 0],
        all_cols[8][:, 0],
        all_cols[9][:, 0],
        all_cols[10][:, 0],
    )
    mlp_sums = (all_mats[4], all_mats[5], all_mats[6], all_cols[11][:, 0], all_cols[12][:, 0])
    return (
        layer_out,
        grad_x,
        attn_sums[0],
        attn_sums[1],
        attn_sums[2],
        attn_sums[3],
        attn_sums[4],
        attn_sums[5],
        attn_sums[6],
        attn_sums[7],
        mlp_sums[0],
        mlp_sums[1],
        mlp_sums[2],
        mlp_sums[3],
        mlp_sums[4],
    )


MESH = pl.DeviceIdType.MESH
VMEM_BYTES = 63 * 2**20
F32 = jnp.float32
BF16 = jnp.bfloat16


def fits_cubes(mesh):
    return dict(mesh.shape) == {"replica": 2, "fsdp": 16}


class Place:
    def __init__(self):
        shard = lax.axis_index("fsdp")
        self.x = lax.axis_index("replica")
        self.shard = shard
        self.c = lax.rem(shard, 2)
        self.y = lax.rem(lax.div(shard, 2), 2)
        self.z = lax.div(shard, 4)
        self.zl = lax.rem(self.z, 2)
        self.zh = lax.div(self.z, 2)

    def at(self, x=None, y=None, z=None, c=None):
        x = self.x if x is None else x
        y = self.y if y is None else y
        z = self.z if z is None else z
        c = self.c if c is None else c
        return (x, (z * 2 + y) * 2 + c)

    def z_xor(self, k):
        low = self.zl if k % 2 == 0 else 1 - self.zl
        high = self.zh if k // 2 == 0 else 1 - self.zh
        return 2 * high + low

    def slice_z(self, z=None):
        z = self.z if z is None else z
        inner = lax.rem(lax.rem(z, 2) + lax.div(z, 2), 2)
        return jnp.where(self.x == 0, 2 * inner, 3 - 2 * inner)

    def cube(self, bits):
        return self.at(
            x=1 - self.x if bits & 4 else self.x,
            y=1 - self.y if bits & 2 else self.y,
            z=self.z_xor(1) if bits & 1 else self.z,
        )


class Wires:
    def __init__(self, send, recv):
        self.send, self.recv, self.used = send, recv, 0

    def remote(self, src, dst, device):
        i = self.used
        self.used += 1
        return pltpu.make_async_remote_copy(
            src_ref=src,
            dst_ref=dst,
            send_sem=self.send.at[i],
            recv_sem=self.recv.at[i],
            device_id=device,
            device_id_type=MESH,
        )

    def local(self, src, dst):
        i = self.used
        self.used += 1
        return pltpu.make_async_copy(src, dst, self.send.at[i])


def greet(devices):
    barrier = pltpu.get_barrier_semaphore()
    for device in devices:
        pl.semaphore_signal(barrier, inc=1, device_id=device, device_id_type=MESH)
    pl.semaphore_wait(barrier, len(devices))


def hbm():
    return pl.BlockSpec(memory_space=pl.ANY)


def vmem():
    return pl.BlockSpec(memory_space=pltpu.VMEM)


def sems(count):
    return [pltpu.SemaphoreType.DMA((count,)), pltpu.SemaphoreType.DMA((count,))]


def params(collective_id):
    return pltpu.CompilerParams(
        collective_id=collective_id, has_side_effects=True, vmem_limit_bytes=VMEM_BYTES
    )


X, Y, Z = 4, 2, 1


def thirds(rows):
    first = -(-rows // 48) * 16
    return ((0, first), (first, first), (2 * first, rows - 2 * first))


def add(left, right):
    return (left.astype(F32) + right.astype(F32)).astype(BF16)


class CubeSum:
    MIDDLE = ((X, Y, Y | Z), (Y, Z, X | Z), (Z, X, X | Y))
    NEAR = ((Y, Z), (Z, X), (X, Y))

    def __init__(self, p, w, parts, third, second, first):
        self.p, self.w, self.parts = p, w, parts
        self.third, self.second, self.first = third, second, first
        self.half = parts.shape[1] // 2
        self.started = []
        self.far, self.mid, self.end = {}, {}, {}

    def push(self, src, dst, bit):
        copy = self.w.remote(src, dst, self.p.cube(bit))
        copy.start()
        self.started.append(copy)
        return copy

    def send_far(self):
        for h in range(2):
            for (start, size), link in zip(thirds(self.half), (X, Y, Z)):
                at = pl.ds(h * self.half + start, size)
                self.far[link, h] = self.push(self.parts.at[7, at], self.third.at[at], link)

    def send_middle(self):
        for h in range(2):
            for i, (link, onward, place) in enumerate(self.MIDDLE):
                start, size = thirds(self.half)[i]
                at = pl.ds(h * self.half + start, size)
                all_at = pl.ds(h * self.half, self.half)
                self.far[link, h].wait_recv()
                self.parts[place, at] = add(self.parts[place, at], self.third[at, :])
                self.mid[onward, h] = self.push(
                    self.parts.at[place, all_at], self.second.at[i, all_at], onward
                )

    def send_near(self):
        for h in range(2):
            at = pl.ds(h * self.half, self.half)
            for i, (came, place) in enumerate(self.NEAR):
                self.mid[came, h].wait_recv()
                self.parts[place, at] = add(self.parts[place, at], self.second[i, at])
                self.end[place, h] = self.push(
                    self.parts.at[place, at], self.first.at[i, at], place
                )

    def finish(self):
        for h in range(2):
            at = pl.ds(h * self.half, self.half)
            value = self.parts[0, at].astype(F32)
            for i, (_, place) in enumerate(self.NEAR):
                self.end[place, h].wait_recv()
                value = value + self.first[i, at].astype(F32)
            yield at, value

    def wait_sent(self):
        for copy in self.started:
            copy.wait_send()
        self.started = []


class LightSum(CubeSum):
    def send_far(self):
        for h, link in ((0, X), (1, Y)):
            at = pl.ds(h * self.half, self.half)
            self.far[link, h] = self.push(self.parts.at[7, at], self.third.at[at], link)

    def send_middle(self):
        for h, link, place in ((0, X, Y | Z), (1, Y, X | Z)):
            at = pl.ds(h * self.half, self.half)
            self.far[link, h].wait_recv()
            self.parts[place, at] = add(self.parts[place, at], self.third[at, :])
        for h in range(2):
            at = pl.ds(h * self.half, self.half)
            for i, (link, place) in enumerate(((X, X | Z), (Y, Y | Z))):
                self.mid[link, h] = self.push(self.parts.at[place, at], self.second.at[i, at], link)
            link = (X, Y)[h]
            self.mid[X | Y, h] = self.push(self.parts.at[X | Y, at], self.second.at[2, at], link)

    def send_near(self):
        for h in range(2):
            at = pl.ds(h * self.half, self.half)
            self.mid[X, h].wait_recv()
            self.mid[Y, h].wait_recv()
            total = self.second[0, at].astype(F32) + self.second[1, at].astype(F32)
            self.parts[Z, at] = add(self.parts[Z, at], total)
            self.end[Z, h] = self.push(self.parts.at[Z, at], self.first.at[0, at], Z)
            self.mid[X | Y, h].wait_recv()
            place = (Y, X)[h]
            self.parts[place, at] = add(self.parts[place, at], self.second[2, at])
            for i, bit in ((1, X), (2, Y)):
                self.end[bit, h] = self.push(self.parts.at[bit, at], self.first.at[i, at], bit)


class CubeGather:
    def __init__(self, p, w, block, every):
        self.p, self.w, self.block, self.every = p, w, block, every
        self.half = block.shape[0] // 2
        self.started = []
        self.near, self.middle, self.far = {}, {}, {}

    def push(self, src, dst, bit):
        copy = self.w.remote(src, dst, self.p.cube(bit))
        copy.start()
        self.started.append(copy)
        return copy

    def send_near(self, h):
        at = pl.ds(h * self.half, self.half)
        for bit in (X, Y, Z):
            self.near[bit, h] = self.push(self.block.at[at], self.every.at[bit, at], bit)

    def send_middle(self, h):
        at = pl.ds(h * self.half, self.half)
        for link, relay in ((X, Y), (Y, Z), (Z, X)):
            self.near[relay, h].wait_recv()
            self.middle[link | relay, h] = self.push(
                self.every.at[relay, at], self.every.at[link | relay, at], link
            )

    def send_far(self, h):
        for (start, size), link, relay in zip(thirds(self.half), (X, Y, Z), (Y | Z, X | Z, X | Y)):
            at = pl.ds(h * self.half + start, size)
            self.middle[relay, h].wait_recv()
            self.far[link, h] = self.push(self.every.at[relay, at], self.every.at[7, at], link)

    def wait_far(self):
        for copy in self.far.values():
            copy.wait_recv()

    def wait_sent(self):
        for copy in self.started:
            copy.wait_send()
        self.started = []


def norm_scale(values):
    return lax.rsqrt(jnp.mean(values * values, axis=-1, keepdims=True) + EPS)


def norm_pull(values, scale, gain, cotangent):
    weighted = gain * cotangent
    lean = jnp.mean(values * weighted, axis=-1, keepdims=True)
    d_values = scale * weighted - values * (scale * scale * scale * lean)
    return d_values, jnp.sum(values * scale * cotangent, axis=0, keepdims=True)


def spread_matrix(width, per):
    column = lax.broadcasted_iota(jnp.int32, (128, width), 1)
    row = lax.broadcasted_iota(jnp.int32, (128, width), 0)
    place = (lax.rem(column, per) == row).astype(F32)
    column = lax.broadcasted_iota(jnp.int32, (16, width), 1)
    row = lax.broadcasted_iota(jnp.int32, (16, width), 0)
    owner = (lax.div(column, per) == row).astype(F32)
    return place, owner


def join_gains(packed, which, width, per):
    place, owner = spread_matrix(width, per)
    shards = packed[:, which, :].astype(BF16)
    wide = jnp.dot(shards, place.astype(BF16), preferred_element_type=F32)
    return jnp.sum(wide * owner, axis=0, keepdims=True)


def turn(values, cosine, sine):
    half = values.shape[-1] // 2
    u, w = values[:, :half], values[:, half:]
    return jnp.concatenate([u * cosine - w * sine, w * cosine + u * sine], axis=1)


def turn_back(values, cosine, sine):
    half = values.shape[-1] // 2
    u, w = values[:, :half], values[:, half:]
    return jnp.concatenate([u * cosine + w * sine, w * cosine - u * sine], axis=1)


def front_kernel(
    tok, seg_row, w_q, w_k, w_v, w_o, g_apre, g_apost, g_mpre, g_mpost, g_q, g_k, w_gate, w_up, w_down,
    qkv_w, out_w, gu_w, dn_w, every, gains_full, a_low, qk_proj, q_low, k_low, v_low,
    probs, o_low, attn_proj, h_mid, tables,
    qkv_s, qkv_own, qkv_send, qkv_got, out_own, gains_own, gains_s, wide_in, wide_send, wide_got,
    wide_out, down_in, down_out, m_low, out_s, send, recv, local,
):
    p = Place()
    w = Wires(send, recv)
    x, y, z, c, zl, zh = p.x, p.y, p.z, p.c, p.zl, p.zh
    sibling = p.at(c=1 - c)
    plane = [p.at(x=1 - x), p.at(y=1 - y)]
    lines = [p.at(y=yy, z=p.z_xor(k)) for yy in (y, 1 - y) for k in range(1, 4)]
    started = []

    def push(src, dst, device):
        copy = w.remote(src, dst, device)
        copy.start()
        started.append(copy)
        return copy

    loads = [
        pltpu.make_async_copy(w_gate, wide_in.at[0], local.at[0]),
        pltpu.make_async_copy(w_up, wide_in.at[1], local.at[1]),
        pltpu.make_async_copy(w_down, down_in, local.at[2]),
    ]
    for copy in loads:
        copy.start()

    rows = w_q.shape[0]
    columns = qkv_s.shape[1] // 4
    out_rows = w_o.shape[0] // 2
    mine = 2 * x + c
    theirs = 2 * x + 1 - c

    all_own = jnp.concatenate([w_q[...], w_k[...], w_v[...]], axis=1)
    for quarter in range(4):
        qkv_own[quarter] = all_own[:, quarter * columns : (quarter + 1) * columns]
    qkv_send[...] = qkv_own[theirs].astype(BF16)
    out_own[...] = w_o[...].astype(BF16)
    gains_own[...] = jnp.zeros_like(gains_own)
    for i, gain in enumerate((g_apre, g_apost, g_mpre, g_mpost, g_q, g_k)):
        gains_own[i, : gain.shape[0]] = gain[...].astype(BF16).astype(F32)
    across = p.at(x=1 - x, z=p.z_xor(3))
    greet([sibling, across] + plane + lines)

    def qkv_at(zz, yy, quarter):
        return qkv_s.at[
            pl.ds(pl.multiple_of((2 * zz + yy) * 2 * rows, 16), 2 * rows),
            pl.ds(pl.multiple_of(quarter * columns, 128), columns),
        ]

    def out_at(zz, yy, quarter):
        return out_s.at[
            pl.ds(pl.multiple_of((2 * zz + yy) * 4 * out_rows + quarter * out_rows, 16), out_rows)
        ]

    swap = push(qkv_send, qkv_got, sibling)

    def gains_at(zz, yy, cc):
        return gains_s.at[(2 * zz + yy) * 2 + cc]

    gains_s[(2 * z + y) * 2 + c] = gains_own[...]
    gain_line = [push(gains_own, gains_at(z, y, c), p.at(z=p.z_xor(k))) for k in range(1, 4)]
    gain_side = [push(gains_own, gains_at(z, y, c), plane[1])]
    holds = x == c
    out_theirs = out_own.at[pl.ds(pl.multiple_of((1 - c) * out_rows, 16), out_rows)]
    out_swap = w.remote(out_theirs, out_at(z, y, theirs), sibling)
    pl.when(holds)(out_swap.start)

    @pl.when(holds)
    def _():
        out_s[pl.ds(pl.multiple_of((2 * z + y) * 4 * out_rows + mine * out_rows, 16), out_rows)] = (
            out_own[pl.ds(pl.multiple_of(c * out_rows, 16), out_rows)]
        )

    swap.wait_recv()
    top, low = qkv_own[mine], qkv_got[...].astype(F32)
    first = jnp.where(c == 0, top, low)
    second = jnp.where(c == 0, low, top)
    base = pl.multiple_of((2 * z + y) * 2 * rows, 16)
    joined = jnp.concatenate([first, second], axis=0).astype(BF16)
    qkv_s[pl.ds(base, 2 * rows), pl.ds(pl.multiple_of(mine * columns, 128), columns)] = joined

    pl.when(jnp.logical_not(holds))(out_swap.wait_recv)
    pl.when(holds)(out_swap.wait_send)

    line = [None]
    for k in range(1, 4):
        to = p.at(z=p.z_xor(k))
        line.append(
            (
                push(qkv_at(z, y, mine), qkv_at(z, y, mine), to),
                push(out_at(z, y, mine), out_at(z, y, mine), to),
            )
        )
    side_x, side_y, corner = {}, {}, {}

    def spread(k):
        zz = p.z_xor(k)
        if k:
            for copy in line[k]:
                copy.wait_recv()
        qkv, out = qkv_at(zz, y, mine), out_at(zz, y, mine)
        side_x[k] = (push(qkv, qkv, plane[0]), push(out, out, plane[0]))
        side_y[k] = (push(qkv, qkv, plane[1]), push(out, out, plane[1]))

    def relay(k):
        zz = p.z_xor(k)
        if k % 2:
            for copy in side_y[k]:
                copy.wait_recv()
            qkv, out, to = qkv_at(zz, 1 - y, mine), out_at(zz, 1 - y, mine), plane[0]
        else:
            for copy in side_x[k]:
                copy.wait_recv()
            other = 2 * (1 - x) + c
            qkv, out, to = qkv_at(zz, y, other), out_at(zz, y, other), plane[1]
        corner[k] = (push(qkv, qkv, to), push(out, out, to))

    pairs = []

    def share(k):
        zz = p.z_xor(k)
        for copy in (side_x[k] if k % 2 else side_y[k]) + corner[k]:
            copy.wait_recv()
        for xx in range(2):
            at = qkv_s.at[
                pl.ds(pl.multiple_of(2 * zz * 2 * rows, 16), 4 * rows),
                pl.ds(pl.multiple_of((2 * xx + c) * columns, 128), columns),
            ]
            pairs.append(push(at, at, sibling))
            for yy in range(2):
                at = out_at(zz, yy, 2 * xx + c)
                pairs.append(push(at, at, sibling))

    spread(0)
    loads[0].wait()
    loads[1].wait()
    part_columns = wide_out.shape[-1]
    for xx in range(2):

        @pl.when(x == xx)
        def _():
            for zz in range(2):
                for yy in range(2):
                    part = (3 - 2 * zz if xx else 2 * zz) * 2 + yy
                    at = slice(part * part_columns, (part + 1) * part_columns)
                    for matrix in range(2):

                        @pl.when(c == 1 - matrix)
                        def _():
                            wide_send[2 * zz + yy] = wide_in[matrix, :, at].astype(BF16)

    wide_swap = push(wide_send, wide_got, sibling)
    loads[2].wait()
    down_out[...] = down_in[...].astype(BF16)
    relay(0)
    spread(1)
    wide_swap.wait_recv()
    for xx in range(2):

        @pl.when(x == xx)
        def _():
            for zz in range(2):
                for yy in range(2):
                    part = (3 - 2 * zz if xx else 2 * zz) * 2 + yy
                    at = slice(part * part_columns, (part + 1) * part_columns)
                    got = wide_got[2 * zz + yy].astype(F32)
                    for matrix in range(2):

                        @pl.when(c == matrix)
                        def _():
                            own = wide_in[matrix, :, at]
                            both = [own, got] if matrix == 0 else [got, own]
                            wide_out[2 * zz + yy] = jnp.concatenate(both, axis=0).astype(BF16)

    def gu_at(zz, yy):
        return gu_w.at[c, pl.ds(pl.multiple_of((2 * zz + yy) * 2 * rows, 16), 2 * rows)]

    down_rows = down_out.shape[0]
    down_at = dn_w.at[pl.ds(pl.multiple_of(c * down_rows, 16), down_rows)]
    down_local = p.slice_z() == z
    down_sends = lax.rem(zl + c, 2) == x
    down_copy = w.remote(down_out, down_at, p.at(x=zl, z=p.z_xor(3)))
    pl.when(down_sends)(down_copy.start)
    own_down = pltpu.make_async_copy(down_out, down_at, local.at[1])
    pl.when(down_local)(own_down.start)

    wide = []
    for k in range(4):
        for other in range(2):
            yy = 1 - y if other else y
            zz = p.z_xor(k)
            inner = lax.rem(lax.rem(zz, 2) + lax.div(zz, 2), 2)
            src = wide_out.at[2 * inner + yy]
            if k == 0 and other == 0:
                own_wide = pltpu.make_async_copy(src, gu_at(z, y), local.at[0])
                own_wide.start()
            else:
                wide.append((zz, yy, push(src, gu_at(z, y), p.at(y=yy, z=zz))))

    tok_f = tok[...].astype(F32)
    length, width = tok_f.shape
    head = k_low.shape[1]
    spread(2)
    relay(1)
    for copy in gain_line:
        copy.wait_recv()
    for k in range(1, 4):
        zz = p.z_xor(k)
        gain_side.append(push(gains_at(zz, y, c), gains_at(zz, y, c), plane[1]))
    row_seg = seg_row[...].astype(F32)
    i_at = lax.broadcasted_iota(jnp.int32, (length, length), 0)
    j_at = lax.broadcasted_iota(jnp.int32, (length, length), 1)
    col_seg = jnp.sum(jnp.where(i_at == j_at, row_seg, 0.0), axis=1, keepdims=True)
    earlier = jnp.sum((row_seg < col_seg).astype(F32), axis=1, keepdims=True)
    index = lax.broadcasted_iota(jnp.int32, (length, 1), 0).astype(F32)
    rate_at = lax.broadcasted_iota(jnp.int32, (1, head // 2), 1).astype(F32)
    rates = jnp.exp(rate_at * (-2.0 * math.log(THETA) / head))
    angles = (index - earlier) * rates
    tables[0] = jnp.cos(angles)
    tables[1] = jnp.sin(angles)
    spread(3)
    relay(2)
    share(0)
    relay(3)
    for copy in gain_side:
        copy.wait_recv()
    gain_pair = []
    for zz in range(4):
        for yy in range(2):
            gain_pair.append(push(gains_at(zz, yy, c), gains_at(zz, yy, c), sibling))
    share(1)
    for copy in gain_pair:
        copy.wait_recv()
    packed = gains_s[...]
    for i, (size, per) in enumerate(
        ((width, rows),) * 4 + ((head, head // 16),) * 2
    ):
        gains_full[i, :, :size] = join_gains(packed, i, size, per)
    a_low[...] = (tok_f * norm_scale(tok_f) * gains_full[0]).astype(BF16)
    share(2)
    share(3)
    for copy in pairs:
        copy.wait_recv()
    saves = [
        pltpu.make_async_copy(qkv_s, qkv_w, local.at[2]),
        pltpu.make_async_copy(out_s, out_w, local.at[3]),
    ]
    for copy in saves:
        copy.start()

    cosine, sine = tables[0], tables[1]
    heads = q_low.shape[1] // head
    for i in range(heads + 2):
        at = slice(i * head, (i + 1) * head)
        value = jnp.dot(a_low[...], qkv_s[:, at], preferred_element_type=F32)
        if i < heads:
            qk_proj[:, at] = value
            q_low[:, at] = turn(
                value * norm_scale(value) * gains_full[4, :, :head], cosine, sine
            ).astype(BF16)
        elif i == heads:
            qk_proj[:, at] = value
            k_low[...] = turn(
                value * norm_scale(value) * gains_full[5, :, :head], cosine, sine
            ).astype(BF16)
        else:
            v_low[...] = value.astype(BF16)
    allowed = (row_seg == col_seg) & (j_at <= i_at)
    for i in range(heads):
        at = slice(i * head, (i + 1) * head)
        scores = SCALE * lax.dot_general(
            q_low[:, at], k_low[...], (((1,), (1,)), ((), ())), preferred_element_type=F32
        )
        scores = jnp.where(allowed, scores, MASKED)
        expo = jnp.exp(scores - jnp.max(scores, axis=1, keepdims=True))
        prob = expo / jnp.sum(expo, axis=1, keepdims=True)
        probs[i] = prob
        o_low[:, at] = jnp.dot(
            prob.astype(BF16), v_low[...], preferred_element_type=F32
        ).astype(BF16)
    third = width // 3
    for i in range(3):
        at = slice(i * third, (i + 1) * third)
        attn_proj[:, at] = jnp.dot(o_low[...], out_s[:, at], preferred_element_type=F32)
    proj = attn_proj[...]
    mid = tok_f + proj * norm_scale(proj) * gains_full[1]
    h_mid[...] = mid
    m_low[...] = (mid * norm_scale(mid) * gains_full[2]).astype(BF16)

    gather = CubeGather(p, w, m_low, every)
    own = pltpu.make_async_copy(m_low, every.at[0], local.at[4])
    own.start()
    gather.send_near(0)
    gather.send_near(1)
    own_wide.wait()
    shared = [push(gu_at(z, y), gu_at(z, y), sibling)]
    gather.send_middle(0)
    gather.send_middle(1)
    gather.send_far(0)
    gather.send_far(1)
    for zz, yy, copy in reversed(wide):
        copy.wait_recv()
        shared.append(push(gu_at(zz, yy), gu_at(zz, yy), sibling))
    pl.when(down_local)(own_down.wait)
    pl.when(jnp.logical_not(down_local))(down_copy.wait_recv)
    shared.append(push(down_at, down_at, sibling))
    gather.wait_far()
    own.wait()
    gather.wait_sent()
    for copy in shared:
        copy.wait_recv()
    for copy in saves:
        copy.wait()
    pl.when(down_sends)(down_copy.wait_send)
    for copy in started:
        copy.wait_send()


def front(tok, segments, w_q, w_k, w_v, w_o, gains, w_gate, w_up, w_down, head):
    length, width = tok.shape
    rows, mix = w_q.shape
    hidden = w_gate.shape[1]
    part = hidden // 8
    down_rows = w_down.shape[0]
    total = mix + 2 * head
    heads = mix // head
    columns = total // 4
    struct = jax.ShapeDtypeStruct
    shapes = (
        struct((16 * rows, total), BF16),
        struct((16 * w_o.shape[0], width), BF16),
        struct((2, 16 * rows, part), BF16),
        struct((2 * down_rows, width), BF16),
        struct((8, length, width), BF16),
        struct((8, 1, width), F32),
        struct((length, width), BF16),
        struct((length, mix + head), F32),
        struct((length, mix), BF16),
        struct((length, head), BF16),
        struct((length, head), BF16),
        struct((heads, length, length), F32),
        struct((length, mix), BF16),
        struct((length, width), F32),
        struct((length, width), F32),
        struct((2, length, head // 2), F32),
    )
    scratch = [
        pltpu.VMEM((16 * rows, total), BF16),
        pltpu.VMEM((4, rows, columns), F32),
        pltpu.VMEM((rows, columns), BF16),
        pltpu.VMEM((rows, columns), BF16),
        pltpu.VMEM(w_o.shape, BF16),
        pltpu.VMEM((8, 128), F32),
        pltpu.VMEM((16, 8, 128), F32),
        pltpu.VMEM((2, rows, hidden), F32),
        pltpu.VMEM((4, rows, part), BF16),
        pltpu.VMEM((4, rows, part), BF16),
        pltpu.VMEM((4, 2 * rows, part), BF16),
        pltpu.VMEM((down_rows, width), F32),
        pltpu.VMEM((down_rows, width), BF16),
        pltpu.VMEM((length, width), BF16),
        pltpu.VMEM((16 * w_o.shape[0], width), BF16),
    ]
    return pl.pallas_call(
        front_kernel,
        out_shape=shapes,
        in_specs=[vmem()] * 12 + [hbm()] * 3,
        out_specs=(hbm(),) * 5 + (vmem(),) * 11,
        scratch_shapes=scratch + sems(128) + [pltpu.SemaphoreType.DMA((5,))],
        compiler_params=params(0),
        name="front",
    )(
        tok, segments, w_q, w_k, w_v, w_o, *gains, w_gate, w_up, w_down
    )


def dot_rows(left, right):
    return lax.dot_general(left, right, (((0,), (0,)), ((), ())), preferred_element_type=F32)


def dot_columns(left, right):
    return lax.dot_general(left, right, (((1,), (1,)), ((), ())), preferred_element_type=F32)


GELU_ROOT = math.sqrt(2.0 / math.pi)


def gelu_parts(gate):
    square = gate * gate
    bend = jnp.tanh(GELU_ROOT * gate * (1.0 + 0.044715 * square))
    half = 0.5 * (1.0 + bend)
    slope = half + 0.5 * gate * (1.0 - bend * bend) * GELU_ROOT * (1.0 + 3 * 0.044715 * square)
    return half * gate, slope


def tiles(size, step):
    return [slice(at, min(at + step, size)) for at in range(0, size, step)]


def tail_kernel(
    tok, d_out, h_mid, gains_full, every, gu, dn, proj_h, o_h, out_h, v_h, probs_h, k_h, q_h, qk_h,
    tables_h, a_h, qkv_h,
    layer_out, grad_x, qe, oe, gains_sum, wide_end, wide_back, down_end,
    dd_own, dd_all, third, second, first, wide_got, wide_sum, wide_far, down_got, down_sum, down_far,
    down_via, d_mid, q1, o1, qa, oa, qb, ob, qc, oc, gain_acc, gain_got, send, recv, local,
):
    p = Place()
    w = Wires(send, recv)
    x, y, z, c, zl, zh = p.x, p.y, p.z, p.c, p.zl, p.zh
    sibling = p.at(c=1 - c)
    plane = [p.at(x=1 - x), p.at(y=1 - y)]
    line = [p.at(z=p.z_xor(k)) for k in range(1, 4)]
    started = []

    def push(src, dst, device):
        copy = w.remote(src, dst, device)
        copy.start()
        started.append(copy)
        return copy

    def rows_of(ref, start, size):
        return ref.at[pl.ds(pl.multiple_of(start, 16), size)]

    chip_rows = wide_sum.shape[0] // 8
    half_rows = 4 * chip_rows
    far_half = half_rows * (1 - zh)
    near_half = half_rows * zh

    pieces = (0, 1, 2, 3)
    order = (3, 1, 2, 0)

    def piece(i, zl):
        to_z = 1 - zl if i // 2 else zl
        to_y = 1 - y if i % 2 else y
        return (2 * to_z + to_y) * chip_rows

    crossing = w.used
    w.used += 5

    def cross(i, src, dst):
        return pltpu.make_async_remote_copy(
            src_ref=src,
            dst_ref=dst,
            send_sem=send.at[crossing + i],
            recv_sem=recv.at[crossing + i],
            device_id=line[2],
            device_id_type=MESH,
        )

    def wide_two(i):
        return cross(
            i,
            rows_of(wide_sum, far_half + piece(i, 1 - zl), chip_rows),
            wide_far.at[pl.ds(i * chip_rows, chip_rows)],
        )

    def down_over():
        return cross(4, down_sum, down_far)

    mine = p.slice_z() == z

    def feed_forward(m_all, wide_w, down_w, wide, hidden, parts):
        blocks = (7, 3, 5, 6, 4, 2, 1, 0)
        loads = {r: pltpu.make_async_copy(every.at[r], m_all.at[r], local.at[r]) for r in blocks}
        wide_load = pltpu.make_async_copy(gu, wide_w, local.at[8])
        down_load = pltpu.make_async_copy(dn, down_w, local.at[9])
        wide_load.start()
        loads[7].start()
        down_load.start()
        for r in blocks[1:]:
            loads[r].start()
        greet([sibling] + plane + line + [p.cube(3), p.cube(5)])
        length, width = m_all.shape[1:]
        part = wide.shape[-1]
        wide_tiles = tiles(part, 256)
        down_tiles = tiles(width, 384)

        def forward(r):
            for at in wide_tiles:
                g = jnp.dot(m_all[r], wide_w[0, :, at], preferred_element_type=F32)
                u = jnp.dot(m_all[r], wide_w[1, :, at], preferred_element_type=F32)
                wide[0, r, :, at] = g.astype(BF16)
                wide[1, r, :, at] = u.astype(BF16)
                value, _ = gelu_parts(g)
                hidden[r, :, at] = (value * u).astype(BF16)
            for at in down_tiles:
                parts[r, :, at] = jnp.dot(
                    hidden[r], down_w[:, at], preferred_element_type=F32
                ).astype(BF16)

        def backward(r):
            for at in wide_tiles:
                d_hidden = dot_columns(dd_all[r], down_w[at, :])
                value, slope = gelu_parts(wide[0, r, :, at].astype(F32))
                up = wide[1, r, :, at].astype(F32)
                wide[0, r, :, at] = (d_hidden * up * slope).astype(BF16)
                wide[1, r, :, at] = (d_hidden * value).astype(BF16)
            d_gate = wide[0, r]
            d_up = wide[1, r]
            for at in down_tiles:
                parts[r, :, at] = (
                    dot_columns(d_gate, wide_w[0, at, :]) + dot_columns(d_up, wide_w[1, at, :])
                ).astype(BF16)

        def several(step, places):
            lax.fori_loop(0, 3, lambda i, _: (step(places(i)), 0)[1], 0)

        def middles(i):
            return 7 - lax.shift_right_logical(jnp.int32(4), i)

        def nears(i):
            return lax.shift_right_logical(jnp.int32(4), i)

        total = CubeSum(p, w, parts, third, second, first)
        wide_load.wait()
        loads[7].wait()
        down_load.wait()
        forward(7)
        total.send_far()
        for r in blocks[1:]:
            loads[r].wait()
        several(forward, middles)
        total.send_middle()
        several(forward, nears)
        total.send_near()
        forward(0)

        gather = CubeGather(p, w, dd_own, dd_all)
        gain = gains_full[3]
        g_rows = 0.0
        for h, (at, value) in enumerate(total.finish()):
            scale = norm_scale(value)
            layer_out[at, :] = (h_mid[at, :] + value * scale * gain).astype(BF16)
            d_value, g_part = norm_pull(value, scale, gain, d_out[at, :].astype(F32))
            dd_own[at, :] = d_value.astype(BF16)
            g_rows = g_rows + g_part
            gather.send_near(h)
        gain_acc[0, 3:4, :] = g_rows
        dd_all[0] = dd_own[...]
        total.wait_sent()
        backward(0)
        gather.send_middle(0)
        gather.send_middle(1)
        several(backward, nears)
        gather.send_far(0)
        gather.send_far(1)
        several(backward, middles)
        gather.wait_far()
        backward(7)

        total = LightSum(p, w, parts, third, second, first)
        total.send_far()
        grad_rows = 384
        all_rows = 8 * length
        for at in down_tiles:
            down_w[:, at] = dot_rows(
                hidden[...].reshape(all_rows, part), dd_all[:, :, at].reshape(all_rows, -1)
            ).astype(BF16)
        down_rows = down_sum.shape[0]
        down_one = w.remote(rows_of(down_w, (1 - c) * down_rows, down_rows), down_got, sibling)
        down_one.start()
        total.send_middle()
        down_one.wait_recv()
        down_sum[...] = add(down_w[pl.ds(pl.multiple_of(c * down_rows, 16), down_rows), :], down_got[...])
        pl.when(jnp.logical_not(mine))(down_over().start)

        def grad_wide(matrix, out):
            def step(i, _):
                at = pl.ds(pl.multiple_of(i * grad_rows, 128), grad_rows)
                left = m_all[:, :, at].reshape(all_rows, grad_rows)
                out[at, :] = dot_rows(left, wide[matrix].reshape(all_rows, part)).astype(BF16)
                return 0

            lax.fori_loop(0, width // grad_rows, step, 0)

        other = wide_w.at[1 - c]
        grad_wide(1 - c, other)
        wide_one = w.remote(other, wide_got, sibling)
        wide_one.start()
        grad_wide(c, wide_sum)
        wide_one.wait_recv()
        wide_sum[...] = add(wide_sum[...], wide_got[...])
        total.send_near()
        for i in pieces:
            wide_two(i).start()
        g_rows = 0.0
        for at, value in total.finish():
            mid = h_mid[at, :]
            d_value, g_part = norm_pull(mid, norm_scale(mid), gains_full[2], value)
            d_mid[at, :] = d_out[at, :].astype(F32) + d_value
            g_rows = g_rows + g_part
        gain_acc[0, 2:3, :] = g_rows
        down_one.wait_send()
        wide_one.wait_send()
        total.wait_sent()
        gather.wait_sent()

    def attention(
        proj, o_low, out_w, v_low, probs, k_low, q_low, qk_proj, tables, a_low, qkv_w,
        d_input, wide_swap, d_attn, d_mix, d_qkv, dqkv, dout, qa_s, oa_s, qb_s, ob_s, qc_s, oc_s,
    ):
        loads = [
            pltpu.make_async_copy(src, dst, local.at[i])
            for i, (src, dst) in enumerate(
                zip(
                    (proj_h, o_h, out_h, v_h, probs_h, k_h, q_h, qk_h, tables_h, a_h, qkv_h),
                    (proj, o_low, out_w, v_low, probs, k_low, q_low, qk_proj, tables, a_low, qkv_w),
                )
            )
        ]
        for copy in loads:
            copy.start()
        down_rows = down_end.shape[0]
        split = down_rows // 32 * 16
        lower, upper = pl.ds(0, split), pl.ds(split, down_rows - split)
        down_copy = w.remote(down_end.at[lower], down_end.at[lower], plane[0])
        down_around = w.remote(down_end.at[upper], down_via, p.cube(5))
        down_relay = w.remote(down_via, down_end.at[upper], line[0])

        @pl.when(mine)
        def _():
            down_over().wait_recv()
            down_end[...] = add(down_sum[...], down_far[...])
            down_copy.start()
            down_around.start()

        loads[0].wait()
        value = proj[...]
        d_value, g_apost = norm_pull(value, norm_scale(value), gains_full[1], d_mid[...])
        d_attn[...] = d_value.astype(BF16)
        gain_acc[0, 1:2, :] = g_apost
        loads[1].wait()

        width = tok.shape[1]
        step = width // 3
        for i in range(3):
            at = slice(i * step, (i + 1) * step)
            dout[:, at] = dot_rows(o_low[...], d_attn[:, at]).astype(BF16)
        out_rows = dout.shape[0] // 32

        def out_at(ref, zz, yy, quarter):
            return rows_of(ref, (2 * zz + yy) * 4 * out_rows + quarter * out_rows, out_rows)

        out_one = {
            k: [
                push(
                    out_at(dout, p.z_xor(k), yy, 2 * xx + 1 - c),
                    o1.at[k, xx, yy],
                    sibling,
                )
                for yy in range(2)
                for xx in range(2)
            ]
            for k in order
        }
        loads[2].wait()
        d_mix[...] = dot_columns(d_attn[...], out_w[...]).astype(BF16)

        columns = dqkv.shape[1] // 4
        first, first_out, then, last_step = {}, {}, {}, {}

        def own_out(k, xx, yy):
            start = ((2 * p.z_xor(k) + yy) * 4 + 2 * xx + c) * out_rows
            rows = pl.ds(pl.multiple_of(start, 16), out_rows)
            return dout[rows, :].astype(F32) + o1[k, xx, yy].astype(F32)

        def own_qkv(k, xx, yy):
            start = (2 * p.z_xor(k) + yy) * chip_rows
            rows = pl.ds(pl.multiple_of(start, 16), chip_rows)
            at = pl.ds(pl.multiple_of((2 * xx + c) * columns, 128), columns)
            got = pl.ds(pl.multiple_of(yy * chip_rows, 16), chip_rows)
            return dqkv[rows, at].astype(F32) + q1[k, xx, got, :].astype(F32)

        for k in order:
            for copy in out_one[k]:
                copy.wait_recv()
            first_out[k] = []
            for j in range(2):
                oa_s[k, j] = own_out(k, x if j == 0 else 1 - x, 1 - y).astype(BF16)
                first_out[k].append(push(oa_s.at[k, j], oa.at[k, j], plane[1]))

        for copy in loads[3:9]:
            copy.wait()
        cosine, sine = tables[0], tables[1]
        head = k_low.shape[1]
        heads = q_low.shape[1] // head
        d_k, d_v, g_q = 0.0, 0.0, 0.0
        for i in range(heads):
            at = slice(i * head, (i + 1) * head)
            prob = probs[i]
            d_probs = dot_columns(d_mix[:, at], v_low[...])
            row_dot = jnp.sum(prob * d_probs, axis=1, keepdims=True)
            d_scores = (prob * (d_probs - row_dot)).astype(BF16)
            d_q = SCALE * jnp.dot(d_scores, k_low[...], preferred_element_type=F32)
            d_k = d_k + dot_rows(d_scores, q_low[:, at])
            d_v = d_v + dot_rows(prob.astype(BF16), d_mix[:, at])
            value = qk_proj[:, at]
            d_value, gain = norm_pull(
                value, norm_scale(value), gains_full[4, :, :head], turn_back(d_q, cosine, sine)
            )
            g_q = g_q + gain
            d_qkv[:, at] = d_value.astype(BF16)
        at = slice(heads * head, (heads + 1) * head)
        value = qk_proj[:, at]
        d_value, g_k = norm_pull(
            value, norm_scale(value), gains_full[5, :, :head], turn_back(SCALE * d_k, cosine, sine)
        )
        d_qkv[:, at] = d_value.astype(BF16)
        d_qkv[:, (heads + 1) * head :] = d_v.astype(BF16)
        gain_acc[0, 4:5, :] = jnp.zeros((1, width), F32)
        gain_acc[0, 5:8, :] = jnp.zeros((3, width), F32)
        gain_acc[0, 4:5, :head] = g_q
        gain_acc[0, 5:6, :head] = g_k
        loads[9].wait()
        for i in range(heads + 2):
            at = slice(i * head, (i + 1) * head)
            dqkv[:, at] = dot_rows(a_low[...], d_qkv[:, at]).astype(BF16)

        qkv_one = {}
        for k in order:
            rows = pl.ds(pl.multiple_of(2 * p.z_xor(k) * chip_rows, 16), 2 * chip_rows)
            qkv_one[k] = [
                push(
                    dqkv.at[
                        rows, pl.ds(pl.multiple_of((2 * xx + 1 - c) * columns, 128), columns)
                    ],
                    q1.at[k, xx],
                    sibling,
                )
                for xx in range(2)
            ]

        def plane_first(k):
            for copy in qkv_one[k]:
                copy.wait_recv()
            first[k] = []
            for j in range(2):
                qa_s[k, j] = own_qkv(k, x if j == 0 else 1 - x, 1 - y).astype(BF16)
                first[k].append(push(qa_s.at[k, j], qa.at[k, j], plane[1]))

        def plane_then(k):
            for copy in first_out[k] + first[k]:
                copy.wait_recv()
            q, o = own_qkv(k, 1 - x, y), own_out(k, 1 - x, y)
            qb_s[k] = (q + qa[k, 1].astype(F32)).astype(BF16)
            ob_s[k] = (o + oa[k, 1].astype(F32)).astype(BF16)
            then[k] = [
                push(qb_s.at[k], qb.at[k], plane[0]),
                push(ob_s.at[k], ob.at[k], plane[0]),
            ]

        def plane_last(k):
            for copy in then[k]:
                copy.wait_recv()
            q, o = own_qkv(k, x, y), own_out(k, x, y)
            q = q + qa[k, 0].astype(F32) + qb[k].astype(F32)
            o = o + oa[k, 0].astype(F32) + ob[k].astype(F32)
            if k == 0:
                return q, o
            qc_s[k] = q.astype(BF16)
            oc_s[k] = o.astype(BF16)
            last_step[k] = [
                push(qc_s.at[k], qc.at[k], line[k - 1]),
                push(oc_s.at[k], oc.at[k], line[k - 1]),
            ]

        for k in order:
            plane_first(k)

        wide_three, wide_four, own_wide = {}, [], []

        def part_of(i):
            return 2 * p.slice_z(2 * zh + (1 - zl if i // 2 else zl)) + (1 - y if i % 2 else y)

        def wide_on(i):
            at = pl.ds(i * chip_rows, chip_rows)
            rows = pl.ds(pl.multiple_of(near_half + piece(i, zl), 16), chip_rows)
            wide_two(i).wait_recv()
            wide_far[at, :] = add(wide_sum[rows, :], wide_far[at, :])
            dst = wide_end.at[part_of(0)]
            if i:
                wide_three[i] = push(wide_far.at[at], dst, p.cube(2 * (i % 2) + i // 2))
            else:
                own_wide.append(pltpu.make_async_copy(wide_far.at[at], dst, local.at[11]))
                own_wide[0].start()
                wide_four.append(push(wide_far.at[at], dst, plane[0]))

        def wide_over(i):
            wide_three[i].wait_recv()
            dst = wide_end.at[part_of(i)]
            wide_four.append(push(dst, dst, plane[0]))

        @pl.when(mine)
        def _():
            down_around.wait_recv()
            down_relay.start()

        wide_on(0)

        loads[10].wait()
        tok_f = tok[...].astype(F32)
        for i in range(3):
            at = slice(i * step, (i + 1) * step)
            d_input[:, at] = dot_columns(d_qkv[...], qkv_w[at, :])
        d_value, g_apre = norm_pull(tok_f, norm_scale(tok_f), gains_full[0], d_input[...])
        grad_x[...] = (d_mid[...] + d_value).astype(BF16)
        gain_acc[0, 0:1, :] = g_apre
        gain_one = push(gain_acc.at[0], gain_got.at[0], sibling)

        for k in order[:2]:
            plane_then(k)
        gain_one.wait_recv()
        gain_acc[1] = gain_acc[0] + gain_got[0]
        gain_two = push(gain_acc.at[1], gain_got.at[1], plane[0])
        wide_on(1)
        for k in order[2:]:
            plane_then(k)
        for k in order[:3]:
            plane_last(k)
        wide_on(2)
        wide_over(1)
        gain_two.wait_recv()
        gain_acc[2] = gain_acc[1] + gain_got[1]
        gain_three = push(gain_acc.at[2], gain_got.at[2], plane[1])
        q, o = plane_last(0)
        for k in order[:3]:
            for copy in last_step[k]:
                copy.wait_recv()
        qe[0] = (q + qc[1].astype(F32) + qc[2].astype(F32) + qc[3].astype(F32)).astype(BF16)
        oe[0] = (o + oc[1].astype(F32) + oc[2].astype(F32) + oc[3].astype(F32)).astype(BF16)
        last = [
            push(qe.at[0], qe.at[4 + i], device)
            for i, device in enumerate((sibling, plane[0]))
        ] + [
            push(oe.at[0], oe.at[4 + i], device)
            for i, device in enumerate((sibling, plane[0]))
        ]
        wide_on(3)
        wide_over(2)
        gain_three.wait_recv()
        gain_acc[3] = gain_acc[2] + gain_got[2]
        gain_four = [push(gain_acc.at[3], gain_got.at[2 + k], line[k - 1]) for k in range(1, 4)]
        for copy in last:
            copy.wait_recv()
        relay = [push(qe.at[5], qe.at[6], sibling), push(oe.at[5], oe.at[6], sibling)]

        wide_over(3)
        for copy in relay:
            copy.wait_recv()
        rows = chip_rows // 2
        for copy in gain_four:
            copy.wait_recv()
        gains_sum[...] = gain_acc[3] + gain_got[3] + gain_got[4] + gain_got[5]

        own_wide[0].wait()
        for copy in wide_four:
            copy.wait_recv()
        for cc in range(2):

            @pl.when(c == cc)
            def _():
                for s in range(8):
                    extra = (rows + 15) // 16 * 16
                    at = slice(0, extra) if cc == 1 else slice(2 * rows - extra, 2 * rows)
                    wide_swap[s] = wide_end[s, at, :]

        final = push(wide_swap, wide_back, sibling)

        @pl.when(jnp.logical_not(mine))
        def _():
            down_copy.wait_recv()
            down_relay.wait_recv()

        final.wait_recv()

        @pl.when(mine)
        def _():
            for copy in (down_copy, down_around, down_relay):
                copy.wait_send()

        pl.when(jnp.logical_not(mine))(down_over().wait_send)
        for i in pieces:
            wide_two(i).wait_send()
        for copy in started:
            copy.wait_send()


    length, width = tok.shape
    blocks = (8, length, width)
    part = wide_sum.shape[1]
    pl.run_scoped(
        feed_forward,
        pltpu.VMEM(blocks, BF16),
        pltpu.VMEM(gu.shape, BF16),
        pltpu.VMEM(dn.shape, BF16),
        pltpu.VMEM((2, 8, length, part), BF16),
        pltpu.VMEM((8, length, part), BF16),
        pltpu.VMEM(blocks, BF16),
    )
    total = qkv_h.shape[1]
    mix = o_h.shape[1]
    q_piece, o_piece = qa.shape[2:], oa.shape[2:]
    saved = (proj_h, o_h, out_h, v_h, probs_h, k_h, q_h, qk_h, tables_h, a_h, qkv_h)
    pl.run_scoped(
        attention,
        *[pltpu.VMEM(ref.shape, ref.dtype) for ref in saved],
        pltpu.VMEM((length, width), F32),
        pltpu.VMEM(wide_back.shape, BF16),
        pltpu.VMEM((length, width), BF16),
        pltpu.VMEM((length, mix), BF16),
        pltpu.VMEM((length, total), BF16),
        pltpu.VMEM((width, total), BF16),
        pltpu.VMEM((mix, width), BF16),
        pltpu.VMEM((4, 2) + q_piece, BF16),
        pltpu.VMEM((4, 2) + o_piece, BF16),
        pltpu.VMEM((4,) + q_piece, BF16),
        pltpu.VMEM((4,) + o_piece, BF16),
        pltpu.VMEM((4,) + q_piece, BF16),
        pltpu.VMEM((4,) + o_piece, BF16),
    )


def tail(tok, d_out, h_mid, gains_full, every, gu, dn, saved):
    length, width = tok.shape
    part = dn.shape[0]
    proj, o_low, out_w, *_, qkv_w = saved
    columns = qkv_w.shape[1] // 4
    mix = out_w.shape[0]
    chip_rows = width // 8
    rows = chip_rows // 2
    extra = (rows + 15) // 16 * 16
    piece = mix // 32
    blocks = (8, length, width)
    struct = jax.ShapeDtypeStruct
    shapes = (
        struct((length, width), BF16),
        struct((length, width), BF16),
        struct((7, chip_rows, columns), BF16),
        struct((7, piece, width), BF16),
        struct((8, width), F32),
        struct((8, chip_rows, part), BF16),
        struct((8, extra, part), BF16),
        struct((part // 2, width), BF16),
    )
    scratch = [
        pltpu.VMEM((length, width), BF16),
        pltpu.VMEM(blocks, BF16),
        pltpu.VMEM((length, width), BF16),
        pltpu.VMEM((3, length, width), BF16),
        pltpu.VMEM((3, length, width), BF16),
        pltpu.VMEM((width, part), BF16),
        pltpu.VMEM((width, part), BF16),
        pltpu.VMEM((width // 2, part), BF16),
        pltpu.VMEM((part // 2, width), BF16),
        pltpu.VMEM((part // 2, width), BF16),
        pltpu.VMEM((part // 2, width), BF16),
        pltpu.VMEM((part // 2 - part // 64 * 16, width), BF16),
        pltpu.VMEM((length, width), F32),
        pltpu.VMEM((4, 2, 2 * chip_rows, columns), BF16),
        pltpu.VMEM((4, 2, 2, piece, width), BF16),
        pltpu.VMEM((4, 2, chip_rows, columns), BF16),
        pltpu.VMEM((4, 2, piece, width), BF16),
        pltpu.VMEM((4, chip_rows, columns), BF16),
        pltpu.VMEM((4, piece, width), BF16),
        pltpu.VMEM((4, chip_rows, columns), BF16),
        pltpu.VMEM((4, piece, width), BF16),
        pltpu.VMEM((4, 8, width), F32),
        pltpu.VMEM((6, 8, width), F32),
    ]
    return pl.pallas_call(
        tail_kernel,
        out_shape=shapes,
        in_specs=[vmem()] * 4 + [hbm()] * 14,
        out_specs=(vmem(),) * 8,
        scratch_shapes=scratch + sems(160) + [pltpu.SemaphoreType.DMA((12,))],
        compiler_params=params(1),
        name="tail",
    )(tok, d_out, h_mid, gains_full, every, gu, dn, *saved)


def place_kernel(
    qe, oe, gains, wide_end, wide_back, down_end,
    w_q, w_k, w_v, w_o, w_gate, w_up, w_down, a_pre, a_post, m_pre, m_post, q_gain, k_gain,
):
    p = Place()
    rows, mix = w_q.shape
    head = w_k.shape[1]
    columns = qe.shape[2]
    piece = oe.shape[1]
    size = wide_end.shape[2]
    extra = wide_back.shape[1]

    def put_columns(start, value):
        for ref, first, width in ((w_q, 0, mix), (w_k, mix, head), (w_v, mix + head, head)):
            low, high = max(start, first), min(start + columns, first + width)
            if low < high:
                ref[:, low - first : high - first] = value[:, low - start : high - start]

    for xx in range(2):
        for cc in range(2):

            @pl.when((p.x == xx) & (p.c == cc))
            def _():
                for i, q in (
                    (0, 2 * xx + cc),
                    (4, 2 * xx + 1 - cc),
                    (5, 2 * (1 - xx) + cc),
                    (6, 2 * (1 - xx) + 1 - cc),
                ):
                    both = qe[i].astype(F32)
                    put_columns(q * columns, both[cc * rows : (cc + 1) * rows])
                    if q // 2 == cc:
                        w_o[(q % 2) * piece : (q % 2 + 1) * piece, :] = oe[i].astype(F32)

    for cc in range(2):

        @pl.when(p.c == cc)
        def _():
            own_ref, other_ref = (w_gate, w_up) if cc == 0 else (w_up, w_gate)
            for s in range(8):
                at = slice(s * size, (s + 1) * size)
                own_ref[:, at] = wide_end[s].astype(F32)[cc * rows : (cc + 1) * rows]
                other = wide_back[s].astype(F32)
                other_ref[:, at] = other[:rows] if cc == 0 else other[extra - rows :]

    w_down[...] = down_end[...].astype(F32)
    sums = gains[...]
    for i, ref in enumerate((a_pre, a_post, m_pre, m_post, q_gain, k_gain)):
        per = ref.shape[0]
        full = 16 * per
        turned = pltpu.roll(sums[:, :full], lax.rem(full - p.shard * per, full), 1)
        ref[...] = turned[i, :per]


def place(summed, shapes):
    return pl.pallas_call(
        place_kernel,
        out_shape=tuple(jax.ShapeDtypeStruct(shape, F32) for shape in shapes),
        in_specs=[vmem()] * 6,
        out_specs=(vmem(),) * 13,
        compiler_params=pltpu.CompilerParams(vmem_limit_bytes=VMEM_BYTES),
        name="place",
    )(*summed)


def cube_body(
    layer_in, d_out, segments, w_q, w_k, w_v, w_o, attn_pre, attn_post, q_gain, k_gain,
    w_gate, w_up, w_down, mlp_pre, mlp_post,
):
    width = layer_in.shape[1]
    head = q_gain.shape[0] * 16
    rows, mix = w_q.shape
    gain_list = [attn_pre, attn_post, mlp_pre, mlp_post, q_gain, k_gain]
    (
        qkv_w, out_w, gu_w, down_w, m_all, gains_full, a_low, qk_proj, q_low, k_low, v_low,
        probs, o_low, attn_proj, h_mid, tables,
    ) = front(
        layer_in, segments, w_q, w_k, w_v, w_o, gain_list, w_gate, w_up, w_down, head
    )
    saved = (
        attn_proj, o_low, out_w, v_low, probs, k_low, q_low, qk_proj, tables, a_low, qkv_w,
    )
    layer_out, grad_x, *summed = tail(
        layer_in, d_out, h_mid, gains_full, m_all, gu_w, down_w, saved
    )
    matrices = [w_q, w_k, w_v, w_o, w_gate, w_up, w_down]
    grads = place(summed, [v.shape for v in matrices + gain_list])
    g_apre, g_apost, g_mpre, g_mpost, g_q, g_k = grads[7:]
    return (
        layer_out,
        grad_x,
        *grads[:4],
        g_apre,
        g_apost,
        g_q,
        g_k,
        *grads[4:7],
        g_mpre,
        g_mpost,
    )


def solution(mesh):
    in_specs = (
        P(("replica", "fsdp"), None),
        P(("replica", "fsdp"), None),
        P(("replica", "fsdp"), None),
        P("fsdp", None),
        P("fsdp", None),
        P("fsdp", None),
        P("fsdp", None),
        P("fsdp"),
        P("fsdp"),
        P("fsdp"),
        P("fsdp"),
        P("fsdp", None),
        P("fsdp", None),
        P("fsdp", None),
        P("fsdp"),
        P("fsdp"),
    )
    out_specs = (
        P(("replica", "fsdp"), None),
        P(("replica", "fsdp"), None),
        P("fsdp", None),
        P("fsdp", None),
        P("fsdp", None),
        P("fsdp", None),
        P("fsdp"),
        P("fsdp"),
        P("fsdp"),
        P("fsdp"),
        P("fsdp", None),
        P("fsdp", None),
        P("fsdp", None),
        P("fsdp"),
        P("fsdp"),
    )
    body = cube_body if fits_cubes(mesh) else general_body
    return jax.shard_map(body, mesh=mesh, in_specs=in_specs, out_specs=out_specs, check_vma=False)
```

```python
from functools import partial
import math

import jax
import jax.numpy as jnp
from jax import lax
from jax.experimental import pallas as pl
from jax.experimental.pallas import tpu as pltpu
from jax.sharding import PartitionSpec as P

EPS = 1e-06
THETA = 1000000.0
SCALE = 0.0625
MASKED = -1e30


def norm_rows(values, gain):
    return values * lax.rsqrt(jnp.mean(values * values, axis=-1, keepdims=True) + EPS) * gain


def positions_of(segments):
    length = segments.shape[-1]
    index = jnp.arange(length, dtype=jnp.int32)
    earlier = jnp.concatenate([segments[:, :1] - 1, segments[:, :-1]], axis=1)
    starts = jnp.where(segments != earlier, index[None, :], jnp.zeros_like(segments))
    return index[None, :] - lax.cummax(starts, axis=1)


def angle_tables(segments, head_size):
    half_size = head_size // 2
    rates = jnp.exp(jnp.arange(half_size, dtype=jnp.float32) * (-2.0 * math.log(THETA) / head_size))
    angles = positions_of(segments).astype(jnp.float32)[..., None] * rates
    return (jnp.cos(angles), jnp.sin(angles))


def rotate(values, cosine, sine):
    half_size = values.shape[-1] // 2
    first_half = values[..., :half_size]
    second_half = values[..., half_size:]
    return jnp.concatenate(
        [first_half * cosine - second_half * sine, second_half * cosine + first_half * sine],
        axis=-1,
    )


def query_path(projected, gain, cosine, sine):
    shaped = projected.reshape(projected.shape[0], projected.shape[1], -1, gain.shape[0])
    return rotate(norm_rows(shaped, gain), cosine[:, :, None, :], sine[:, :, None, :])


def key_path(projected, gain, cosine, sine):
    return rotate(norm_rows(projected, gain), cosine, sine)


def gelu_product(gate_val, up_val):
    return jax.nn.gelu(gate_val, approximate=True) * up_val


def to_low(values):
    return values.astype(jnp.bfloat16)


def matmul(left, right):
    return jnp.dot(left, right, preferred_element_type=jnp.float32)


def matmul_left_t(left, right):
    return lax.dot_general(
        left, right, (((0,), (0,)), ((), ())), preferred_element_type=jnp.float32
    )


def matmul_right_t(left, right):
    return lax.dot_general(
        left, right, (((1,), (1,)), ((), ())), preferred_element_type=jnp.float32
    )


def attention_masks(segments):
    length = segments.shape[1]
    index = jnp.arange(length, dtype=jnp.int32)
    causal = index[None, :] <= index[:, None]
    return (segments[:, :, None] == segments[:, None, :]) & causal[None]


def scores_of(q_low, k_low, masks):
    scores = SCALE * jnp.einsum("nqhd,nkd->nhqk", q_low, k_low, preferred_element_type=jnp.float32)
    return jnp.where(masks[:, None], scores, MASKED)


def spread_gain(values):
    return jnp.broadcast_to(values[:, None], (values.shape[0], lax.axis_size("replica")))


def general_body(
    layer_in,
    d_out,
    segments,
    w_q,
    w_k,
    w_v,
    w_o,
    attn_pre,
    attn_post,
    q_gain,
    k_gain,
    w_gate,
    w_up,
    w_down,
    mlp_pre,
    mlp_post,
):
    attn_set = (
        lax.all_gather(to_low(w_q), "fsdp", axis=0, tiled=True),
        lax.all_gather(to_low(w_k), "fsdp", axis=0, tiled=True),
        lax.all_gather(to_low(w_v), "fsdp", axis=0, tiled=True),
        lax.all_gather(to_low(w_o), "fsdp", axis=0, tiled=True),
        lax.all_gather(to_low(attn_pre), "fsdp", axis=0, tiled=True),
        lax.all_gather(to_low(attn_post), "fsdp", axis=0, tiled=True),
        lax.all_gather(to_low(q_gain), "fsdp", axis=0, tiled=True),
        lax.all_gather(to_low(k_gain), "fsdp", axis=0, tiled=True),
    )
    q_full, k_full, v_full, o_full = (attn_set[0], attn_set[1], attn_set[2], attn_set[3])
    gain_apre = attn_set[4].astype(jnp.float32)
    gain_apost = attn_set[5].astype(jnp.float32)
    gain_q = attn_set[6].astype(jnp.float32)
    gain_k = attn_set[7].astype(jnp.float32)
    mlp_set = (
        lax.all_gather(to_low(w_gate), "fsdp", axis=0, tiled=True),
        lax.all_gather(to_low(w_up), "fsdp", axis=0, tiled=True),
        lax.all_gather(to_low(w_down), "fsdp", axis=0, tiled=True),
        lax.all_gather(to_low(mlp_pre), "fsdp", axis=0, tiled=True),
        lax.all_gather(to_low(mlp_post), "fsdp", axis=0, tiled=True),
    )
    gate_full, up_full, down_full = (mlp_set[0], mlp_set[1], mlp_set[2])
    gain_mpre = mlp_set[3].astype(jnp.float32)
    gain_mpost = mlp_set[4].astype(jnp.float32)
    seq_count, seq_len = segments.shape
    tok_flat = layer_in.astype(jnp.float32)
    cosine, sine = angle_tables(segments, gain_q.shape[0])
    masks = attention_masks(segments)
    normed_a, pull_a = jax.vjp(norm_rows, tok_flat, gain_apre)
    a_low = to_low(normed_a)
    q_proj = matmul(a_low, q_full).reshape(seq_count, seq_len, -1)
    k_proj = matmul(a_low, k_full).reshape(seq_count, seq_len, -1)
    v_proj = matmul(a_low, v_full)
    q_rot, pull_q = jax.vjp(partial(query_path, cosine=cosine, sine=sine), q_proj, gain_q)
    k_rot, pull_k = jax.vjp(partial(key_path, cosine=cosine, sine=sine), k_proj, gain_k)
    q_low = to_low(q_rot)
    k_low = to_low(k_rot)
    v_low = to_low(v_proj).reshape(seq_count, seq_len, -1)
    scores = scores_of(q_low, k_low, masks)
    top_val = jnp.max(scores, axis=-1, keepdims=True)
    log_total = top_val + jnp.log(jnp.sum(jnp.exp(scores - top_val), axis=-1, keepdims=True))
    p_low = to_low(jnp.exp(scores - log_total))
    attn_mix = jnp.einsum("nhqk,nkd->nqhd", p_low, v_low, preferred_element_type=jnp.float32)
    o_low = to_low(attn_mix.reshape(seq_count * seq_len, -1))
    attn_proj = matmul(o_low, o_full)
    post_attn, pull_pa = jax.vjp(norm_rows, attn_proj, gain_apost)
    h_mid = tok_flat + post_attn
    normed_m, pull_m = jax.vjp(norm_rows, h_mid, gain_mpre)
    m_low = to_low(normed_m)
    gate_val = matmul(m_low, gate_full)
    up_val = matmul(m_low, up_full)
    hidden, pull_h = jax.vjp(gelu_product, gate_val, up_val)
    h_low = to_low(hidden)
    down_val = matmul(h_low, down_full)
    post_mlp, pull_pm = jax.vjp(norm_rows, down_val, gain_mpost)
    layer_out = (h_mid + post_mlp).astype(jnp.bfloat16)
    gate_full, up_full, down_full = (
        lax.all_gather(to_low(w_gate), "fsdp", axis=0, tiled=True),
        lax.all_gather(to_low(w_up), "fsdp", axis=0, tiled=True),
        lax.all_gather(to_low(w_down), "fsdp", axis=0, tiled=True),
    )
    grad_top = d_out.astype(jnp.float32)
    d_down, grad_mpost = pull_pm(grad_top)
    d_down_low = to_low(d_down)
    grad_wdown = matmul_left_t(h_low, d_down_low)
    d_hidden = matmul_right_t(d_down_low, down_full)
    d_gate, d_up = pull_h(d_hidden)
    d_gate_low = to_low(d_gate)
    d_up_low = to_low(d_up)
    grad_wgate = matmul_left_t(m_low, d_gate_low)
    grad_wup = matmul_left_t(m_low, d_up_low)
    d_normed = matmul_right_t(d_gate_low, gate_full) + matmul_right_t(d_up_low, up_full)
    d_mid_norm, grad_mpre = pull_m(d_normed)
    d_mid = grad_top + d_mid_norm
    q_full, k_full, v_full, o_full = (
        lax.all_gather(to_low(w_q), "fsdp", axis=0, tiled=True),
        lax.all_gather(to_low(w_k), "fsdp", axis=0, tiled=True),
        lax.all_gather(to_low(w_v), "fsdp", axis=0, tiled=True),
        lax.all_gather(to_low(w_o), "fsdp", axis=0, tiled=True),
    )
    d_attn, grad_apost = pull_pa(d_mid)
    d_attn_low = to_low(d_attn)
    grad_wo = matmul_left_t(o_low, d_attn_low)
    d_mix_low = to_low(matmul_right_t(d_attn_low, o_full)).reshape(
        seq_count, seq_len, -1, k_low.shape[-1]
    )
    probs = jnp.exp(scores_of(q_low, k_low, masks) - log_total)
    d_probs = jnp.einsum("nqhd,nkd->nhqk", d_mix_low, v_low, preferred_element_type=jnp.float32)
    row_dot = jnp.sum(probs * d_probs, axis=-1, keepdims=True)
    d_scores_low = to_low(probs * (d_probs - row_dot))
    d_query = SCALE * jnp.einsum(
        "nhqk,nkd->nqhd", d_scores_low, k_low, preferred_element_type=jnp.float32
    )
    d_key = SCALE * jnp.einsum(
        "nhqk,nqhd->nkd", d_scores_low, q_low, preferred_element_type=jnp.float32
    )
    d_value = jnp.einsum("nhqk,nqhd->nkd", p_low, d_mix_low, preferred_element_type=jnp.float32)
    d_qproj, grad_qgain = pull_q(d_query)
    d_kproj, grad_kgain = pull_k(d_key)
    d_q_low = to_low(d_qproj.reshape(seq_count * seq_len, -1))
    d_k_low = to_low(d_kproj.reshape(seq_count * seq_len, -1))
    d_v_low = to_low(d_value.reshape(seq_count * seq_len, -1))
    grad_wq = matmul_left_t(a_low, d_q_low)
    grad_wk = matmul_left_t(a_low, d_k_low)
    grad_wv = matmul_left_t(a_low, d_v_low)
    d_normed_a = (
        matmul_right_t(d_q_low, q_full)
        + matmul_right_t(d_k_low, k_full)
        + matmul_right_t(d_v_low, v_full)
    )
    d_input_norm, grad_apre = pull_a(d_normed_a)
    grad_x = (d_mid + d_input_norm).astype(jnp.bfloat16)
    all_shards = (
        lax.psum_scatter(grad_wq, "fsdp", scatter_dimension=0, tiled=True),
        lax.psum_scatter(grad_wk, "fsdp", scatter_dimension=0, tiled=True),
        lax.psum_scatter(grad_wv, "fsdp", scatter_dimension=0, tiled=True),
        lax.psum_scatter(grad_wo, "fsdp", scatter_dimension=0, tiled=True),
        lax.psum_scatter(grad_apre, "fsdp", scatter_dimension=0, tiled=True),
        lax.psum_scatter(grad_apost, "fsdp", scatter_dimension=0, tiled=True),
        lax.psum_scatter(grad_qgain, "fsdp", scatter_dimension=0, tiled=True),
        lax.psum_scatter(grad_kgain, "fsdp", scatter_dimension=0, tiled=True),
        lax.psum_scatter(grad_wgate, "fsdp", scatter_dimension=0, tiled=True),
        lax.psum_scatter(grad_wup, "fsdp", scatter_dimension=0, tiled=True),
        lax.psum_scatter(grad_wdown, "fsdp", scatter_dimension=0, tiled=True),
        lax.psum_scatter(grad_mpre, "fsdp", scatter_dimension=0, tiled=True),
        lax.psum_scatter(grad_mpost, "fsdp", scatter_dimension=0, tiled=True),
    )
    all_cols = (
        lax.psum_scatter(
            all_shards[0].astype(jnp.bfloat16), "replica", scatter_dimension=1, tiled=True
        ).astype(jnp.float32),
        lax.psum_scatter(
            all_shards[1].astype(jnp.bfloat16), "replica", scatter_dimension=1, tiled=True
        ).astype(jnp.float32),
        lax.psum_scatter(
            all_shards[2].astype(jnp.bfloat16), "replica", scatter_dimension=1, tiled=True
        ).astype(jnp.float32),
        lax.psum_scatter(
            all_shards[3].astype(jnp.bfloat16), "replica", scatter_dimension=1, tiled=True
        ).astype(jnp.float32),
        lax.psum_scatter(
            all_shards[8].astype(jnp.bfloat16), "replica", scatter_dimension=1, tiled=True
        ).astype(jnp.float32),
        lax.psum_scatter(
            all_shards[9].astype(jnp.bfloat16), "replica", scatter_dimension=1, tiled=True
        ).astype(jnp.float32),
        lax.psum_scatter(
            all_shards[10].astype(jnp.bfloat16), "replica", scatter_dimension=1, tiled=True
        ).astype(jnp.float32),
        lax.psum_scatter(
            spread_gain(all_shards[4]).astype(jnp.bfloat16),
            "replica",
            scatter_dimension=1,
            tiled=True,
        ).astype(jnp.float32),
        lax.psum_scatter(
            spread_gain(all_shards[5]).astype(jnp.bfloat16),
            "replica",
            scatter_dimension=1,
            tiled=True,
        ).astype(jnp.float32),
        lax.psum_scatter(
            spread_gain(all_shards[6]).astype(jnp.bfloat16),
            "replica",
            scatter_dimension=1,
            tiled=True,
        ).astype(jnp.float32),
        lax.psum_scatter(
            spread_gain(all_shards[7]).astype(jnp.bfloat16),
            "replica",
            scatter_dimension=1,
            tiled=True,
        ).astype(jnp.float32),
        lax.psum_scatter(
            spread_gain(all_shards[11]).astype(jnp.bfloat16),
            "replica",
            scatter_dimension=1,
            tiled=True,
        ).astype(jnp.float32),
        lax.psum_scatter(
            spread_gain(all_shards[12]).astype(jnp.bfloat16),
            "replica",
            scatter_dimension=1,
            tiled=True,
        ).astype(jnp.float32),
    )
    all_mats = (
        lax.all_gather(all_cols[0].astype(jnp.bfloat16), "replica", axis=1, tiled=True).astype(
            jnp.float32
        ),
        lax.all_gather(all_cols[1].astype(jnp.bfloat16), "replica", axis=1, tiled=True).astype(
            jnp.float32
        ),
        lax.all_gather(all_cols[2].astype(jnp.bfloat16), "replica", axis=1, tiled=True).astype(
            jnp.float32
        ),
        lax.all_gather(all_cols[3].astype(jnp.bfloat16), "replica", axis=1, tiled=True).astype(
            jnp.float32
        ),
        lax.all_gather(all_cols[4].astype(jnp.bfloat16), "replica", axis=1, tiled=True).astype(
            jnp.float32
        ),
        lax.all_gather(all_cols[5].astype(jnp.bfloat16), "replica", axis=1, tiled=True).astype(
            jnp.float32
        ),
        lax.all_gather(all_cols[6].astype(jnp.bfloat16), "replica", axis=1, tiled=True).astype(
            jnp.float32
        ),
    )
    attn_sums = (
        all_mats[0],
        all_mats[1],
        all_mats[2],
        all_mats[3],
        all_cols[7][:, 0],
        all_cols[8][:, 0],
        all_cols[9][:, 0],
        all_cols[10][:, 0],
    )
    mlp_sums = (all_mats[4], all_mats[5], all_mats[6], all_cols[11][:, 0], all_cols[12][:, 0])
    return (
        layer_out,
        grad_x,
        attn_sums[0],
        attn_sums[1],
        attn_sums[2],
        attn_sums[3],
        attn_sums[4],
        attn_sums[5],
        attn_sums[6],
        attn_sums[7],
        mlp_sums[0],
        mlp_sums[1],
        mlp_sums[2],
        mlp_sums[3],
        mlp_sums[4],
    )


MESH = pl.DeviceIdType.MESH
VMEM_BYTES = 63 * 2**20
F32 = jnp.float32
BF16 = jnp.bfloat16


def fits_cubes(mesh):
    return dict(mesh.shape) == {"replica": 2, "fsdp": 16}


class Place:
    def __init__(self):
        shard = lax.axis_index("fsdp")
        self.x = lax.axis_index("replica")
        self.shard = shard
        self.c = lax.rem(shard, 2)
        self.y = lax.rem(lax.div(shard, 2), 2)
        self.z = lax.div(shard, 4)
        self.zl = lax.rem(self.z, 2)
        self.zh = lax.div(self.z, 2)

    def at(self, x=None, y=None, z=None, c=None):
        x = self.x if x is None else x
        y = self.y if y is None else y
        z = self.z if z is None else z
        c = self.c if c is None else c
        return (x, (z * 2 + y) * 2 + c)

    def z_xor(self, k):
        low = self.zl if k % 2 == 0 else 1 - self.zl
        high = self.zh if k // 2 == 0 else 1 - self.zh
        return 2 * high + low

    def slice_z(self, z=None):
        z = self.z if z is None else z
        inner = lax.rem(lax.rem(z, 2) + lax.div(z, 2), 2)
        return jnp.where(self.x == 0, 2 * inner, 3 - 2 * inner)

    def cube(self, bits):
        return self.at(
            x=1 - self.x if bits & 4 else self.x,
            y=1 - self.y if bits & 2 else self.y,
            z=self.z_xor(1) if bits & 1 else self.z,
        )


class Wires:
    def __init__(self, send, recv):
        self.send, self.recv, self.used = send, recv, 0

    def remote(self, src, dst, device):
        i = self.used
        self.used += 1
        return pltpu.make_async_remote_copy(
            src_ref=src,
            dst_ref=dst,
            send_sem=self.send.at[i],
            recv_sem=self.recv.at[i],
            device_id=device,
            device_id_type=MESH,
        )

    def local(self, src, dst):
        i = self.used
        self.used += 1
        return pltpu.make_async_copy(src, dst, self.send.at[i])


def greet(devices):
    barrier = pltpu.get_barrier_semaphore()
    for device in devices:
        pl.semaphore_signal(barrier, inc=1, device_id=device, device_id_type=MESH)
    pl.semaphore_wait(barrier, len(devices))


def hbm():
    return pl.BlockSpec(memory_space=pl.ANY)


def vmem():
    return pl.BlockSpec(memory_space=pltpu.VMEM)


def sems(count):
    return [pltpu.SemaphoreType.DMA((count,)), pltpu.SemaphoreType.DMA((count,))]


def params(collective_id):
    return pltpu.CompilerParams(
        collective_id=collective_id, has_side_effects=True, vmem_limit_bytes=VMEM_BYTES
    )


X, Y, Z = 4, 2, 1


def thirds(rows):
    first = -(-rows // 48) * 16
    return ((0, first), (first, first), (2 * first, rows - 2 * first))


def add(left, right):
    return (left.astype(F32) + right.astype(F32)).astype(BF16)


class CubeSum:
    MIDDLE = ((X, Y, Y | Z), (Y, Z, X | Z), (Z, X, X | Y))
    NEAR = ((Y, Z), (Z, X), (X, Y))

    def __init__(self, p, w, parts, third, second, first):
        self.p, self.w, self.parts = p, w, parts
        self.third, self.second, self.first = third, second, first
        self.half = parts.shape[1] // 2
        self.started = []
        self.far, self.mid, self.end = {}, {}, {}

    def push(self, src, dst, bit):
        copy = self.w.remote(src, dst, self.p.cube(bit))
        copy.start()
        self.started.append(copy)
        return copy

    def send_far(self):
        for h in range(2):
            for (start, size), link in zip(thirds(self.half), (X, Y, Z)):
                at = pl.ds(h * self.half + start, size)
                self.far[link, h] = self.push(self.parts.at[7, at], self.third.at[at], link)

    def send_middle(self):
        for h in range(2):
            for i, (link, onward, place) in enumerate(self.MIDDLE):
                start, size = thirds(self.half)[i]
                at = pl.ds(h * self.half + start, size)
                all_at = pl.ds(h * self.half, self.half)
                self.far[link, h].wait_recv()
                self.parts[place, at] = add(self.parts[place, at], self.third[at, :])
                self.mid[onward, h] = self.push(
                    self.parts.at[place, all_at], self.second.at[i, all_at], onward
                )

    def send_near(self):
        for h in range(2):
            at = pl.ds(h * self.half, self.half)
            for i, (came, place) in enumerate(self.NEAR):
                self.mid[came, h].wait_recv()
                self.parts[place, at] = add(self.parts[place, at], self.second[i, at])
                self.end[place, h] = self.push(
                    self.parts.at[place, at], self.first.at[i, at], place
                )

    def finish(self):
        for h in range(2):
            at = pl.ds(h * self.half, self.half)
            value = self.parts[0, at].astype(F32)
            for i, (_, place) in enumerate(self.NEAR):
                self.end[place, h].wait_recv()
                value = value + self.first[i, at].astype(F32)
            yield at, value

    def wait_sent(self):
        for copy in self.started:
            copy.wait_send()
        self.started = []


class LightSum(CubeSum):
    def send_far(self):
        for h, link in ((0, X), (1, Y)):
            at = pl.ds(h * self.half, self.half)
            self.far[link, h] = self.push(self.parts.at[7, at], self.third.at[at], link)

    def send_middle(self):
        for h, link, place in ((0, X, Y | Z), (1, Y, X | Z)):
            at = pl.ds(h * self.half, self.half)
            self.far[link, h].wait_recv()
            self.parts[place, at] = add(self.parts[place, at], self.third[at, :])
        for h in range(2):
            at = pl.ds(h * self.half, self.half)
            for i, (link, place) in enumerate(((X, X | Z), (Y, Y | Z))):
                self.mid[link, h] = self.push(self.parts.at[place, at], self.second.at[i, at], link)
            link = (X, Y)[h]
            self.mid[X | Y, h] = self.push(self.parts.at[X | Y, at], self.second.at[2, at], link)

    def send_near(self):
        for h in range(2):
            at = pl.ds(h * self.half, self.half)
            self.mid[X, h].wait_recv()
            self.mid[Y, h].wait_recv()
            total = self.second[0, at].astype(F32) + self.second[1, at].astype(F32)
            self.parts[Z, at] = add(self.parts[Z, at], total)
            self.end[Z, h] = self.push(self.parts.at[Z, at], self.first.at[0, at], Z)
            self.mid[X | Y, h].wait_recv()
            place = (Y, X)[h]
            self.parts[place, at] = add(self.parts[place, at], self.second[2, at])
            for i, bit in ((1, X), (2, Y)):
                self.end[bit, h] = self.push(self.parts.at[bit, at], self.first.at[i, at], bit)


class CubeGather:
    def __init__(self, p, w, block, every):
        self.p, self.w, self.block, self.every = p, w, block, every
        self.half = block.shape[0] // 2
        self.started = []
        self.near, self.middle, self.far = {}, {}, {}

    def push(self, src, dst, bit):
        copy = self.w.remote(src, dst, self.p.cube(bit))
        copy.start()
        self.started.append(copy)
        return copy

    def send_near(self, h):
        at = pl.ds(h * self.half, self.half)
        for bit in (X, Y, Z):
            self.near[bit, h] = self.push(self.block.at[at], self.every.at[bit, at], bit)

    def send_middle(self, h):
        at = pl.ds(h * self.half, self.half)
        for link, relay in ((X, Y), (Y, Z), (Z, X)):
            self.near[relay, h].wait_recv()
            self.middle[link | relay, h] = self.push(
                self.every.at[relay, at], self.every.at[link | relay, at], link
            )

    def send_far(self, h):
        for (start, size), link, relay in zip(thirds(self.half), (X, Y, Z), (Y | Z, X | Z, X | Y)):
            at = pl.ds(h * self.half + start, size)
            self.middle[relay, h].wait_recv()
            self.far[link, h] = self.push(self.every.at[relay, at], self.every.at[7, at], link)

    def wait_far(self):
        for copy in self.far.values():
            copy.wait_recv()

    def wait_sent(self):
        for copy in self.started:
            copy.wait_send()
        self.started = []


def norm_scale(values):
    return lax.rsqrt(jnp.mean(values * values, axis=-1, keepdims=True) + EPS)


def norm_pull(values, scale, gain, cotangent):
    weighted = gain * cotangent
    lean = jnp.mean(values * weighted, axis=-1, keepdims=True)
    d_values = scale * weighted - values * (scale * scale * scale * lean)
    return d_values, jnp.sum(values * scale * cotangent, axis=0, keepdims=True)


def spread_matrix(width, per):
    column = lax.broadcasted_iota(jnp.int32, (128, width), 1)
    row = lax.broadcasted_iota(jnp.int32, (128, width), 0)
    place = (lax.rem(column, per) == row).astype(F32)
    column = lax.broadcasted_iota(jnp.int32, (16, width), 1)
    row = lax.broadcasted_iota(jnp.int32, (16, width), 0)
    owner = (lax.div(column, per) == row).astype(F32)
    return place, owner


def join_gains(packed, which, width, per):
    place, owner = spread_matrix(width, per)
    shards = packed[:, which, :].astype(BF16)
    wide = jnp.dot(shards, place.astype(BF16), preferred_element_type=F32)
    return jnp.sum(wide * owner, axis=0, keepdims=True)


def turn(values, cosine, sine):
    half = values.shape[-1] // 2
    u, w = values[:, :half], values[:, half:]
    return jnp.concatenate([u * cosine - w * sine, w * cosine + u * sine], axis=1)


def turn_back(values, cosine, sine):
    half = values.shape[-1] // 2
    u, w = values[:, :half], values[:, half:]
    return jnp.concatenate([u * cosine + w * sine, w * cosine - u * sine], axis=1)


def front_kernel(
    tok, seg_row, w_q, w_k, w_v, w_o, g_apre, g_apost, g_mpre, g_mpost, g_q, g_k, w_gate, w_up, w_down,
    qkv_w, out_w, gu_w, dn_w, every, gains_full, a_low, qk_proj, q_low, k_low, v_low,
    probs, o_low, attn_proj, h_mid, tables,
    qkv_s, qkv_own, qkv_send, qkv_got, out_own, gains_own, gains_s, wide_in, wide_send, wide_got,
    wide_out, down_in, down_out, m_low, out_s, send, recv, local,
):
    p = Place()
    w = Wires(send, recv)
    x, y, z, c, zl, zh = p.x, p.y, p.z, p.c, p.zl, p.zh
    sibling = p.at(c=1 - c)
    plane = [p.at(x=1 - x), p.at(y=1 - y)]
    lines = [p.at(y=yy, z=p.z_xor(k)) for yy in (y, 1 - y) for k in range(1, 4)]
    started = []

    def push(src, dst, device):
        copy = w.remote(src, dst, device)
        copy.start()
        started.append(copy)
        return copy

    loads = [
        pltpu.make_async_copy(w_gate, wide_in.at[0], local.at[0]),
        pltpu.make_async_copy(w_up, wide_in.at[1], local.at[1]),
        pltpu.make_async_copy(w_down, down_in, local.at[2]),
    ]
    for copy in loads:
        copy.start()

    rows = w_q.shape[0]
    columns = qkv_s.shape[1] // 4
    out_rows = w_o.shape[0] // 2
    mine = 2 * x + c
    theirs = 2 * x + 1 - c

    all_own = jnp.concatenate([w_q[...], w_k[...], w_v[...]], axis=1)
    for quarter in range(4):
        qkv_own[quarter] = all_own[:, quarter * columns : (quarter + 1) * columns]
    qkv_send[...] = qkv_own[theirs].astype(BF16)
    out_own[...] = w_o[...].astype(BF16)
    gains_own[...] = jnp.zeros_like(gains_own)
    for i, gain in enumerate((g_apre, g_apost, g_mpre, g_mpost, g_q, g_k)):
        gains_own[i, : gain.shape[0]] = gain[...].astype(BF16).astype(F32)
    across = p.at(x=1 - x, z=p.z_xor(3))
    greet([sibling, across] + plane + lines)

    def qkv_at(zz, yy, quarter):
        return qkv_s.at[
            pl.ds(pl.multiple_of((2 * zz + yy) * 2 * rows, 16), 2 * rows),
            pl.ds(pl.multiple_of(quarter * columns, 128), columns),
        ]

    def out_at(zz, yy, quarter):
        return out_s.at[
            pl.ds(pl.multiple_of((2 * zz + yy) * 4 * out_rows + quarter * out_rows, 16), out_rows)
        ]

    swap = push(qkv_send, qkv_got, sibling)

    def gains_at(zz, yy, cc):
        return gains_s.at[(2 * zz + yy) * 2 + cc]

    gains_s[(2 * z + y) * 2 + c] = gains_own[...]
    gain_line = [push(gains_own, gains_at(z, y, c), p.at(z=p.z_xor(k))) for k in range(1, 4)]
    gain_side = [push(gains_own, gains_at(z, y, c), plane[1])]
    holds = x == c
    out_theirs = out_own.at[pl.ds(pl.multiple_of((1 - c) * out_rows, 16), out_rows)]
    out_swap = w.remote(out_theirs, out_at(z, y, theirs), sibling)
    pl.when(holds)(out_swap.start)

    @pl.when(holds)
    def _():
        out_s[pl.ds(pl.multiple_of((2 * z + y) * 4 * out_rows + mine * out_rows, 16), out_rows)] = (
            out_own[pl.ds(pl.multiple_of(c * out_rows, 16), out_rows)]
        )

    swap.wait_recv()
    top, low = qkv_own[mine], qkv_got[...].astype(F32)
    first = jnp.where(c == 0, top, low)
    second = jnp.where(c == 0, low, top)
    base = pl.multiple_of((2 * z + y) * 2 * rows, 16)
    joined = jnp.concatenate([first, second], axis=0).astype(BF16)
    qkv_s[pl.ds(base, 2 * rows), pl.ds(pl.multiple_of(mine * columns, 128), columns)] = joined

    pl.when(jnp.logical_not(holds))(out_swap.wait_recv)
    pl.when(holds)(out_swap.wait_send)

    line = [None]
    for k in range(1, 4):
        to = p.at(z=p.z_xor(k))
        line.append(
            (
                push(qkv_at(z, y, mine), qkv_at(z, y, mine), to),
                push(out_at(z, y, mine), out_at(z, y, mine), to),
            )
        )
    side_x, side_y, corner = {}, {}, {}

    def spread(k):
        zz = p.z_xor(k)
        if k:
            for copy in line[k]:
                copy.wait_recv()
        qkv, out = qkv_at(zz, y, mine), out_at(zz, y, mine)
        side_x[k] = (push(qkv, qkv, plane[0]), push(out, out, plane[0]))
        side_y[k] = (push(qkv, qkv, plane[1]), push(out, out, plane[1]))

    def relay(k):
        zz = p.z_xor(k)
        if k % 2:
            for copy in side_y[k]:
                copy.wait_recv()
            qkv, out, to = qkv_at(zz, 1 - y, mine), out_at(zz, 1 - y, mine), plane[0]
        else:
            for copy in side_x[k]:
                copy.wait_recv()
            other = 2 * (1 - x) + c
            qkv, out, to = qkv_at(zz, y, other), out_at(zz, y, other), plane[1]
        corner[k] = (push(qkv, qkv, to), push(out, out, to))

    pairs = []

    def share(k):
        zz = p.z_xor(k)
        for copy in (side_x[k] if k % 2 else side_y[k]) + corner[k]:
            copy.wait_recv()
        for xx in range(2):
            at = qkv_s.at[
                pl.ds(pl.multiple_of(2 * zz * 2 * rows, 16), 4 * rows),
                pl.ds(pl.multiple_of((2 * xx + c) * columns, 128), columns),
            ]
            pairs.append(push(at, at, sibling))
            for yy in range(2):
                at = out_at(zz, yy, 2 * xx + c)
                pairs.append(push(at, at, sibling))

    spread(0)
    loads[0].wait()
    loads[1].wait()
    part_columns = wide_out.shape[-1]
    for xx in range(2):

        @pl.when(x == xx)
        def _():
            for zz in range(2):
                for yy in range(2):
                    part = (3 - 2 * zz if xx else 2 * zz) * 2 + yy
                    at = slice(part * part_columns, (part + 1) * part_columns)
                    for matrix in range(2):

                        @pl.when(c == 1 - matrix)
                        def _():
                            wide_send[2 * zz + yy] = wide_in[matrix, :, at].astype(BF16)

    wide_swap = push(wide_send, wide_got, sibling)
    loads[2].wait()
    down_out[...] = down_in[...].astype(BF16)
    relay(0)
    spread(1)
    wide_swap.wait_recv()
    for xx in range(2):

        @pl.when(x == xx)
        def _():
            for zz in range(2):
                for yy in range(2):
                    part = (3 - 2 * zz if xx else 2 * zz) * 2 + yy
                    at = slice(part * part_columns, (part + 1) * part_columns)
                    got = wide_got[2 * zz + yy].astype(F32)
                    for matrix in range(2):

                        @pl.when(c == matrix)
                        def _():
                            own = wide_in[matrix, :, at]
                            both = [own, got] if matrix == 0 else [got, own]
                            wide_out[2 * zz + yy] = jnp.concatenate(both, axis=0).astype(BF16)

    def gu_at(zz, yy):
        return gu_w.at[c, pl.ds(pl.multiple_of((2 * zz + yy) * 2 * rows, 16), 2 * rows)]

    down_rows = down_out.shape[0]
    down_at = dn_w.at[pl.ds(pl.multiple_of(c * down_rows, 16), down_rows)]
    down_local = p.slice_z() == z
    down_sends = lax.rem(zl + c, 2) == x
    down_copy = w.remote(down_out, down_at, p.at(x=zl, z=p.z_xor(3)))
    pl.when(down_sends)(down_copy.start)
    own_down = pltpu.make_async_copy(down_out, down_at, local.at[1])
    pl.when(down_local)(own_down.start)

    wide = []
    for k in range(4):
        for other in range(2):
            yy = 1 - y if other else y
            zz = p.z_xor(k)
            inner = lax.rem(lax.rem(zz, 2) + lax.div(zz, 2), 2)
            src = wide_out.at[2 * inner + yy]
            if k == 0 and other == 0:
                own_wide = pltpu.make_async_copy(src, gu_at(z, y), local.at[0])
                own_wide.start()
            else:
                wide.append((zz, yy, push(src, gu_at(z, y), p.at(y=yy, z=zz))))

    tok_f = tok[...].astype(F32)
    length, width = tok_f.shape
    head = k_low.shape[1]
    spread(2)
    relay(1)
    for copy in gain_line:
        copy.wait_recv()
    for k in range(1, 4):
        zz = p.z_xor(k)
        gain_side.append(push(gains_at(zz, y, c), gains_at(zz, y, c), plane[1]))
    row_seg = seg_row[...].astype(F32)
    i_at = lax.broadcasted_iota(jnp.int32, (length, length), 0)
    j_at = lax.broadcasted_iota(jnp.int32, (length, length), 1)
    col_seg = jnp.sum(jnp.where(i_at == j_at, row_seg, 0.0), axis=1, keepdims=True)
    earlier = jnp.sum((row_seg < col_seg).astype(F32), axis=1, keepdims=True)
    index = lax.broadcasted_iota(jnp.int32, (length, 1), 0).astype(F32)
    rate_at = lax.broadcasted_iota(jnp.int32, (1, head // 2), 1).astype(F32)
    rates = jnp.exp(rate_at * (-2.0 * math.log(THETA) / head))
    angles = (index - earlier) * rates
    tables[0] = jnp.cos(angles)
    tables[1] = jnp.sin(angles)
    spread(3)
    relay(2)
    share(0)
    relay(3)
    for copy in gain_side:
        copy.wait_recv()
    gain_pair = []
    for zz in range(4):
        for yy in range(2):
            gain_pair.append(push(gains_at(zz, yy, c), gains_at(zz, yy, c), sibling))
    share(1)
    for copy in gain_pair:
        copy.wait_recv()
    packed = gains_s[...]
    for i, (size, per) in enumerate(
        ((width, rows),) * 4 + ((head, head // 16),) * 2
    ):
        gains_full[i, :, :size] = join_gains(packed, i, size, per)
    a_low[...] = (tok_f * norm_scale(tok_f) * gains_full[0]).astype(BF16)
    share(2)
    share(3)
    for copy in pairs:
        copy.wait_recv()
    saves = [
        pltpu.make_async_copy(qkv_s, qkv_w, local.at[2]),
        pltpu.make_async_copy(out_s, out_w, local.at[3]),
    ]
    for copy in saves:
        copy.start()

    cosine, sine = tables[0], tables[1]
    heads = q_low.shape[1] // head
    for i in range(heads + 2):
        at = slice(i * head, (i + 1) * head)
        value = jnp.dot(a_low[...], qkv_s[:, at], preferred_element_type=F32)
        if i < heads:
            qk_proj[:, at] = value
            q_low[:, at] = turn(
                value * norm_scale(value) * gains_full[4, :, :head], cosine, sine
            ).astype(BF16)
        elif i == heads:
            qk_proj[:, at] = value
            k_low[...] = turn(
                value * norm_scale(value) * gains_full[5, :, :head], cosine, sine
            ).astype(BF16)
        else:
            v_low[...] = value.astype(BF16)
    allowed = (row_seg == col_seg) & (j_at <= i_at)
    for i in range(heads):
        at = slice(i * head, (i + 1) * head)
        scores = SCALE * lax.dot_general(
            q_low[:, at], k_low[...], (((1,), (1,)), ((), ())), preferred_element_type=F32
        )
        scores = jnp.where(allowed, scores, MASKED)
        expo = jnp.exp(scores - jnp.max(scores, axis=1, keepdims=True))
        prob = expo / jnp.sum(expo, axis=1, keepdims=True)
        probs[i] = prob
        o_low[:, at] = jnp.dot(
            prob.astype(BF16), v_low[...], preferred_element_type=F32
        ).astype(BF16)
    third = width // 3
    for i in range(3):
        at = slice(i * third, (i + 1) * third)
        attn_proj[:, at] = jnp.dot(o_low[...], out_s[:, at], preferred_element_type=F32)
    proj = attn_proj[...]
    mid = tok_f + proj * norm_scale(proj) * gains_full[1]
    h_mid[...] = mid
    m_low[...] = (mid * norm_scale(mid) * gains_full[2]).astype(BF16)

    gather = CubeGather(p, w, m_low, every)
    own = pltpu.make_async_copy(m_low, every.at[0], local.at[4])
    own.start()
    gather.send_near(0)
    gather.send_near(1)
    own_wide.wait()
    shared = [push(gu_at(z, y), gu_at(z, y), sibling)]
    gather.send_middle(0)
    gather.send_middle(1)
    gather.send_far(0)
    gather.send_far(1)
    for zz, yy, copy in reversed(wide):
        copy.wait_recv()
        shared.append(push(gu_at(zz, yy), gu_at(zz, yy), sibling))
    pl.when(down_local)(own_down.wait)
    pl.when(jnp.logical_not(down_local))(down_copy.wait_recv)
    shared.append(push(down_at, down_at, sibling))
    gather.wait_far()
    own.wait()
    gather.wait_sent()
    for copy in shared:
        copy.wait_recv()
    for copy in saves:
        copy.wait()
    pl.when(down_sends)(down_copy.wait_send)
    for copy in started:
        copy.wait_send()


def front(tok, segments, w_q, w_k, w_v, w_o, gains, w_gate, w_up, w_down, head):
    length, width = tok.shape
    rows, mix = w_q.shape
    hidden = w_gate.shape[1]
    part = hidden // 8
    down_rows = w_down.shape[0]
    total = mix + 2 * head
    heads = mix // head
    columns = total // 4
    struct = jax.ShapeDtypeStruct
    shapes = (
        struct((16 * rows, total), BF16),
        struct((16 * w_o.shape[0], width), BF16),
        struct((2, 16 * rows, part), BF16),
        struct((2 * down_rows, width), BF16),
        struct((8, length, width), BF16),
        struct((8, 1, width), F32),
        struct((length, width), BF16),
        struct((length, mix + head), F32),
        struct((length, mix), BF16),
        struct((length, head), BF16),
        struct((length, head), BF16),
        struct((heads, length, length), F32),
        struct((length, mix), BF16),
        struct((length, width), F32),
        struct((length, width), F32),
        struct((2, length, head // 2), F32),
    )
    scratch = [
        pltpu.VMEM((16 * rows, total), BF16),
        pltpu.VMEM((4, rows, columns), F32),
        pltpu.VMEM((rows, columns), BF16),
        pltpu.VMEM((rows, columns), BF16),
        pltpu.VMEM(w_o.shape, BF16),
        pltpu.VMEM((8, 128), F32),
        pltpu.VMEM((16, 8, 128), F32),
        pltpu.VMEM((2, rows, hidden), F32),
        pltpu.VMEM((4, rows, part), BF16),
        pltpu.VMEM((4, rows, part), BF16),
        pltpu.VMEM((4, 2 * rows, part), BF16),
        pltpu.VMEM((down_rows, width), F32),
        pltpu.VMEM((down_rows, width), BF16),
        pltpu.VMEM((length, width), BF16),
        pltpu.VMEM((16 * w_o.shape[0], width), BF16),
    ]
    return pl.pallas_call(
        front_kernel,
        out_shape=shapes,
        in_specs=[vmem()] * 12 + [hbm()] * 3,
        out_specs=(hbm(),) * 5 + (vmem(),) * 11,
        scratch_shapes=scratch + sems(128) + [pltpu.SemaphoreType.DMA((5,))],
        compiler_params=params(0),
        name="front",
    )(
        tok, segments, w_q, w_k, w_v, w_o, *gains, w_gate, w_up, w_down
    )


def dot_rows(left, right):
    return lax.dot_general(left, right, (((0,), (0,)), ((), ())), preferred_element_type=F32)


def dot_columns(left, right):
    return lax.dot_general(left, right, (((1,), (1,)), ((), ())), preferred_element_type=F32)


GELU_ROOT = math.sqrt(2.0 / math.pi)


def gelu_parts(gate):
    square = gate * gate
    bend = jnp.tanh(GELU_ROOT * gate * (1.0 + 0.044715 * square))
    half = 0.5 * (1.0 + bend)
    slope = half + 0.5 * gate * (1.0 - bend * bend) * GELU_ROOT * (1.0 + 3 * 0.044715 * square)
    return half * gate, slope


def tiles(size, step):
    return [slice(at, min(at + step, size)) for at in range(0, size, step)]


def tail_kernel(
    tok, d_out, h_mid, gains_full, every, gu, dn, proj_h, o_h, out_h, v_h, probs_h, k_h, q_h, qk_h,
    tables_h, a_h, qkv_h,
    layer_out, grad_x, qe, oe, gains_sum, wide_end, wide_back, down_end,
    dd_own, dd_all, third, second, first, wide_got, wide_sum, wide_far, down_got, down_sum, down_far,
    down_via, d_mid, q1, o1, qa, oa, qb, ob, qc, oc, gain_acc, gain_got, send, recv, local,
):
    p = Place()
    w = Wires(send, recv)
    x, y, z, c, zl, zh = p.x, p.y, p.z, p.c, p.zl, p.zh
    sibling = p.at(c=1 - c)
    plane = [p.at(x=1 - x), p.at(y=1 - y)]
    line = [p.at(z=p.z_xor(k)) for k in range(1, 4)]
    started = []

    def push(src, dst, device):
        copy = w.remote(src, dst, device)
        copy.start()
        started.append(copy)
        return copy

    def rows_of(ref, start, size):
        return ref.at[pl.ds(pl.multiple_of(start, 16), size)]

    chip_rows = wide_sum.shape[0] // 8
    half_rows = 4 * chip_rows
    far_half = half_rows * (1 - zh)
    near_half = half_rows * zh

    pieces = (0, 1, 2, 3)
    order = (3, 1, 2, 0)

    def piece(i, zl):
        to_z = 1 - zl if i // 2 else zl
        to_y = 1 - y if i % 2 else y
        return (2 * to_z + to_y) * chip_rows

    crossing = w.used
    w.used += 5

    def cross(i, src, dst):
        return pltpu.make_async_remote_copy(
            src_ref=src,
            dst_ref=dst,
            send_sem=send.at[crossing + i],
            recv_sem=recv.at[crossing + i],
            device_id=line[2],
            device_id_type=MESH,
        )

    def wide_two(i):
        return cross(
            i,
            rows_of(wide_sum, far_half + piece(i, 1 - zl), chip_rows),
            wide_far.at[pl.ds(i * chip_rows, chip_rows)],
        )

    def down_over():
        return cross(4, down_sum, down_far)

    mine = p.slice_z() == z

    def feed_forward(m_all, wide_w, down_w, wide, hidden, parts):
        blocks = (7, 3, 5, 6, 4, 2, 1, 0)
        loads = {r: pltpu.make_async_copy(every.at[r], m_all.at[r], local.at[r]) for r in blocks}
        wide_load = pltpu.make_async_copy(gu, wide_w, local.at[8])
        down_load = pltpu.make_async_copy(dn, down_w, local.at[9])
        wide_load.start()
        loads[7].start()
        down_load.start()
        for r in blocks[1:]:
            loads[r].start()
        greet([sibling] + plane + line + [p.cube(3), p.cube(5)])
        length, width = m_all.shape[1:]
        part = wide.shape[-1]
        wide_tiles = tiles(part, 256)
        down_tiles = tiles(width, 384)

        def forward(r):
            for at in wide_tiles:
                g = jnp.dot(m_all[r], wide_w[0, :, at], preferred_element_type=F32)
                u = jnp.dot(m_all[r], wide_w[1, :, at], preferred_element_type=F32)
                wide[0, r, :, at] = g.astype(BF16)
                wide[1, r, :, at] = u.astype(BF16)
                value, _ = gelu_parts(g)
                hidden[r, :, at] = (value * u).astype(BF16)
            for at in down_tiles:
                parts[r, :, at] = jnp.dot(
                    hidden[r], down_w[:, at], preferred_element_type=F32
                ).astype(BF16)

        def backward(r):
            for at in wide_tiles:
                d_hidden = dot_columns(dd_all[r], down_w[at, :])
                value, slope = gelu_parts(wide[0, r, :, at].astype(F32))
                up = wide[1, r, :, at].astype(F32)
                wide[0, r, :, at] = (d_hidden * up * slope).astype(BF16)
                wide[1, r, :, at] = (d_hidden * value).astype(BF16)
            d_gate = wide[0, r]
            d_up = wide[1, r]
            for at in down_tiles:
                parts[r, :, at] = (
                    dot_columns(d_gate, wide_w[0, at, :]) + dot_columns(d_up, wide_w[1, at, :])
                ).astype(BF16)

        def several(step, places):
            lax.fori_loop(0, 3, lambda i, _: (step(places(i)), 0)[1], 0)

        def middles(i):
            return 7 - lax.shift_right_logical(jnp.int32(4), i)

        def nears(i):
            return lax.shift_right_logical(jnp.int32(4), i)

        total = CubeSum(p, w, parts, third, second, first)
        wide_load.wait()
        loads[7].wait()
        down_load.wait()
        forward(7)
        total.send_far()
        for r in blocks[1:]:
            loads[r].wait()
        several(forward, middles)
        total.send_middle()
        several(forward, nears)
        total.send_near()
        forward(0)

        gather = CubeGather(p, w, dd_own, dd_all)
        gain = gains_full[3]
        g_rows = 0.0
        for h, (at, value) in enumerate(total.finish()):
            scale = norm_scale(value)
            layer_out[at, :] = (h_mid[at, :] + value * scale * gain).astype(BF16)
            d_value, g_part = norm_pull(value, scale, gain, d_out[at, :].astype(F32))
            dd_own[at, :] = d_value.astype(BF16)
            g_rows = g_rows + g_part
            gather.send_near(h)
        gain_acc[0, 3:4, :] = g_rows
        dd_all[0] = dd_own[...]
        total.wait_sent()
        backward(0)
        gather.send_middle(0)
        gather.send_middle(1)
        several(backward, nears)
        gather.send_far(0)
        gather.send_far(1)
        several(backward, middles)
        gather.wait_far()
        backward(7)

        total = LightSum(p, w, parts, third, second, first)
        total.send_far()
        grad_rows = 384
        all_rows = 8 * length
        for at in down_tiles:
            down_w[:, at] = dot_rows(
                hidden[...].reshape(all_rows, part), dd_all[:, :, at].reshape(all_rows, -1)
            ).astype(BF16)
        down_rows = down_sum.shape[0]
        down_one = w.remote(rows_of(down_w, (1 - c) * down_rows, down_rows), down_got, sibling)
        down_one.start()
        total.send_middle()
        down_one.wait_recv()
        down_sum[...] = add(down_w[pl.ds(pl.multiple_of(c * down_rows, 16), down_rows), :], down_got[...])
        pl.when(jnp.logical_not(mine))(down_over().start)

        def grad_wide(matrix, out):
            def step(i, _):
                at = pl.ds(pl.multiple_of(i * grad_rows, 128), grad_rows)
                left = m_all[:, :, at].reshape(all_rows, grad_rows)
                out[at, :] = dot_rows(left, wide[matrix].reshape(all_rows, part)).astype(BF16)
                return 0

            lax.fori_loop(0, width // grad_rows, step, 0)

        other = wide_w.at[1 - c]
        grad_wide(1 - c, other)
        wide_one = w.remote(other, wide_got, sibling)
        wide_one.start()
        grad_wide(c, wide_sum)
        wide_one.wait_recv()
        wide_sum[...] = add(wide_sum[...], wide_got[...])
        total.send_near()
        wide_two(0).start()
        wide_two(1).start()
        g_rows = 0.0
        for at, value in total.finish():
            mid = h_mid[at, :]
            d_value, g_part = norm_pull(mid, norm_scale(mid), gains_full[2], value)
            d_mid[at, :] = d_out[at, :].astype(F32) + d_value
            g_rows = g_rows + g_part
        gain_acc[0, 2:3, :] = g_rows
        down_one.wait_send()
        wide_one.wait_send()
        total.wait_sent()
        gather.wait_sent()

    def attention(
        proj, o_low, out_w, v_low, probs, k_low, q_low, qk_proj, tables, a_low, qkv_w,
        d_input, wide_swap, d_attn, d_mix, d_qkv, dqkv, dout, qa_s, oa_s, qb_s, ob_s, qc_s, oc_s,
    ):
        loads = [
            pltpu.make_async_copy(src, dst, local.at[i])
            for i, (src, dst) in enumerate(
                zip(
                    (proj_h, o_h, out_h, v_h, probs_h, k_h, q_h, qk_h, tables_h, a_h, qkv_h),
                    (proj, o_low, out_w, v_low, probs, k_low, q_low, qk_proj, tables, a_low, qkv_w),
                )
            )
        ]
        for copy in loads:
            copy.start()
        down_rows = down_end.shape[0]
        split = down_rows // 32 * 16
        lower, upper = pl.ds(0, split), pl.ds(split, down_rows - split)
        down_copy = w.remote(down_end.at[lower], down_end.at[lower], plane[0])
        down_around = w.remote(down_end.at[upper], down_via, p.cube(5))
        down_relay = w.remote(down_via, down_end.at[upper], line[0])

        @pl.when(mine)
        def _():
            down_over().wait_recv()
            down_end[...] = add(down_sum[...], down_far[...])
            down_copy.start()
            down_around.start()

        loads[0].wait()
        value = proj[...]
        d_value, g_apost = norm_pull(value, norm_scale(value), gains_full[1], d_mid[...])
        d_attn[...] = d_value.astype(BF16)
        gain_acc[0, 1:2, :] = g_apost
        loads[1].wait()

        width = tok.shape[1]
        step = width // 3
        for i in range(3):
            at = slice(i * step, (i + 1) * step)
            dout[:, at] = dot_rows(o_low[...], d_attn[:, at]).astype(BF16)
        out_rows = dout.shape[0] // 32

        def out_at(ref, zz, yy, quarter):
            return rows_of(ref, (2 * zz + yy) * 4 * out_rows + quarter * out_rows, out_rows)

        out_one = {
            k: [
                push(
                    out_at(dout, p.z_xor(k), yy, 2 * xx + 1 - c),
                    o1.at[k, xx, yy],
                    sibling,
                )
                for yy in range(2)
                for xx in range(2)
            ]
            for k in order
        }
        loads[2].wait()
        d_mix[...] = dot_columns(d_attn[...], out_w[...]).astype(BF16)

        def y_first(k):
            return k % 2 == 1

        columns = dqkv.shape[1] // 4
        first, first_out, then, last_step = {}, {}, {}, {}

        def own_out(k, xx, yy):
            start = ((2 * p.z_xor(k) + yy) * 4 + 2 * xx + c) * out_rows
            rows = pl.ds(pl.multiple_of(start, 16), out_rows)
            return dout[rows, :].astype(F32) + o1[k, xx, yy].astype(F32)

        def own_qkv(k, xx, yy):
            start = (2 * p.z_xor(k) + yy) * chip_rows
            rows = pl.ds(pl.multiple_of(start, 16), chip_rows)
            at = pl.ds(pl.multiple_of((2 * xx + c) * columns, 128), columns)
            got = pl.ds(pl.multiple_of(yy * chip_rows, 16), chip_rows)
            return dqkv[rows, at].astype(F32) + q1[k, xx, got, :].astype(F32)

        for k in order:
            for copy in out_one[k]:
                copy.wait_recv()
            first_out[k] = []
            for j in range(2):
                if y_first(k):
                    xx, yy, to = x if j == 0 else 1 - x, 1 - y, plane[1]
                else:
                    xx, yy, to = 1 - x, y if j == 0 else 1 - y, plane[0]
                oa_s[k, j] = own_out(k, xx, yy).astype(BF16)
                first_out[k].append(push(oa_s.at[k, j], oa.at[k, j], to))

        wide_two(2).start()
        for copy in loads[3:9]:
            copy.wait()
        cosine, sine = tables[0], tables[1]
        head = k_low.shape[1]
        heads = q_low.shape[1] // head
        d_k, d_v, g_q = 0.0, 0.0, 0.0
        for i in range(heads):
            at = slice(i * head, (i + 1) * head)
            prob = probs[i]
            d_probs = dot_columns(d_mix[:, at], v_low[...])
            row_dot = jnp.sum(prob * d_probs, axis=1, keepdims=True)
            d_scores = (prob * (d_probs - row_dot)).astype(BF16)
            d_q = SCALE * jnp.dot(d_scores, k_low[...], preferred_element_type=F32)
            d_k = d_k + dot_rows(d_scores, q_low[:, at])
            d_v = d_v + dot_rows(prob.astype(BF16), d_mix[:, at])
            value = qk_proj[:, at]
            d_value, gain = norm_pull(
                value, norm_scale(value), gains_full[4, :, :head], turn_back(d_q, cosine, sine)
            )
            g_q = g_q + gain
            d_qkv[:, at] = d_value.astype(BF16)
        at = slice(heads * head, (heads + 1) * head)
        value = qk_proj[:, at]
        d_value, g_k = norm_pull(
            value, norm_scale(value), gains_full[5, :, :head], turn_back(SCALE * d_k, cosine, sine)
        )
        d_qkv[:, at] = d_value.astype(BF16)
        d_qkv[:, (heads + 1) * head :] = d_v.astype(BF16)
        gain_acc[0, 4:5, :] = jnp.zeros((1, width), F32)
        gain_acc[0, 5:8, :] = jnp.zeros((3, width), F32)
        gain_acc[0, 4:5, :head] = g_q
        gain_acc[0, 5:6, :head] = g_k
        loads[9].wait()
        for i in range(heads + 2):
            at = slice(i * head, (i + 1) * head)
            dqkv[:, at] = dot_rows(a_low[...], d_qkv[:, at]).astype(BF16)

        qkv_one = {}
        for k in order:
            rows = pl.ds(pl.multiple_of(2 * p.z_xor(k) * chip_rows, 16), 2 * chip_rows)
            qkv_one[k] = [
                push(
                    dqkv.at[
                        rows, pl.ds(pl.multiple_of((2 * xx + 1 - c) * columns, 128), columns)
                    ],
                    q1.at[k, xx],
                    sibling,
                )
                for xx in range(2)
            ]

        def plane_first(k):
            for copy in qkv_one[k]:
                copy.wait_recv()
            first[k] = []
            for j in range(2):
                qa_s[k, j] = own_qkv(k, x if j == 0 else 1 - x, 1 - y).astype(BF16)
                first[k].append(push(qa_s.at[k, j], qa.at[k, j], plane[1]))

        def plane_then(k):
            for copy in first_out[k] + first[k]:
                copy.wait_recv()
            q = own_qkv(k, 1 - x, y)
            if y_first(k):
                o, to = own_out(k, 1 - x, y), plane[0]
            else:
                o, to = own_out(k, x, 1 - y), plane[1]
            qb_s[k] = (q + qa[k, 1].astype(F32)).astype(BF16)
            ob_s[k] = (o + oa[k, 1].astype(F32)).astype(BF16)
            then[k] = [
                push(qb_s.at[k], qb.at[k], plane[0]),
                push(ob_s.at[k], ob.at[k], to),
            ]

        def plane_last(k):
            for copy in then[k]:
                copy.wait_recv()
            q, o = own_qkv(k, x, y), own_out(k, x, y)
            q = q + qa[k, 0].astype(F32) + qb[k].astype(F32)
            o = o + oa[k, 0].astype(F32) + ob[k].astype(F32)
            if k == 0:
                return q, o
            qc_s[k] = q.astype(BF16)
            oc_s[k] = o.astype(BF16)
            last_step[k] = [
                push(qc_s.at[k], qc.at[k], line[k - 1]),
                push(oc_s.at[k], oc.at[k], line[k - 1]),
            ]

        for k in order:
            plane_first(k)
        wide_two(3).start()

        wide_three, wide_four, own_wide = {}, [], []

        def part_of(i):
            return 2 * p.slice_z(2 * zh + (1 - zl if i // 2 else zl)) + (1 - y if i % 2 else y)

        def wide_on(i):
            at = pl.ds(i * chip_rows, chip_rows)
            rows = pl.ds(pl.multiple_of(near_half + piece(i, zl), 16), chip_rows)
            wide_two(i).wait_recv()
            wide_far[at, :] = add(wide_sum[rows, :], wide_far[at, :])
            dst = wide_end.at[part_of(0)]
            if i:
                wide_three[i] = push(wide_far.at[at], dst, p.cube(2 * (i % 2) + i // 2))
            else:
                own_wide.append(pltpu.make_async_copy(wide_far.at[at], dst, local.at[11]))
                own_wide[0].start()
                wide_four.append(push(wide_far.at[at], dst, plane[0]))

        def wide_over(i):
            wide_three[i].wait_recv()
            dst = wide_end.at[part_of(i)]
            wide_four.append(push(dst, dst, plane[0]))

        @pl.when(mine)
        def _():
            down_around.wait_recv()
            down_relay.start()

        wide_on(0)

        loads[10].wait()
        tok_f = tok[...].astype(F32)
        for i in range(3):
            at = slice(i * step, (i + 1) * step)
            d_input[:, at] = dot_columns(d_qkv[...], qkv_w[at, :])
        d_value, g_apre = norm_pull(tok_f, norm_scale(tok_f), gains_full[0], d_input[...])
        grad_x[...] = (d_mid[...] + d_value).astype(BF16)
        gain_acc[0, 0:1, :] = g_apre
        gain_one = push(gain_acc.at[0], gain_got.at[0], sibling)

        for k in order[:2]:
            plane_then(k)
        gain_one.wait_recv()
        gain_acc[1] = gain_acc[0] + gain_got[0]
        gain_two = push(gain_acc.at[1], gain_got.at[1], plane[0])
        wide_on(1)
        for k in order[2:]:
            plane_then(k)
        for k in order[:3]:
            plane_last(k)
        wide_on(2)
        wide_over(1)
        gain_two.wait_recv()
        gain_acc[2] = gain_acc[1] + gain_got[1]
        gain_three = push(gain_acc.at[2], gain_got.at[2], plane[1])
        q, o = plane_last(0)
        for k in order[:3]:
            for copy in last_step[k]:
                copy.wait_recv()
        qe[0] = (q + qc[1].astype(F32) + qc[2].astype(F32) + qc[3].astype(F32)).astype(BF16)
        oe[0] = (o + oc[1].astype(F32) + oc[2].astype(F32) + oc[3].astype(F32)).astype(BF16)
        last = [
            push(qe.at[0], qe.at[4 + i], device)
            for i, device in enumerate((sibling, plane[0]))
        ] + [
            push(oe.at[0], oe.at[4 + i], device)
            for i, device in enumerate((sibling, plane[0]))
        ]
        wide_on(3)
        wide_over(2)
        gain_three.wait_recv()
        gain_acc[3] = gain_acc[2] + gain_got[2]
        gain_four = [push(gain_acc.at[3], gain_got.at[2 + k], line[k - 1]) for k in range(1, 4)]
        for copy in last:
            copy.wait_recv()
        relay = [push(qe.at[5], qe.at[6], sibling), push(oe.at[5], oe.at[6], sibling)]

        wide_over(3)
        for copy in relay:
            copy.wait_recv()
        rows = chip_rows // 2
        for copy in gain_four:
            copy.wait_recv()
        gains_sum[...] = gain_acc[3] + gain_got[3] + gain_got[4] + gain_got[5]

        own_wide[0].wait()
        for copy in wide_four:
            copy.wait_recv()
        for cc in range(2):

            @pl.when(c == cc)
            def _():
                for s in range(8):
                    extra = (rows + 15) // 16 * 16
                    at = slice(0, extra) if cc == 1 else slice(2 * rows - extra, 2 * rows)
                    wide_swap[s] = wide_end[s, at, :]

        final = push(wide_swap, wide_back, sibling)

        @pl.when(jnp.logical_not(mine))
        def _():
            down_copy.wait_recv()
            down_relay.wait_recv()

        final.wait_recv()

        @pl.when(mine)
        def _():
            for copy in (down_copy, down_around, down_relay):
                copy.wait_send()

        pl.when(jnp.logical_not(mine))(down_over().wait_send)
        for i in pieces:
            wide_two(i).wait_send()
        for copy in started:
            copy.wait_send()


    length, width = tok.shape
    blocks = (8, length, width)
    part = wide_sum.shape[1]
    pl.run_scoped(
        feed_forward,
        pltpu.VMEM(blocks, BF16),
        pltpu.VMEM(gu.shape, BF16),
        pltpu.VMEM(dn.shape, BF16),
        pltpu.VMEM((2, 8, length, part), BF16),
        pltpu.VMEM((8, length, part), BF16),
        pltpu.VMEM(blocks, BF16),
    )
    total = qkv_h.shape[1]
    mix = o_h.shape[1]
    q_piece, o_piece = qa.shape[2:], oa.shape[2:]
    saved = (proj_h, o_h, out_h, v_h, probs_h, k_h, q_h, qk_h, tables_h, a_h, qkv_h)
    pl.run_scoped(
        attention,
        *[pltpu.VMEM(ref.shape, ref.dtype) for ref in saved],
        pltpu.VMEM((length, width), F32),
        pltpu.VMEM(wide_back.shape, BF16),
        pltpu.VMEM((length, width), BF16),
        pltpu.VMEM((length, mix), BF16),
        pltpu.VMEM((length, total), BF16),
        pltpu.VMEM((width, total), BF16),
        pltpu.VMEM((mix, width), BF16),
        pltpu.VMEM((4, 2) + q_piece, BF16),
        pltpu.VMEM((4, 2) + o_piece, BF16),
        pltpu.VMEM((4,) + q_piece, BF16),
        pltpu.VMEM((4,) + o_piece, BF16),
        pltpu.VMEM((4,) + q_piece, BF16),
        pltpu.VMEM((4,) + o_piece, BF16),
    )


def tail(tok, d_out, h_mid, gains_full, every, gu, dn, saved):
    length, width = tok.shape
    part = dn.shape[0]
    proj, o_low, out_w, *_, qkv_w = saved
    columns = qkv_w.shape[1] // 4
    mix = out_w.shape[0]
    chip_rows = width // 8
    rows = chip_rows // 2
    extra = (rows + 15) // 16 * 16
    piece = mix // 32
    blocks = (8, length, width)
    struct = jax.ShapeDtypeStruct
    shapes = (
        struct((length, width), BF16),
        struct((length, width), BF16),
        struct((7, chip_rows, columns), BF16),
        struct((7, piece, width), BF16),
        struct((8, width), F32),
        struct((8, chip_rows, part), BF16),
        struct((8, extra, part), BF16),
        struct((part // 2, width), BF16),
    )
    scratch = [
        pltpu.VMEM((length, width), BF16),
        pltpu.VMEM(blocks, BF16),
        pltpu.VMEM((length, width), BF16),
        pltpu.VMEM((3, length, width), BF16),
        pltpu.VMEM((3, length, width), BF16),
        pltpu.VMEM((width, part), BF16),
        pltpu.VMEM((width, part), BF16),
        pltpu.VMEM((width // 2, part), BF16),
        pltpu.VMEM((part // 2, width), BF16),
        pltpu.VMEM((part // 2, width), BF16),
        pltpu.VMEM((part // 2, width), BF16),
        pltpu.VMEM((part // 2 - part // 64 * 16, width), BF16),
        pltpu.VMEM((length, width), F32),
        pltpu.VMEM((4, 2, 2 * chip_rows, columns), BF16),
        pltpu.VMEM((4, 2, 2, piece, width), BF16),
        pltpu.VMEM((4, 2, chip_rows, columns), BF16),
        pltpu.VMEM((4, 2, piece, width), BF16),
        pltpu.VMEM((4, chip_rows, columns), BF16),
        pltpu.VMEM((4, piece, width), BF16),
        pltpu.VMEM((4, chip_rows, columns), BF16),
        pltpu.VMEM((4, piece, width), BF16),
        pltpu.VMEM((4, 8, width), F32),
        pltpu.VMEM((6, 8, width), F32),
    ]
    return pl.pallas_call(
        tail_kernel,
        out_shape=shapes,
        in_specs=[vmem()] * 4 + [hbm()] * 14,
        out_specs=(vmem(),) * 8,
        scratch_shapes=scratch + sems(160) + [pltpu.SemaphoreType.DMA((12,))],
        compiler_params=params(1),
        name="tail",
    )(tok, d_out, h_mid, gains_full, every, gu, dn, *saved)


def place_kernel(
    qe, oe, gains, wide_end, wide_back, down_end,
    w_q, w_k, w_v, w_o, w_gate, w_up, w_down, a_pre, a_post, m_pre, m_post, q_gain, k_gain,
):
    p = Place()
    rows, mix = w_q.shape
    head = w_k.shape[1]
    columns = qe.shape[2]
    piece = oe.shape[1]
    size = wide_end.shape[2]
    extra = wide_back.shape[1]

    def put_columns(start, value):
        for ref, first, width in ((w_q, 0, mix), (w_k, mix, head), (w_v, mix + head, head)):
            low, high = max(start, first), min(start + columns, first + width)
            if low < high:
                ref[:, low - first : high - first] = value[:, low - start : high - start]

    for xx in range(2):
        for cc in range(2):

            @pl.when((p.x == xx) & (p.c == cc))
            def _():
                for i, q in (
                    (0, 2 * xx + cc),
                    (4, 2 * xx + 1 - cc),
                    (5, 2 * (1 - xx) + cc),
                    (6, 2 * (1 - xx) + 1 - cc),
                ):
                    both = qe[i].astype(F32)
                    put_columns(q * columns, both[cc * rows : (cc + 1) * rows])
                    if q // 2 == cc:
                        w_o[(q % 2) * piece : (q % 2 + 1) * piece, :] = oe[i].astype(F32)

    for cc in range(2):

        @pl.when(p.c == cc)
        def _():
            own_ref, other_ref = (w_gate, w_up) if cc == 0 else (w_up, w_gate)
            for s in range(8):
                at = slice(s * size, (s + 1) * size)
                own_ref[:, at] = wide_end[s].astype(F32)[cc * rows : (cc + 1) * rows]
                other = wide_back[s].astype(F32)
                other_ref[:, at] = other[:rows] if cc == 0 else other[extra - rows :]

    w_down[...] = down_end[...].astype(F32)
    sums = gains[...]
    for i, ref in enumerate((a_pre, a_post, m_pre, m_post, q_gain, k_gain)):
        per = ref.shape[0]
        full = 16 * per
        turned = pltpu.roll(sums[:, :full], lax.rem(full - p.shard * per, full), 1)
        ref[...] = turned[i, :per]


def place(summed, shapes):
    return pl.pallas_call(
        place_kernel,
        out_shape=tuple(jax.ShapeDtypeStruct(shape, F32) for shape in shapes),
        in_specs=[vmem()] * 6,
        out_specs=(vmem(),) * 13,
        compiler_params=pltpu.CompilerParams(vmem_limit_bytes=VMEM_BYTES),
        name="place",
    )(*summed)


def cube_body(
    layer_in, d_out, segments, w_q, w_k, w_v, w_o, attn_pre, attn_post, q_gain, k_gain,
    w_gate, w_up, w_down, mlp_pre, mlp_post,
):
    width = layer_in.shape[1]
    head = q_gain.shape[0] * 16
    rows, mix = w_q.shape
    gain_list = [attn_pre, attn_post, mlp_pre, mlp_post, q_gain, k_gain]
    (
        qkv_w, out_w, gu_w, down_w, m_all, gains_full, a_low, qk_proj, q_low, k_low, v_low,
        probs, o_low, attn_proj, h_mid, tables,
    ) = front(
        layer_in, segments, w_q, w_k, w_v, w_o, gain_list, w_gate, w_up, w_down, head
    )
    saved = (
        attn_proj, o_low, out_w, v_low, probs, k_low, q_low, qk_proj, tables, a_low, qkv_w,
    )
    layer_out, grad_x, *summed = tail(
        layer_in, d_out, h_mid, gains_full, m_all, gu_w, down_w, saved
    )
    matrices = [w_q, w_k, w_v, w_o, w_gate, w_up, w_down]
    grads = place(summed, [v.shape for v in matrices + gain_list])
    g_apre, g_apost, g_mpre, g_mpost, g_q, g_k = grads[7:]
    return (
        layer_out,
        grad_x,
        *grads[:4],
        g_apre,
        g_apost,
        g_q,
        g_k,
        *grads[4:7],
        g_mpre,
        g_mpost,
    )


def solution(mesh):
    in_specs = (
        P(("replica", "fsdp"), None),
        P(("replica", "fsdp"), None),
        P(("replica", "fsdp"), None),
        P("fsdp", None),
        P("fsdp", None),
        P("fsdp", None),
        P("fsdp", None),
        P("fsdp"),
        P("fsdp"),
        P("fsdp"),
        P("fsdp"),
        P("fsdp", None),
        P("fsdp", None),
        P("fsdp", None),
        P("fsdp"),
        P("fsdp"),
    )
    out_specs = (
        P(("replica", "fsdp"), None),
        P(("replica", "fsdp"), None),
        P("fsdp", None),
        P("fsdp", None),
        P("fsdp", None),
        P("fsdp", None),
        P("fsdp"),
        P("fsdp"),
        P("fsdp"),
        P("fsdp"),
        P("fsdp", None),
        P("fsdp", None),
        P("fsdp", None),
        P("fsdp"),
        P("fsdp"),
    )
    body = cube_body if fits_cubes(mesh) else general_body
    return jax.shard_map(body, mesh=mesh, in_specs=in_specs, out_specs=out_specs, check_vma=False)
```

```python
from functools import partial
import math

import jax
import jax.numpy as jnp
from jax import lax
from jax.experimental import pallas as pl
from jax.experimental.pallas import tpu as pltpu
from jax.sharding import PartitionSpec as P

EPS = 1e-06
THETA = 1000000.0
SCALE = 0.0625
MASKED = -1e30


def norm_rows(values, gain):
    return values * lax.rsqrt(jnp.mean(values * values, axis=-1, keepdims=True) + EPS) * gain


def positions_of(segments):
    length = segments.shape[-1]
    index = jnp.arange(length, dtype=jnp.int32)
    earlier = jnp.concatenate([segments[:, :1] - 1, segments[:, :-1]], axis=1)
    starts = jnp.where(segments != earlier, index[None, :], jnp.zeros_like(segments))
    return index[None, :] - lax.cummax(starts, axis=1)


def angle_tables(segments, head_size):
    half_size = head_size // 2
    rates = jnp.exp(jnp.arange(half_size, dtype=jnp.float32) * (-2.0 * math.log(THETA) / head_size))
    angles = positions_of(segments).astype(jnp.float32)[..., None] * rates
    return (jnp.cos(angles), jnp.sin(angles))


def rotate(values, cosine, sine):
    half_size = values.shape[-1] // 2
    first_half = values[..., :half_size]
    second_half = values[..., half_size:]
    return jnp.concatenate(
        [first_half * cosine - second_half * sine, second_half * cosine + first_half * sine],
        axis=-1,
    )


def query_path(projected, gain, cosine, sine):
    shaped = projected.reshape(projected.shape[0], projected.shape[1], -1, gain.shape[0])
    return rotate(norm_rows(shaped, gain), cosine[:, :, None, :], sine[:, :, None, :])


def key_path(projected, gain, cosine, sine):
    return rotate(norm_rows(projected, gain), cosine, sine)


def gelu_product(gate_val, up_val):
    return jax.nn.gelu(gate_val, approximate=True) * up_val


def to_low(values):
    return values.astype(jnp.bfloat16)


def matmul(left, right):
    return jnp.dot(left, right, preferred_element_type=jnp.float32)


def matmul_left_t(left, right):
    return lax.dot_general(
        left, right, (((0,), (0,)), ((), ())), preferred_element_type=jnp.float32
    )


def matmul_right_t(left, right):
    return lax.dot_general(
        left, right, (((1,), (1,)), ((), ())), preferred_element_type=jnp.float32
    )


def attention_masks(segments):
    length = segments.shape[1]
    index = jnp.arange(length, dtype=jnp.int32)
    causal = index[None, :] <= index[:, None]
    return (segments[:, :, None] == segments[:, None, :]) & causal[None]


def scores_of(q_low, k_low, masks):
    scores = SCALE * jnp.einsum("nqhd,nkd->nhqk", q_low, k_low, preferred_element_type=jnp.float32)
    return jnp.where(masks[:, None], scores, MASKED)


def spread_gain(values):
    return jnp.broadcast_to(values[:, None], (values.shape[0], lax.axis_size("replica")))


def general_body(
    layer_in,
    d_out,
    segments,
    w_q,
    w_k,
    w_v,
    w_o,
    attn_pre,
    attn_post,
    q_gain,
    k_gain,
    w_gate,
    w_up,
    w_down,
    mlp_pre,
    mlp_post,
):
    attn_set = (
        lax.all_gather(to_low(w_q), "fsdp", axis=0, tiled=True),
        lax.all_gather(to_low(w_k), "fsdp", axis=0, tiled=True),
        lax.all_gather(to_low(w_v), "fsdp", axis=0, tiled=True),
        lax.all_gather(to_low(w_o), "fsdp", axis=0, tiled=True),
        lax.all_gather(to_low(attn_pre), "fsdp", axis=0, tiled=True),
        lax.all_gather(to_low(attn_post), "fsdp", axis=0, tiled=True),
        lax.all_gather(to_low(q_gain), "fsdp", axis=0, tiled=True),
        lax.all_gather(to_low(k_gain), "fsdp", axis=0, tiled=True),
    )
    q_full, k_full, v_full, o_full = (attn_set[0], attn_set[1], attn_set[2], attn_set[3])
    gain_apre = attn_set[4].astype(jnp.float32)
    gain_apost = attn_set[5].astype(jnp.float32)
    gain_q = attn_set[6].astype(jnp.float32)
    gain_k = attn_set[7].astype(jnp.float32)
    mlp_set = (
        lax.all_gather(to_low(w_gate), "fsdp", axis=0, tiled=True),
        lax.all_gather(to_low(w_up), "fsdp", axis=0, tiled=True),
        lax.all_gather(to_low(w_down), "fsdp", axis=0, tiled=True),
        lax.all_gather(to_low(mlp_pre), "fsdp", axis=0, tiled=True),
        lax.all_gather(to_low(mlp_post), "fsdp", axis=0, tiled=True),
    )
    gate_full, up_full, down_full = (mlp_set[0], mlp_set[1], mlp_set[2])
    gain_mpre = mlp_set[3].astype(jnp.float32)
    gain_mpost = mlp_set[4].astype(jnp.float32)
    seq_count, seq_len = segments.shape
    tok_flat = layer_in.astype(jnp.float32)
    cosine, sine = angle_tables(segments, gain_q.shape[0])
    masks = attention_masks(segments)
    normed_a, pull_a = jax.vjp(norm_rows, tok_flat, gain_apre)
    a_low = to_low(normed_a)
    q_proj = matmul(a_low, q_full).reshape(seq_count, seq_len, -1)
    k_proj = matmul(a_low, k_full).reshape(seq_count, seq_len, -1)
    v_proj = matmul(a_low, v_full)
    q_rot, pull_q = jax.vjp(partial(query_path, cosine=cosine, sine=sine), q_proj, gain_q)
    k_rot, pull_k = jax.vjp(partial(key_path, cosine=cosine, sine=sine), k_proj, gain_k)
    q_low = to_low(q_rot)
    k_low = to_low(k_rot)
    v_low = to_low(v_proj).reshape(seq_count, seq_len, -1)
    scores = scores_of(q_low, k_low, masks)
    top_val = jnp.max(scores, axis=-1, keepdims=True)
    log_total = top_val + jnp.log(jnp.sum(jnp.exp(scores - top_val), axis=-1, keepdims=True))
    p_low = to_low(jnp.exp(scores - log_total))
    attn_mix = jnp.einsum("nhqk,nkd->nqhd", p_low, v_low, preferred_element_type=jnp.float32)
    o_low = to_low(attn_mix.reshape(seq_count * seq_len, -1))
    attn_proj = matmul(o_low, o_full)
    post_attn, pull_pa = jax.vjp(norm_rows, attn_proj, gain_apost)
    h_mid = tok_flat + post_attn
    normed_m, pull_m = jax.vjp(norm_rows, h_mid, gain_mpre)
    m_low = to_low(normed_m)
    gate_val = matmul(m_low, gate_full)
    up_val = matmul(m_low, up_full)
    hidden, pull_h = jax.vjp(gelu_product, gate_val, up_val)
    h_low = to_low(hidden)
    down_val = matmul(h_low, down_full)
    post_mlp, pull_pm = jax.vjp(norm_rows, down_val, gain_mpost)
    layer_out = (h_mid + post_mlp).astype(jnp.bfloat16)
    gate_full, up_full, down_full = (
        lax.all_gather(to_low(w_gate), "fsdp", axis=0, tiled=True),
        lax.all_gather(to_low(w_up), "fsdp", axis=0, tiled=True),
        lax.all_gather(to_low(w_down), "fsdp", axis=0, tiled=True),
    )
    grad_top = d_out.astype(jnp.float32)
    d_down, grad_mpost = pull_pm(grad_top)
    d_down_low = to_low(d_down)
    grad_wdown = matmul_left_t(h_low, d_down_low)
    d_hidden = matmul_right_t(d_down_low, down_full)
    d_gate, d_up = pull_h(d_hidden)
    d_gate_low = to_low(d_gate)
    d_up_low = to_low(d_up)
    grad_wgate = matmul_left_t(m_low, d_gate_low)
    grad_wup = matmul_left_t(m_low, d_up_low)
    d_normed = matmul_right_t(d_gate_low, gate_full) + matmul_right_t(d_up_low, up_full)
    d_mid_norm, grad_mpre = pull_m(d_normed)
    d_mid = grad_top + d_mid_norm
    q_full, k_full, v_full, o_full = (
        lax.all_gather(to_low(w_q), "fsdp", axis=0, tiled=True),
        lax.all_gather(to_low(w_k), "fsdp", axis=0, tiled=True),
        lax.all_gather(to_low(w_v), "fsdp", axis=0, tiled=True),
        lax.all_gather(to_low(w_o), "fsdp", axis=0, tiled=True),
    )
    d_attn, grad_apost = pull_pa(d_mid)
    d_attn_low = to_low(d_attn)
    grad_wo = matmul_left_t(o_low, d_attn_low)
    d_mix_low = to_low(matmul_right_t(d_attn_low, o_full)).reshape(
        seq_count, seq_len, -1, k_low.shape[-1]
    )
    probs = jnp.exp(scores_of(q_low, k_low, masks) - log_total)
    d_probs = jnp.einsum("nqhd,nkd->nhqk", d_mix_low, v_low, preferred_element_type=jnp.float32)
    row_dot = jnp.sum(probs * d_probs, axis=-1, keepdims=True)
    d_scores_low = to_low(probs * (d_probs - row_dot))
    d_query = SCALE * jnp.einsum(
        "nhqk,nkd->nqhd", d_scores_low, k_low, preferred_element_type=jnp.float32
    )
    d_key = SCALE * jnp.einsum(
        "nhqk,nqhd->nkd", d_scores_low, q_low, preferred_element_type=jnp.float32
    )
    d_value = jnp.einsum("nhqk,nqhd->nkd", p_low, d_mix_low, preferred_element_type=jnp.float32)
    d_qproj, grad_qgain = pull_q(d_query)
    d_kproj, grad_kgain = pull_k(d_key)
    d_q_low = to_low(d_qproj.reshape(seq_count * seq_len, -1))
    d_k_low = to_low(d_kproj.reshape(seq_count * seq_len, -1))
    d_v_low = to_low(d_value.reshape(seq_count * seq_len, -1))
    grad_wq = matmul_left_t(a_low, d_q_low)
    grad_wk = matmul_left_t(a_low, d_k_low)
    grad_wv = matmul_left_t(a_low, d_v_low)
    d_normed_a = (
        matmul_right_t(d_q_low, q_full)
        + matmul_right_t(d_k_low, k_full)
        + matmul_right_t(d_v_low, v_full)
    )
    d_input_norm, grad_apre = pull_a(d_normed_a)
    grad_x = (d_mid + d_input_norm).astype(jnp.bfloat16)
    all_shards = (
        lax.psum_scatter(grad_wq, "fsdp", scatter_dimension=0, tiled=True),
        lax.psum_scatter(grad_wk, "fsdp", scatter_dimension=0, tiled=True),
        lax.psum_scatter(grad_wv, "fsdp", scatter_dimension=0, tiled=True),
        lax.psum_scatter(grad_wo, "fsdp", scatter_dimension=0, tiled=True),
        lax.psum_scatter(grad_apre, "fsdp", scatter_dimension=0, tiled=True),
        lax.psum_scatter(grad_apost, "fsdp", scatter_dimension=0, tiled=True),
        lax.psum_scatter(grad_qgain, "fsdp", scatter_dimension=0, tiled=True),
        lax.psum_scatter(grad_kgain, "fsdp", scatter_dimension=0, tiled=True),
        lax.psum_scatter(grad_wgate, "fsdp", scatter_dimension=0, tiled=True),
        lax.psum_scatter(grad_wup, "fsdp", scatter_dimension=0, tiled=True),
        lax.psum_scatter(grad_wdown, "fsdp", scatter_dimension=0, tiled=True),
        lax.psum_scatter(grad_mpre, "fsdp", scatter_dimension=0, tiled=True),
        lax.psum_scatter(grad_mpost, "fsdp", scatter_dimension=0, tiled=True),
    )
    all_cols = (
        lax.psum_scatter(
            all_shards[0].astype(jnp.bfloat16), "replica", scatter_dimension=1, tiled=True
        ).astype(jnp.float32),
        lax.psum_scatter(
            all_shards[1].astype(jnp.bfloat16), "replica", scatter_dimension=1, tiled=True
        ).astype(jnp.float32),
        lax.psum_scatter(
            all_shards[2].astype(jnp.bfloat16), "replica", scatter_dimension=1, tiled=True
        ).astype(jnp.float32),
        lax.psum_scatter(
            all_shards[3].astype(jnp.bfloat16), "replica", scatter_dimension=1, tiled=True
        ).astype(jnp.float32),
        lax.psum_scatter(
            all_shards[8].astype(jnp.bfloat16), "replica", scatter_dimension=1, tiled=True
        ).astype(jnp.float32),
        lax.psum_scatter(
            all_shards[9].astype(jnp.bfloat16), "replica", scatter_dimension=1, tiled=True
        ).astype(jnp.float32),
        lax.psum_scatter(
            all_shards[10].astype(jnp.bfloat16), "replica", scatter_dimension=1, tiled=True
        ).astype(jnp.float32),
        lax.psum_scatter(
            spread_gain(all_shards[4]).astype(jnp.bfloat16),
            "replica",
            scatter_dimension=1,
            tiled=True,
        ).astype(jnp.float32),
        lax.psum_scatter(
            spread_gain(all_shards[5]).astype(jnp.bfloat16),
            "replica",
            scatter_dimension=1,
            tiled=True,
        ).astype(jnp.float32),
        lax.psum_scatter(
            spread_gain(all_shards[6]).astype(jnp.bfloat16),
            "replica",
            scatter_dimension=1,
            tiled=True,
        ).astype(jnp.float32),
        lax.psum_scatter(
            spread_gain(all_shards[7]).astype(jnp.bfloat16),
            "replica",
            scatter_dimension=1,
            tiled=True,
        ).astype(jnp.float32),
        lax.psum_scatter(
            spread_gain(all_shards[11]).astype(jnp.bfloat16),
            "replica",
            scatter_dimension=1,
            tiled=True,
        ).astype(jnp.float32),
        lax.psum_scatter(
            spread_gain(all_shards[12]).astype(jnp.bfloat16),
            "replica",
            scatter_dimension=1,
            tiled=True,
        ).astype(jnp.float32),
    )
    all_mats = (
        lax.all_gather(all_cols[0].astype(jnp.bfloat16), "replica", axis=1, tiled=True).astype(
            jnp.float32
        ),
        lax.all_gather(all_cols[1].astype(jnp.bfloat16), "replica", axis=1, tiled=True).astype(
            jnp.float32
        ),
        lax.all_gather(all_cols[2].astype(jnp.bfloat16), "replica", axis=1, tiled=True).astype(
            jnp.float32
        ),
        lax.all_gather(all_cols[3].astype(jnp.bfloat16), "replica", axis=1, tiled=True).astype(
            jnp.float32
        ),
        lax.all_gather(all_cols[4].astype(jnp.bfloat16), "replica", axis=1, tiled=True).astype(
            jnp.float32
        ),
        lax.all_gather(all_cols[5].astype(jnp.bfloat16), "replica", axis=1, tiled=True).astype(
            jnp.float32
        ),
        lax.all_gather(all_cols[6].astype(jnp.bfloat16), "replica", axis=1, tiled=True).astype(
            jnp.float32
        ),
    )
    attn_sums = (
        all_mats[0],
        all_mats[1],
        all_mats[2],
        all_mats[3],
        all_cols[7][:, 0],
        all_cols[8][:, 0],
        all_cols[9][:, 0],
        all_cols[10][:, 0],
    )
    mlp_sums = (all_mats[4], all_mats[5], all_mats[6], all_cols[11][:, 0], all_cols[12][:, 0])
    return (
        layer_out,
        grad_x,
        attn_sums[0],
        attn_sums[1],
        attn_sums[2],
        attn_sums[3],
        attn_sums[4],
        attn_sums[5],
        attn_sums[6],
        attn_sums[7],
        mlp_sums[0],
        mlp_sums[1],
        mlp_sums[2],
        mlp_sums[3],
        mlp_sums[4],
    )


MESH = pl.DeviceIdType.MESH
VMEM_BYTES = 63 * 2**20
F32 = jnp.float32
BF16 = jnp.bfloat16


def fits_cubes(mesh):
    return dict(mesh.shape) == {"replica": 2, "fsdp": 16}


class Place:
    def __init__(self):
        shard = lax.axis_index("fsdp")
        self.x = lax.axis_index("replica")
        self.shard = shard
        self.c = lax.rem(shard, 2)
        self.y = lax.rem(lax.div(shard, 2), 2)
        self.z = lax.div(shard, 4)
        self.zl = lax.rem(self.z, 2)
        self.zh = lax.div(self.z, 2)

    def at(self, x=None, y=None, z=None, c=None):
        x = self.x if x is None else x
        y = self.y if y is None else y
        z = self.z if z is None else z
        c = self.c if c is None else c
        return (x, (z * 2 + y) * 2 + c)

    def z_xor(self, k):
        low = self.zl if k % 2 == 0 else 1 - self.zl
        high = self.zh if k // 2 == 0 else 1 - self.zh
        return 2 * high + low

    def slice_z(self, z=None):
        z = self.z if z is None else z
        inner = lax.rem(lax.rem(z, 2) + lax.div(z, 2), 2)
        return jnp.where(self.x == 0, 2 * inner, 3 - 2 * inner)

    def cube(self, bits):
        return self.at(
            x=1 - self.x if bits & 4 else self.x,
            y=1 - self.y if bits & 2 else self.y,
            z=self.z_xor(1) if bits & 1 else self.z,
        )


class Wires:
    def __init__(self, send, recv):
        self.send, self.recv, self.used = send, recv, 0

    def remote(self, src, dst, device):
        i = self.used
        self.used += 1
        return pltpu.make_async_remote_copy(
            src_ref=src,
            dst_ref=dst,
            send_sem=self.send.at[i],
            recv_sem=self.recv.at[i],
            device_id=device,
            device_id_type=MESH,
        )

    def local(self, src, dst):
        i = self.used
        self.used += 1
        return pltpu.make_async_copy(src, dst, self.send.at[i])


def greet(devices):
    barrier = pltpu.get_barrier_semaphore()
    for device in devices:
        pl.semaphore_signal(barrier, inc=1, device_id=device, device_id_type=MESH)
    pl.semaphore_wait(barrier, len(devices))


def hbm():
    return pl.BlockSpec(memory_space=pl.ANY)


def vmem():
    return pl.BlockSpec(memory_space=pltpu.VMEM)


def sems(count):
    return [pltpu.SemaphoreType.DMA((count,)), pltpu.SemaphoreType.DMA((count,))]


def params(collective_id):
    return pltpu.CompilerParams(
        collective_id=collective_id, has_side_effects=True, vmem_limit_bytes=VMEM_BYTES
    )


X, Y, Z = 4, 2, 1


def thirds(rows):
    first = -(-rows // 48) * 16
    return ((0, first), (first, first), (2 * first, rows - 2 * first))


def add(left, right):
    return (left.astype(F32) + right.astype(F32)).astype(BF16)


class CubeSum:
    MIDDLE = ((X, Y, Y | Z), (Y, Z, X | Z), (Z, X, X | Y))
    NEAR = ((Y, Z), (Z, X), (X, Y))

    def __init__(self, p, w, parts, third, second, first):
        self.p, self.w, self.parts = p, w, parts
        self.third, self.second, self.first = third, second, first
        self.half = parts.shape[1] // 2
        self.started = []
        self.far, self.mid, self.end = {}, {}, {}

    def push(self, src, dst, bit):
        copy = self.w.remote(src, dst, self.p.cube(bit))
        copy.start()
        self.started.append(copy)
        return copy

    def send_far(self):
        for h in range(2):
            for (start, size), link in zip(thirds(self.half), (X, Y, Z)):
                at = pl.ds(h * self.half + start, size)
                self.far[link, h] = self.push(self.parts.at[7, at], self.third.at[at], link)

    def send_middle(self):
        for h in range(2):
            for i, (link, onward, place) in enumerate(self.MIDDLE):
                start, size = thirds(self.half)[i]
                at = pl.ds(h * self.half + start, size)
                all_at = pl.ds(h * self.half, self.half)
                self.far[link, h].wait_recv()
                self.parts[place, at] = add(self.parts[place, at], self.third[at, :])
                self.mid[onward, h] = self.push(
                    self.parts.at[place, all_at], self.second.at[i, all_at], onward
                )

    def send_near(self):
        for h in range(2):
            at = pl.ds(h * self.half, self.half)
            for i, (came, place) in enumerate(self.NEAR):
                self.mid[came, h].wait_recv()
                self.parts[place, at] = add(self.parts[place, at], self.second[i, at])
                self.end[place, h] = self.push(
                    self.parts.at[place, at], self.first.at[i, at], place
                )

    def finish(self):
        for h in range(2):
            at = pl.ds(h * self.half, self.half)
            value = self.parts[0, at].astype(F32)
            for i, (_, place) in enumerate(self.NEAR):
                self.end[place, h].wait_recv()
                value = value + self.first[i, at].astype(F32)
            yield at, value

    def wait_sent(self):
        for copy in self.started:
            copy.wait_send()
        self.started = []


class LightSum(CubeSum):
    def send_far(self):
        for h, link in ((0, X), (1, Y)):
            at = pl.ds(h * self.half, self.half)
            self.far[link, h] = self.push(self.parts.at[7, at], self.third.at[at], link)

    def send_middle(self):
        for h, link, place in ((0, X, Y | Z), (1, Y, X | Z)):
            at = pl.ds(h * self.half, self.half)
            self.far[link, h].wait_recv()
            self.parts[place, at] = add(self.parts[place, at], self.third[at, :])
        for h in range(2):
            at = pl.ds(h * self.half, self.half)
            for i, (link, place) in enumerate(((X, X | Z), (Y, Y | Z))):
                self.mid[link, h] = self.push(self.parts.at[place, at], self.second.at[i, at], link)
            link = (X, Y)[h]
            self.mid[X | Y, h] = self.push(self.parts.at[X | Y, at], self.second.at[2, at], link)

    def send_near(self):
        for h in range(2):
            at = pl.ds(h * self.half, self.half)
            self.mid[X, h].wait_recv()
            self.mid[Y, h].wait_recv()
            total = self.second[0, at].astype(F32) + self.second[1, at].astype(F32)
            self.parts[Z, at] = add(self.parts[Z, at], total)
            self.end[Z, h] = self.push(self.parts.at[Z, at], self.first.at[0, at], Z)
            self.mid[X | Y, h].wait_recv()
            place = (Y, X)[h]
            self.parts[place, at] = add(self.parts[place, at], self.second[2, at])
            for i, bit in ((1, X), (2, Y)):
                self.end[bit, h] = self.push(self.parts.at[bit, at], self.first.at[i, at], bit)


class CubeGather:
    def __init__(self, p, w, block, every):
        self.p, self.w, self.block, self.every = p, w, block, every
        self.half = block.shape[0] // 2
        self.started = []
        self.near, self.middle, self.far = {}, {}, {}

    def push(self, src, dst, bit):
        copy = self.w.remote(src, dst, self.p.cube(bit))
        copy.start()
        self.started.append(copy)
        return copy

    def send_near(self, h):
        at = pl.ds(h * self.half, self.half)
        for bit in (X, Y, Z):
            self.near[bit, h] = self.push(self.block.at[at], self.every.at[bit, at], bit)

    def send_middle(self, h):
        at = pl.ds(h * self.half, self.half)
        for link, relay in ((X, Y), (Y, Z), (Z, X)):
            self.near[relay, h].wait_recv()
            self.middle[link | relay, h] = self.push(
                self.every.at[relay, at], self.every.at[link | relay, at], link
            )

    def send_far(self, h):
        for (start, size), link, relay in zip(thirds(self.half), (X, Y, Z), (Y | Z, X | Z, X | Y)):
            at = pl.ds(h * self.half + start, size)
            self.middle[relay, h].wait_recv()
            self.far[link, h] = self.push(self.every.at[relay, at], self.every.at[7, at], link)

    def wait_far(self):
        for copy in self.far.values():
            copy.wait_recv()

    def wait_sent(self):
        for copy in self.started:
            copy.wait_send()
        self.started = []


def norm_scale(values):
    return lax.rsqrt(jnp.mean(values * values, axis=-1, keepdims=True) + EPS)


def norm_pull(values, scale, gain, cotangent):
    weighted = gain * cotangent
    lean = jnp.mean(values * weighted, axis=-1, keepdims=True)
    d_values = scale * weighted - values * (scale * scale * scale * lean)
    return d_values, jnp.sum(values * scale * cotangent, axis=0, keepdims=True)


def spread_matrix(width, per):
    column = lax.broadcasted_iota(jnp.int32, (128, width), 1)
    row = lax.broadcasted_iota(jnp.int32, (128, width), 0)
    place = (lax.rem(column, per) == row).astype(F32)
    column = lax.broadcasted_iota(jnp.int32, (16, width), 1)
    row = lax.broadcasted_iota(jnp.int32, (16, width), 0)
    owner = (lax.div(column, per) == row).astype(F32)
    return place, owner


def join_gains(packed, which, width, per):
    place, owner = spread_matrix(width, per)
    shards = packed[:, which, :].astype(BF16)
    wide = jnp.dot(shards, place.astype(BF16), preferred_element_type=F32)
    return jnp.sum(wide * owner, axis=0, keepdims=True)


def turn(values, cosine, sine):
    half = values.shape[-1] // 2
    u, w = values[:, :half], values[:, half:]
    return jnp.concatenate([u * cosine - w * sine, w * cosine + u * sine], axis=1)


def turn_back(values, cosine, sine):
    half = values.shape[-1] // 2
    u, w = values[:, :half], values[:, half:]
    return jnp.concatenate([u * cosine + w * sine, w * cosine - u * sine], axis=1)


def front_kernel(
    tok, seg_row, w_q, w_k, w_v, w_o, g_apre, g_apost, g_mpre, g_mpost, g_q, g_k, w_gate, w_up, w_down,
    qkv_w, out_w, gu_w, dn_w, every, gains_full, a_low, qk_proj, q_low, k_low, v_low,
    probs, o_low, attn_proj, h_mid, tables,
    qkv_s, qkv_own, qkv_send, qkv_got, out_own, gains_own, gains_s, wide_in, wide_send, wide_got,
    wide_out, down_in, down_out, m_low, out_s, send, recv, local,
):
    p = Place()
    w = Wires(send, recv)
    x, y, z, c, zl, zh = p.x, p.y, p.z, p.c, p.zl, p.zh
    sibling = p.at(c=1 - c)
    plane = [p.at(x=1 - x), p.at(y=1 - y)]
    lines = [p.at(y=yy, z=p.z_xor(k)) for yy in (y, 1 - y) for k in range(1, 4)]
    started = []

    def push(src, dst, device):
        copy = w.remote(src, dst, device)
        copy.start()
        started.append(copy)
        return copy

    loads = [
        pltpu.make_async_copy(w_gate, wide_in.at[0], local.at[0]),
        pltpu.make_async_copy(w_up, wide_in.at[1], local.at[1]),
        pltpu.make_async_copy(w_down, down_in, local.at[2]),
    ]
    for copy in loads:
        copy.start()

    rows = w_q.shape[0]
    columns = qkv_s.shape[1] // 4
    out_rows = w_o.shape[0] // 2
    mine = 2 * x + c
    theirs = 2 * x + 1 - c

    all_own = jnp.concatenate([w_q[...], w_k[...], w_v[...]], axis=1)
    for quarter in range(4):
        qkv_own[quarter] = all_own[:, quarter * columns : (quarter + 1) * columns]
    qkv_send[...] = qkv_own[theirs].astype(BF16)
    out_own[...] = w_o[...].astype(BF16)
    gains_own[...] = jnp.zeros_like(gains_own)
    for i, gain in enumerate((g_apre, g_apost, g_mpre, g_mpost, g_q, g_k)):
        gains_own[i, : gain.shape[0]] = gain[...].astype(BF16).astype(F32)
    across = p.at(x=1 - x, z=p.z_xor(3))
    greet([sibling, across] + plane + lines)

    def qkv_at(zz, yy, quarter):
        return qkv_s.at[
            pl.ds(pl.multiple_of((2 * zz + yy) * 2 * rows, 16), 2 * rows),
            pl.ds(pl.multiple_of(quarter * columns, 128), columns),
        ]

    def out_at(zz, yy, quarter):
        return out_s.at[
            pl.ds(pl.multiple_of((2 * zz + yy) * 4 * out_rows + quarter * out_rows, 16), out_rows)
        ]

    swap = push(qkv_send, qkv_got, sibling)

    def gains_at(zz, yy, cc):
        return gains_s.at[(2 * zz + yy) * 2 + cc]

    gains_s[(2 * z + y) * 2 + c] = gains_own[...]
    gain_line = [push(gains_own, gains_at(z, y, c), p.at(z=p.z_xor(k))) for k in range(1, 4)]
    gain_side = [push(gains_own, gains_at(z, y, c), plane[1])]
    holds = x == c
    out_theirs = out_own.at[pl.ds(pl.multiple_of((1 - c) * out_rows, 16), out_rows)]
    out_swap = w.remote(out_theirs, out_at(z, y, theirs), sibling)
    pl.when(holds)(out_swap.start)

    @pl.when(holds)
    def _():
        out_s[pl.ds(pl.multiple_of((2 * z + y) * 4 * out_rows + mine * out_rows, 16), out_rows)] = (
            out_own[pl.ds(pl.multiple_of(c * out_rows, 16), out_rows)]
        )

    swap.wait_recv()
    top, low = qkv_own[mine], qkv_got[...].astype(F32)
    first = jnp.where(c == 0, top, low)
    second = jnp.where(c == 0, low, top)
    base = pl.multiple_of((2 * z + y) * 2 * rows, 16)
    joined = jnp.concatenate([first, second], axis=0).astype(BF16)
    qkv_s[pl.ds(base, 2 * rows), pl.ds(pl.multiple_of(mine * columns, 128), columns)] = joined

    pl.when(jnp.logical_not(holds))(out_swap.wait_recv)
    pl.when(holds)(out_swap.wait_send)

    line = [None]
    for k in range(1, 4):
        to = p.at(z=p.z_xor(k))
        line.append(
            (
                push(qkv_at(z, y, mine), qkv_at(z, y, mine), to),
                push(out_at(z, y, mine), out_at(z, y, mine), to),
            )
        )
    side_x, side_y, corner = {}, {}, {}

    def spread(k):
        zz = p.z_xor(k)
        if k:
            for copy in line[k]:
                copy.wait_recv()
        qkv, out = qkv_at(zz, y, mine), out_at(zz, y, mine)
        side_x[k] = (push(qkv, qkv, plane[0]), push(out, out, plane[0]))
        side_y[k] = (push(qkv, qkv, plane[1]), push(out, out, plane[1]))

    def relay(k):
        zz = p.z_xor(k)
        if k % 2:
            for copy in side_y[k]:
                copy.wait_recv()
            qkv, out, to = qkv_at(zz, 1 - y, mine), out_at(zz, 1 - y, mine), plane[0]
        else:
            for copy in side_x[k]:
                copy.wait_recv()
            other = 2 * (1 - x) + c
            qkv, out, to = qkv_at(zz, y, other), out_at(zz, y, other), plane[1]
        corner[k] = (push(qkv, qkv, to), push(out, out, to))

    pairs = []

    def share(k):
        zz = p.z_xor(k)
        for copy in (side_x[k] if k % 2 else side_y[k]) + corner[k]:
            copy.wait_recv()
        for xx in range(2):
            at = qkv_s.at[
                pl.ds(pl.multiple_of(2 * zz * 2 * rows, 16), 4 * rows),
                pl.ds(pl.multiple_of((2 * xx + c) * columns, 128), columns),
            ]
            pairs.append(push(at, at, sibling))
            for yy in range(2):
                at = out_at(zz, yy, 2 * xx + c)
                pairs.append(push(at, at, sibling))

    spread(0)
    loads[0].wait()
    loads[1].wait()
    part_columns = wide_out.shape[-1]
    for xx in range(2):

        @pl.when(x == xx)
        def _():
            for zz in range(2):
                for yy in range(2):
                    part = (3 - 2 * zz if xx else 2 * zz) * 2 + yy
                    at = slice(part * part_columns, (part + 1) * part_columns)
                    for matrix in range(2):

                        @pl.when(c == 1 - matrix)
                        def _():
                            wide_send[2 * zz + yy] = wide_in[matrix, :, at].astype(BF16)

    wide_swap = push(wide_send, wide_got, sibling)
    loads[2].wait()
    down_out[...] = down_in[...].astype(BF16)
    relay(0)
    spread(1)
    wide_swap.wait_recv()
    for xx in range(2):

        @pl.when(x == xx)
        def _():
            for zz in range(2):
                for yy in range(2):
                    part = (3 - 2 * zz if xx else 2 * zz) * 2 + yy
                    at = slice(part * part_columns, (part + 1) * part_columns)
                    got = wide_got[2 * zz + yy].astype(F32)
                    for matrix in range(2):

                        @pl.when(c == matrix)
                        def _():
                            own = wide_in[matrix, :, at]
                            both = [own, got] if matrix == 0 else [got, own]
                            wide_out[2 * zz + yy] = jnp.concatenate(both, axis=0).astype(BF16)

    def gu_at(zz, yy):
        return gu_w.at[c, pl.ds(pl.multiple_of((2 * zz + yy) * 2 * rows, 16), 2 * rows)]

    down_rows = down_out.shape[0]
    down_at = dn_w.at[pl.ds(pl.multiple_of(c * down_rows, 16), down_rows)]
    down_local = p.slice_z() == z
    down_sends = lax.rem(zl + c, 2) == x
    down_copy = w.remote(down_out, down_at, p.at(x=zl, z=p.z_xor(3)))
    pl.when(down_sends)(down_copy.start)
    own_down = pltpu.make_async_copy(down_out, down_at, local.at[1])
    pl.when(down_local)(own_down.start)

    wide = []
    for k in range(4):
        for other in range(2):
            yy = 1 - y if other else y
            zz = p.z_xor(k)
            inner = lax.rem(lax.rem(zz, 2) + lax.div(zz, 2), 2)
            src = wide_out.at[2 * inner + yy]
            if k == 0 and other == 0:
                own_wide = pltpu.make_async_copy(src, gu_at(z, y), local.at[0])
                own_wide.start()
            else:
                wide.append((zz, yy, push(src, gu_at(z, y), p.at(y=yy, z=zz))))

    tok_f = tok[...].astype(F32)
    length, width = tok_f.shape
    head = k_low.shape[1]
    spread(2)
    relay(1)
    for copy in gain_line:
        copy.wait_recv()
    for k in range(1, 4):
        zz = p.z_xor(k)
        gain_side.append(push(gains_at(zz, y, c), gains_at(zz, y, c), plane[1]))
    row_seg = seg_row[...].astype(F32)
    i_at = lax.broadcasted_iota(jnp.int32, (length, length), 0)
    j_at = lax.broadcasted_iota(jnp.int32, (length, length), 1)
    col_seg = jnp.sum(jnp.where(i_at == j_at, row_seg, 0.0), axis=1, keepdims=True)
    earlier = jnp.sum((row_seg < col_seg).astype(F32), axis=1, keepdims=True)
    index = lax.broadcasted_iota(jnp.int32, (length, 1), 0).astype(F32)
    rate_at = lax.broadcasted_iota(jnp.int32, (1, head // 2), 1).astype(F32)
    rates = jnp.exp(rate_at * (-2.0 * math.log(THETA) / head))
    angles = (index - earlier) * rates
    tables[0] = jnp.cos(angles)
    tables[1] = jnp.sin(angles)
    spread(3)
    relay(2)
    share(0)
    relay(3)
    for copy in gain_side:
        copy.wait_recv()
    gain_pair = []
    for zz in range(4):
        for yy in range(2):
            gain_pair.append(push(gains_at(zz, yy, c), gains_at(zz, yy, c), sibling))
    share(1)
    for copy in gain_pair:
        copy.wait_recv()
    packed = gains_s[...]
    for i, (size, per) in enumerate(
        ((width, rows),) * 4 + ((head, head // 16),) * 2
    ):
        gains_full[i, :, :size] = join_gains(packed, i, size, per)
    a_low[...] = (tok_f * norm_scale(tok_f) * gains_full[0]).astype(BF16)
    share(2)
    share(3)
    for copy in pairs:
        copy.wait_recv()
    saves = [
        pltpu.make_async_copy(qkv_s, qkv_w, local.at[2]),
        pltpu.make_async_copy(out_s, out_w, local.at[3]),
    ]
    for copy in saves:
        copy.start()

    cosine, sine = tables[0], tables[1]
    heads = q_low.shape[1] // head
    for i in range(heads + 2):
        at = slice(i * head, (i + 1) * head)
        value = jnp.dot(a_low[...], qkv_s[:, at], preferred_element_type=F32)
        if i < heads:
            qk_proj[:, at] = value
            q_low[:, at] = turn(
                value * norm_scale(value) * gains_full[4, :, :head], cosine, sine
            ).astype(BF16)
        elif i == heads:
            qk_proj[:, at] = value
            k_low[...] = turn(
                value * norm_scale(value) * gains_full[5, :, :head], cosine, sine
            ).astype(BF16)
        else:
            v_low[...] = value.astype(BF16)
    allowed = (row_seg == col_seg) & (j_at <= i_at)
    for i in range(heads):
        at = slice(i * head, (i + 1) * head)
        scores = SCALE * lax.dot_general(
            q_low[:, at], k_low[...], (((1,), (1,)), ((), ())), preferred_element_type=F32
        )
        scores = jnp.where(allowed, scores, MASKED)
        expo = jnp.exp(scores - jnp.max(scores, axis=1, keepdims=True))
        prob = expo / jnp.sum(expo, axis=1, keepdims=True)
        probs[i] = prob
        o_low[:, at] = jnp.dot(
            prob.astype(BF16), v_low[...], preferred_element_type=F32
        ).astype(BF16)
    third = width // 3
    for i in range(3):
        at = slice(i * third, (i + 1) * third)
        attn_proj[:, at] = jnp.dot(o_low[...], out_s[:, at], preferred_element_type=F32)
    proj = attn_proj[...]
    mid = tok_f + proj * norm_scale(proj) * gains_full[1]
    h_mid[...] = mid
    m_low[...] = (mid * norm_scale(mid) * gains_full[2]).astype(BF16)

    gather = CubeGather(p, w, m_low, every)
    own = pltpu.make_async_copy(m_low, every.at[0], local.at[4])
    own.start()
    gather.send_near(0)
    gather.send_near(1)
    own_wide.wait()
    shared = [push(gu_at(z, y), gu_at(z, y), sibling)]
    gather.send_middle(0)
    gather.send_middle(1)
    gather.send_far(0)
    gather.send_far(1)
    for zz, yy, copy in reversed(wide):
        copy.wait_recv()
        shared.append(push(gu_at(zz, yy), gu_at(zz, yy), sibling))
    pl.when(down_local)(own_down.wait)
    pl.when(jnp.logical_not(down_local))(down_copy.wait_recv)
    shared.append(push(down_at, down_at, sibling))
    gather.wait_far()
    own.wait()
    gather.wait_sent()
    for copy in shared:
        copy.wait_recv()
    for copy in saves:
        copy.wait()
    pl.when(down_sends)(down_copy.wait_send)
    for copy in started:
        copy.wait_send()


def front(tok, segments, w_q, w_k, w_v, w_o, gains, w_gate, w_up, w_down, head):
    length, width = tok.shape
    rows, mix = w_q.shape
    hidden = w_gate.shape[1]
    part = hidden // 8
    down_rows = w_down.shape[0]
    total = mix + 2 * head
    heads = mix // head
    columns = total // 4
    struct = jax.ShapeDtypeStruct
    shapes = (
        struct((16 * rows, total), BF16),
        struct((16 * w_o.shape[0], width), BF16),
        struct((2, 16 * rows, part), BF16),
        struct((2 * down_rows, width), BF16),
        struct((8, length, width), BF16),
        struct((8, 1, width), F32),
        struct((length, width), BF16),
        struct((length, mix + head), F32),
        struct((length, mix), BF16),
        struct((length, head), BF16),
        struct((length, head), BF16),
        struct((heads, length, length), F32),
        struct((length, mix), BF16),
        struct((length, width), F32),
        struct((length, width), F32),
        struct((2, length, head // 2), F32),
    )
    scratch = [
        pltpu.VMEM((16 * rows, total), BF16),
        pltpu.VMEM((4, rows, columns), F32),
        pltpu.VMEM((rows, columns), BF16),
        pltpu.VMEM((rows, columns), BF16),
        pltpu.VMEM(w_o.shape, BF16),
        pltpu.VMEM((8, 128), F32),
        pltpu.VMEM((16, 8, 128), F32),
        pltpu.VMEM((2, rows, hidden), F32),
        pltpu.VMEM((4, rows, part), BF16),
        pltpu.VMEM((4, rows, part), BF16),
        pltpu.VMEM((4, 2 * rows, part), BF16),
        pltpu.VMEM((down_rows, width), F32),
        pltpu.VMEM((down_rows, width), BF16),
        pltpu.VMEM((length, width), BF16),
        pltpu.VMEM((16 * w_o.shape[0], width), BF16),
    ]
    return pl.pallas_call(
        front_kernel,
        out_shape=shapes,
        in_specs=[vmem()] * 12 + [hbm()] * 3,
        out_specs=(hbm(),) * 5 + (vmem(),) * 11,
        scratch_shapes=scratch + sems(128) + [pltpu.SemaphoreType.DMA((5,))],
        compiler_params=params(0),
        name="front",
    )(
        tok, segments, w_q, w_k, w_v, w_o, *gains, w_gate, w_up, w_down
    )


def dot_rows(left, right):
    return lax.dot_general(left, right, (((0,), (0,)), ((), ())), preferred_element_type=F32)


def dot_columns(left, right):
    return lax.dot_general(left, right, (((1,), (1,)), ((), ())), preferred_element_type=F32)


GELU_ROOT = math.sqrt(2.0 / math.pi)


def gelu_parts(gate):
    square = gate * gate
    bend = jnp.tanh(GELU_ROOT * gate * (1.0 + 0.044715 * square))
    half = 0.5 * (1.0 + bend)
    slope = half + 0.5 * gate * (1.0 - bend * bend) * GELU_ROOT * (1.0 + 3 * 0.044715 * square)
    return half * gate, slope


def tiles(size, step):
    return [slice(at, min(at + step, size)) for at in range(0, size, step)]


def tail_kernel(
    tok, d_out, h_mid, gains_full, every, gu, dn, proj_h, o_h, out_h, v_h, probs_h, k_h, q_h, qk_h,
    tables_h, a_h, qkv_h,
    layer_out, grad_x, qe, oe, gains_sum, wide_end, wide_back, down_end,
    dd_own, dd_all, third, second, first, wide_got, wide_sum, wide_far, down_got, down_sum, down_far,
    down_via, d_mid, q1, o1, qa, oa, qb, ob, qc, oc, gain_acc, gain_got, send, recv, local,
):
    p = Place()
    w = Wires(send, recv)
    x, y, z, c, zl, zh = p.x, p.y, p.z, p.c, p.zl, p.zh
    sibling = p.at(c=1 - c)
    plane = [p.at(x=1 - x), p.at(y=1 - y)]
    line = [p.at(z=p.z_xor(k)) for k in range(1, 4)]
    started = []

    def push(src, dst, device):
        copy = w.remote(src, dst, device)
        copy.start()
        started.append(copy)
        return copy

    def rows_of(ref, start, size):
        return ref.at[pl.ds(pl.multiple_of(start, 16), size)]

    chip_rows = wide_sum.shape[0] // 8
    half_rows = 4 * chip_rows
    far_half = half_rows * (1 - zh)
    near_half = half_rows * zh

    pieces = (0, 1, 2, 3)
    order = (3, 1, 2, 0)

    def piece(i, zl):
        to_z = 1 - zl if i // 2 else zl
        to_y = 1 - y if i % 2 else y
        return (2 * to_z + to_y) * chip_rows

    crossing = w.used
    w.used += 5

    def cross(i, src, dst):
        return pltpu.make_async_remote_copy(
            src_ref=src,
            dst_ref=dst,
            send_sem=send.at[crossing + i],
            recv_sem=recv.at[crossing + i],
            device_id=line[2],
            device_id_type=MESH,
        )

    def wide_two(i):
        return cross(
            i,
            rows_of(wide_sum, far_half + piece(i, 1 - zl), chip_rows),
            wide_far.at[pl.ds(i * chip_rows, chip_rows)],
        )

    def down_over():
        return cross(4, down_sum, down_far)

    mine = p.slice_z() == z

    def feed_forward(m_all, wide_w, down_w, wide, hidden, parts):
        blocks = (7, 3, 5, 6, 4, 2, 1, 0)
        loads = {r: pltpu.make_async_copy(every.at[r], m_all.at[r], local.at[r]) for r in blocks}
        wide_load = pltpu.make_async_copy(gu, wide_w, local.at[8])
        down_load = pltpu.make_async_copy(dn, down_w, local.at[9])
        wide_load.start()
        loads[7].start()
        down_load.start()
        for r in blocks[1:]:
            loads[r].start()
        greet([sibling] + plane + line + [p.cube(3), p.cube(5)])
        length, width = m_all.shape[1:]
        part = wide.shape[-1]
        wide_tiles = tiles(part, 256)
        down_tiles = tiles(width, 384)

        def forward(r):
            for at in wide_tiles:
                g = jnp.dot(m_all[r], wide_w[0, :, at], preferred_element_type=F32)
                u = jnp.dot(m_all[r], wide_w[1, :, at], preferred_element_type=F32)
                wide[0, r, :, at] = g.astype(BF16)
                wide[1, r, :, at] = u.astype(BF16)
                value, _ = gelu_parts(g)
                hidden[r, :, at] = (value * u).astype(BF16)
            for at in down_tiles:
                parts[r, :, at] = jnp.dot(
                    hidden[r], down_w[:, at], preferred_element_type=F32
                ).astype(BF16)

        def backward(r):
            for at in wide_tiles:
                d_hidden = dot_columns(dd_all[r], down_w[at, :])
                value, slope = gelu_parts(wide[0, r, :, at].astype(F32))
                up = wide[1, r, :, at].astype(F32)
                wide[0, r, :, at] = (d_hidden * up * slope).astype(BF16)
                wide[1, r, :, at] = (d_hidden * value).astype(BF16)
            d_gate = wide[0, r]
            d_up = wide[1, r]
            for at in down_tiles:
                parts[r, :, at] = (
                    dot_columns(d_gate, wide_w[0, at, :]) + dot_columns(d_up, wide_w[1, at, :])
                ).astype(BF16)

        def several(step, places):
            lax.fori_loop(0, 3, lambda i, _: (step(places(i)), 0)[1], 0)

        def middles(i):
            return 7 - lax.shift_right_logical(jnp.int32(4), i)

        def nears(i):
            return lax.shift_right_logical(jnp.int32(4), i)

        total = CubeSum(p, w, parts, third, second, first)
        wide_load.wait()
        loads[7].wait()
        down_load.wait()
        forward(7)
        total.send_far()
        for r in blocks[1:]:
            loads[r].wait()
        several(forward, middles)
        total.send_middle()
        several(forward, nears)
        total.send_near()
        forward(0)

        gather = CubeGather(p, w, dd_own, dd_all)
        gain = gains_full[3]
        g_rows = 0.0
        for h, (at, value) in enumerate(total.finish()):
            scale = norm_scale(value)
            layer_out[at, :] = (h_mid[at, :] + value * scale * gain).astype(BF16)
            d_value, g_part = norm_pull(value, scale, gain, d_out[at, :].astype(F32))
            dd_own[at, :] = d_value.astype(BF16)
            g_rows = g_rows + g_part
            gather.send_near(h)
        gain_acc[0, 3:4, :] = g_rows
        dd_all[0] = dd_own[...]
        total.wait_sent()
        backward(0)
        gather.send_middle(0)
        gather.send_middle(1)
        several(backward, nears)
        gather.send_far(0)
        gather.send_far(1)
        several(backward, middles)
        gather.wait_far()
        backward(7)

        total = LightSum(p, w, parts, third, second, first)
        total.send_far()
        grad_rows = 384
        all_rows = 8 * length
        for at in down_tiles:
            down_w[:, at] = dot_rows(
                hidden[...].reshape(all_rows, part), dd_all[:, :, at].reshape(all_rows, -1)
            ).astype(BF16)
        down_rows = down_sum.shape[0]
        down_one = w.remote(rows_of(down_w, (1 - c) * down_rows, down_rows), down_got, sibling)
        down_one.start()
        total.send_middle()
        down_one.wait_recv()
        down_sum[...] = add(down_w[pl.ds(pl.multiple_of(c * down_rows, 16), down_rows), :], down_got[...])
        pl.when(jnp.logical_not(mine))(down_over().start)

        def grad_wide(matrix, out):
            def step(i, _):
                at = pl.ds(pl.multiple_of(i * grad_rows, 128), grad_rows)
                left = m_all[:, :, at].reshape(all_rows, grad_rows)
                out[at, :] = dot_rows(left, wide[matrix].reshape(all_rows, part)).astype(BF16)
                return 0

            lax.fori_loop(0, width // grad_rows, step, 0)

        other = wide_w.at[1 - c]
        grad_wide(1 - c, other)
        wide_one = w.remote(other, wide_got, sibling)
        wide_one.start()
        grad_wide(c, wide_sum)
        wide_one.wait_recv()
        wide_sum[...] = add(wide_sum[...], wide_got[...])
        total.send_near()
        wide_two(0).start()
        wide_two(1).start()
        g_rows = 0.0
        for at, value in total.finish():
            mid = h_mid[at, :]
            d_value, g_part = norm_pull(mid, norm_scale(mid), gains_full[2], value)
            d_mid[at, :] = d_out[at, :].astype(F32) + d_value
            g_rows = g_rows + g_part
        gain_acc[0, 2:3, :] = g_rows
        down_one.wait_send()
        wide_one.wait_send()
        total.wait_sent()
        gather.wait_sent()

    def attention(
        proj, o_low, out_w, v_low, probs, k_low, q_low, qk_proj, tables, a_low, qkv_w,
        d_input, wide_swap, d_attn, d_mix, d_qkv, dqkv, dout, qa_s, oa_s, qb_s, ob_s, qc_s, oc_s,
    ):
        loads = [
            pltpu.make_async_copy(src, dst, local.at[i])
            for i, (src, dst) in enumerate(
                zip(
                    (proj_h, o_h, out_h, v_h, probs_h, k_h, q_h, qk_h, tables_h, a_h, qkv_h),
                    (proj, o_low, out_w, v_low, probs, k_low, q_low, qk_proj, tables, a_low, qkv_w),
                )
            )
        ]
        for copy in loads:
            copy.start()
        down_rows = down_end.shape[0]
        split = down_rows // 32 * 16
        lower, upper = pl.ds(0, split), pl.ds(split, down_rows - split)
        down_copy = w.remote(down_end.at[lower], down_end.at[lower], plane[0])
        down_around = w.remote(down_end.at[upper], down_via, p.cube(5))
        down_relay = w.remote(down_via, down_end.at[upper], line[0])

        @pl.when(mine)
        def _():
            down_over().wait_recv()
            down_end[...] = add(down_sum[...], down_far[...])
            down_copy.start()
            down_around.start()

        loads[0].wait()
        value = proj[...]
        d_value, g_apost = norm_pull(value, norm_scale(value), gains_full[1], d_mid[...])
        d_attn[...] = d_value.astype(BF16)
        gain_acc[0, 1:2, :] = g_apost
        loads[1].wait()

        width = tok.shape[1]
        step = width // 3
        for i in range(3):
            at = slice(i * step, (i + 1) * step)
            dout[:, at] = dot_rows(o_low[...], d_attn[:, at]).astype(BF16)
        out_rows = dout.shape[0] // 32

        def out_at(ref, zz, yy, quarter):
            return rows_of(ref, (2 * zz + yy) * 4 * out_rows + quarter * out_rows, out_rows)

        out_one = {
            k: [
                push(
                    out_at(dout, p.z_xor(k), yy, 2 * xx + 1 - c),
                    o1.at[k, xx, yy],
                    sibling,
                )
                for yy in range(2)
                for xx in range(2)
            ]
            for k in order
        }
        loads[2].wait()
        d_mix[...] = dot_columns(d_attn[...], out_w[...]).astype(BF16)

        def y_first(k):
            return k % 2 == 1

        columns = dqkv.shape[1] // 4
        first, first_out, then, last_step = {}, {}, {}, {}

        def own_out(k, xx, yy):
            start = ((2 * p.z_xor(k) + yy) * 4 + 2 * xx + c) * out_rows
            rows = pl.ds(pl.multiple_of(start, 16), out_rows)
            return dout[rows, :].astype(F32) + o1[k, xx, yy].astype(F32)

        def own_qkv(k, xx, yy):
            start = (2 * p.z_xor(k) + yy) * chip_rows
            rows = pl.ds(pl.multiple_of(start, 16), chip_rows)
            at = pl.ds(pl.multiple_of((2 * xx + c) * columns, 128), columns)
            got = pl.ds(pl.multiple_of(yy * chip_rows, 16), chip_rows)
            return dqkv[rows, at].astype(F32) + q1[k, xx, got, :].astype(F32)

        for k in order:
            for copy in out_one[k]:
                copy.wait_recv()
            first_out[k] = []
            for j in range(2):
                if y_first(k):
                    xx, yy, to = x if j == 0 else 1 - x, 1 - y, plane[1]
                else:
                    xx, yy, to = 1 - x, y if j == 0 else 1 - y, plane[0]
                oa_s[k, j] = own_out(k, xx, yy).astype(BF16)
                first_out[k].append(push(oa_s.at[k, j], oa.at[k, j], to))

        wide_two(2).start()
        for copy in loads[3:9]:
            copy.wait()
        cosine, sine = tables[0], tables[1]
        head = k_low.shape[1]
        heads = q_low.shape[1] // head
        d_k, d_v, g_q = 0.0, 0.0, 0.0
        for i in range(heads):
            at = slice(i * head, (i + 1) * head)
            prob = probs[i]
            d_probs = dot_columns(d_mix[:, at], v_low[...])
            row_dot = jnp.sum(prob * d_probs, axis=1, keepdims=True)
            d_scores = (prob * (d_probs - row_dot)).astype(BF16)
            d_q = SCALE * jnp.dot(d_scores, k_low[...], preferred_element_type=F32)
            d_k = d_k + dot_rows(d_scores, q_low[:, at])
            d_v = d_v + dot_rows(prob.astype(BF16), d_mix[:, at])
            value = qk_proj[:, at]
            d_value, gain = norm_pull(
                value, norm_scale(value), gains_full[4, :, :head], turn_back(d_q, cosine, sine)
            )
            g_q = g_q + gain
            d_qkv[:, at] = d_value.astype(BF16)
        at = slice(heads * head, (heads + 1) * head)
        value = qk_proj[:, at]
        d_value, g_k = norm_pull(
            value, norm_scale(value), gains_full[5, :, :head], turn_back(SCALE * d_k, cosine, sine)
        )
        d_qkv[:, at] = d_value.astype(BF16)
        d_qkv[:, (heads + 1) * head :] = d_v.astype(BF16)
        gain_acc[0, 4:5, :] = jnp.zeros((1, width), F32)
        gain_acc[0, 5:8, :] = jnp.zeros((3, width), F32)
        gain_acc[0, 4:5, :head] = g_q
        gain_acc[0, 5:6, :head] = g_k
        loads[9].wait()
        for i in range(heads + 2):
            at = slice(i * head, (i + 1) * head)
            dqkv[:, at] = dot_rows(a_low[...], d_qkv[:, at]).astype(BF16)

        qkv_one = {}
        for k in order:
            rows = pl.ds(pl.multiple_of(2 * p.z_xor(k) * chip_rows, 16), 2 * chip_rows)
            qkv_one[k] = [
                push(
                    dqkv.at[
                        rows, pl.ds(pl.multiple_of((2 * xx + 1 - c) * columns, 128), columns)
                    ],
                    q1.at[k, xx],
                    sibling,
                )
                for xx in range(2)
            ]

        def plane_first(k):
            for copy in qkv_one[k]:
                copy.wait_recv()
            first[k] = []
            for j in range(2):
                qa_s[k, j] = own_qkv(k, x if j == 0 else 1 - x, 1 - y).astype(BF16)
                first[k].append(push(qa_s.at[k, j], qa.at[k, j], plane[1]))

        def plane_then(k):
            for copy in first_out[k] + first[k]:
                copy.wait_recv()
            q = own_qkv(k, 1 - x, y)
            if y_first(k):
                o, to = own_out(k, 1 - x, y), plane[0]
            else:
                o, to = own_out(k, x, 1 - y), plane[1]
            qb_s[k] = (q + qa[k, 1].astype(F32)).astype(BF16)
            ob_s[k] = (o + oa[k, 1].astype(F32)).astype(BF16)
            then[k] = [
                push(qb_s.at[k], qb.at[k], plane[0]),
                push(ob_s.at[k], ob.at[k], to),
            ]

        def plane_last(k):
            for copy in then[k]:
                copy.wait_recv()
            q, o = own_qkv(k, x, y), own_out(k, x, y)
            q = q + qa[k, 0].astype(F32) + qb[k].astype(F32)
            o = o + oa[k, 0].astype(F32) + ob[k].astype(F32)
            if k == 0:
                return q, o
            qc_s[k] = q.astype(BF16)
            oc_s[k] = o.astype(BF16)
            last_step[k] = [
                push(qc_s.at[k], qc.at[k], line[k - 1]),
                push(oc_s.at[k], oc.at[k], line[k - 1]),
            ]

        for k in order:
            plane_first(k)
        wide_two(3).start()

        wide_three, wide_four, own_wide = {}, [], []

        def part_of(i):
            return 2 * p.slice_z(2 * zh + (1 - zl if i // 2 else zl)) + (1 - y if i % 2 else y)

        def wide_on(i):
            at = pl.ds(i * chip_rows, chip_rows)
            rows = pl.ds(pl.multiple_of(near_half + piece(i, zl), 16), chip_rows)
            wide_two(i).wait_recv()
            wide_far[at, :] = add(wide_sum[rows, :], wide_far[at, :])
            dst = wide_end.at[part_of(0)]
            if i:
                wide_three[i] = push(wide_far.at[at], dst, p.cube(2 * (i % 2) + i // 2))
            else:
                own_wide.append(pltpu.make_async_copy(wide_far.at[at], dst, local.at[11]))
                own_wide[0].start()
                wide_four.append(push(wide_far.at[at], dst, plane[0]))

        def wide_over(i):
            wide_three[i].wait_recv()
            dst = wide_end.at[part_of(i)]
            wide_four.append(push(dst, dst, plane[0]))

        @pl.when(mine)
        def _():
            down_around.wait_recv()
            down_relay.start()

        wide_on(0)

        loads[10].wait()
        tok_f = tok[...].astype(F32)
        for i in range(3):
            at = slice(i * step, (i + 1) * step)
            d_input[:, at] = dot_columns(d_qkv[...], qkv_w[at, :])
        d_value, g_apre = norm_pull(tok_f, norm_scale(tok_f), gains_full[0], d_input[...])
        grad_x[...] = (d_mid[...] + d_value).astype(BF16)
        gain_acc[0, 0:1, :] = g_apre
        gain_one = push(gain_acc.at[0], gain_got.at[0], sibling)

        for k in order[:2]:
            plane_then(k)
        gain_one.wait_recv()
        gain_acc[1] = gain_acc[0] + gain_got[0]
        gain_two = push(gain_acc.at[1], gain_got.at[1], plane[0])
        wide_on(1)
        for k in order[2:]:
            plane_then(k)
        for k in order[:3]:
            plane_last(k)
        wide_on(2)
        wide_over(1)
        gain_two.wait_recv()
        gain_acc[2] = gain_acc[1] + gain_got[1]
        gain_three = push(gain_acc.at[2], gain_got.at[2], plane[1])
        q, o = plane_last(0)
        for k in order[:3]:
            for copy in last_step[k]:
                copy.wait_recv()
        qe[0] = (q + qc[1].astype(F32) + qc[2].astype(F32) + qc[3].astype(F32)).astype(BF16)
        oe[0] = (o + oc[1].astype(F32) + oc[2].astype(F32) + oc[3].astype(F32)).astype(BF16)
        last = [
            push(qe.at[0], qe.at[4 + i], device)
            for i, device in enumerate((sibling, plane[0]))
        ] + [
            push(oe.at[0], oe.at[4 + i], device)
            for i, device in enumerate((sibling, plane[0]))
        ]
        wide_on(3)
        wide_over(2)
        gain_three.wait_recv()
        gain_acc[3] = gain_acc[2] + gain_got[2]
        gain_four = [push(gain_acc.at[3], gain_got.at[2 + k], line[k - 1]) for k in range(1, 4)]
        for copy in last:
            copy.wait_recv()
        relay = [push(qe.at[5], qe.at[6], sibling), push(oe.at[5], oe.at[6], sibling)]

        wide_over(3)
        for copy in relay:
            copy.wait_recv()
        rows = chip_rows // 2
        for copy in gain_four:
            copy.wait_recv()
        gains_sum[...] = gain_acc[3] + gain_got[3] + gain_got[4] + gain_got[5]

        own_wide[0].wait()
        for copy in wide_four:
            copy.wait_recv()
        for cc in range(2):

            @pl.when(c == cc)
            def _():
                for s in range(8):
                    extra = (rows + 15) // 16 * 16
                    at = slice(0, extra) if cc == 1 else slice(2 * rows - extra, 2 * rows)
                    wide_swap[s] = wide_end[s, at, :]

        final = push(wide_swap, wide_back, sibling)

        @pl.when(jnp.logical_not(mine))
        def _():
            down_copy.wait_recv()
            down_relay.wait_recv()

        final.wait_recv()

        @pl.when(mine)
        def _():
            for copy in (down_copy, down_around, down_relay):
                copy.wait_send()

        pl.when(jnp.logical_not(mine))(down_over().wait_send)
        for i in pieces:
            wide_two(i).wait_send()
        for copy in started:
            copy.wait_send()


    length, width = tok.shape
    blocks = (8, length, width)
    part = wide_sum.shape[1]
    pl.run_scoped(
        feed_forward,
        pltpu.VMEM(blocks, BF16),
        pltpu.VMEM(gu.shape, BF16),
        pltpu.VMEM(dn.shape, BF16),
        pltpu.VMEM((2, 8, length, part), BF16),
        pltpu.VMEM((8, length, part), BF16),
        pltpu.VMEM(blocks, BF16),
    )
    total = qkv_h.shape[1]
    mix = o_h.shape[1]
    q_piece, o_piece = qa.shape[2:], oa.shape[2:]
    saved = (proj_h, o_h, out_h, v_h, probs_h, k_h, q_h, qk_h, tables_h, a_h, qkv_h)
    pl.run_scoped(
        attention,
        *[pltpu.VMEM(ref.shape, ref.dtype) for ref in saved],
        pltpu.VMEM((length, width), F32),
        pltpu.VMEM(wide_back.shape, BF16),
        pltpu.VMEM((length, width), BF16),
        pltpu.VMEM((length, mix), BF16),
        pltpu.VMEM((length, total), BF16),
        pltpu.VMEM((width, total), BF16),
        pltpu.VMEM((mix, width), BF16),
        pltpu.VMEM((4, 2) + q_piece, BF16),
        pltpu.VMEM((4, 2) + o_piece, BF16),
        pltpu.VMEM((4,) + q_piece, BF16),
        pltpu.VMEM((4,) + o_piece, BF16),
        pltpu.VMEM((4,) + q_piece, BF16),
        pltpu.VMEM((4,) + o_piece, BF16),
    )


def tail(tok, d_out, h_mid, gains_full, every, gu, dn, saved):
    length, width = tok.shape
    part = dn.shape[0]
    proj, o_low, out_w, *_, qkv_w = saved
    columns = qkv_w.shape[1] // 4
    mix = out_w.shape[0]
    chip_rows = width // 8
    rows = chip_rows // 2
    extra = (rows + 15) // 16 * 16
    piece = mix // 32
    blocks = (8, length, width)
    struct = jax.ShapeDtypeStruct
    shapes = (
        struct((length, width), BF16),
        struct((length, width), BF16),
        struct((7, chip_rows, columns), BF16),
        struct((7, piece, width), BF16),
        struct((8, width), F32),
        struct((8, chip_rows, part), BF16),
        struct((8, extra, part), BF16),
        struct((part // 2, width), BF16),
    )
    scratch = [
        pltpu.VMEM((length, width), BF16),
        pltpu.VMEM(blocks, BF16),
        pltpu.VMEM((length, width), BF16),
        pltpu.VMEM((3, length, width), BF16),
        pltpu.VMEM((3, length, width), BF16),
        pltpu.VMEM((width, part), BF16),
        pltpu.VMEM((width, part), BF16),
        pltpu.VMEM((width // 2, part), BF16),
        pltpu.VMEM((part // 2, width), BF16),
        pltpu.VMEM((part // 2, width), BF16),
        pltpu.VMEM((part // 2, width), BF16),
        pltpu.VMEM((part // 2 - part // 64 * 16, width), BF16),
        pltpu.VMEM((length, width), F32),
        pltpu.VMEM((4, 2, 2 * chip_rows, columns), BF16),
        pltpu.VMEM((4, 2, 2, piece, width), BF16),
        pltpu.VMEM((4, 2, chip_rows, columns), BF16),
        pltpu.VMEM((4, 2, piece, width), BF16),
        pltpu.VMEM((4, chip_rows, columns), BF16),
        pltpu.VMEM((4, piece, width), BF16),
        pltpu.VMEM((4, chip_rows, columns), BF16),
        pltpu.VMEM((4, piece, width), BF16),
        pltpu.VMEM((4, 8, width), F32),
        pltpu.VMEM((6, 8, width), F32),
    ]
    return pl.pallas_call(
        tail_kernel,
        out_shape=shapes,
        in_specs=[vmem()] * 4 + [hbm()] * 14,
        out_specs=(vmem(),) * 8,
        scratch_shapes=scratch + sems(160) + [pltpu.SemaphoreType.DMA((12,))],
        compiler_params=params(1),
        name="tail",
    )(tok, d_out, h_mid, gains_full, every, gu, dn, *saved)


def place_kernel(
    qe, oe, gains, wide_end_h, wide_back_h, down_end_h, layer_h, grad_h,
    w_q, w_k, w_v, w_o, w_gate_h, w_up_h, w_down_h, a_pre, a_post, m_pre, m_post, q_gain, k_gain,
    layer_out, grad_x,
    wide_end, wide_back, down_end, w_gate, w_up, w_down, sem,
):
    pairs = (
        (down_end_h, down_end), (wide_end_h, wide_end), (wide_back_h, wide_back),
        (layer_h, layer_out), (grad_h, grad_x),
        (w_down, w_down_h), (w_gate, w_gate_h), (w_up, w_up_h),
    )
    copies = [pltpu.make_async_copy(*pair, sem.at[i]) for i, pair in enumerate(pairs)]
    for copy in copies[:5]:
        copy.start()
    p = Place()
    rows, mix = w_q.shape
    head = w_k.shape[1]
    columns = qe.shape[2]
    piece = oe.shape[1]
    size = wide_end.shape[2]
    extra = wide_back.shape[1]

    copies[0].wait()
    w_down[...] = down_end[...].astype(F32)
    copies[5].start()
    copies[1].wait()
    copies[2].wait()
    for cc in range(2):

        @pl.when(p.c == cc)
        def _():
            own_ref, other_ref = (w_gate, w_up) if cc == 0 else (w_up, w_gate)
            for s in range(8):
                at = slice(s * size, (s + 1) * size)
                own_ref[:, at] = wide_end[s].astype(F32)[cc * rows : (cc + 1) * rows]
                other = wide_back[s].astype(F32)
                other_ref[:, at] = other[:rows] if cc == 0 else other[extra - rows :]

    copies[6].start()
    copies[7].start()

    def put_columns(start, value):
        for ref, first, width in ((w_q, 0, mix), (w_k, mix, head), (w_v, mix + head, head)):
            low, high = max(start, first), min(start + columns, first + width)
            if low < high:
                ref[:, low - first : high - first] = value[:, low - start : high - start]

    for xx in range(2):
        for cc in range(2):

            @pl.when((p.x == xx) & (p.c == cc))
            def _():
                for i, q in (
                    (0, 2 * xx + cc),
                    (4, 2 * xx + 1 - cc),
                    (5, 2 * (1 - xx) + cc),
                    (6, 2 * (1 - xx) + 1 - cc),
                ):
                    both = qe[i].astype(F32)
                    put_columns(q * columns, both[cc * rows : (cc + 1) * rows])
                    if q // 2 == cc:
                        w_o[(q % 2) * piece : (q % 2 + 1) * piece, :] = oe[i].astype(F32)

    sums = gains[...]
    for i, ref in enumerate((a_pre, a_post, m_pre, m_post, q_gain, k_gain)):
        per = ref.shape[0]
        full = 16 * per
        turned = pltpu.roll(sums[:, :full], lax.rem(full - p.shard * per, full), 1)
        ref[...] = turned[i, :per]
    for copy in copies[3:]:
        copy.wait()


def place(summed, results, shapes):
    outs = [jax.ShapeDtypeStruct(shape, F32) for shape in shapes]
    staged = [pltpu.VMEM(v.shape, v.dtype) for v in summed[3:]]
    staged += [pltpu.VMEM(shape, F32) for shape in shapes[4:7]]
    outs += [jax.ShapeDtypeStruct(v.shape, v.dtype) for v in results]
    return pl.pallas_call(
        place_kernel,
        out_shape=tuple(outs),
        in_specs=[vmem()] * 3 + [hbm()] * 5,
        out_specs=(vmem(),) * 4 + (hbm(),) * 3 + (vmem(),) * 6 + (hbm(),) * 2,
        scratch_shapes=staged + [pltpu.SemaphoreType.DMA((8,))],
        compiler_params=pltpu.CompilerParams(vmem_limit_bytes=VMEM_BYTES),
        name="place",
    )(*summed, *results)


def cube_body(
    layer_in, d_out, segments, w_q, w_k, w_v, w_o, attn_pre, attn_post, q_gain, k_gain,
    w_gate, w_up, w_down, mlp_pre, mlp_post,
):
    width = layer_in.shape[1]
    head = q_gain.shape[0] * 16
    rows, mix = w_q.shape
    gain_list = [attn_pre, attn_post, mlp_pre, mlp_post, q_gain, k_gain]
    (
        qkv_w, out_w, gu_w, down_w, m_all, gains_full, a_low, qk_proj, q_low, k_low, v_low,
        probs, o_low, attn_proj, h_mid, tables,
    ) = front(
        layer_in, segments, w_q, w_k, w_v, w_o, gain_list, w_gate, w_up, w_down, head
    )
    saved = (
        attn_proj, o_low, out_w, v_low, probs, k_low, q_low, qk_proj, tables, a_low, qkv_w,
    )
    layer_out, grad_x, *summed = tail(
        layer_in, d_out, h_mid, gains_full, m_all, gu_w, down_w, saved
    )
    matrices = [w_q, w_k, w_v, w_o, w_gate, w_up, w_down]
    grads = place(summed, (layer_out, grad_x), [v.shape for v in matrices + gain_list])
    g_apre, g_apost, g_mpre, g_mpost, g_q, g_k, layer_out, grad_x = grads[7:]
    return (
        layer_out,
        grad_x,
        *grads[:4],
        g_apre,
        g_apost,
        g_q,
        g_k,
        *grads[4:7],
        g_mpre,
        g_mpost,
    )


def solution(mesh):
    in_specs = (
        P(("replica", "fsdp"), None),
        P(("replica", "fsdp"), None),
        P(("replica", "fsdp"), None),
        P("fsdp", None),
        P("fsdp", None),
        P("fsdp", None),
        P("fsdp", None),
        P("fsdp"),
        P("fsdp"),
        P("fsdp"),
        P("fsdp"),
        P("fsdp", None),
        P("fsdp", None),
        P("fsdp", None),
        P("fsdp"),
        P("fsdp"),
    )
    out_specs = (
        P(("replica", "fsdp"), None),
        P(("replica", "fsdp"), None),
        P("fsdp", None),
        P("fsdp", None),
        P("fsdp", None),
        P("fsdp", None),
        P("fsdp"),
        P("fsdp"),
        P("fsdp"),
        P("fsdp"),
        P("fsdp", None),
        P("fsdp", None),
        P("fsdp", None),
        P("fsdp"),
        P("fsdp"),
    )
    body = cube_body if fits_cubes(mesh) else general_body
    return jax.shard_map(body, mesh=mesh, in_specs=in_specs, out_specs=out_specs, check_vma=False)
```
